32 devices in a mesh: grp: 8 (over y, x, core), rep: 4 (over z).
Axes of the slice: x: 2, y: 2, z: 4, core: 2. Of those that a mesh axis runs over, the one named last changes fastest.
Arguments:
- tokens: bfloat16 [16384, 1536], P(('grp', 'rep')), may hold values from -6 to 6
- condition: bfloat16 [64, 1536], P(('grp', 'rep')), may hold values from -6 to 6
- caption: bfloat16 [64, 128, 4096], P(('grp', 'rep')), may hold values from -6 to 6
- caption_len: int32 [64], P(('grp', 'rep')), may hold values from 16 to 128, as said below
- item_kind: int32 [64], P(('grp', 'rep')), may hold values 0 or 1
- out_cotangent: bfloat16 [16384, 1536], P(('grp', 'rep')), may hold values from -6 to 6
- norm_gains: bfloat16 [6, 1536], P(None, ('grp', 'rep')), may hold values from 0.099609375 to 1.8984375
- ada_weight: bfloat16 [1536, 6144], P(('grp', 'rep')), may hold values from -0.15625 to 0.15625
- qkv_weight: bfloat16 [1536, 4608], P(('grp', 'rep')), may hold values from -0.15625 to 0.15625
- out_weight: bfloat16 [1536, 1536], P(('grp', 'rep')), may hold values from -1.25 to 1.25
- text_weight: bfloat16 [4096, 3072], P(('grp', 'rep')), may hold values from -0.09375 to 0.09375
- gate_up_weight: bfloat16 [1536, 8192], P(('grp', 'rep')), may hold values from -0.15625 to 0.15625
- down_weight: bfloat16 [4096, 1536], P(('grp', 'rep')), may hold values from -0.1875 to 0.1875
Outputs:
- layer_out: bfloat16 [16384, 1536], P(('grp', 'rep'))
- tokens_grad: float32 [16384, 1536], P(('grp', 'rep'))
- norm_gains_grad: float32 [6, 1536], P(None, ('grp', 'rep'))
- ada_weight_grad: float32 [1536, 6144], P(('grp', 'rep'))
- qkv_weight_grad: float32 [1536, 4608], P(('grp', 'rep'))
- out_weight_grad: float32 [1536, 1536], P(('grp', 'rep'))
- text_weight_grad: float32 [4096, 3072], P(('grp', 'rep'))
- gate_up_weight_grad: float32 [1536, 8192], P(('grp', 'rep'))
- down_weight_grad: float32 [4096, 1536], P(('grp', 'rep'))
The draws below stay inside these ranges and needn't reach their ends.
Inputs may be any that keep to these rules, and one draw needn't show every extreme that they name: Slots below caption_len of an item hold its caption, the rest of its 128 slots are padding; some item uses all 128. `item_kind`: 1 marks a clip of four frames of (8) x (8) patches, 0 an image of 16 x 16 patches.
All inputs are finite; a program needn't handle non-finite values. No bound on the sum of `item_kind` on one device may be relied on, other than what follows from the above.
Results may differ from the reference program's by a relative error of at most 0.02.
Values may be sent and summed in bfloat16 or wider, within the bound.
No kernel may reach another device: no remote copies, remote signals or barrier semaphores. Data moves between devices by JAX's collectives and lax.ppermute only.
A program may use at most 384 MiB of HBM per device.

```python
import math
import jax
import jax.numpy as jnp
from jax import lax

D = 1536
HEADS = 24
HEAD_DIM = 64
FF = 4096
TEXT_DIM = 4096
TEXT = 128
SIDE = 16
SEQ = 256
ITEMS = 64
TOKENS = 16384


def draw_caption_len(key, part):
    key = jax.random.fold_in(key, 7)
    first_key, second_key = jax.random.split(key)
    lengths = jax.random.randint(first_key, (ITEMS,), max(1, TEXT // 8), TEXT + 1, dtype=jnp.int32)
    longest = jax.random.randint(second_key, (), 0, ITEMS, dtype=jnp.int32)
    return lengths.at[longest].set(TEXT)


def place_ends(entries, key, low, largest):
    extent = entries.shape
    place = [jax.random.randint(jax.random.fold_in(key, axis), (), 0, extent[axis]) for axis in range(len(extent))]
    entries = entries.at[tuple(place)].set(low)
    longest = extent.index(max(extent))
    place[longest] = (place[longest] + 1) % extent[longest]
    return entries.at[tuple(place)].set(largest)


def levels(own_key, dims, shards, smallest, high):
    def one(axis_at, blocks):
        draws = jax.random.uniform(jax.random.fold_in(jax.random.fold_in(own_key, 6), axis_at), (blocks,), jnp.float32, smallest / len(shards), high / len(shards))
        return jnp.repeat(jnp.exp(draws), dims[axis_at] // blocks).reshape((-1,) + (1,) * (len(dims) - axis_at - 1))

    level = one(*shards[0])
    for cut in shards[1:]:
        level = level * one(*cut)
    return level


def gaussian(key, shape, width, reach, cuts=(), held_as=jnp.bfloat16):
    values = jax.random.normal(key, shape, jnp.float32) * width
    if len(cuts) > 0:
        values = levels(key, shape, cuts, -0.22, 0.18) * values
    return jnp.clip(values, min=-reach, max=reach).astype(held_as)


def setup_inputs(seed: int = 0) -> dict:
    keys = jax.random.split(jax.random.key(seed), 14)
    return {
        "tokens": gaussian(keys[0], (TOKENS, D), 1.0, 6.0, ((0, 32),)),
        "condition": gaussian(keys[1], (ITEMS, D), 1.0, 6.0, ((0, 32),)),
        "caption": gaussian(keys[2], (ITEMS, TEXT, TEXT_DIM), 1.0, 6.0, ((0, 32),)),
        "caption_len": draw_caption_len(jax.random.fold_in(keys[13], 71), 0),
        "item_kind": place_ends((jax.random.randint(keys[4], (ITEMS,), 0, 8) < 1).astype(jnp.int32), jax.random.fold_in(keys[4], 1), 0, 1),
        "out_cotangent": gaussian(keys[5], (TOKENS, D), 1.0, 6.0, ((0, 32),)),
        "norm_gains": jnp.clip(1.0 + 0.18 * jax.random.normal(keys[6], (6, D), jnp.float32), 0.099609375, 1.8984375).astype(jnp.bfloat16),
        "ada_weight": gaussian(keys[7], (D, 4 * D), D ** -0.5, 0.15625, ((0, 32),)),
        "qkv_weight": gaussian(keys[8], (D, 3 * D), D ** -0.5, 0.15625, ((0, 32),)),
        "out_weight": gaussian(keys[9], (D, D), (D // 64) ** -0.5, 1.25, ((0, 32),)),
        "text_weight": gaussian(keys[10], (TEXT_DIM, 2 * D), TEXT_DIM ** -0.5, 0.09375, ((0, 32),)),
        "gate_up_weight": gaussian(keys[11], (D, 2 * FF), D ** -0.5, 0.15625, ((0, 32),)),
        "down_weight": gaussian(keys[12], (FF, D), (FF // 4) ** -0.5, 0.1875, ((0, 32),)),
    }


EPSILON = 1e-06
HIGHEST = lax.Precision.HIGHEST

@jax.custom_vjp
def low(v):
    return lax.optimization_barrier(v.astype(jnp.bfloat16)).astype(jnp.float32)

@jax.custom_vjp
def low_back(v):
    return v

def low_keep(v):
    return (low(v), None)

def low_pass(kept, grad):
    return (grad,)

def back_keep(v):
    return (v, None)

def back_low(kept, grad):
    return (low(grad),)
low.defvjp(low_keep, low_pass)
low_back.defvjp(back_keep, back_low)

def norm_rows(values, gain_row):
    return values * lax.rsqrt(lax.optimization_barrier(jnp.mean(values * values, axis=-1, keepdims=True)) + EPSILON) * gain_row

def turn_half(values):
    first_q, second, third_q, fourth = jnp.split(values, 4, axis=-1)
    return jnp.concatenate([-second, first_q, -fourth, third_q], axis=-1)

def rotate(values, cosine, sine_table):
    return values * cosine[:, None, :] + turn_half(values) * sine_table[:, None, :]

def rope_tables(item_kind):
    position = jnp.arange(SEQ, dtype=jnp.int32)
    half_side = SIDE // 2
    frame_index = position // (half_side * half_side)
    within = position % (half_side * half_side)
    row_index = jnp.where(item_kind == 1, frame_index * half_side + within // half_side, position // SIDE)
    columns = jnp.where(item_kind == 1, within % half_side, position % SIDE)
    lane_index = jnp.arange(HEAD_DIM, dtype=jnp.int32)
    quarter = HEAD_DIM // 4
    frequency = jnp.exp(-(lane_index % quarter).astype(jnp.float32) * (math.log(10000.0) / quarter))
    coordinate = jnp.where(lane_index[None, :] < 2 * quarter, row_index[:, None], columns[:, None]).astype(jnp.float32)
    angles = coordinate * frequency[None, :]
    return (jnp.cos(angles), jnp.sin(angles))

def softmax_rows(scores):
    row_max = lax.optimization_barrier(jnp.max(scores, axis=-1, keepdims=True))
    shifted = jnp.exp(scores - row_max)
    return shifted / lax.optimization_barrier(jnp.sum(shifted, axis=-1, keepdims=True))

def item_forward(token_block, condition, caption, caption_len, item_kind, weight_set):
    gains, ada_weight, qkv_weight, out_weight, text_weight, gate_up_weight, down_weight = weight_set
    scaling = HEAD_DIM ** (-0.5)
    head_shape = (HEADS, HEAD_DIM)
    activated = low(jax.nn.silu(condition))
    modulation = low_back(jnp.dot(activated[None, :], ada_weight, precision=HIGHEST))[0]
    scale_attn, gate_attn, scale_mlp, gate_mlp = jnp.split(modulation, 4)
    cosine, sine_table = rope_tables(item_kind)
    normed = low(norm_rows(token_block, gains[0]) * (1.0 + scale_attn))
    qkv_rows = low_back(jnp.dot(normed, qkv_weight, precision=HIGHEST))
    query_raw, key_raw, value_raw = jnp.split(qkv_rows, 3, axis=1)
    queries = low(rotate(norm_rows(query_raw.reshape(SEQ, HEADS, HEAD_DIM), gains[1].reshape(head_shape)), cosine, sine_table))
    key_rows = low(rotate(norm_rows(key_raw.reshape(SEQ, HEADS, HEAD_DIM), gains[2].reshape(head_shape)), cosine, sine_table))
    values = low(value_raw).reshape(SEQ, HEADS, HEAD_DIM)
    text_proj = low_back(jnp.dot(caption, text_weight, precision=HIGHEST))
    text_key_raw, text_value_raw = jnp.split(text_proj, 2, axis=1)
    text_keys = low(norm_rows(text_key_raw.reshape(TEXT, HEADS, HEAD_DIM), gains[3].reshape(head_shape)))
    text_values = low(text_value_raw).reshape(TEXT, HEADS, HEAD_DIM)
    own_scores = low_back(jnp.einsum('shd,thd->hst', queries, key_rows, precision=HIGHEST) * scaling)
    own_probs = low(softmax_rows(own_scores))
    own_out = jnp.einsum('hst,thd->shd', own_probs, values, precision=HIGHEST).reshape(SEQ, D)
    text_scores = low_back(jnp.einsum('shd,thd->hst', queries, text_keys, precision=HIGHEST) * scaling)
    text_valid = jnp.arange(TEXT, dtype=jnp.int32) < caption_len
    text_scores = jnp.where(text_valid[None, None, :], text_scores, -1e+30)
    text_probs = low(softmax_rows(text_scores))
    text_out = jnp.einsum('hst,thd->shd', text_probs, text_values, precision=HIGHEST).reshape(SEQ, D)
    mixed_heads = low(low_back(own_out) + jnp.tanh(gains[5]) * low_back(text_out))
    branch = low_back(jnp.dot(mixed_heads, out_weight, precision=HIGHEST))
    middle = token_block + jnp.tanh(gate_attn) * branch
    mlp_input = low(norm_rows(middle, gains[4]) * (1.0 + scale_mlp))
    gate_up = low_back(jnp.dot(mlp_input, gate_up_weight, precision=HIGHEST))
    gate_half, up_half = jnp.split(gate_up, 2, axis=1)
    hidden = low(jax.nn.silu(gate_half) * up_half)
    result = low_back(jnp.dot(hidden, down_weight, precision=HIGHEST))
    return middle + jnp.tanh(gate_mlp) * result

def reference(tokens, condition, caption, caption_len, item_kind, out_cotangent, norm_gains, ada_weight, qkv_weight, out_weight, text_weight, gate_up_weight, down_weight):
    weights = (norm_gains.astype(jnp.float32), ada_weight.astype(jnp.float32), qkv_weight.astype(jnp.float32), out_weight.astype(jnp.float32), text_weight.astype(jnp.float32), gate_up_weight.astype(jnp.float32), down_weight.astype(jnp.float32))
    token_blocks = tokens.astype(jnp.float32).reshape(ITEMS, SEQ, D)
    conditions = condition.astype(jnp.float32)
    captions = caption.astype(jnp.float32)

    def forward(blocks, weight_set):

        def one_item(section):
            return item_forward(section[0], section[1], section[2], section[3], section[4], weight_set)
        return lax.map(jax.checkpoint(one_item), (blocks, conditions, captions, caption_len, item_kind))
    outputs, pull_back = jax.vjp(forward, token_blocks, weights)
    grad_tokens, grad_weights = pull_back(out_cotangent.astype(jnp.float32).reshape(ITEMS, SEQ, D))
    return (outputs.reshape(TOKENS, D).astype(jnp.bfloat16), grad_tokens.reshape(TOKENS, D), grad_weights[0], grad_weights[1], grad_weights[2], grad_weights[3], grad_weights[4], grad_weights[5], grad_weights[6])
```

```python
import math

import jax
import jax.numpy as jnp
from jax import lax
from jax.sharding import Mesh
from jax.sharding import PartitionSpec as P

D = 1536
HEADS = 24
HEAD_DIM = 64
TEXT_DIM = 4096
FF = 4096
SIDE = 16
RANKS = 4
AXES = ("hi", "mid", "core", "rep")


EPSILON = 1e-06


def norm_rows(values, gain_row):
    return (
        values * lax.rsqrt(jnp.mean(values * values, axis=-1, keepdims=True) + EPSILON) * gain_row
    )


def turn_half(values):
    first_q, second, third_q, fourth = jnp.split(values, 4, axis=-1)
    return jnp.concatenate([-second, first_q, -fourth, third_q], axis=-1)


def rope_tables(item_kind, item_len):
    position = jnp.arange(item_len, dtype=jnp.int32)[None, :]
    half_side = SIDE // 2
    frame_index = position // (half_side * half_side)
    within = position % (half_side * half_side)
    is_clip = item_kind[:, None] == 1
    row_index = jnp.where(is_clip, frame_index * half_side + within // half_side, position // SIDE)
    columns = jnp.where(is_clip, within % half_side, position % SIDE)
    lane_index = jnp.arange(HEAD_DIM, dtype=jnp.int32)
    quarter = HEAD_DIM // 4
    frequency = jnp.exp(-(lane_index % quarter).astype(jnp.float32) * (math.log(10000.0) / quarter))
    coordinate = jnp.where(
        lane_index[None, None, :] < 2 * quarter, row_index[:, :, None], columns[:, :, None]
    ).astype(jnp.float32)
    angles = coordinate * frequency
    return (jnp.cos(angles), jnp.sin(angles))


def modulate(values, gain_row, scaling):
    return norm_rows(values, gain_row) * (1.0 + scaling[:, None, :])


def rotated_norm(values, gain_row, cosine, sine_table):
    normal_rows = norm_rows(values, gain_row)
    return normal_rows * cosine[:, :, None, :] + turn_half(normal_rows) * sine_table[:, :, None, :]


def silu_product(gate_half, up_half):
    return jax.nn.silu(gate_half) * up_half


def score_rows(queries, key_rows, text_valid, scaling):
    scores = (
        jnp.einsum("ishd,ithd->ihst", queries, key_rows, preferred_element_type=jnp.float32)
        * scaling
    )
    if text_valid is not None:
        scores = jnp.where(text_valid, scores, -1e30)
    return scores


def attend(queries, key_rows, values, text_valid, scaling):
    scores = score_rows(queries, key_rows, text_valid, scaling)
    row_max = jnp.max(scores, axis=-1, keepdims=True)
    shifted = jnp.exp(scores - row_max)
    row_sum = jnp.sum(shifted, axis=-1, keepdims=True)
    attn_probs = (shifted / row_sum).astype(jnp.bfloat16)
    attended = jnp.einsum("ihst,ithd->ishd", attn_probs, values, preferred_element_type=jnp.float32)
    return (attended, row_max + jnp.log(row_sum))


def attend_back(queries, key_rows, values, text_valid, scaling, log_sum, grad_attended):
    scores = score_rows(queries, key_rows, text_valid, scaling)
    attn_probs = jnp.exp(scores - log_sum)
    grad_values = jnp.einsum(
        "ihst,ishd->ithd",
        attn_probs.astype(jnp.bfloat16),
        grad_attended,
        preferred_element_type=jnp.float32,
    )
    grad_probs = jnp.einsum(
        "ishd,ithd->ihst", grad_attended, values, preferred_element_type=jnp.float32
    )
    inner_sum = jnp.sum(attn_probs * grad_probs, axis=-1, keepdims=True)
    grad_scores = (attn_probs * (grad_probs - inner_sum)).astype(jnp.bfloat16)
    grad_queries = (
        jnp.einsum("ihst,ithd->ishd", grad_scores, key_rows, preferred_element_type=jnp.float32)
        * scaling
    )
    grad_keys = (
        jnp.einsum("ihst,ishd->ithd", grad_scores, queries, preferred_element_type=jnp.float32)
        * scaling
    )
    return (grad_queries, grad_keys, grad_values)


def dot(left, right):
    return jnp.dot(left, right, preferred_element_type=jnp.float32)


def dot_left(left, right):
    return lax.dot_general(left, right, (((0,), (0,)), ((), ())), preferred_element_type=jnp.float32)


def dot_right(left, right):
    return lax.dot_general(left, right, (((1,), (1,)), ((), ())), preferred_element_type=jnp.float32)


def swap(block, axis, count=2, step=1):
    return lax.ppermute(block, axis, [(at, at ^ step) for at in range(count)])


def spread(block, axis, count):
    if count & (count - 1):
        return lax.all_gather(block, axis)
    block, step = block[None], 1
    while step < count:
        other = swap(block, axis, count, step)
        low = (lax.axis_index(axis) & step) == 0
        block = jnp.where(
            low, jnp.concatenate([block, other]), jnp.concatenate([other, block])
        )
        step *= 2
    return block


def fold(block, axis, count):
    if count & (count - 1):
        return lax.psum_scatter(block, axis, scatter_dimension=0)
    step = count // 2
    while step:
        half = block.shape[0] // 2
        low = (lax.axis_index(axis) & step) == 0
        lower, upper = block[:half], block[half:]
        block = jnp.where(low, lower, upper) + swap(
            jnp.where(low, upper, lower), axis, count, step
        )
        step //= 2
    return block[0]


def trade(block, axis):
    low = lax.axis_index(axis) == 0
    kept = jnp.where(low, block[0], block[1])
    got = swap(jnp.where(low, block[1], block[0]), axis)
    return jnp.where(low, jnp.stack([kept, got]), jnp.stack([got, kept]))


def trade_ranks(block):
    block = trade(block, "mid")
    return jnp.swapaxes(trade(jnp.swapaxes(block, 0, 1), "core"), 0, 1)


def pick(stack, index):
    return lax.dynamic_index_in_dim(stack, index, 0, keepdims=False)


def share(rows):
    far = swap(rows, "mid")
    return (
        jnp.concatenate([rows, swap(rows, "core")]),
        jnp.concatenate([far, swap(far, "core")]),
    )


def settle(near, far):
    half = near.shape[0] // 2
    across = far[:half] + swap(far[half:].astype(jnp.bfloat16), "core").astype(jnp.float32)
    moved = swap(across.astype(jnp.bfloat16), "mid").astype(jnp.float32)
    return near[:half] + swap(near[half:].astype(jnp.bfloat16), "core").astype(jnp.float32) + moved


class Layout:
    def __init__(self, hi, rep, out_rows):
        self.hi, self.rep = hi, rep
        self.aligned = (rep * out_rows) % HEAD_DIM == 0
        self.head_groups = hi if self.aligned else 1
        self.rank = lax.axis_index("mid") * 2 + lax.axis_index("core")

    def by_rank(self, weight, sections, groups):
        rows, columns = weight.shape
        width = columns // (sections * groups * RANKS)
        view = weight.reshape(rows, sections * groups, RANKS, width)
        view = jnp.transpose(view, (2, 0, 1, 3))
        return view.reshape(2, 2, rows, sections * groups * width)

    def from_ranks(self, blocks, sections, groups):
        _, _, rows, per_rank = blocks.shape
        width = per_rank // (sections * groups)
        view = blocks.reshape(RANKS, rows, sections * groups, width)
        return jnp.transpose(view, (1, 2, 0, 3)).reshape(rows, RANKS * per_rank)

    def gather_columns(self, blocks):
        stacked = spread(lax.all_gather(blocks, "rep"), "hi", self.hi)
        natural = jnp.transpose(stacked, (0, 2, 3, 1, 4, 5))
        return natural.reshape(-1, blocks.shape[-1])

    def reduce_columns(self, grad, rows):
        view = grad.astype(jnp.bfloat16).reshape(self.hi, 2, 2, self.rep, rows, -1)
        view = jnp.transpose(view, (0, 3, 1, 2, 4, 5))
        summed = fold(view, "hi", self.hi)
        return lax.psum_scatter(summed, "rep", scatter_dimension=0)

    def gather_rows(self, block):
        stacked = spread(lax.all_gather(block, "rep", tiled=True), "hi", self.hi)
        return stacked.reshape(-1, block.shape[-1])

    def reduce_rows(self, grad):
        summed = fold(grad.astype(jnp.bfloat16).reshape(self.hi, -1, grad.shape[-1]), "hi", self.hi)
        return lax.psum_scatter(summed, "rep", scatter_dimension=0, tiled=True)

    def rank_lanes(self, rows, groups):
        view = rows.reshape(rows.shape[0], groups, RANKS, -1)
        return lax.dynamic_index_in_dim(view, self.rank, 2, keepdims=False).reshape(rows.shape[0], -1)

    def place_lanes(self, row):
        view = row.reshape(self.head_groups, 1, -1)
        at = (jnp.arange(RANKS) == self.rank).astype(row.dtype)[None, :, None]
        return (view * at).reshape(-1)


def local(
    hi_count,
    rep_count,
    tokens,
    condition,
    caption,
    caption_len,
    item_kind,
    out_cotangent,
    norm_gains,
    ada_weight,
    qkv_weight,
    out_weight,
    text_weight,
    gate_up_weight,
    down_weight,
):
    bf16, f32 = jnp.bfloat16, jnp.float32
    item_count = condition.shape[0]
    item_len = tokens.shape[0] // item_count
    text_len = caption.shape[1]
    row_count = item_count * item_len
    rows = qkv_weight.shape[0]
    scaling = HEAD_DIM ** (-0.5)
    plan = Layout(hi_count, rep_count, out_weight.shape[0])
    rank_heads = HEADS // RANKS
    rank_width = rank_heads * HEAD_DIM
    head_shape = (rank_heads, HEAD_DIM)
    hi_at, mid_at, core_at, rep_at = [lax.axis_index(name) for name in AXES]
    device_shape = (hi_count, 2, 2, rep_count)

    qkv_mine = trade_ranks(plan.by_rank(qkv_weight, 3, plan.head_groups))
    text_mine = trade_ranks(plan.by_rank(text_weight, 2, plan.head_groups))
    gate_up_mine = trade_ranks(plan.by_rank(gate_up_weight, 2, hi_count))
    qkv_rank = plan.gather_columns(qkv_mine)
    if plan.aligned:
        out_rank = plan.gather_rows(out_weight)
    else:
        out_whole = lax.all_gather(out_weight, AXES, axis=0, tiled=True)
        out_rank = pick(out_whole.reshape(RANKS, rank_width, D), plan.rank)
    text_rank = plan.gather_columns(text_mine)
    gate_up_rank = plan.gather_columns(gate_up_mine)
    down_rank = plan.gather_rows(down_weight)

    small = jnp.concatenate(
        [
            condition.reshape(-1),
            norm_gains.reshape(-1),
            caption_len.astype(bf16),
            item_kind.astype(bf16),
        ]
    )
    for axis, count in (("rep", rep_count), ("core", 2), ("mid", 2), ("hi", hi_count)):
        small = spread(small, axis, count)
    cut = [condition.size, condition.size + norm_gains.size]
    cut.append(cut[1] + item_count)
    conditions, gains, lengths, kinds = jnp.split(small, cut, axis=-1)
    activated = jax.nn.silu(conditions.astype(f32)).astype(bf16).reshape(-1, D)
    gain_rows = jnp.moveaxis(
        gains.astype(f32).reshape(device_shape + (6, norm_gains.shape[1])), 4, 0
    ).reshape(6, D)
    block_at = ((hi_at * 2 + mid_at) * 2 + core_at) * rep_count + rep_at
    activated_mine = lax.dynamic_slice_in_dim(activated, block_at * rows, rows, axis=1)

    def group_items(values):
        view = lax.dynamic_index_in_dim(pick(values, hi_at), rep_at, 2, keepdims=False)
        near, far = pick(view, mid_at), pick(view, 1 - mid_at)
        order = [core_at, 1 - core_at]
        return [
            jnp.concatenate([pick(side, at) for at in order]).astype(jnp.int32)
            for side in (near, far)
        ]

    near_len, far_len = group_items(lengths)
    near_kind, far_kind = group_items(kinds)

    partial = dot(activated_mine, ada_weight).reshape(device_shape + (item_count, 4 * D))
    partial = fold(jnp.moveaxis(partial, 2, 0), "core", 2)
    partial = fold(jnp.moveaxis(partial, 1, 0), "mid", 2)
    partial = fold(partial, "hi", hi_count)
    modulation = fold(partial, "rep", rep_count)
    scale_attn, gate_attn, scale_mlp, gate_mlp = jnp.split(modulation, 4, axis=1)

    token_rows = tokens.astype(f32).reshape(item_count, item_len, D)
    normed = (
        modulate(token_rows, gain_rows[0], scale_attn).astype(bf16).reshape(row_count, D)
    )
    mlp_gate = jnp.tanh(gate_mlp)[:, None, :]
    grad_top = out_cotangent.astype(f32).reshape(item_count, item_len, D)
    grad_result = (mlp_gate * grad_top).astype(bf16).reshape(row_count, D)
    head_gains = plan.rank_lanes(gain_rows, plan.head_groups)
    query_gain, key_gain, text_gain = [head_gains[at].reshape(head_shape) for at in (1, 2, 3)]
    cross_gate = jnp.tanh(head_gains[5])

    normed_sides = share(normed)
    caption_sides = share(caption.reshape(-1, TEXT_DIM))
    result_sides = share(grad_result)

    def attention(normed_side, caption_side, kind, length):
        count = kind.shape[0]
        full_shape = (count, item_len) + head_shape
        text_shape = (count, text_len) + head_shape
        cosine, sine_table = rope_tables(kind, item_len)
        qkv_rows = dot(normed_side, qkv_rank)
        query_raw, key_raw, value_raw = [
            section.reshape(full_shape) for section in jnp.split(qkv_rows, 3, axis=1)
        ]
        queries = rotated_norm(query_raw, query_gain, cosine, sine_table).astype(bf16)
        key_rows = rotated_norm(key_raw, key_gain, cosine, sine_table).astype(bf16)
        values = value_raw.astype(bf16)
        text_proj = dot(caption_side, text_rank)
        text_key_raw, text_value_raw = [
            section.reshape(text_shape) for section in jnp.split(text_proj, 2, axis=1)
        ]
        text_keys = norm_rows(text_key_raw, text_gain).astype(bf16)
        text_values = text_value_raw.astype(bf16)
        text_valid = (jnp.arange(text_len, dtype=jnp.int32)[None, :] < length[:, None])[
            :, None, None, :
        ]
        own_out, own_logsum = attend(queries, key_rows, values, None, scaling)
        text_out, text_logsum = attend(queries, text_keys, text_values, text_valid, scaling)
        text_flat = text_out.reshape(-1, rank_width)
        mixed = (own_out.reshape(-1, rank_width) + cross_gate * text_flat).astype(bf16)

        def back(grad_branch_side):
            grad_mixed = dot_right(grad_branch_side, out_rank)
            grad_cross_gate = jnp.sum(grad_mixed * text_flat, axis=0) * (1.0 - cross_gate**2)
            grad_own = grad_mixed.astype(bf16).reshape(full_shape)
            grad_read = (cross_gate * grad_mixed).astype(bf16).reshape(full_shape)
            own_queries, own_keys, own_values = attend_back(
                queries, key_rows, values, None, scaling, own_logsum, grad_own
            )
            read_queries, read_keys, read_values = attend_back(
                queries, text_keys, text_values, text_valid, scaling, text_logsum, grad_read
            )

            def rotate_rows(values, gain_row):
                return rotated_norm(values, gain_row, cosine, sine_table)

            _, pull_query = jax.vjp(rotate_rows, query_raw, query_gain)
            grad_query_raw, grad_query_gain = pull_query(own_queries + read_queries)
            _, pull_key = jax.vjp(rotate_rows, key_raw, key_gain)
            grad_key_raw, grad_key_gain = pull_key(own_keys)
            _, pull_text = jax.vjp(norm_rows, text_key_raw, text_gain)
            grad_text_key, grad_text_gain = pull_text(read_keys)
            grad_qkv_rows = jnp.concatenate(
                [part.reshape(-1, rank_width) for part in (grad_query_raw, grad_key_raw, own_values)],
                axis=1,
            ).astype(bf16)
            grad_text_rows = jnp.concatenate(
                [part.reshape(-1, rank_width) for part in (grad_text_key, read_values)], axis=1
            ).astype(bf16)
            gain_terms = jnp.stack(
                [
                    grad_query_gain.reshape(-1),
                    grad_key_gain.reshape(-1),
                    grad_text_gain.reshape(-1),
                    grad_cross_gate,
                ]
            )
            return grad_qkv_rows, grad_text_rows, gain_terms

        return mixed, back

    mixed_far, back_far = attention(normed_sides[1], caption_sides[1], far_kind, far_len)
    mixed_near, back_near = attention(normed_sides[0], caption_sides[0], near_kind, near_len)
    branch = settle(dot(mixed_near, out_rank), dot(mixed_far, out_rank)).reshape(
        item_count, item_len, D
    )
    attn_gate = jnp.tanh(gate_attn)[:, None, :]
    middle = token_rows + attn_gate * branch
    mlp_input = modulate(middle, gain_rows[4], scale_mlp).astype(bf16).reshape(row_count, D)
    input_sides = share(mlp_input)

    def feed(input_side, result_side):
        gate_half, up_half = jnp.split(dot(input_side, gate_up_rank), 2, axis=1)
        hidden = silu_product(gate_half, up_half).astype(bf16)
        grad_hidden = dot_right(result_side, down_rank)
        _, pull_silu = jax.vjp(silu_product, gate_half, up_half)
        grad_gate_rows = jnp.concatenate(pull_silu(grad_hidden), axis=1).astype(bf16)
        return hidden, grad_gate_rows, dot_right(grad_gate_rows, gate_up_rank)

    hidden_near, gate_rows_near, grad_input_near = feed(input_sides[0], result_sides[0])
    hidden_far, gate_rows_far, grad_input_far = feed(input_sides[1], result_sides[1])
    grad_mlp_input = settle(grad_input_near, grad_input_far)
    input_all = jnp.concatenate(input_sides)
    gate_up_grad = dot_left(input_all, jnp.concatenate([gate_rows_near, gate_rows_far]))
    gate_up_parts = plan.reduce_columns(gate_up_grad, rows)
    hidden_all = jnp.concatenate([hidden_near, hidden_far])
    down_grad = dot_left(hidden_all, jnp.concatenate(result_sides))
    down_weight_grad = plan.reduce_rows(down_grad).astype(f32)
    result = settle(dot(hidden_near, down_rank), dot(hidden_far, down_rank)).reshape(
        item_count, item_len, D
    )
    layer_out = (middle + mlp_gate * result).astype(bf16).reshape(row_count, D)
    grad_mlp_gate = jnp.sum(grad_top * result, axis=1) * (1.0 - jnp.tanh(gate_mlp) ** 2)
    _, pull_mlp_norm = jax.vjp(modulate, middle, gain_rows[4], scale_mlp)
    grad_middle_norm, grad_mlp_gain, grad_scale_mlp = pull_mlp_norm(
        grad_mlp_input.reshape(item_count, item_len, D)
    )
    grad_middle = grad_top + grad_middle_norm

    grad_attn_gate = jnp.sum(grad_middle * branch, axis=1) * (1.0 - jnp.tanh(gate_attn) ** 2)
    grad_branch = (attn_gate * grad_middle).astype(bf16).reshape(row_count, D)
    branch_sides = share(grad_branch)
    qkv_rows_near, text_rows_near, gain_terms_near = back_near(branch_sides[0])
    qkv_rows_far, text_rows_far, gain_terms_far = back_far(branch_sides[1])
    grad_normed = settle(dot_right(qkv_rows_near, qkv_rank), dot_right(qkv_rows_far, qkv_rank))
    out_grad = dot_left(jnp.concatenate([mixed_near, mixed_far]), jnp.concatenate(branch_sides))
    if plan.aligned:
        out_weight_grad = plan.reduce_rows(out_grad).astype(f32)
    else:
        at = (jnp.arange(RANKS) == plan.rank).astype(bf16)[:, None, None]
        placed = (out_grad.astype(bf16)[None] * at).reshape(D, D)
        out_weight_grad = lax.psum_scatter(placed, AXES, scatter_dimension=0, tiled=True).astype(f32)
    qkv_grad = dot_left(jnp.concatenate(normed_sides), jnp.concatenate([qkv_rows_near, qkv_rows_far]))
    qkv_parts = plan.reduce_columns(qkv_grad, rows)
    text_grad = dot_left(
        jnp.concatenate(caption_sides), jnp.concatenate([text_rows_near, text_rows_far])
    )
    text_parts = plan.reduce_columns(text_grad, text_weight.shape[0])

    _, pull_attn_norm = jax.vjp(modulate, token_rows, gain_rows[0], scale_attn)
    grad_token_norm, grad_attn_gain, grad_scale_attn = pull_attn_norm(
        grad_normed.reshape(item_count, item_len, D)
    )
    tokens_grad = (grad_middle + grad_token_norm).reshape(row_count, D)

    grad_modulation = jnp.concatenate(
        [grad_scale_attn, grad_attn_gate, grad_scale_mlp, grad_mlp_gate], axis=1
    ).astype(bf16)
    gain_terms = [plan.place_lanes(row) for row in gain_terms_near + gain_terms_far]
    gains_grad = jnp.stack(
        [grad_attn_gain, gain_terms[0], gain_terms[1], gain_terms[2], grad_mlp_gain, gain_terms[3]]
    ).astype(bf16)
    for axis, count in (("rep", rep_count), ("core", 2), ("mid", 2), ("hi", hi_count)):
        both = spread(
            jnp.concatenate([grad_modulation.reshape(-1), gains_grad.reshape(-1)]), axis, count
        )
        grad_modulation = both[:, : grad_modulation.size]
        gains_grad = jnp.sum(
            both[:, grad_modulation[0].size :].astype(f32), axis=0
        ).astype(bf16)
    ada_weight_grad = dot_left(activated_mine, grad_modulation.reshape(-1, 4 * D))
    norm_gains_grad = lax.dynamic_slice_in_dim(
        gains_grad.reshape(6, D), block_at * norm_gains.shape[1], norm_gains.shape[1], axis=1
    ).astype(f32)

    qkv_weight_grad = plan.from_ranks(trade_ranks(qkv_parts), 3, plan.head_groups).astype(f32)
    text_weight_grad = plan.from_ranks(trade_ranks(text_parts), 2, plan.head_groups).astype(f32)
    gate_up_weight_grad = plan.from_ranks(trade_ranks(gate_up_parts), 2, hi_count).astype(f32)
    return (
        layer_out,
        tokens_grad,
        norm_gains_grad,
        ada_weight_grad,
        qkv_weight_grad,
        out_weight_grad,
        text_weight_grad,
        gate_up_weight_grad,
        down_weight_grad,
    )


def solution(mesh):
    grp, rep = mesh.devices.shape
    hi = grp // RANKS
    inner = Mesh(mesh.devices.reshape(hi, 2, 2, rep), AXES)
    rows = P(AXES, None)

    def step(*arrays):
        return local(hi, rep, *arrays)

    return jax.shard_map(
        step,
        mesh=inner,
        in_specs=(
            rows,
            rows,
            P(AXES, None, None),
            P(AXES),
            P(AXES),
            rows,
            P(None, AXES),
            rows,
            rows,
            rows,
            rows,
            rows,
            rows,
        ),
        out_specs=(rows, rows, P(None, AXES), rows, rows, rows, rows, rows, rows),
        check_vma=False,
    )
```

```python
import math

import jax
import jax.numpy as jnp
from jax import lax
from jax.experimental import pallas as pl
from jax.experimental.pallas import tpu as pltpu
from jax.sharding import Mesh
from jax.sharding import PartitionSpec as P

D = 1536
HEADS = 24
HEAD_DIM = 64
TEXT_DIM = 4096
FF = 4096
SIDE = 16
RANKS = 4
LANES = 128
MIB = 1 << 20
AXES = ("hi", "mid", "core", "rep")


EPSILON = 1e-06


def norm_rows(values, gain_row):
    return (
        values * lax.rsqrt(jnp.mean(values * values, axis=-1, keepdims=True) + EPSILON) * gain_row
    )


def rope_tables(item_kind, item_len):
    position = jnp.arange(item_len, dtype=jnp.int32)[None, :]
    half_side = SIDE // 2
    frame_index = position // (half_side * half_side)
    within = position % (half_side * half_side)
    is_clip = item_kind[:, None] == 1
    row_index = jnp.where(is_clip, frame_index * half_side + within // half_side, position // SIDE)
    columns = jnp.where(is_clip, within % half_side, position % SIDE)
    lane_index = jnp.arange(HEAD_DIM, dtype=jnp.int32)
    quarter = HEAD_DIM // 4
    frequency = jnp.exp(-(lane_index % quarter).astype(jnp.float32) * (math.log(10000.0) / quarter))
    coordinate = jnp.where(
        lane_index[None, None, :] < 2 * quarter, row_index[:, :, None], columns[:, :, None]
    ).astype(jnp.float32)
    angles = coordinate * frequency
    return (jnp.cos(angles), jnp.sin(angles))


def modulate(values, gain_row, scaling):
    return norm_rows(values, gain_row) * (1.0 + scaling[:, None, :])


def silu_product(gate_half, up_half):
    return jax.nn.silu(gate_half) * up_half


def dot(left, right):
    return jnp.dot(left, right, preferred_element_type=jnp.float32)


def dot_left(left, right):
    return lax.dot_general(left, right, (((0,), (0,)), ((), ())), preferred_element_type=jnp.float32)


def dot_right(left, right):
    return lax.dot_general(left, right, (((1,), (1,)), ((), ())), preferred_element_type=jnp.float32)


def lane_index(shape):
    return lax.broadcasted_iota(jnp.int32, shape, len(shape) - 1)

def head_sums(values):
    first = lane_index(values.shape) < HEAD_DIM
    low = jnp.sum(jnp.where(first, values, 0.0), axis=-1, keepdims=True)
    high = jnp.sum(jnp.where(first, 0.0, values), axis=-1, keepdims=True)
    return jnp.where(first, low, high)

def partner(values):
    quarter = HEAD_DIM // 4
    width = values.shape[-1]
    low = lane_index(values.shape) % (2 * quarter) < quarter
    return jnp.where(low, pltpu.roll(values, width - quarter, 1), pltpu.roll(values, quarter, 1))

def stack_heads(values):
    first = lane_index(values.shape) < HEAD_DIM
    zero = jnp.zeros_like(values)
    return jnp.concatenate([jnp.where(first, values, zero), jnp.where(first, zero, values)])

def join_heads(stacked):
    rows = stacked.shape[0] // 2
    first = lane_index((rows, stacked.shape[1])) < HEAD_DIM
    return jnp.where(first, stacked[:rows], stacked[rows:])

def inverse_rms(raw):
    return lax.rsqrt(head_sums(raw * raw) * (1.0 / HEAD_DIM) + EPSILON)

def attend_kernel(kind_ref, len_ref, qkv_ref, text_ref, text_value_ref, gain_ref, cos_ref, sin_ref, q_ref, k_ref, tk_ref, mixed_ref, read_ref):
    item = pl.program_id(0)
    kind, length = kind_ref[item], len_ref[item]
    width = q_ref.shape[1]
    cosine, sine = cos_ref[kind], sin_ref[kind]
    scaling = HEAD_DIM ** (-0.5)
    for at in range(0, width, LANES):
        lanes = slice(at, at + LANES)
        turned = []
        for part, out_ref in ((0, q_ref), (1, k_ref)):
            raw = qkv_ref[:, part * width + at : part * width + at + LANES]
            normal = raw * inverse_rms(raw) * gain_ref[part : part + 1, lanes]
            rows = (normal * cosine + partner(normal) * sine).astype(jnp.bfloat16)
            out_ref[:, lanes] = rows
            turned.append(rows)
        queries, keys = turned
        values = qkv_ref[:, 2 * width + at : 2 * width + at + LANES].astype(jnp.bfloat16)
        text_raw = text_ref[:, lanes]
        text_keys = (text_raw * inverse_rms(text_raw) * gain_ref[2:3, lanes]).astype(jnp.bfloat16)
        tk_ref[:, lanes] = text_keys
        text_values = text_value_ref[:, lanes].astype(jnp.bfloat16)
        stacked = stack_heads(queries)
        own = dot_right(stacked, keys) * scaling
        own = jnp.exp(own - jnp.max(own, axis=-1, keepdims=True))
        own_out = dot(own.astype(jnp.bfloat16), values) / jnp.sum(own, axis=-1, keepdims=True)
        text = dot_right(stacked, text_keys) * scaling
        text = jnp.where(lane_index(text.shape) < length, text, -1e30)
        text = jnp.exp(text - jnp.max(text, axis=-1, keepdims=True))
        text_out = dot(text.astype(jnp.bfloat16), text_values) / jnp.sum(text, axis=-1, keepdims=True)
        read = join_heads(text_out)
        read_ref[:, lanes] = read
        mixed_ref[:, lanes] = (join_heads(own_out) + gain_ref[3:4, lanes] * read).astype(jnp.bfloat16)

def head_norm_back(grad, raw, gain_row):
    inverse = inverse_rms(raw)
    scaled = grad * gain_row
    normal = raw * inverse
    inner = head_sums(scaled * normal) * (1.0 / HEAD_DIM)
    return inverse * (scaled - normal * inner), jnp.sum(grad * normal, axis=0, keepdims=True)

def attend_back_kernel(kind_ref, len_ref, qkv_ref, text_ref, text_value_ref, gain_ref, cos_ref, sin_ref, q_ref, k_ref, tk_ref, read_ref, grad_ref, gqkv_ref, gtext_ref, gains_ref):
    item = pl.program_id(0)
    kind, length = kind_ref[item], len_ref[item]
    width = q_ref.shape[1]
    cosine, sine = cos_ref[kind], sin_ref[kind]
    scaling = HEAD_DIM ** (-0.5)

    @pl.when(item == 0)
    def _():
        gains_ref[...] = jnp.zeros_like(gains_ref)

    def one(stacked, keys, values, stacked_grad, valid):
        scores = dot_right(keys, stacked) * scaling
        if valid is not None:
            scores = jnp.where(valid(scores.shape), scores, -1e30)
        probs = jnp.exp(scores - jnp.max(scores, axis=0, keepdims=True))
        probs = probs * (1.0 / jnp.sum(probs, axis=0, keepdims=True))
        grad_values = dot(probs.astype(jnp.bfloat16), stacked_grad)
        grad_probs = dot_right(values, stacked_grad)
        inner = jnp.sum(probs * grad_probs, axis=0, keepdims=True)
        grad_scores = (probs * (grad_probs - inner)).astype(jnp.bfloat16)
        grad_keys = dot(grad_scores, stacked) * scaling
        grad_queries = dot_left(keys, grad_scores)
        return grad_queries, grad_keys, grad_values

    for at in range(0, width, LANES):
        lanes = slice(at, at + LANES)
        grad = grad_ref[:, lanes]
        cross = gain_ref[3:4, lanes]
        values = qkv_ref[:, 2 * width + at : 2 * width + at + LANES].astype(jnp.bfloat16)
        text_values = text_value_ref[:, lanes].astype(jnp.bfloat16)
        stacked = stack_heads(q_ref[:, lanes])
        own_queries, own_keys, own_values = one(
            stacked, k_ref[:, lanes], values, stack_heads(grad.astype(jnp.bfloat16)), None
        )
        read_queries, read_keys, read_values = one(
            stacked, tk_ref[:, lanes], text_values, stack_heads((cross * grad).astype(jnp.bfloat16)),
            lambda shape: lax.broadcasted_iota(jnp.int32, shape, 0) < length,
        )
        grad_queries = join_heads((own_queries + read_queries).T) * scaling
        for part, turned in ((0, grad_queries), (1, own_keys)):
            raw = qkv_ref[:, part * width + at : part * width + at + LANES]
            back = turned * cosine + partner(turned * sine)
            grad_raw, gain = head_norm_back(back, raw, gain_ref[part : part + 1, lanes])
            gqkv_ref[:, part * width + at : part * width + at + LANES] = grad_raw.astype(jnp.bfloat16)
            gains_ref[part : part + 1, lanes] += gain
        gqkv_ref[:, 2 * width + at : 2 * width + at + LANES] = own_values.astype(jnp.bfloat16)
        grad_text, gain = head_norm_back(read_keys, text_ref[:, lanes], gain_ref[2:3, lanes])
        gtext_ref[:, lanes] = grad_text.astype(jnp.bfloat16)
        gains_ref[2:3, lanes] += gain
        gtext_ref[:, width + at : width + at + LANES] = read_values.astype(jnp.bfloat16)
        gains_ref[3:4, lanes] += jnp.sum(grad * read_ref[:, lanes], axis=0, keepdims=True)

def item_call(kernel, items, operands, outs, name):
    def rows(shape):
        return pl.BlockSpec((shape[0] // items, shape[1]), lambda i, *_: (i, 0))
    def full(shape):
        return pl.BlockSpec(shape, lambda i, *_: (0,) * len(shape))
    def call(scalars, *arrays):
        in_specs = [rows(a.shape) if i in operands else full(a.shape) for i, a in enumerate(arrays)]
        return pl.pallas_call(
            kernel,
            grid_spec=pltpu.PrefetchScalarGridSpec(
                num_scalar_prefetch=len(scalars), grid=(items,), in_specs=in_specs,
                out_specs=[rows(s.shape) if cut else full(s.shape) for s, cut in outs]),
            out_shape=[s for s, _ in outs],
            compiler_params=pltpu.CompilerParams(dimension_semantics=("arbitrary",), vmem_limit_bytes=48*MIB),
            name=name,
        )(*scalars, *arrays)
    return call

def attend(kind, length, qkv_raw, text_raw, text_value_raw, gains, cosine, sine):
    items=kind.shape[0]; n=qkv_raw.shape[0]; width=qkv_raw.shape[1]//3; t=text_raw.shape[0]
    S=jax.ShapeDtypeStruct
    outs=[(S((n,width),jnp.bfloat16),True),(S((n,width),jnp.bfloat16),True),(S((t,width),jnp.bfloat16),True),(S((n,width),jnp.bfloat16),True),(S((n,width),jnp.float32),True)]
    return item_call(attend_kernel, items, (0,1,2), outs, "attend")((kind,length), qkv_raw, text_raw, text_value_raw, gains, cosine, sine)

def attend_back(kind, length, qkv_raw, text_raw, text_value_raw, gains, cosine, sine, q, k, tk, read, grad):
    items=kind.shape[0]; n=qkv_raw.shape[0]; width=qkv_raw.shape[1]//3; t=text_raw.shape[0]
    S=jax.ShapeDtypeStruct
    outs=[(S((n,3*width),jnp.bfloat16),True),(S((t,2*width),jnp.bfloat16),True),(S((4,width),jnp.float32),False)]
    return item_call(attend_back_kernel, items, (0,1,2,6,7,8,9,10), outs, "attend_back")((kind,length), qkv_raw, text_raw, text_value_raw, gains, cosine, sine, q,k,tk,read,grad)


def feed_kernel(input_ref, result_ref, gate_ref, up_ref, down_ref, hidden_ref, grad_gate_ref, grad_up_ref, grad_ref):
    rows = input_ref[...]
    gate = dot(rows, gate_ref[...])
    up = dot(rows, up_ref[...])
    grad_hidden = dot_right(result_ref[...], down_ref[...])
    sigmoid = 1.0 / (1.0 + jnp.exp(-gate))
    silu = gate * sigmoid
    hidden_ref[...] = (silu * up).astype(jnp.bfloat16)
    grad_gate = (grad_hidden * up * (sigmoid + silu * (1.0 - sigmoid))).astype(jnp.bfloat16)
    grad_up = (grad_hidden * silu).astype(jnp.bfloat16)
    grad_gate_ref[...] = grad_gate
    grad_up_ref[...] = grad_up
    grad_ref[...] = dot_right(grad_gate, gate_ref[...]) + dot_right(grad_up, up_ref[...])


def feed(rows, grad_result, gate_rank, up_rank, down_rank):
    count, width = rows.shape[0], gate_rank.shape[1]
    block = 256

    def cut(columns):
        return pl.BlockSpec((block, columns), lambda i: (i, 0))

    def whole(array):
        return pl.BlockSpec(array.shape, lambda i: (0, 0), pipeline_mode=pl.Buffered(1))

    hidden = jax.ShapeDtypeStruct((count, width), jnp.bfloat16)
    return pl.pallas_call(
        feed_kernel,
        grid=(count // block,),
        in_specs=[cut(D), cut(D), whole(gate_rank), whole(up_rank), whole(down_rank)],
        out_specs=[cut(width), cut(width), cut(width), cut(D)],
        out_shape=[hidden, hidden, hidden, jax.ShapeDtypeStruct((count, D), jnp.float32)],
        compiler_params=pltpu.CompilerParams(
            dimension_semantics=("arbitrary",), vmem_limit_bytes=56 * MIB
        ),
        name="feed",
    )(rows, grad_result, gate_rank, up_rank, down_rank)


def swap(block, axis, count=2, step=1):
    return lax.ppermute(block, axis, [(at, at ^ step) for at in range(count)])


def spread(block, axis, count):
    if count & (count - 1):
        return lax.all_gather(block, axis)
    block, step = block[None], 1
    while step < count:
        other = swap(block, axis, count, step)
        low = (lax.axis_index(axis) & step) == 0
        block = jnp.where(
            low, jnp.concatenate([block, other]), jnp.concatenate([other, block])
        )
        step *= 2
    return block


def fold(block, axis, count):
    if count & (count - 1):
        return lax.psum_scatter(block, axis, scatter_dimension=0)
    step = count // 2
    while step:
        half = block.shape[0] // 2
        low = (lax.axis_index(axis) & step) == 0
        lower, upper = block[:half], block[half:]
        block = jnp.where(low, lower, upper) + swap(
            jnp.where(low, upper, lower), axis, count, step
        )
        step //= 2
    return block[0]


def trade_ranks(block):
    return lax.all_to_all(block, ("mid", "core"), 0, 0, tiled=True)


def pick(stack, index):
    return lax.dynamic_index_in_dim(stack, index, 0, keepdims=False)


def pair(rows):
    return jnp.concatenate([rows, swap(rows, "core")])


def settle_far(far):
    half = far.shape[0] // 2
    return far[:half] + swap(far[half:].astype(jnp.bfloat16), "core").astype(jnp.float32)


def settle_near(near):
    half = near.shape[0] // 2
    return near[:half] + swap(near[half:].astype(jnp.bfloat16), "core").astype(jnp.float32)


def settle_move(across):
    return swap(across.astype(jnp.bfloat16), "mid").astype(jnp.float32)


class Layout:
    def __init__(self, hi, rep, out_rows):
        self.hi, self.rep = hi, rep
        self.aligned = (rep * out_rows) % HEAD_DIM == 0
        self.head_groups = hi if self.aligned else 1
        self.rank = lax.axis_index("mid") * 2 + lax.axis_index("core")

    def by_rank(self, weight, sections, groups):
        rows, columns = weight.shape
        width = columns // (sections * groups * RANKS)
        view = weight.reshape(rows, sections * groups, RANKS, width)
        view = jnp.transpose(view, (2, 0, 1, 3))
        return view.reshape(RANKS, rows, sections * groups * width)

    def from_ranks(self, blocks, sections, groups):
        _, rows, per_rank = blocks.shape
        width = per_rank // (sections * groups)
        view = blocks.reshape(RANKS, rows, sections * groups, width)
        return jnp.transpose(view, (1, 2, 0, 3)).reshape(rows, RANKS * per_rank)

    def ordered(self, values):
        if self.hi != 2:
            return values
        half = values.shape[-1] // 2
        turned = jnp.concatenate([values[..., half:], values[..., :half]], axis=-1)
        return jnp.where(lax.axis_index("hi") == 0, values, turned)

    def across_hi(self, block):
        if self.hi == 2:
            return jnp.stack([block, swap(block, "hi")])
        return spread(block, "hi", self.hi)

    def natural_rows(self, stacked):
        view = stacked.reshape(self.hi, self.rep, RANKS, -1, stacked.shape[-1])
        return jnp.transpose(view, (0, 2, 1, 3, 4)).reshape(-1, stacked.shape[-1])

    def product(self, left_sides, right_sides, cut):
        near, far = [
            dot_left(cut(left), right) for left, right in zip(left_sides, right_sides, strict=True)
        ]
        return near + far

    def product_moved(self, left_sides, right_sides):
        half = left_sides[0].shape[1] // 2 if self.hi == 2 else 0
        return self.product(left_sides, right_sides, lambda left: left[:, half:]).astype(jnp.bfloat16)

    def move(self, moved):
        if self.hi == 2:
            return swap(moved, "hi")
        return fold(moved.reshape(self.hi, -1, moved.shape[1]), "hi", self.hi)

    def product_kept(self, left_sides, right_sides):
        if self.hi != 2:
            return None
        half = left_sides[0].shape[1] // 2
        return self.product(left_sides, right_sides, lambda left: left[:, :half])

    def total(self, kept, arrived):
        if kept is None:
            return arrived
        return (kept + arrived.astype(jnp.float32)).astype(jnp.bfloat16)

    def by_rep(self, summed):
        view = summed.reshape(RANKS, self.rep, -1, summed.shape[1])
        return jnp.transpose(view, (1, 0, 2, 3)).reshape(self.rep, -1, summed.shape[1])

    def reduce(self, blocks):
        flat = blocks.reshape(-1, blocks.shape[-1])
        return lax.psum_scatter(flat, "rep", scatter_dimension=0, tiled=True)

    def rank_lanes(self, rows, groups):
        view = rows.reshape(rows.shape[0], groups, RANKS, -1)
        return lax.dynamic_index_in_dim(view, self.rank, 2, keepdims=False).reshape(rows.shape[0], -1)

    def place_lanes(self, row):
        view = row.reshape(self.head_groups, 1, -1)
        at = (jnp.arange(RANKS) == self.rank).astype(row.dtype)[None, :, None]
        return (view * at).reshape(-1)


def fence(*values):
    return lax.optimization_barrier(values)


def local(
    hi_count,
    rep_count,
    tokens,
    condition,
    caption,
    caption_len,
    item_kind,
    out_cotangent,
    norm_gains,
    ada_weight,
    qkv_weight,
    out_weight,
    text_weight,
    gate_up_weight,
    down_weight,
):
    bf16, f32 = jnp.bfloat16, jnp.float32
    item_count = condition.shape[0]
    item_len = tokens.shape[0] // item_count
    row_count = item_count * item_len
    rows = qkv_weight.shape[0]
    plan = Layout(hi_count, rep_count, out_weight.shape[0])
    rank_width = HEADS // RANKS * HEAD_DIM
    hi_at, mid_at, core_at, rep_at = [lax.axis_index(name) for name in AXES]
    device_shape = (hi_count, 2, 2, rep_count)

    feed_width = FF // RANKS
    devices = hi_count * RANKS * rep_count
    block_at = (hi_at * RANKS + plan.rank) * rep_count + rep_at

    def z_gather(block):
        return lax.all_gather(block.reshape(-1, block.shape[-1]), "rep", tiled=True)

    down_z = z_gather(down_weight)
    qkv_mine = trade_ranks(plan.by_rank(qkv_weight, 3, plan.head_groups))
    qkv_mine = qkv_mine.reshape(RANKS * rows, 3 * rank_width)
    if plan.aligned:
        qkv_mine = jnp.concatenate([qkv_mine, out_weight.reshape(-1, 3 * rank_width)])
    else:
        out_whole = lax.all_gather(out_weight, AXES, axis=0, tiled=True)
        out_rank = pick(out_whole.reshape(RANKS, rank_width, D), plan.rank)

    head = condition.reshape(item_count, devices, rows)
    head = jnp.transpose(head, (1, 0, 2)).reshape(devices, -1)
    rest = jnp.concatenate(
        [norm_gains.reshape(-1), caption_len.astype(bf16), item_kind.astype(bf16)]
    )
    small = jnp.concatenate([head, jnp.broadcast_to(rest, (devices, rest.size))], axis=1)
    qkv_mine, small = fence(qkv_mine, small)
    qkv_z = z_gather(qkv_mine)
    small = lax.all_to_all(small, AXES, 0, 0, tiled=True)
    cut = [head.shape[1], head.shape[1] + norm_gains.size]
    cut.append(cut[1] + item_count)
    conditions, gains, lengths, kinds = jnp.split(small, cut, axis=-1)
    activated_mine = jax.nn.silu(conditions.astype(f32)).astype(bf16).reshape(-1, rows)
    gain_rows = jnp.moveaxis(gains.astype(f32).reshape(devices, 6, -1), 1, 0).reshape(6, D)
    lengths, kinds = [
        values.reshape(device_shape + (item_count,)) for values in (lengths, kinds)
    ]

    def group_items(values):
        view = lax.dynamic_index_in_dim(pick(values, hi_at), rep_at, 2, keepdims=False)
        near, far = pick(view, mid_at), pick(view, 1 - mid_at)
        order = [core_at, 1 - core_at]
        return [
            jnp.concatenate([pick(side, at) for at in order]).astype(jnp.int32)
            for side in (near, far)
        ]

    lengths_sides = group_items(lengths)
    kinds_sides = group_items(kinds)
    cosine, sine = rope_tables(jnp.arange(2), item_len)
    signs = jnp.where(jnp.arange(HEAD_DIM) % (HEAD_DIM // 2) < HEAD_DIM // 4, -1.0, 1.0)
    cosine, sine = jnp.tile(cosine, (1, 1, 2)), jnp.tile(sine * signs, (1, 1, 2))
    head_gains = plan.rank_lanes(gain_rows, plan.head_groups)
    cross_gate = jnp.tanh(head_gains[5])
    head_gains = jnp.concatenate([head_gains[1:4], cross_gate[None]])
    tables = (head_gains, cosine, sine)
    scalars = list(zip(kinds_sides, lengths_sides, strict=True))

    text_weight, conditions = fence(text_weight, activated_mine)
    text_mine = trade_ranks(plan.by_rank(text_weight, 2, plan.head_groups))
    partial = dot(conditions, ada_weight).astype(bf16).reshape(devices, item_count, 4 * D)
    text_mine, partial, down_z = fence(text_mine, partial, down_z)
    down_rank = plan.across_hi(down_z)
    modulation = jnp.sum(lax.all_to_all(partial, AXES, 0, 0, tiled=True).astype(f32), axis=0)
    qkv_z, down_rank, modulation, text_mine = fence(qkv_z, down_rank, modulation, text_mine)

    scale_attn, gate_attn, scale_mlp, gate_mlp = jnp.split(modulation, 4, axis=1)
    captions = plan.ordered(caption.reshape(-1, TEXT_DIM))
    text_key_z = z_gather(text_mine[..., :rank_width])
    captions_far = swap(captions, "mid")
    qkv_rank = plan.across_hi(qkv_z)
    gate_up_mine = trade_ranks(plan.by_rank(gate_up_weight, 2, hi_count))
    token_rows = tokens.astype(f32).reshape(item_count, item_len, D)
    normed = modulate(token_rows, gain_rows[0], scale_attn)
    normed = plan.ordered(normed.astype(bf16).reshape(row_count, D))
    mlp_gate = jnp.tanh(gate_mlp)[:, None, :]
    grad_top = out_cotangent.astype(f32).reshape(item_count, item_len, D)
    grad_result = (mlp_gate * grad_top).astype(bf16).reshape(row_count, D)
    text_key_z, captions_far, qkv_rank, gate_up_mine, normed, grad_result = fence(
        text_key_z, captions_far, qkv_rank, gate_up_mine, normed, grad_result
    )

    text_value_z = z_gather(text_mine[..., rank_width:])
    text_key_rank = plan.across_hi(text_key_z)
    normed_far = swap(normed, "mid")
    caption_sides = (pair(captions), pair(captions_far))
    normed_near = pair(normed)
    if plan.aligned:
        blocks = qkv_rank.reshape(hi_count, rep_count, -1, 3 * rank_width)
        out_rank = blocks[:, :, RANKS * rows :].reshape(hi_count, -1)
        if hi_count == 2:
            out_rank = jnp.where(hi_at == 0, out_rank, out_rank[::-1])
        out_rank = out_rank.reshape(rank_width, D)
        qkv_rank = blocks[:, :, : RANKS * rows]
    qkv_rank = plan.natural_rows(qkv_rank)
    text_value_z, text_key_rank, normed_far, caption_sides, normed_near, qkv_rank, out_rank = fence(
        text_value_z, text_key_rank, normed_far, caption_sides, normed_near, qkv_rank, out_rank
    )

    gate_z = z_gather(gate_up_mine[..., :feed_width])
    text_value_rank = plan.across_hi(text_value_z)
    result_far = swap(grad_result, "mid")
    normed_sides = (normed_near, pair(normed_far))
    text_key_rank = plan.natural_rows(text_key_rank)
    qkv_raw = [dot(side, qkv_rank) for side in normed_sides]
    text_key_raw = [dot(side, text_key_rank) for side in caption_sides]
    down_rank = down_rank.reshape(hi_count, -1)
    if hi_count == 2:
        down_rank = jnp.where(hi_at == 0, down_rank, down_rank[::-1])
    down_rank = down_rank.reshape(feed_width, D)
    gate_z, text_value_rank, result_far, normed_sides, qkv_raw, text_key_raw, down_rank = fence(
        gate_z, text_value_rank, result_far, normed_sides, qkv_raw, text_key_raw, down_rank
    )

    up_z = z_gather(gate_up_mine[..., feed_width:])
    gate_rank = plan.across_hi(gate_z)
    text_value_rank = plan.natural_rows(text_value_rank)
    text_value_raw = [dot(side, text_value_rank) for side in caption_sides]
    raw_near, raw_far = zip(qkv_raw, text_key_raw, text_value_raw, strict=True)
    kept_far = attend(*scalars[1], *raw_far, *tables)
    up_z, gate_rank, raw_near, raw_far, kept_far = fence(
        up_z, gate_rank, raw_near, raw_far, kept_far
    )

    across = settle_far(dot(kept_far[3], out_rank))
    across, raw_near, up_z = fence(across, raw_near, up_z)
    up_rank = plan.across_hi(up_z)
    arrived = settle_move(across)
    kept_near = attend(*scalars[0], *raw_near, *tables)
    up_rank, arrived, kept_near = fence(up_rank, arrived, kept_near)

    branch = settle_near(dot(kept_near[3], out_rank)) + arrived
    branch = branch.reshape(item_count, item_len, D)
    attn_gate = jnp.tanh(gate_attn)[:, None, :]
    middle = token_rows + attn_gate * branch
    mlp_input = modulate(middle, gain_rows[4], scale_mlp)
    mlp_input = plan.ordered(mlp_input.astype(bf16).reshape(row_count, D))
    feed_weights = (plan.natural_rows(gate_rank), plan.natural_rows(up_rank), down_rank)
    result_sides = (pair(grad_result), pair(result_far))
    input_near = pair(mlp_input)
    feed_weights, mlp_input, input_near, result_sides = fence(
        feed_weights, mlp_input, input_near, result_sides
    )

    input_far = swap(mlp_input, "mid")
    hidden_near, gate_near, up_near, partial_near = feed(input_near, result_sides[0], *feed_weights)
    input_far, hidden_near, gate_near, up_near, partial_near = fence(
        input_far, hidden_near, gate_near, up_near, partial_near
    )
    input_sides = (input_near, pair(input_far))
    hidden_far, gate_far, up_far, partial_far = feed(input_sides[1], result_sides[1], *feed_weights)
    across = settle_far(partial_far)
    across, gate_far, up_far, hidden_far = fence(across, gate_far, up_far, hidden_far)
    arrived = settle_move(across)
    gate_sides, up_sides, hidden_sides = (gate_near, gate_far), (up_near, up_far), (hidden_near, hidden_far)
    hidden_turned = [plan.ordered(side) for side in hidden_sides]
    gate_moved = plan.product_moved(input_sides, gate_sides)
    up_moved = plan.product_moved(input_sides, up_sides)
    near = settle_near(partial_near)
    arrived, gate_moved, up_moved, near = fence(arrived, gate_moved, up_moved, near)

    gate_moved = plan.move(gate_moved)
    grad_mlp_input = plan.ordered(near + arrived)
    _, pull_mlp_norm = jax.vjp(modulate, middle, gain_rows[4], scale_mlp)
    grad_middle_norm, grad_mlp_gain, grad_scale_mlp = pull_mlp_norm(
        grad_mlp_input.reshape(item_count, item_len, D)
    )
    grad_middle = grad_top + grad_middle_norm
    grad_attn_gate = jnp.sum(grad_middle * branch, axis=1) * (1.0 - jnp.tanh(gate_attn) ** 2)
    grad_branch = (attn_gate * grad_middle).astype(bf16).reshape(row_count, D)
    branch_near = pair(grad_branch)
    mixed_near = dot_right(branch_near, out_rank)
    gate_kept = plan.product_kept(input_sides, gate_sides)
    gate_moved, gate_kept, grad_branch, branch_near, mixed_near = fence(
        gate_moved, gate_kept, grad_branch, branch_near, mixed_near
    )

    def attention_back(at, kept, raw, grad_mixed):
        queries, key_rows, text_keys, _, read = kept
        return attend_back(
            *scalars[at], *raw, *tables, queries, key_rows, text_keys, read, grad_mixed
        )

    gate_grad = plan.by_rep(plan.total(gate_kept, gate_moved))
    gate_grad, up_moved, grad_branch, mixed_near = fence(
        gate_grad, up_moved, grad_branch, mixed_near
    )
    gate_parts = plan.reduce(gate_grad)
    branch_far = swap(grad_branch, "mid")
    up_moved = plan.move(up_moved)
    qkv_near, text_near, gain_near = attention_back(0, kept_near, raw_near, mixed_near)
    branch_far, up_moved, qkv_near, text_near, gain_near = fence(
        branch_far, up_moved, qkv_near, text_near, gain_near
    )

    branch_sides = (branch_near, pair(branch_far))
    up_grad = plan.by_rep(plan.total(plan.product_kept(input_sides, up_sides), up_moved))
    mixed_far = dot_right(branch_sides[1], out_rank)
    down_moved = plan.product_moved(hidden_turned, result_sides)
    up_grad, mixed_far, down_moved = fence(up_grad, mixed_far, down_moved)
    up_parts = plan.reduce(up_grad)
    down_moved = plan.move(down_moved)
    qkv_far, text_far, gain_far = attention_back(1, kept_far, raw_far, mixed_far)
    down_moved, qkv_far, text_far, gain_far = fence(down_moved, qkv_far, text_far, gain_far)

    text_sides, qkv_sides, mixed_sides = (text_near, text_far), (qkv_near, qkv_far), (kept_near[3], kept_far[3])
    mixed_sides = [plan.ordered(side) for side in mixed_sides]
    down_kept = plan.product_kept(hidden_turned, result_sides)
    down_grad = plan.total(down_kept, down_moved).reshape(rep_count, -1, D)
    across = settle_far(dot_right(qkv_far, qkv_rank))
    text_moved = plan.product_moved(caption_sides, text_sides)
    down_grad, across, text_moved, hidden_sides = fence(down_grad, across, text_moved, hidden_sides)
    down_weight_grad = plan.reduce(down_grad).astype(f32)
    arrived = settle_move(across)
    text_moved = plan.move(text_moved)
    text_kept = plan.product_kept(caption_sides, text_sides)
    qkv_moved = plan.product_moved(normed_sides, qkv_sides)
    grad_normed = settle_near(dot_right(qkv_near, qkv_rank))
    partial_result = [dot(side, down_rank) for side in hidden_sides]
    result_near, across = settle_near(partial_result[0]), settle_far(partial_result[1])
    if plan.aligned:
        out_moved = plan.product_moved(mixed_sides, branch_sides)
    if plan.aligned and hi_count == 2:
        qkv_moved = jnp.concatenate([qkv_moved.reshape(-1), out_moved.reshape(-1)])
        qkv_moved = qkv_moved.reshape(-1, 3 * rank_width)
    arrived, text_moved, text_kept, qkv_moved, grad_normed, result_near, across = fence(
        arrived, text_moved, text_kept, qkv_moved, grad_normed, result_near, across
    )

    text_grad = plan.by_rep(plan.total(text_kept, text_moved))
    text_grad, qkv_moved, grad_normed, across = fence(text_grad, qkv_moved, grad_normed, across)
    text_parts = plan.reduce(text_grad)
    qkv_moved = plan.move(qkv_moved)
    if plan.aligned and hi_count != 2:
        out_moved = plan.move(out_moved)
    result = (result_near + settle_move(across)).reshape(item_count, item_len, D)
    layer_out = (middle + mlp_gate * result).astype(bf16).reshape(row_count, D)
    grad_mlp_gate = jnp.sum(grad_top * result, axis=1) * (1.0 - jnp.tanh(gate_mlp) ** 2)
    grad_normed = plan.ordered(grad_normed + arrived)
    _, pull_attn_norm = jax.vjp(modulate, token_rows, gain_rows[0], scale_attn)
    grad_token_norm, grad_attn_gain, grad_scale_attn = pull_attn_norm(
        grad_normed.reshape(item_count, item_len, D)
    )
    tokens_grad = (grad_middle + grad_token_norm).reshape(row_count, D)
    qkv_kept = plan.product_kept(normed_sides, qkv_sides)
    if plan.aligned:
        out_kept = plan.product_kept(mixed_sides, branch_sides)
        if out_kept is not None:
            split = qkv_kept.shape[0]
            qkv_moved, out_moved = qkv_moved[:split], qkv_moved[split:].reshape(out_kept.shape)
        qkv_grad = plan.total(qkv_kept, qkv_moved)
        out_grad = plan.total(out_kept, out_moved)
        qkv_grad = jnp.concatenate(
            [plan.by_rep(qkv_grad), out_grad.reshape(rep_count, -1, 3 * rank_width)], axis=1
        )
    else:
        qkv_grad = plan.by_rep(plan.total(qkv_kept, qkv_moved))
        at = (jnp.arange(RANKS) == plan.rank).astype(bf16)[:, None, None]
        out_grad = plan.product(mixed_sides, branch_sides, lambda left: left)
        placed = (out_grad.astype(bf16)[None] * at).reshape(D, D)
        out_weight_grad = lax.psum_scatter(placed, AXES, scatter_dimension=0, tiled=True).astype(f32)
    qkv_parts = plan.reduce(qkv_grad)
    if plan.aligned:
        out_weight_grad = qkv_parts[RANKS * rows :].reshape(-1, D).astype(f32)
        qkv_parts = qkv_parts[: RANKS * rows]

    grad_modulation = jnp.concatenate(
        [grad_scale_attn, grad_attn_gate, grad_scale_mlp, grad_mlp_gate], axis=1
    ).astype(bf16)
    gain_terms = gain_near + gain_far
    gain_terms = gain_terms.at[3].multiply(1.0 - cross_gate**2)
    gain_terms = [plan.place_lanes(row) for row in gain_terms]
    gains_grad = jnp.stack(
        [grad_attn_gain, gain_terms[0], gain_terms[1], gain_terms[2], grad_mlp_gain, gain_terms[3]]
    ).astype(bf16)
    gain_blocks = jnp.moveaxis(gains_grad.reshape(6, devices, -1), 1, 0).reshape(devices, -1)
    modulations = jnp.broadcast_to(grad_modulation.reshape(-1), (devices, grad_modulation.size))
    both = lax.all_to_all(
        jnp.concatenate([modulations, gain_blocks], axis=1), AXES, 0, 0, tiled=True
    )
    ada_weight_grad = dot_left(activated_mine, both[:, : modulations.shape[1]].reshape(-1, 4 * D))
    norm_gains_grad = jnp.sum(both[:, modulations.shape[1] :].astype(f32), axis=0).reshape(6, -1)

    def whole(parts, weight, sections, groups):
        blocks = trade_ranks(parts.reshape(RANKS, weight.shape[0], -1))
        return plan.from_ranks(blocks, sections, groups).astype(f32)

    gate_up_weight_grad = whole(
        jnp.concatenate([gate_parts, up_parts], axis=-1), gate_up_weight, 2, hi_count
    )
    text_weight_grad = whole(text_parts, text_weight, 2, plan.head_groups)
    qkv_weight_grad = whole(qkv_parts, qkv_weight, 3, plan.head_groups)
    return (
        layer_out,
        tokens_grad,
        norm_gains_grad,
        ada_weight_grad,
        qkv_weight_grad,
        out_weight_grad,
        text_weight_grad,
        gate_up_weight_grad,
        down_weight_grad,
    )


def solution(mesh):
    grp, rep = mesh.devices.shape
    hi = grp // RANKS
    inner = Mesh(mesh.devices.reshape(hi, 2, 2, rep), AXES)
    rows = P(AXES, None)

    def step(*arrays):
        return local(hi, rep, *arrays)

    return jax.shard_map(
        step,
        mesh=inner,
        in_specs=(
            rows,
            rows,
            P(AXES, None, None),
            P(AXES),
            P(AXES),
            rows,
            P(None, AXES),
            rows,
            rows,
            rows,
            rows,
            rows,
            rows,
        ),
        out_specs=(rows, rows, P(None, AXES), rows, rows, rows, rows, rows, rows),
        check_vma=False,
    )
```

```python
import math

import jax
import jax.numpy as jnp
from jax import lax
from jax.experimental import pallas as pl
from jax.experimental.pallas import tpu as pltpu
from jax.sharding import Mesh
from jax.sharding import PartitionSpec as P

D = 1536
HEADS = 24
HEAD_DIM = 64
TEXT_DIM = 4096
FF = 4096
SIDE = 16
RANKS = 4
LANES = 128
MIB = 1 << 20
AXES = ("hi", "mid", "core", "rep")


EPSILON = 1e-06


def norm_rows(values, gain_row):
    return (
        values * lax.rsqrt(jnp.mean(values * values, axis=-1, keepdims=True) + EPSILON) * gain_row
    )


def rope_tables(item_kind, item_len):
    position = jnp.arange(item_len, dtype=jnp.int32)[None, :]
    half_side = SIDE // 2
    frame_index = position // (half_side * half_side)
    within = position % (half_side * half_side)
    is_clip = item_kind[:, None] == 1
    row_index = jnp.where(is_clip, frame_index * half_side + within // half_side, position // SIDE)
    columns = jnp.where(is_clip, within % half_side, position % SIDE)
    lane_index = jnp.arange(HEAD_DIM, dtype=jnp.int32)
    quarter = HEAD_DIM // 4
    frequency = jnp.exp(-(lane_index % quarter).astype(jnp.float32) * (math.log(10000.0) / quarter))
    coordinate = jnp.where(
        lane_index[None, None, :] < 2 * quarter, row_index[:, :, None], columns[:, :, None]
    ).astype(jnp.float32)
    angles = coordinate * frequency
    return (jnp.cos(angles), jnp.sin(angles))


def modulate(values, gain_row, scaling):
    return norm_rows(values, gain_row) * (1.0 + scaling[:, None, :])


def silu_product(gate_half, up_half):
    return jax.nn.silu(gate_half) * up_half


def dot(left, right):
    return jnp.dot(left, right, preferred_element_type=jnp.float32)


def dot_left(left, right):
    return lax.dot_general(left, right, (((0,), (0,)), ((), ())), preferred_element_type=jnp.float32)


def dot_right(left, right):
    return lax.dot_general(left, right, (((1,), (1,)), ((), ())), preferred_element_type=jnp.float32)


def lane_index(shape):
    return lax.broadcasted_iota(jnp.int32, shape, len(shape) - 1)

def head_sums(values):
    first = lane_index(values.shape) < HEAD_DIM
    low = jnp.sum(jnp.where(first, values, 0.0), axis=-1, keepdims=True)
    high = jnp.sum(jnp.where(first, 0.0, values), axis=-1, keepdims=True)
    return jnp.where(first, low, high)

def partner(values):
    quarter = HEAD_DIM // 4
    width = values.shape[-1]
    low = lane_index(values.shape) % (2 * quarter) < quarter
    return jnp.where(low, pltpu.roll(values, width - quarter, 1), pltpu.roll(values, quarter, 1))

def stack_heads(values):
    first = lane_index(values.shape) < HEAD_DIM
    zero = jnp.zeros_like(values)
    return jnp.concatenate([jnp.where(first, values, zero), jnp.where(first, zero, values)])

def join_heads(stacked):
    rows = stacked.shape[0] // 2
    first = lane_index((rows, stacked.shape[1])) < HEAD_DIM
    return jnp.where(first, stacked[:rows], stacked[rows:])

def inverse_rms(raw):
    return lax.rsqrt(head_sums(raw * raw) * (1.0 / HEAD_DIM) + EPSILON)

def attend_kernel(
    kind_ref,
    len_ref,
    rows_ref,
    caption_ref,
    qkv_weight_ref,
    key_weight_ref,
    value_weight_ref,
    out_weight_ref,
    gain_ref,
    cos_ref,
    sin_ref,
    qkv_ref,
    text_ref,
    text_value_ref,
    q_ref,
    k_ref,
    tk_ref,
    mixed_ref,
    read_ref,
    branch_ref,
):
    item = pl.program_id(0)
    kind, length = kind_ref[item], len_ref[item]
    width = q_ref.shape[1]
    cosine, sine = cos_ref[kind], sin_ref[kind]
    scaling = HEAD_DIM ** (-0.5)
    qkv_ref[...] = dot(rows_ref[...], qkv_weight_ref[...])
    text_ref[...] = dot(caption_ref[...], key_weight_ref[...])
    text_value_ref[...] = dot(caption_ref[...], value_weight_ref[...])
    for at in range(0, width, LANES):
        lanes = slice(at, at + LANES)
        turned = []
        for part, out_ref in ((0, q_ref), (1, k_ref)):
            raw = qkv_ref[:, part * width + at : part * width + at + LANES]
            normal = raw * inverse_rms(raw) * gain_ref[part : part + 1, lanes]
            rows = (normal * cosine + partner(normal) * sine).astype(jnp.bfloat16)
            out_ref[:, lanes] = rows
            turned.append(rows)
        queries, keys = turned
        values = qkv_ref[:, 2 * width + at : 2 * width + at + LANES].astype(jnp.bfloat16)
        text_raw = text_ref[:, lanes]
        text_keys = (text_raw * inverse_rms(text_raw) * gain_ref[2:3, lanes]).astype(jnp.bfloat16)
        tk_ref[:, lanes] = text_keys
        text_values = text_value_ref[:, lanes].astype(jnp.bfloat16)
        stacked = stack_heads(queries)
        own = dot_right(stacked, keys) * scaling
        own = jnp.exp(own - jnp.max(own, axis=-1, keepdims=True))
        own_out = dot(own.astype(jnp.bfloat16), values) / jnp.sum(own, axis=-1, keepdims=True)
        text = dot_right(stacked, text_keys) * scaling
        text = jnp.where(lane_index(text.shape) < length, text, -1e30)
        text = jnp.exp(text - jnp.max(text, axis=-1, keepdims=True))
        text_out = dot(text.astype(jnp.bfloat16), text_values) / jnp.sum(text, axis=-1, keepdims=True)
        read = join_heads(text_out)
        read_ref[:, lanes] = read
        mixed_ref[:, lanes] = (join_heads(own_out) + gain_ref[3:4, lanes] * read).astype(jnp.bfloat16)
    branch_ref[...] = dot(mixed_ref[...], out_weight_ref[...])


def head_norm_back(grad, raw, gain_row):
    inverse = inverse_rms(raw)
    scaled = grad * gain_row
    normal = raw * inverse
    inner = head_sums(scaled * normal) * (1.0 / HEAD_DIM)
    return inverse * (scaled - normal * inner), jnp.sum(grad * normal, axis=0, keepdims=True)

def attend_back_kernel(
    kind_ref,
    len_ref,
    branch_ref,
    qkv_ref,
    text_ref,
    text_value_ref,
    q_ref,
    k_ref,
    tk_ref,
    read_ref,
    qkv_weight_ref,
    out_weight_ref,
    gain_ref,
    cos_ref,
    sin_ref,
    gqkv_ref,
    gtext_ref,
    grad_rows_ref,
    gains_ref,
):
    item = pl.program_id(0)
    kind, length = kind_ref[item], len_ref[item]
    width = q_ref.shape[1]
    cosine, sine = cos_ref[kind], sin_ref[kind]
    scaling = HEAD_DIM ** (-0.5)
    grad_mixed = dot_right(branch_ref[...], out_weight_ref[...])

    @pl.when(item == 0)
    def _():
        gains_ref[...] = jnp.zeros_like(gains_ref)

    def one(stacked, keys, values, stacked_grad, valid):
        scores = dot_right(keys, stacked) * scaling
        if valid is not None:
            scores = jnp.where(valid(scores.shape), scores, -1e30)
        probs = jnp.exp(scores - jnp.max(scores, axis=0, keepdims=True))
        probs = probs * (1.0 / jnp.sum(probs, axis=0, keepdims=True))
        grad_values = dot(probs.astype(jnp.bfloat16), stacked_grad)
        grad_probs = dot_right(values, stacked_grad)
        inner = jnp.sum(probs * grad_probs, axis=0, keepdims=True)
        grad_scores = (probs * (grad_probs - inner)).astype(jnp.bfloat16)
        grad_keys = dot(grad_scores, stacked) * scaling
        grad_queries = dot_left(keys, grad_scores)
        return grad_queries, grad_keys, grad_values

    for at in range(0, width, LANES):
        lanes = slice(at, at + LANES)
        grad = grad_mixed[:, lanes]
        cross = gain_ref[3:4, lanes]
        values = qkv_ref[:, 2 * width + at : 2 * width + at + LANES].astype(jnp.bfloat16)
        text_values = text_value_ref[:, lanes].astype(jnp.bfloat16)
        stacked = stack_heads(q_ref[:, lanes])
        own_queries, own_keys, own_values = one(
            stacked, k_ref[:, lanes], values, stack_heads(grad.astype(jnp.bfloat16)), None
        )
        read_queries, read_keys, read_values = one(
            stacked, tk_ref[:, lanes], text_values, stack_heads((cross * grad).astype(jnp.bfloat16)),
            lambda shape: lax.broadcasted_iota(jnp.int32, shape, 0) < length,
        )
        grad_queries = join_heads((own_queries + read_queries).T) * scaling
        for part, turned in ((0, grad_queries), (1, own_keys)):
            raw = qkv_ref[:, part * width + at : part * width + at + LANES]
            back = turned * cosine + partner(turned * sine)
            grad_raw, gain = head_norm_back(back, raw, gain_ref[part : part + 1, lanes])
            gqkv_ref[:, part * width + at : part * width + at + LANES] = grad_raw.astype(jnp.bfloat16)
            gains_ref[part : part + 1, lanes] += gain
        gqkv_ref[:, 2 * width + at : 2 * width + at + LANES] = own_values.astype(jnp.bfloat16)
        grad_text, gain = head_norm_back(read_keys, text_ref[:, lanes], gain_ref[2:3, lanes])
        gtext_ref[:, lanes] = grad_text.astype(jnp.bfloat16)
        gains_ref[2:3, lanes] += gain
        gtext_ref[:, width + at : width + at + LANES] = read_values.astype(jnp.bfloat16)
        gains_ref[3:4, lanes] += jnp.sum(grad * read_ref[:, lanes], axis=0, keepdims=True)
    grad_rows_ref[...] = dot_right(gqkv_ref[...], qkv_weight_ref[...])

def item_call(kernel, scalars, by_item, whole, outs, summed, name):
    items = scalars[0].shape[0]

    def cut(array):
        return pl.BlockSpec((array.shape[0] // items, array.shape[1]), lambda i, *_: (i, 0))

    def all_of(array):
        zeros = (0,) * len(array.shape)
        return pl.BlockSpec(array.shape, lambda i, *_: zeros, pipeline_mode=pl.Buffered(1))

    return pl.pallas_call(
        kernel,
        grid_spec=pltpu.PrefetchScalarGridSpec(
            num_scalar_prefetch=len(scalars),
            grid=(items,),
            in_specs=[cut(array) for array in by_item] + [all_of(array) for array in whole],
            out_specs=[cut(array) for array in outs]
            + [pl.BlockSpec(array.shape, lambda i, *_: (0, 0)) for array in summed],
        ),
        out_shape=outs + summed,
        compiler_params=pltpu.CompilerParams(
            dimension_semantics=("arbitrary",), vmem_limit_bytes=56 * MIB
        ),
        name=name,
    )(*scalars, *by_item, *whole)


def attend(scalars, rows, captions, qkv_rank, key_rank, value_rank, out_rank, tables):
    count, width = rows.shape[0], key_rank.shape[1]
    text_count = captions.shape[0]

    def shape(count, columns, dtype=jnp.bfloat16):
        return jax.ShapeDtypeStruct((count, columns), dtype)

    outs = [
        shape(count, 3 * width, jnp.float32),
        shape(text_count, width, jnp.float32),
        shape(text_count, width, jnp.float32),
        shape(count, width),
        shape(count, width),
        shape(text_count, width),
        shape(count, width),
        shape(count, width, jnp.float32),
        shape(count, D, jnp.float32),
    ]
    whole = [qkv_rank, key_rank, value_rank, out_rank, *tables]
    *kept, branch = item_call(attend_kernel, scalars, [rows, captions], whole, outs, [], "attend")
    return kept, branch


def attend_back(scalars, grad_branch, kept, qkv_rank, out_rank, tables):
    qkv_raw, text_raw, text_value_raw, queries, keys, text_keys, _, read = kept
    count, width = queries.shape
    outs = [
        jax.ShapeDtypeStruct((count, 3 * width), jnp.bfloat16),
        jax.ShapeDtypeStruct((text_raw.shape[0], 2 * width), jnp.bfloat16),
        jax.ShapeDtypeStruct((count, D), jnp.float32),
    ]
    by_item = [grad_branch, qkv_raw, text_raw, text_value_raw, queries, keys, text_keys, read]
    summed = [jax.ShapeDtypeStruct((4, width), jnp.float32)]
    whole = [qkv_rank, out_rank, *tables]
    return item_call(attend_back_kernel, scalars, by_item, whole, outs, summed, "attend_back")


def product_kernel(first_ref, left_near, left_far, right_near, right_far, out_ref):
    near = dot_left(left_near[...], right_near[...])
    out_ref[...] = (near + dot_left(left_far[...], right_far[...])).astype(out_ref.dtype)


def product(left_sides, right_sides, first, lanes, dtype):
    count, columns = right_sides[0].shape
    block = math.gcd(lanes, 384) if lanes % 384 == 0 else math.gcd(lanes, 512)
    cut = pl.BlockSpec((count, block), lambda i, first: (0, first[0] // block + i))
    whole = pl.BlockSpec((count, columns), lambda i, first: (0, 0), pipeline_mode=pl.Buffered(1))
    return pl.pallas_call(
        product_kernel,
        grid_spec=pltpu.PrefetchScalarGridSpec(
            num_scalar_prefetch=1,
            grid=(lanes // block,),
            in_specs=[cut, cut, whole, whole],
            out_specs=pl.BlockSpec((block, columns), lambda i, first: (i, 0)),
        ),
        out_shape=jax.ShapeDtypeStruct((lanes, columns), dtype),
        compiler_params=pltpu.CompilerParams(
            dimension_semantics=("arbitrary",), vmem_limit_bytes=48 * MIB
        ),
        name="product",
    )(jnp.reshape(first, (1,)).astype(jnp.int32), *left_sides, *right_sides)


def feed_kernel(input_ref, result_ref, gate_ref, up_ref, down_ref, hidden_ref, grad_gate_ref, grad_up_ref, grad_ref):
    rows = input_ref[...]
    gate = dot(rows, gate_ref[...])
    up = dot(rows, up_ref[...])
    grad_hidden = dot_right(result_ref[...], down_ref[...])
    sigmoid = 1.0 / (1.0 + jnp.exp(-gate))
    silu = gate * sigmoid
    hidden_ref[...] = (silu * up).astype(jnp.bfloat16)
    grad_gate = (grad_hidden * up * (sigmoid + silu * (1.0 - sigmoid))).astype(jnp.bfloat16)
    grad_up = (grad_hidden * silu).astype(jnp.bfloat16)
    grad_gate_ref[...] = grad_gate
    grad_up_ref[...] = grad_up
    grad_ref[...] = dot_right(grad_gate, gate_ref[...]) + dot_right(grad_up, up_ref[...])


def feed(rows, grad_result, gate_rank, up_rank, down_rank):
    count, width = rows.shape[0], gate_rank.shape[1]
    block = 256

    def cut(columns):
        return pl.BlockSpec((block, columns), lambda i: (i, 0))

    def whole(array):
        return pl.BlockSpec(array.shape, lambda i: (0, 0), pipeline_mode=pl.Buffered(1))

    hidden = jax.ShapeDtypeStruct((count, width), jnp.bfloat16)
    return pl.pallas_call(
        feed_kernel,
        grid=(count // block,),
        in_specs=[cut(D), cut(D), whole(gate_rank), whole(up_rank), whole(down_rank)],
        out_specs=[cut(width), cut(width), cut(width), cut(D)],
        out_shape=[hidden, hidden, hidden, jax.ShapeDtypeStruct((count, D), jnp.float32)],
        compiler_params=pltpu.CompilerParams(
            dimension_semantics=("arbitrary",), vmem_limit_bytes=56 * MIB
        ),
        name="feed",
    )(rows, grad_result, gate_rank, up_rank, down_rank)


def swap(block, axis, count=2, step=1):
    return lax.ppermute(block, axis, [(at, at ^ step) for at in range(count)])


def spread(block, axis, count):
    if count & (count - 1):
        return lax.all_gather(block, axis)
    block, step = block[None], 1
    while step < count:
        other = swap(block, axis, count, step)
        low = (lax.axis_index(axis) & step) == 0
        block = jnp.where(
            low, jnp.concatenate([block, other]), jnp.concatenate([other, block])
        )
        step *= 2
    return block


def fold(block, axis, count):
    if count & (count - 1):
        return lax.psum_scatter(block, axis, scatter_dimension=0)
    step = count // 2
    while step:
        half = block.shape[0] // 2
        low = (lax.axis_index(axis) & step) == 0
        lower, upper = block[:half], block[half:]
        block = jnp.where(low, lower, upper) + swap(
            jnp.where(low, upper, lower), axis, count, step
        )
        step //= 2
    return block[0]


def trade_ranks(block):
    return lax.all_to_all(block, ("mid", "core"), 0, 0, tiled=True)


def pick(stack, index):
    return lax.dynamic_index_in_dim(stack, index, 0, keepdims=False)


def pair(rows):
    return jnp.concatenate([rows, swap(rows, "core")])


def settle_far(far):
    half = far.shape[0] // 2
    return far[:half] + swap(far[half:].astype(jnp.bfloat16), "core").astype(jnp.float32)


def settle_near(near):
    half = near.shape[0] // 2
    return near[:half] + swap(near[half:].astype(jnp.bfloat16), "core").astype(jnp.float32)


def settle_move(across):
    return swap(across.astype(jnp.bfloat16), "mid").astype(jnp.float32)


class Layout:
    def __init__(self, hi, rep, out_rows):
        self.hi, self.rep = hi, rep
        self.aligned = (rep * out_rows) % HEAD_DIM == 0
        self.head_groups = hi if self.aligned else 1
        self.rank = lax.axis_index("mid") * 2 + lax.axis_index("core")

    def by_rank(self, weight, sections, groups):
        rows, columns = weight.shape
        width = columns // (sections * groups * RANKS)
        view = weight.reshape(rows, sections * groups, RANKS, width)
        view = jnp.transpose(view, (2, 0, 1, 3))
        return view.reshape(RANKS, rows, sections * groups * width)

    def from_ranks(self, blocks, sections, groups):
        _, rows, per_rank = blocks.shape
        width = per_rank // (sections * groups)
        view = blocks.reshape(RANKS, rows, sections * groups, width)
        return jnp.transpose(view, (1, 2, 0, 3)).reshape(rows, RANKS * per_rank)

    def ordered(self, values):
        if self.hi != 2:
            return values
        half = values.shape[-1] // 2
        turned = jnp.concatenate([values[..., half:], values[..., :half]], axis=-1)
        return jnp.where(lax.axis_index("hi") == 0, values, turned)

    def across_hi(self, block):
        if self.hi == 2:
            return jnp.stack([block, swap(block, "hi")])
        return spread(block, "hi", self.hi)

    def natural_hi(self, stacked):
        if self.hi != 2:
            return stacked
        mine, other = stacked[0], stacked[1]
        low = lax.axis_index("hi") == 0
        return jnp.stack([jnp.where(low, mine, other), jnp.where(low, other, mine)])

    def natural_rows(self, stacked):
        view = stacked.reshape(self.hi, self.rep, RANKS, -1, stacked.shape[-1])
        return jnp.transpose(view, (0, 2, 1, 3, 4)).reshape(-1, stacked.shape[-1])

    def product_moved(self, left_sides, right_sides, first=None):
        lanes = left_sides[0].shape[1]
        if self.hi != 2:
            return product(left_sides, right_sides, 0, lanes, jnp.bfloat16)
        first = lanes // 2 if first is None else first
        return product(left_sides, right_sides, first, lanes // 2, jnp.bfloat16)

    def move(self, moved):
        if self.hi == 2:
            return swap(moved, "hi")
        return fold(moved.reshape(self.hi, -1, moved.shape[1]), "hi", self.hi)

    def product_kept(self, left_sides, right_sides, first=0):
        if self.hi != 2:
            return None
        return product(left_sides, right_sides, first, left_sides[0].shape[1] // 2, jnp.float32)

    def total(self, kept, arrived):
        if kept is None:
            return arrived
        return (kept + arrived.astype(jnp.float32)).astype(jnp.bfloat16)

    def by_rep(self, summed):
        view = summed.reshape(RANKS, self.rep, -1, summed.shape[1])
        return jnp.transpose(view, (1, 0, 2, 3)).reshape(self.rep, -1, summed.shape[1])

    def reduce(self, blocks):
        flat = blocks.reshape(-1, blocks.shape[-1])
        return lax.psum_scatter(flat, "rep", scatter_dimension=0, tiled=True)

    def rank_lanes(self, rows, groups):
        view = rows.reshape(rows.shape[0], groups, RANKS, -1)
        return lax.dynamic_index_in_dim(view, self.rank, 2, keepdims=False).reshape(rows.shape[0], -1)

    def place_lanes(self, row):
        view = row.reshape(self.head_groups, 1, -1)
        at = (jnp.arange(RANKS) == self.rank).astype(row.dtype)[None, :, None]
        return (view * at).reshape(-1)


def fence(*values):
    return lax.optimization_barrier(values)


def local(
    hi_count,
    rep_count,
    tokens,
    condition,
    caption,
    caption_len,
    item_kind,
    out_cotangent,
    norm_gains,
    ada_weight,
    qkv_weight,
    out_weight,
    text_weight,
    gate_up_weight,
    down_weight,
):
    bf16, f32 = jnp.bfloat16, jnp.float32
    item_count = condition.shape[0]
    item_len = tokens.shape[0] // item_count
    row_count = item_count * item_len
    rows = qkv_weight.shape[0]
    plan = Layout(hi_count, rep_count, out_weight.shape[0])
    rank_width = HEADS // RANKS * HEAD_DIM
    hi_at, mid_at, core_at, rep_at = [lax.axis_index(name) for name in AXES]
    device_shape = (hi_count, 2, 2, rep_count)

    feed_width = FF // RANKS
    devices = hi_count * RANKS * rep_count
    block_at = (hi_at * RANKS + plan.rank) * rep_count + rep_at

    def z_gather(block):
        return lax.all_gather(block.reshape(-1, block.shape[-1]), "rep", tiled=True)

    qkv_mine = trade_ranks(plan.by_rank(qkv_weight, 3, plan.head_groups))
    qkv_mine = qkv_mine.reshape(RANKS * rows, 3 * rank_width)
    if plan.aligned:
        qkv_mine = jnp.concatenate([qkv_mine, out_weight.reshape(-1, 3 * rank_width)])
    else:
        out_whole = lax.all_gather(out_weight, AXES, axis=0, tiled=True)
        out_rank = pick(out_whole.reshape(RANKS, rank_width, D), plan.rank)

    head = condition.reshape(item_count, devices, rows)
    head = jnp.transpose(head, (1, 0, 2)).reshape(devices, -1)
    rest = jnp.concatenate(
        [norm_gains.reshape(-1), caption_len.astype(bf16), item_kind.astype(bf16)]
    )
    small = jnp.concatenate([head, jnp.broadcast_to(rest, (devices, rest.size))], axis=1)
    qkv_mine, small = fence(qkv_mine, small)
    qkv_z = z_gather(qkv_mine)
    small = lax.all_to_all(small, AXES, 0, 0, tiled=True)
    cut = [head.shape[1], head.shape[1] + norm_gains.size]
    cut.append(cut[1] + item_count)
    conditions, gains, lengths, kinds = jnp.split(small, cut, axis=-1)
    activated_mine = jax.nn.silu(conditions.astype(f32)).astype(bf16).reshape(-1, rows)
    gain_rows = jnp.moveaxis(gains.astype(f32).reshape(devices, 6, -1), 1, 0).reshape(6, D)
    lengths, kinds = [
        values.reshape(device_shape + (item_count,)) for values in (lengths, kinds)
    ]

    def group_items(values):
        view = lax.dynamic_index_in_dim(pick(values, hi_at), rep_at, 2, keepdims=False)
        near, far = pick(view, mid_at), pick(view, 1 - mid_at)
        order = [core_at, 1 - core_at]
        return [
            jnp.concatenate([pick(side, at) for at in order]).astype(jnp.int32)
            for side in (near, far)
        ]

    lengths_sides = group_items(lengths)
    kinds_sides = group_items(kinds)
    cosine, sine = rope_tables(jnp.arange(2), item_len)
    signs = jnp.where(jnp.arange(HEAD_DIM) % (HEAD_DIM // 2) < HEAD_DIM // 4, -1.0, 1.0)
    cosine, sine = jnp.tile(cosine, (1, 1, 2)), jnp.tile(sine * signs, (1, 1, 2))
    head_gains = plan.rank_lanes(gain_rows, plan.head_groups)
    cross_gate = jnp.tanh(head_gains[5])
    head_gains = jnp.concatenate([head_gains[1:4], cross_gate[None]])
    tables = (head_gains, cosine, sine)
    scalars = list(zip(kinds_sides, lengths_sides, strict=True))

    text_weight, conditions = fence(text_weight, activated_mine)
    text_mine = trade_ranks(plan.by_rank(text_weight, 2, plan.head_groups))
    partial = dot(conditions, ada_weight).astype(bf16).reshape(devices, item_count, 4 * D)
    text_mine, partial = fence(text_mine, partial)
    modulation = jnp.sum(lax.all_to_all(partial, AXES, 0, 0, tiled=True).astype(f32), axis=0)
    qkv_z, modulation, text_mine = fence(qkv_z, modulation, text_mine)

    scale_attn, gate_attn, scale_mlp, gate_mlp = jnp.split(modulation, 4, axis=1)
    captions = plan.ordered(caption.reshape(-1, TEXT_DIM))
    text_key_z = z_gather(text_mine[..., :rank_width])
    captions_far = swap(captions, "mid")
    qkv_rank = plan.across_hi(qkv_z)
    gate_up_mine = trade_ranks(plan.by_rank(gate_up_weight, 2, hi_count))
    token_rows = tokens.astype(f32).reshape(item_count, item_len, D)
    normed = modulate(token_rows, gain_rows[0], scale_attn)
    normed = plan.ordered(normed.astype(bf16).reshape(row_count, D))
    mlp_gate = jnp.tanh(gate_mlp)[:, None, :]
    grad_top = out_cotangent.astype(f32).reshape(item_count, item_len, D)
    grad_result = (mlp_gate * grad_top).astype(bf16).reshape(row_count, D)
    text_key_z, captions_far, qkv_rank, gate_up_mine, normed, grad_result = fence(
        text_key_z, captions_far, qkv_rank, gate_up_mine, normed, grad_result
    )

    text_value_z = z_gather(text_mine[..., rank_width:])
    text_key_rank = plan.across_hi(text_key_z)
    normed_far = swap(normed, "mid")
    caption_sides = (pair(captions), pair(captions_far))
    normed_near = pair(normed)
    if plan.aligned:
        blocks = qkv_rank.reshape(hi_count, rep_count, -1, 3 * rank_width)
        out_rank = plan.natural_hi(blocks[:, :, RANKS * rows :]).reshape(rank_width, D)
        qkv_rank = blocks[:, :, : RANKS * rows]
    qkv_rank = plan.natural_rows(qkv_rank)
    text_value_z, text_key_rank, normed_far, caption_sides, normed_near, qkv_rank, out_rank = fence(
        text_value_z, text_key_rank, normed_far, caption_sides, normed_near, qkv_rank, out_rank
    )

    gate_z = z_gather(gate_up_mine[..., :feed_width])
    text_value_rank = plan.across_hi(text_value_z)
    result_far = swap(grad_result, "mid")
    normed_sides = (normed_near, pair(normed_far))
    text_key_rank = plan.natural_rows(text_key_rank)
    gate_z, text_value_rank, result_far, normed_sides, text_key_rank = fence(
        gate_z, text_value_rank, result_far, normed_sides, text_key_rank
    )

    up_z = z_gather(gate_up_mine[..., feed_width:])
    gate_rank = plan.across_hi(gate_z)
    text_value_rank = plan.natural_rows(text_value_rank)
    attend_weights = (qkv_rank, text_key_rank, text_value_rank, out_rank, tables)
    kept_far, branch_far = attend(scalars[1], normed_sides[1], caption_sides[1], *attend_weights)
    up_z, gate_rank, kept_far, branch_far, attend_weights = fence(
        up_z, gate_rank, kept_far, branch_far, attend_weights
    )

    across = settle_far(branch_far)
    across, normed_near, up_z = fence(across, normed_sides[0], up_z)
    normed_sides = (normed_near, normed_sides[1])
    down_z = z_gather(down_weight)
    up_rank = plan.across_hi(up_z)
    arrived = settle_move(across)
    kept_near, branch_near = attend(scalars[0], normed_near, caption_sides[0], *attend_weights)
    result_sides = (pair(grad_result), pair(result_far))
    gate_rank = plan.natural_rows(gate_rank)
    down_z, up_rank, arrived, kept_near, branch_near, result_sides, gate_rank = fence(
        down_z, up_rank, arrived, kept_near, branch_near, result_sides, gate_rank
    )

    down_rank = plan.across_hi(down_z)
    branch = (settle_near(branch_near) + arrived).reshape(item_count, item_len, D)
    attn_gate = jnp.tanh(gate_attn)[:, None, :]
    middle = token_rows + attn_gate * branch
    mlp_input = modulate(middle, gain_rows[4], scale_mlp)
    mlp_input = plan.ordered(mlp_input.astype(bf16).reshape(row_count, D))
    up_rank = plan.natural_rows(up_rank)
    input_far = swap(mlp_input, "mid")
    input_near = pair(mlp_input)
    down_rank, input_far, input_near, up_rank = fence(down_rank, input_far, input_near, up_rank)

    down_rank = plan.natural_hi(down_rank).reshape(feed_width, D)
    feed_weights = (gate_rank, up_rank, down_rank)
    input_sides = (input_near, pair(input_far))
    hidden_far, gate_far, up_far, partial_far = feed(input_sides[1], result_sides[1], *feed_weights)
    across = settle_far(partial_far)
    across, input_near = fence(across, input_near)
    arrived = settle_move(across)
    hidden_near, gate_near, up_near, partial_near = feed(input_near, result_sides[0], *feed_weights)
    input_sides = (input_near, input_sides[1])
    gate_sides, up_sides, hidden_sides = (gate_near, gate_far), (up_near, up_far), (hidden_near, hidden_far)
    gate_moved = plan.product_moved(input_sides, gate_sides)
    arrived, gate_sides, up_sides, hidden_sides, partial_near, gate_moved = fence(
        arrived, gate_sides, up_sides, hidden_sides, partial_near, gate_moved
    )

    gate_moved = plan.move(gate_moved)
    grad_mlp_input = plan.ordered(settle_near(partial_near) + arrived)
    _, pull_mlp_norm = jax.vjp(modulate, middle, gain_rows[4], scale_mlp)
    grad_middle_norm, grad_mlp_gain, grad_scale_mlp = pull_mlp_norm(
        grad_mlp_input.reshape(item_count, item_len, D)
    )
    grad_middle = grad_top + grad_middle_norm
    grad_attn_gate = jnp.sum(grad_middle * branch, axis=1) * (1.0 - jnp.tanh(gate_attn) ** 2)
    grad_branch = (attn_gate * grad_middle).astype(bf16).reshape(row_count, D)
    branch_near = pair(grad_branch)
    up_moved = plan.product_moved(input_sides, up_sides)
    gate_kept = plan.product_kept(input_sides, gate_sides)
    gate_moved, up_moved, gate_kept, grad_branch, branch_near = fence(
        gate_moved, up_moved, gate_kept, grad_branch, branch_near
    )

    gate_grad = plan.by_rep(plan.total(gate_kept, gate_moved))
    gate_grad, up_moved, grad_branch, branch_near = fence(
        gate_grad, up_moved, grad_branch, branch_near
    )
    gate_parts = plan.reduce(gate_grad)
    branch_far = swap(grad_branch, "mid")
    up_moved = plan.move(up_moved)
    back_weights = (qkv_rank, out_rank, tables)
    qkv_near, text_near, rows_near, gain_near = attend_back(
        scalars[0], branch_near, kept_near, *back_weights
    )
    up_kept = plan.product_kept(input_sides, up_sides)
    hidden_first = hi_at * (feed_width // 2)
    down_moved = plan.product_moved(hidden_sides, result_sides, feed_width // 2 - hidden_first)
    branch_far, up_moved, qkv_near, text_near, rows_near, gain_near, up_kept, down_moved = fence(
        branch_far, up_moved, qkv_near, text_near, rows_near, gain_near, up_kept, down_moved
    )

    branch_sides = (branch_near, pair(branch_far))
    up_grad = plan.by_rep(plan.total(up_kept, up_moved))
    up_grad, branch_far, down_moved = fence(up_grad, branch_sides[1], down_moved)
    up_parts = plan.reduce(up_grad)
    down_moved = plan.move(down_moved)
    qkv_far, text_far, rows_far, gain_far = attend_back(
        scalars[1], branch_far, kept_far, *back_weights
    )
    text_sides, qkv_sides = (text_near, text_far), (qkv_near, qkv_far)
    text_moved = plan.product_moved(caption_sides, text_sides)
    down_moved, text_moved, text_sides, qkv_sides, rows_far, gain_far = fence(
        down_moved, text_moved, text_sides, qkv_sides, rows_far, gain_far
    )

    text_moved = plan.move(text_moved)
    down_kept = plan.product_kept(hidden_sides, result_sides, hidden_first)
    down_grad = plan.total(down_kept, down_moved).reshape(rep_count, -1, D)
    across = settle_far(rows_far)
    across, down_grad, text_sides, qkv_sides = fence(across, down_grad, text_sides, qkv_sides)
    down_weight_grad = plan.reduce(down_grad).astype(f32)
    arrived = settle_move(across)
    qkv_moved = plan.product_moved(normed_sides, qkv_sides)
    text_kept = plan.product_kept(caption_sides, text_sides)
    qkv_kept = plan.product_kept(normed_sides, qkv_sides)
    grad_normed = settle_near(rows_near)
    arrived, text_moved, text_kept, qkv_moved, qkv_kept, grad_normed = fence(
        arrived, text_moved, text_kept, qkv_moved, qkv_kept, grad_normed
    )

    text_grad = plan.by_rep(plan.total(text_kept, text_moved))
    text_grad, qkv_moved, arrived = fence(text_grad, qkv_moved, arrived)
    text_parts = plan.reduce(text_grad)
    qkv_moved = plan.move(qkv_moved)
    mixed_sides = [plan.ordered(kept[6]) for kept in (kept_near, kept_far)]
    if plan.aligned:
        out_halves = [
            dot_left(mixed_sides[0][:, lanes], branch_sides[0])
            + dot_left(mixed_sides[1][:, lanes], branch_sides[1])
            for lanes in (slice(0, rank_width // 2), slice(rank_width // 2, None))
        ]
        if hi_count == 2:
            out_kept, out_moved = out_halves[0], swap(out_halves[1].astype(bf16), "hi")
        else:
            out_kept, out_moved = None, plan.move(jnp.concatenate(out_halves).astype(bf16))
    partial_result = [dot(side, down_rank) for side in hidden_sides]
    result = settle_near(partial_result[0]) + settle_move(settle_far(partial_result[1]))
    result = result.reshape(item_count, item_len, D)
    layer_out = (middle + mlp_gate * result).astype(bf16).reshape(row_count, D)
    grad_mlp_gate = jnp.sum(grad_top * result, axis=1) * (1.0 - jnp.tanh(gate_mlp) ** 2)
    grad_normed = plan.ordered(grad_normed + arrived)
    _, pull_attn_norm = jax.vjp(modulate, token_rows, gain_rows[0], scale_attn)
    grad_token_norm, grad_attn_gain, grad_scale_attn = pull_attn_norm(
        grad_normed.reshape(item_count, item_len, D)
    )
    tokens_grad = (grad_middle + grad_token_norm).reshape(row_count, D)
    qkv_grad = plan.by_rep(plan.total(qkv_kept, qkv_moved))
    if plan.aligned:
        out_grad = plan.total(out_kept, out_moved).reshape(rep_count, -1, 3 * rank_width)
        qkv_grad = jnp.concatenate([qkv_grad, out_grad], axis=1)
    else:
        at = (jnp.arange(RANKS) == plan.rank).astype(bf16)[:, None, None]
        out_grad = dot_left(mixed_sides[0], branch_sides[0]) + dot_left(mixed_sides[1], branch_sides[1])
        placed = (out_grad.astype(bf16)[None] * at).reshape(D, D)
        out_weight_grad = lax.psum_scatter(placed, AXES, scatter_dimension=0, tiled=True).astype(f32)
    qkv_grad, grad_mlp_gate, grad_scale_attn, grad_attn_gain = fence(
        qkv_grad, grad_mlp_gate, grad_scale_attn, grad_attn_gain
    )
    qkv_parts = plan.reduce(qkv_grad)
    if plan.aligned:
        out_weight_grad = qkv_parts[RANKS * rows :].reshape(-1, D).astype(f32)
        qkv_parts = qkv_parts[: RANKS * rows]

    grad_modulation = jnp.concatenate(
        [grad_scale_attn, grad_attn_gate, grad_scale_mlp, grad_mlp_gate], axis=1
    ).astype(bf16)
    gain_terms = gain_near + gain_far
    gain_terms = gain_terms.at[3].multiply(1.0 - cross_gate**2)
    gain_terms = [plan.place_lanes(row) for row in gain_terms]
    gains_grad = jnp.stack(
        [grad_attn_gain, gain_terms[0], gain_terms[1], gain_terms[2], grad_mlp_gain, gain_terms[3]]
    ).astype(bf16)
    gain_blocks = jnp.moveaxis(gains_grad.reshape(6, devices, -1), 1, 0).reshape(devices, -1)
    modulations = jnp.broadcast_to(grad_modulation.reshape(-1), (devices, grad_modulation.size))
    both = lax.all_to_all(
        jnp.concatenate([modulations, gain_blocks], axis=1), AXES, 0, 0, tiled=True
    )
    ada_weight_grad = dot_left(activated_mine, both[:, : modulations.shape[1]].reshape(-1, 4 * D))
    norm_gains_grad = jnp.sum(both[:, modulations.shape[1] :].astype(f32), axis=0).reshape(6, -1)

    def whole(parts, weight, sections, groups):
        blocks = trade_ranks(parts.reshape(RANKS, weight.shape[0], -1))
        return plan.from_ranks(blocks, sections, groups).astype(f32)

    gate_up_weight_grad = whole(
        jnp.concatenate([gate_parts, up_parts], axis=-1), gate_up_weight, 2, hi_count
    )
    text_weight_grad = whole(text_parts, text_weight, 2, plan.head_groups)
    qkv_weight_grad = whole(qkv_parts, qkv_weight, 3, plan.head_groups)
    return (
        layer_out,
        tokens_grad,
        norm_gains_grad,
        ada_weight_grad,
        qkv_weight_grad,
        out_weight_grad,
        text_weight_grad,
        gate_up_weight_grad,
        down_weight_grad,
    )


def solution(mesh):
    grp, rep = mesh.devices.shape
    hi = grp // RANKS
    inner = Mesh(mesh.devices.reshape(hi, 2, 2, rep), AXES)
    rows = P(AXES, None)

    def step(*arrays):
        return local(hi, rep, *arrays)

    return jax.shard_map(
        step,
        mesh=inner,
        in_specs=(
            rows,
            rows,
            P(AXES, None, None),
            P(AXES),
            P(AXES),
            rows,
            P(None, AXES),
            rows,
            rows,
            rows,
            rows,
            rows,
            rows,
        ),
        out_specs=(rows, rows, P(None, AXES), rows, rows, rows, rows, rows, rows),
        check_vma=False,
    )
```

```python
import math

import jax
import jax.numpy as jnp
from jax import lax
from jax.experimental import pallas as pl
from jax.experimental.pallas import tpu as pltpu
from jax.sharding import Mesh
from jax.sharding import PartitionSpec as P

D = 1536
HEADS = 24
HEAD_DIM = 64
TEXT_DIM = 4096
FF = 4096
SIDE = 16
RANKS = 4
LANES = 128
MIB = 1 << 20
AXES = ("hi", "mid", "core", "rep")


EPSILON = 1e-06


def norm_rows(values, gain_row):
    return (
        values * lax.rsqrt(jnp.mean(values * values, axis=-1, keepdims=True) + EPSILON) * gain_row
    )


def rope_tables(item_kind, item_len):
    position = jnp.arange(item_len, dtype=jnp.int32)[None, :]
    half_side = SIDE // 2
    frame_index = position // (half_side * half_side)
    within = position % (half_side * half_side)
    is_clip = item_kind[:, None] == 1
    row_index = jnp.where(is_clip, frame_index * half_side + within // half_side, position // SIDE)
    columns = jnp.where(is_clip, within % half_side, position % SIDE)
    lane_index = jnp.arange(HEAD_DIM, dtype=jnp.int32)
    quarter = HEAD_DIM // 4
    frequency = jnp.exp(-(lane_index % quarter).astype(jnp.float32) * (math.log(10000.0) / quarter))
    coordinate = jnp.where(
        lane_index[None, None, :] < 2 * quarter, row_index[:, :, None], columns[:, :, None]
    ).astype(jnp.float32)
    angles = coordinate * frequency
    return (jnp.cos(angles), jnp.sin(angles))


def modulate(values, gain_row, scaling):
    return norm_rows(values, gain_row) * (1.0 + scaling[:, None, :])


def silu_product(gate_half, up_half):
    return jax.nn.silu(gate_half) * up_half


def dot(left, right):
    return jnp.dot(left, right, preferred_element_type=jnp.float32)


def dot_left(left, right):
    return lax.dot_general(left, right, (((0,), (0,)), ((), ())), preferred_element_type=jnp.float32)


def dot_right(left, right):
    return lax.dot_general(left, right, (((1,), (1,)), ((), ())), preferred_element_type=jnp.float32)


def lane_index(shape):
    return lax.broadcasted_iota(jnp.int32, shape, len(shape) - 1)

def head_sums(values):
    first = lane_index(values.shape) < HEAD_DIM
    low = jnp.sum(jnp.where(first, values, 0.0), axis=-1, keepdims=True)
    high = jnp.sum(jnp.where(first, 0.0, values), axis=-1, keepdims=True)
    return jnp.where(first, low, high)

def partner(values):
    quarter = HEAD_DIM // 4
    width = values.shape[-1]
    low = lane_index(values.shape) % (2 * quarter) < quarter
    return jnp.where(low, pltpu.roll(values, width - quarter, 1), pltpu.roll(values, quarter, 1))

def stack_heads(values):
    first = lane_index(values.shape) < HEAD_DIM
    zero = jnp.zeros_like(values)
    return jnp.concatenate([jnp.where(first, values, zero), jnp.where(first, zero, values)])

def join_heads(stacked):
    rows = stacked.shape[0] // 2
    first = lane_index((rows, stacked.shape[1])) < HEAD_DIM
    return jnp.where(first, stacked[:rows], stacked[rows:])

def inverse_rms(raw):
    return lax.rsqrt(head_sums(raw * raw) * (1.0 / HEAD_DIM) + EPSILON)

def dot_cut(rows, mine, other):
    half = mine.shape[0]
    return dot(rows[:, :half], mine[...]) + dot(rows[:, half:], other[...])


def attend_kernel(
    kind_ref,
    len_ref,
    rows_ref,
    core_rows_ref,
    caption_ref,
    core_caption_ref,
    qkv_mine_ref,
    qkv_other_ref,
    key_mine_ref,
    key_other_ref,
    value_mine_ref,
    value_other_ref,
    out_weight_ref,
    gain_ref,
    cos_ref,
    sin_ref,
    qkv_ref,
    text_ref,
    text_value_ref,
    q_ref,
    k_ref,
    tk_ref,
    mixed_ref,
    read_ref,
    branch_ref,
    core_branch_ref,
):
    item = pl.program_id(0)
    own = item < pl.num_programs(0) // 2
    kind, length = kind_ref[item], len_ref[item]
    width = q_ref.shape[1]
    cosine, sine = cos_ref[kind], sin_ref[kind]
    scaling = HEAD_DIM ** (-0.5)

    def project(rows, captions):
        qkv_ref[...] = dot_cut(rows, qkv_mine_ref, qkv_other_ref)
        text_ref[...] = dot_cut(captions, key_mine_ref, key_other_ref)
        text_value_ref[...] = dot_cut(captions, value_mine_ref, value_other_ref)

    @pl.when(own)
    def _():
        project(rows_ref, caption_ref)

    @pl.when(jnp.logical_not(own))
    def _():
        project(core_rows_ref, core_caption_ref)

    for at in range(0, width, LANES):
        lanes = slice(at, at + LANES)
        turned = []
        for part, out_ref in ((0, q_ref), (1, k_ref)):
            raw = qkv_ref[:, part * width + at : part * width + at + LANES]
            normal = raw * inverse_rms(raw) * gain_ref[part : part + 1, lanes]
            rows = (normal * cosine + partner(normal) * sine).astype(jnp.bfloat16)
            out_ref[:, lanes] = rows
            turned.append(rows)
        queries, keys = turned
        values = qkv_ref[:, 2 * width + at : 2 * width + at + LANES].astype(jnp.bfloat16)
        text_raw = text_ref[:, lanes]
        text_keys = (text_raw * inverse_rms(text_raw) * gain_ref[2:3, lanes]).astype(jnp.bfloat16)
        tk_ref[:, lanes] = text_keys
        text_values = text_value_ref[:, lanes].astype(jnp.bfloat16)
        stacked = stack_heads(queries)
        scores = dot_right(stacked, keys) * scaling
        scores = jnp.exp(scores - jnp.max(scores, axis=-1, keepdims=True))
        own_out = dot(scores.astype(jnp.bfloat16), values) / jnp.sum(scores, axis=-1, keepdims=True)
        text = dot_right(stacked, text_keys) * scaling
        text = jnp.where(lane_index(text.shape) < length, text, -1e30)
        text = jnp.exp(text - jnp.max(text, axis=-1, keepdims=True))
        text_out = dot(text.astype(jnp.bfloat16), text_values) / jnp.sum(text, axis=-1, keepdims=True)
        read = join_heads(text_out)
        read_ref[:, lanes] = read
        mixed_ref[:, lanes] = (join_heads(own_out) + gain_ref[3:4, lanes] * read).astype(jnp.bfloat16)

    @pl.when(own)
    def _():
        branch_ref[...] = dot(mixed_ref[...], out_weight_ref[...])

    @pl.when(jnp.logical_not(own))
    def _():
        core_branch_ref[...] = dot(mixed_ref[...], out_weight_ref[...]).astype(jnp.bfloat16)


def head_norm_back(grad, raw, gain_row):
    inverse = inverse_rms(raw)
    scaled = grad * gain_row
    normal = raw * inverse
    inner = head_sums(scaled * normal) * (1.0 / HEAD_DIM)
    return inverse * (scaled - normal * inner), jnp.sum(grad * normal, axis=0, keepdims=True)

def attend_back_kernel(
    kind_ref,
    len_ref,
    branch_ref,
    core_branch_ref,
    qkv_ref,
    text_ref,
    text_value_ref,
    q_ref,
    k_ref,
    tk_ref,
    read_ref,
    qkv_mine_ref,
    qkv_other_ref,
    out_weight_ref,
    gain_ref,
    cos_ref,
    sin_ref,
    gqkv_ref,
    gtext_ref,
    gtext_value_ref,
    grad_rows_ref,
    core_grad_rows_ref,
    gains_ref,
    mixed_ref,
):
    item = pl.program_id(0)
    own = item < pl.num_programs(0) // 2
    kind, length = kind_ref[item], len_ref[item]
    width = q_ref.shape[1]
    cosine, sine = cos_ref[kind], sin_ref[kind]
    scaling = HEAD_DIM ** (-0.5)

    @pl.when(own)
    def _():
        mixed_ref[...] = dot_right(branch_ref[...], out_weight_ref[...])

    @pl.when(jnp.logical_not(own))
    def _():
        mixed_ref[...] = dot_right(core_branch_ref[...], out_weight_ref[...])

    @pl.when(item == 0)
    def _():
        gains_ref[...] = jnp.zeros_like(gains_ref)

    def one(stacked, keys, values, stacked_grad, valid):
        scores = dot_right(keys, stacked) * scaling
        if valid is not None:
            scores = jnp.where(valid(scores.shape), scores, -1e30)
        probs = jnp.exp(scores - jnp.max(scores, axis=0, keepdims=True))
        probs = probs * (1.0 / jnp.sum(probs, axis=0, keepdims=True))
        grad_values = dot(probs.astype(jnp.bfloat16), stacked_grad)
        grad_probs = dot_right(values, stacked_grad)
        inner = jnp.sum(probs * grad_probs, axis=0, keepdims=True)
        grad_scores = (probs * (grad_probs - inner)).astype(jnp.bfloat16)
        grad_keys = dot(grad_scores, stacked) * scaling
        grad_queries = dot_left(keys, grad_scores)
        return grad_queries, grad_keys, grad_values

    for at in range(0, width, LANES):
        lanes = slice(at, at + LANES)
        grad = mixed_ref[:, lanes]
        cross = gain_ref[3:4, lanes]
        values = qkv_ref[:, 2 * width + at : 2 * width + at + LANES].astype(jnp.bfloat16)
        text_values = text_value_ref[:, lanes].astype(jnp.bfloat16)
        stacked = stack_heads(q_ref[:, lanes])
        own_queries, own_keys, own_values = one(
            stacked, k_ref[:, lanes], values, stack_heads(grad.astype(jnp.bfloat16)), None
        )
        read_queries, read_keys, read_values = one(
            stacked, tk_ref[:, lanes], text_values, stack_heads((cross * grad).astype(jnp.bfloat16)),
            lambda shape: lax.broadcasted_iota(jnp.int32, shape, 0) < length,
        )
        grad_queries = join_heads((own_queries + read_queries).T) * scaling
        for part, turned in ((0, grad_queries), (1, own_keys)):
            raw = qkv_ref[:, part * width + at : part * width + at + LANES]
            back = turned * cosine + partner(turned * sine)
            grad_raw, gain = head_norm_back(back, raw, gain_ref[part : part + 1, lanes])
            gqkv_ref[:, part * width + at : part * width + at + LANES] = grad_raw.astype(jnp.bfloat16)
            gains_ref[part : part + 1, lanes] += gain
        gqkv_ref[:, 2 * width + at : 2 * width + at + LANES] = own_values.astype(jnp.bfloat16)
        grad_text, gain = head_norm_back(read_keys, text_ref[:, lanes], gain_ref[2:3, lanes])
        gtext_ref[:, lanes] = grad_text.astype(jnp.bfloat16)
        gains_ref[2:3, lanes] += gain
        gtext_value_ref[:, lanes] = read_values.astype(jnp.bfloat16)
        gains_ref[3:4, lanes] += jnp.sum(grad * read_ref[:, lanes], axis=0, keepdims=True)

    half = qkv_mine_ref.shape[0]

    @pl.when(own)
    def _():
        grad_rows_ref[:, :half] = dot_right(gqkv_ref[...], qkv_mine_ref[...])
        grad_rows_ref[:, half:] = dot_right(gqkv_ref[...], qkv_other_ref[...])

    @pl.when(jnp.logical_not(own))
    def _():
        rows = gqkv_ref[...]
        core_grad_rows_ref[:, :half] = dot_right(rows, qkv_mine_ref[...]).astype(jnp.bfloat16)
        core_grad_rows_ref[:, half:] = dot_right(rows, qkv_other_ref[...]).astype(jnp.bfloat16)

def whole_spec(array):
    zeros = (0,) * len(array.shape)
    return pl.BlockSpec(array.shape, lambda *_: zeros, pipeline_mode=pl.Buffered(1))


def mine_spec(array, steps):
    half = steps // 2
    return pl.BlockSpec(
        (array.shape[0] // half, array.shape[1]), lambda i, *_: (jnp.minimum(i, half - 1), 0)
    )


def core_spec(array, steps):
    half = steps // 2
    return pl.BlockSpec(
        (array.shape[0] // half, array.shape[1]), lambda i, *_: (jnp.maximum(i - half, 0), 0)
    )


def pair_specs(pair_of_arrays, steps):
    return [mine_spec(pair_of_arrays[0], steps), core_spec(pair_of_arrays[1], steps)]


def step_spec(array, steps):
    return pl.BlockSpec((array.shape[0] // steps, array.shape[1]), lambda i, *_: (i, 0))


def summed_spec(array):
    return pl.BlockSpec(array.shape, lambda i, *_: (0, 0))


def shaped(count, columns, dtype=jnp.bfloat16):
    return jax.ShapeDtypeStruct((count, columns), dtype)


def parameters():
    return pltpu.CompilerParams(dimension_semantics=("arbitrary",), vmem_limit_bytes=58 * MIB)


def attend(scalars, rows, captions, qkv_rank, key_rank, value_rank, out_rank, tables):
    items = scalars[0].shape[0]
    count, width = 2 * rows[0].shape[0], out_rank.shape[0]
    text_count = 2 * captions[0].shape[0]
    outs = [
        shaped(count, 3 * width, jnp.float32),
        shaped(text_count, width, jnp.float32),
        shaped(text_count, width, jnp.float32),
        shaped(count, width),
        shaped(count, width),
        shaped(text_count, width),
        shaped(count, width),
        shaped(count, width, jnp.float32),
    ]
    branch = (shaped(count // 2, D, jnp.float32), shaped(count // 2, D))
    whole = [*qkv_rank, *key_rank, *value_rank, out_rank, *tables]
    *kept, branch_mine, branch_core = pl.pallas_call(
        attend_kernel,
        grid_spec=pltpu.PrefetchScalarGridSpec(
            num_scalar_prefetch=2,
            grid=(items,),
            in_specs=pair_specs(rows, items)
            + pair_specs(captions, items)
            + [whole_spec(array) for array in whole],
            out_specs=[step_spec(array, items) for array in outs] + pair_specs(branch, items),
        ),
        out_shape=[*outs, *branch],
        compiler_params=parameters(),
        name="attend",
    )(*scalars, *rows, *captions, *whole)
    return kept, (branch_mine, branch_core)


def attend_back(scalars, grad_branch, kept, qkv_rank, out_rank, tables):
    items = scalars[0].shape[0]
    qkv_raw, text_raw, text_value_raw, queries, keys, text_keys, _, read = kept
    count, width = queries.shape
    outs = [
        shaped(count, 3 * width),
        shaped(text_raw.shape[0], width),
        shaped(text_raw.shape[0], width),
    ]
    rows = (shaped(count // 2, D, jnp.float32), shaped(count // 2, D))
    gains = shaped(4, width, jnp.float32)
    by_item = [qkv_raw, text_raw, text_value_raw, queries, keys, text_keys, read]
    whole = [*qkv_rank, out_rank, *tables]
    qkv, text, text_value, rows_mine, rows_core, gains = pl.pallas_call(
        attend_back_kernel,
        grid_spec=pltpu.PrefetchScalarGridSpec(
            num_scalar_prefetch=2,
            grid=(items,),
            in_specs=pair_specs(grad_branch, items)
            + [step_spec(array, items) for array in by_item]
            + [whole_spec(array) for array in whole],
            out_specs=[step_spec(array, items) for array in outs]
            + pair_specs(rows, items)
            + [summed_spec(gains)],
            scratch_shapes=[pltpu.VMEM((count // items, width), jnp.float32)],
        ),
        out_shape=[*outs, *rows, gains],
        compiler_params=parameters(),
        name="attend_back",
    )(*scalars, *grad_branch, *by_item, *whole)
    return qkv, text, text_value, (rows_mine, rows_core), gains


def row_cuts(lefts, rights):
    cuts, left, right, left_row, right_row = [], 0, 0, 0, 0
    while left < len(lefts):
        count = min(lefts[left].shape[0] - left_row, rights[right].shape[0] - right_row)
        cuts.append((left, left_row, right, right_row, count))
        left_row, right_row = left_row + count, right_row + count
        if left_row == lefts[left].shape[0]:
            left, left_row = left + 1, 0
        if right_row == rights[right].shape[0]:
            right, right_row = right + 1, 0
    return cuts


def product(lefts, rights, first, lanes, dtype):
    columns = rights[0].shape[1]
    if lanes % LANES:
        block = lanes
    else:
        block = 384 if lanes % 384 == 0 else math.gcd(lanes, 512)
    cuts = row_cuts(lefts, rights)

    def kernel(first_ref, *refs):
        left_refs, right_refs, out_ref = refs[: len(lefts)], refs[len(lefts) : -1], refs[-1]
        total = None
        for left, left_row, right, right_row, count in cuts:
            term = dot_left(
                left_refs[left][left_row : left_row + count, :],
                right_refs[right][right_row : right_row + count, :],
            )
            total = term if total is None else total + term
        out_ref[...] = total.astype(out_ref.dtype)

    return pl.pallas_call(
        kernel,
        grid_spec=pltpu.PrefetchScalarGridSpec(
            num_scalar_prefetch=1,
            grid=(lanes // block,),
            in_specs=[
                pl.BlockSpec((array.shape[0], block), lambda i, first: (0, first[0] // block + i))
                for array in lefts
            ]
            + [whole_spec(array) for array in rights],
            out_specs=pl.BlockSpec((block, columns), lambda i, first: (i, 0)),
        ),
        out_shape=shaped(lanes, columns, dtype),
        compiler_params=parameters(),
        name="product",
    )(jnp.reshape(first, (1,)).astype(jnp.int32), *lefts, *rights)


def feed_kernel(
    rows_ref,
    core_rows_ref,
    result_ref,
    core_result_ref,
    gate_mine_ref,
    gate_other_ref,
    up_mine_ref,
    up_other_ref,
    down_ref,
    hidden_ref,
    grad_gate_ref,
    grad_up_ref,
    grad_ref,
    core_grad_ref,
    rows,
    result,
):
    own = pl.program_id(0) < pl.num_programs(0) // 2

    @pl.when(own)
    def _():
        rows[...] = rows_ref[...]
        result[...] = result_ref[...]

    @pl.when(jnp.logical_not(own))
    def _():
        rows[...] = core_rows_ref[...]
        result[...] = core_result_ref[...]

    gate = dot_cut(rows, gate_mine_ref, gate_other_ref)
    up = dot_cut(rows, up_mine_ref, up_other_ref)
    grad_hidden = dot_right(result[...], down_ref[...])
    sigmoid = 1.0 / (1.0 + jnp.exp(-gate))
    silu = gate * sigmoid
    hidden_ref[...] = (silu * up).astype(jnp.bfloat16)
    grad_gate = (grad_hidden * up * (sigmoid + silu * (1.0 - sigmoid))).astype(jnp.bfloat16)
    grad_up = (grad_hidden * silu).astype(jnp.bfloat16)
    grad_gate_ref[...] = grad_gate
    grad_up_ref[...] = grad_up
    half = gate_mine_ref.shape[0]
    low = dot_right(grad_gate, gate_mine_ref[...]) + dot_right(grad_up, up_mine_ref[...])
    high = dot_right(grad_gate, gate_other_ref[...]) + dot_right(grad_up, up_other_ref[...])

    @pl.when(own)
    def _():
        grad_ref[:, :half] = low
        grad_ref[:, half:] = high

    @pl.when(jnp.logical_not(own))
    def _():
        core_grad_ref[:, :half] = low.astype(jnp.bfloat16)
        core_grad_ref[:, half:] = high.astype(jnp.bfloat16)


def feed(rows, grad_result, gate_rank, up_rank, down_rank):
    count, width = 2 * rows[0].shape[0], down_rank.shape[0]
    block = 256
    steps = count // block
    outs = [shaped(count, width)] * 3
    grads = (shaped(count // 2, D, jnp.float32), shaped(count // 2, D))
    whole = [*gate_rank, *up_rank, down_rank]
    hidden, grad_gate, grad_up, grad_mine, grad_core = pl.pallas_call(
        feed_kernel,
        grid=(steps,),
        in_specs=pair_specs(rows, steps)
        + pair_specs(grad_result, steps)
        + [whole_spec(array) for array in whole],
        out_specs=[step_spec(array, steps) for array in outs] + pair_specs(grads, steps),
        out_shape=[*outs, *grads],
        scratch_shapes=[pltpu.VMEM((block, D), jnp.bfloat16)] * 2,
        compiler_params=parameters(),
        name="feed",
    )(*rows, *grad_result, *whole)
    return hidden, grad_gate, grad_up, (grad_mine, grad_core)


def swap(block, axis, count=2, step=1):
    return lax.ppermute(block, axis, [(at, at ^ step) for at in range(count)])


def spread(block, axis, count):
    if count & (count - 1):
        return lax.all_gather(block, axis)
    block, step = block[None], 1
    while step < count:
        other = swap(block, axis, count, step)
        low = (lax.axis_index(axis) & step) == 0
        block = jnp.where(
            low, jnp.concatenate([block, other]), jnp.concatenate([other, block])
        )
        step *= 2
    return block


def fold(block, axis, count):
    if count & (count - 1):
        return lax.psum_scatter(block, axis, scatter_dimension=0)
    step = count // 2
    while step:
        half = block.shape[0] // 2
        low = (lax.axis_index(axis) & step) == 0
        lower, upper = block[:half], block[half:]
        block = jnp.where(low, lower, upper) + swap(
            jnp.where(low, upper, lower), axis, count, step
        )
        step //= 2
    return block[0]


def trade_ranks(block):
    return lax.all_to_all(block, ("mid", "core"), 0, 0, tiled=True)


def pick(stack, index):
    return lax.dynamic_index_in_dim(stack, index, 0, keepdims=False)


def pair(rows):
    return (rows, swap(rows, "core"))


def settle(partial):
    mine, core = partial
    return mine + swap(core, "core").astype(jnp.float32)


def settle_move(across):
    return swap(across, "mid").astype(jnp.float32)


class Layout:
    def __init__(self, hi, rep, out_rows):
        self.hi, self.rep = hi, rep
        self.aligned = (rep * out_rows) % HEAD_DIM == 0
        self.head_groups = hi if self.aligned else 1
        self.rank = lax.axis_index("mid") * 2 + lax.axis_index("core")

    def by_rank(self, weight, sections, groups):
        rows, columns = weight.shape
        width = columns // (sections * groups * RANKS)
        view = weight.reshape(rows, sections * groups, RANKS, width)
        view = jnp.transpose(view, (2, 0, 1, 3))
        return view.reshape(RANKS, rows, sections * groups * width)

    def from_ranks(self, blocks, sections, groups):
        _, rows, per_rank = blocks.shape
        width = per_rank // (sections * groups)
        view = blocks.reshape(RANKS, rows, sections * groups, width)
        return jnp.transpose(view, (1, 2, 0, 3)).reshape(rows, RANKS * per_rank)

    def ordered(self, values):
        if self.hi != 2:
            return values
        half = values.shape[-1] // 2
        turned = jnp.concatenate([values[..., half:], values[..., :half]], axis=-1)
        return jnp.where(lax.axis_index("hi") == 0, values, turned)

    def across_hi(self, block):
        if self.hi == 2:
            return (block, swap(block, "hi"))
        return spread(block, "hi", self.hi)

    def natural_hi(self, blocks):
        if self.hi != 2:
            return blocks
        mine, other = blocks
        low = lax.axis_index("hi") == 0
        return jnp.stack([jnp.where(low, mine, other), jnp.where(low, other, mine)])

    def halves(self, blocks):
        if self.hi == 2:
            return tuple(self.natural_rows(block[None]) for block in blocks)
        return tuple(jnp.split(self.natural_rows(blocks), 2))

    def natural_rows(self, stacked):
        view = stacked.reshape(stacked.shape[0], self.rep, RANKS, -1, stacked.shape[-1])
        return jnp.transpose(view, (0, 2, 1, 3, 4)).reshape(-1, stacked.shape[-1])

    def product_moved(self, lefts, rights, first=None):
        lanes = lefts[0].shape[1]
        if self.hi != 2:
            return product(lefts, rights, 0, lanes, jnp.bfloat16)
        return product(lefts, rights, lanes // 2 if first is None else first, lanes // 2, jnp.bfloat16)

    def move(self, moved):
        if self.hi == 2:
            return swap(moved, "hi")
        return fold(moved.reshape(self.hi, -1, moved.shape[1]), "hi", self.hi)

    def product_kept(self, lefts, rights, first=0):
        if self.hi != 2:
            return None
        return product(lefts, rights, first, lefts[0].shape[1] // 2, jnp.float32)

    def total(self, kept, arrived):
        if kept is None:
            return arrived
        return (kept + arrived.astype(jnp.float32)).astype(jnp.bfloat16)

    def by_rep(self, summed):
        view = summed.reshape(RANKS, self.rep, -1, summed.shape[1])
        return jnp.transpose(view, (1, 0, 2, 3)).reshape(self.rep, -1, summed.shape[1])

    def reduce(self, blocks):
        flat = blocks.reshape(-1, blocks.shape[-1])
        return lax.psum_scatter(flat, "rep", scatter_dimension=0, tiled=True)

    def rank_lanes(self, rows, groups):
        view = rows.reshape(rows.shape[0], groups, RANKS, -1)
        return lax.dynamic_index_in_dim(view, self.rank, 2, keepdims=False).reshape(rows.shape[0], -1)

    def place_lanes(self, row):
        view = row.reshape(self.head_groups, 1, -1)
        at = (jnp.arange(RANKS) == self.rank).astype(row.dtype)[None, :, None]
        return (view * at).reshape(-1)


def fence(*values):
    return lax.optimization_barrier(values)


def local(
    hi_count,
    rep_count,
    tokens,
    condition,
    caption,
    caption_len,
    item_kind,
    out_cotangent,
    norm_gains,
    ada_weight,
    qkv_weight,
    out_weight,
    text_weight,
    gate_up_weight,
    down_weight,
):
    bf16, f32 = jnp.bfloat16, jnp.float32
    item_count = condition.shape[0]
    item_len = tokens.shape[0] // item_count
    row_count = item_count * item_len
    rows = qkv_weight.shape[0]
    plan = Layout(hi_count, rep_count, out_weight.shape[0])
    rank_width = HEADS // RANKS * HEAD_DIM
    hi_at, mid_at, core_at, rep_at = [lax.axis_index(name) for name in AXES]
    device_shape = (hi_count, 2, 2, rep_count)

    feed_width = FF // RANKS
    devices = hi_count * RANKS * rep_count
    block_at = (hi_at * RANKS + plan.rank) * rep_count + rep_at

    def z_gather(block):
        return lax.all_gather(block.reshape(-1, block.shape[-1]), "rep", tiled=True)

    qkv_mine = trade_ranks(plan.by_rank(qkv_weight, 3, plan.head_groups))
    qkv_mine = qkv_mine.reshape(RANKS * rows, 3 * rank_width)
    if plan.aligned:
        qkv_mine = jnp.concatenate([qkv_mine, out_weight.reshape(-1, 3 * rank_width)])
    else:
        out_whole = lax.all_gather(out_weight, AXES, axis=0, tiled=True)
        out_rank = pick(out_whole.reshape(RANKS, rank_width, D), plan.rank)

    head = condition.reshape(item_count, devices, rows)
    head = jnp.transpose(head, (1, 0, 2)).reshape(devices, -1)
    rest = jnp.concatenate(
        [norm_gains.reshape(-1), caption_len.astype(bf16), item_kind.astype(bf16)]
    )
    small = jnp.concatenate([head, jnp.broadcast_to(rest, (devices, rest.size))], axis=1)
    qkv_mine, small = fence(qkv_mine, small)
    qkv_z = z_gather(qkv_mine)
    small = lax.all_to_all(small, AXES, 0, 0, tiled=True)
    cut = [head.shape[1], head.shape[1] + norm_gains.size]
    cut.append(cut[1] + item_count)
    conditions, gains, lengths, kinds = jnp.split(small, cut, axis=-1)
    activated_mine = jax.nn.silu(conditions.astype(f32)).astype(bf16).reshape(-1, rows)
    gain_rows = jnp.moveaxis(gains.astype(f32).reshape(devices, 6, -1), 1, 0).reshape(6, D)
    lengths, kinds = [
        values.reshape(device_shape + (item_count,)) for values in (lengths, kinds)
    ]

    def group_items(values):
        view = lax.dynamic_index_in_dim(pick(values, hi_at), rep_at, 2, keepdims=False)
        near, far = pick(view, mid_at), pick(view, 1 - mid_at)
        order = [core_at, 1 - core_at]
        return [
            jnp.concatenate([pick(side, at) for at in order]).astype(jnp.int32)
            for side in (near, far)
        ]

    lengths_sides = group_items(lengths)
    kinds_sides = group_items(kinds)
    cosine, sine = rope_tables(jnp.arange(2), item_len)
    signs = jnp.where(jnp.arange(HEAD_DIM) % (HEAD_DIM // 2) < HEAD_DIM // 4, -1.0, 1.0)
    cosine, sine = jnp.tile(cosine, (1, 1, 2)), jnp.tile(sine * signs, (1, 1, 2))
    head_gains = plan.rank_lanes(gain_rows, plan.head_groups)
    cross_gate = jnp.tanh(head_gains[5])
    head_gains = jnp.concatenate([head_gains[1:4], cross_gate[None]])
    tables = (head_gains, cosine, sine)
    scalars = list(zip(kinds_sides, lengths_sides, strict=True))

    captions = plan.ordered(caption.reshape(-1, TEXT_DIM))
    text_weight, conditions, captions = fence(text_weight, activated_mine, captions)
    text_mine = trade_ranks(plan.by_rank(text_weight, 2, plan.head_groups))
    captions_near = pair(captions)
    partial = dot(conditions, ada_weight).astype(bf16).reshape(devices, item_count, 4 * D)
    text_mine, partial, captions_near = fence(text_mine, partial, captions_near)
    text_key_mine, text_value_mine = text_mine[..., :rank_width], text_mine[..., rank_width:]
    modulation = jnp.sum(lax.all_to_all(partial, AXES, 0, 0, tiled=True).astype(f32), axis=0)
    qkv_z, modulation, text_key_mine, text_value_mine = fence(
        qkv_z, modulation, text_key_mine, text_value_mine
    )

    scale_attn, gate_attn, scale_mlp, gate_mlp = jnp.split(modulation, 4, axis=1)
    text_key_z = z_gather(text_key_mine)
    captions_far = swap(captions, "mid")
    qkv_rank = plan.across_hi(qkv_z)
    gate_up_mine = trade_ranks(plan.by_rank(gate_up_weight, 2, hi_count))
    gate_mine, up_mine = gate_up_mine[..., :feed_width], gate_up_mine[..., feed_width:]
    token_rows = tokens.astype(f32).reshape(item_count, item_len, D)
    normed = modulate(token_rows, gain_rows[0], scale_attn)
    normed = plan.ordered(normed.astype(bf16).reshape(row_count, D))
    mlp_gate = jnp.tanh(gate_mlp)[:, None, :]
    grad_top = out_cotangent.astype(f32).reshape(item_count, item_len, D)
    grad_result = (mlp_gate * grad_top).astype(bf16).reshape(row_count, D)
    normed_near, result_near = pair(normed), pair(grad_result)
    text_key_z, captions_far, qkv_rank, gate_mine, up_mine, normed_near, result_near = fence(
        text_key_z, captions_far, qkv_rank, gate_mine, up_mine, normed_near, result_near
    )

    text_value_z = z_gather(text_value_mine)
    text_key_rank = plan.across_hi(text_key_z)
    normed_far = swap(normed_near[0], "mid")
    captions_far = pair(captions_far)
    text_value_z, text_key_rank, normed_far, captions_far = fence(
        text_value_z, text_key_rank, normed_far, captions_far
    )

    gate_z = z_gather(gate_mine)
    text_value_rank = plan.across_hi(text_value_z)
    result_far = swap(result_near[0], "mid")
    normed_far = pair(normed_far)
    if plan.aligned:
        blocks = [block.reshape(rep_count, -1, 3 * rank_width) for block in qkv_rank]
        out_rank = plan.natural_hi([block[:, RANKS * rows :].reshape(-1, D) for block in blocks])
        out_rank = out_rank.reshape(rank_width, D)
        qkv_rank = [block[:, : RANKS * rows].reshape(-1, 3 * rank_width) for block in blocks]
        qkv_rank = qkv_rank if hi_count == 2 else jnp.stack(qkv_rank)
    qkv_rank, text_key_rank = plan.halves(qkv_rank), plan.halves(text_key_rank)
    gate_z, text_value_rank, result_far, normed_far, qkv_rank, out_rank, text_key_rank = fence(
        gate_z, text_value_rank, result_far, normed_far, qkv_rank, out_rank, text_key_rank
    )

    up_z = z_gather(up_mine)
    gate_rank = plan.across_hi(gate_z)
    attend_weights = (qkv_rank, text_key_rank, plan.halves(text_value_rank), out_rank, tables)
    kept_far, partial_far = attend(scalars[1], normed_far, captions_far, *attend_weights)
    up_z, gate_rank, kept_far, partial_far, attend_weights = fence(
        up_z, gate_rank, kept_far, partial_far, attend_weights
    )

    across = settle(partial_far).astype(bf16)
    across, normed_near, up_z = fence(across, normed_near, up_z)
    down_z = z_gather(down_weight)
    up_rank = plan.across_hi(up_z)
    arrived = settle_move(across)
    kept_near, partial_near = attend(scalars[0], normed_near, captions_near, *attend_weights)
    result_far = pair(result_far)
    down_z, up_rank, arrived, kept_near, partial_near, result_far = fence(
        down_z, up_rank, arrived, kept_near, partial_near, result_far
    )

    down_rank = plan.across_hi(down_z)
    branch = (settle(partial_near) + arrived).reshape(item_count, item_len, D)
    attn_gate = jnp.tanh(gate_attn)[:, None, :]
    middle = token_rows + attn_gate * branch
    mlp_input = modulate(middle, gain_rows[4], scale_mlp)
    mlp_input = plan.ordered(mlp_input.astype(bf16).reshape(row_count, D))
    input_far = swap(mlp_input, "mid")
    input_near = pair(mlp_input)
    gate_rank, up_rank = plan.halves(gate_rank), plan.halves(up_rank)
    down_rank, input_far, input_near, gate_rank, up_rank = fence(
        down_rank, input_far, input_near, gate_rank, up_rank
    )

    down_rank = plan.natural_hi(down_rank).reshape(feed_width, D)
    feed_weights = (gate_rank, up_rank, down_rank)
    input_far = pair(input_far)
    hidden_far, gate_far, up_far, partial_far = feed(input_far, result_far, *feed_weights)
    across = settle(partial_far).astype(bf16)
    across, input_near = fence(across, input_near)
    arrived = settle_move(across)
    hidden_near, gate_near, up_near, partial_near = feed(input_near, result_near, *feed_weights)
    inputs, results = (*input_near, *input_far), (*result_near, *result_far)
    gate_rows, up_rows, hidden_rows = (gate_near, gate_far), (up_near, up_far), (hidden_near, hidden_far)
    gate_moved = plan.product_moved(inputs, gate_rows)
    arrived, gate_rows, up_rows, hidden_rows, partial_near, gate_moved = fence(
        arrived, gate_rows, up_rows, hidden_rows, partial_near, gate_moved
    )

    gate_moved = plan.move(gate_moved)
    grad_mlp_input = plan.ordered(settle(partial_near) + arrived)
    _, pull_mlp_norm = jax.vjp(modulate, middle, gain_rows[4], scale_mlp)
    grad_middle_norm, grad_mlp_gain, grad_scale_mlp = pull_mlp_norm(
        grad_mlp_input.reshape(item_count, item_len, D)
    )
    grad_middle = grad_top + grad_middle_norm
    grad_attn_gate = jnp.sum(grad_middle * branch, axis=1) * (1.0 - jnp.tanh(gate_attn) ** 2)
    grad_branch = (attn_gate * grad_middle).astype(bf16).reshape(row_count, D)
    branch_near = pair(grad_branch)
    up_moved = plan.product_moved(inputs, up_rows)
    gate_kept = plan.product_kept(inputs, gate_rows)
    hidden_first = hi_at * (feed_width // 2)
    down_moved = plan.product_moved(hidden_rows, results, feed_width // 2 - hidden_first)
    gate_moved, up_moved, gate_kept, branch_near, down_moved = fence(
        gate_moved, up_moved, gate_kept, branch_near, down_moved
    )

    gate_grad = plan.by_rep(plan.total(gate_kept, gate_moved))
    gate_grad, up_moved, branch_near = fence(gate_grad, up_moved, branch_near)
    gate_parts = plan.reduce(gate_grad)
    branch_far = swap(branch_near[0], "mid")
    up_moved = plan.move(up_moved)
    back_weights = (qkv_rank, out_rank, tables)
    qkv_near, key_near, value_near, rows_near, gain_near = attend_back(
        scalars[0], branch_near, kept_near, *back_weights
    )
    up_kept = plan.product_kept(inputs, up_rows)
    gate_parts, branch_far, up_moved, qkv_near, key_near, value_near, rows_near, gain_near, up_kept = fence(
        gate_parts, branch_far, up_moved, qkv_near, key_near, value_near, rows_near, gain_near, up_kept
    )

    branch_far = pair(branch_far)
    up_grad = plan.by_rep(plan.total(up_kept, up_moved))
    up_grad, branch_far, down_moved = fence(up_grad, branch_far, down_moved)
    up_parts = plan.reduce(up_grad)
    down_moved = plan.move(down_moved)
    qkv_far, key_far, value_far, rows_far, gain_far = attend_back(
        scalars[1], branch_far, kept_far, *back_weights
    )
    qkv_rows, key_rows, value_rows = (qkv_near, qkv_far), (key_near, key_far), (value_near, value_far)
    all_captions, all_normed = (*captions_near, *captions_far), (*normed_near, *normed_far)
    key_moved = plan.product_moved(all_captions, key_rows)
    down_kept = plan.product_kept(hidden_rows, results, hidden_first)
    up_parts, down_moved, key_moved, down_kept, qkv_rows, value_rows, rows_far, gain_far = fence(
        up_parts, down_moved, key_moved, down_kept, qkv_rows, value_rows, rows_far, gain_far
    )

    across = settle(rows_far).astype(bf16)
    down_grad = plan.total(down_kept, down_moved).reshape(rep_count, -1, D)
    across, down_grad, key_moved, qkv_rows, value_rows = fence(
        across, down_grad, key_moved, qkv_rows, value_rows
    )
    down_parts = plan.reduce(down_grad)
    arrived = settle_move(across)
    key_moved = plan.move(key_moved)
    value_moved = plan.product_moved(all_captions, value_rows)
    key_kept = plan.product_kept(all_captions, key_rows)
    qkv_moved = plan.product_moved(all_normed, qkv_rows)
    value_kept = plan.product_kept(all_captions, value_rows)
    down_parts, arrived, key_moved, value_moved, key_kept, qkv_moved, value_kept, rows_near = fence(
        down_parts, arrived, key_moved, value_moved, key_kept, qkv_moved, value_kept, rows_near
    )

    key_grad = plan.by_rep(plan.total(key_kept, key_moved))
    key_grad, value_moved, qkv_moved, hidden_rows = fence(key_grad, value_moved, qkv_moved, hidden_rows)
    key_parts = plan.reduce(key_grad)
    value_moved = plan.move(value_moved)
    qkv_kept = plan.product_kept(all_normed, qkv_rows)
    mixed_rows = [plan.ordered(kept[6]) for kept in (kept_near, kept_far)]
    branches = (*branch_near, *branch_far)
    if plan.aligned:
        out_halves = [
            product([rows[:, lanes] for rows in mixed_rows], branches, 0, rank_width // 2, bf16)
            for lanes in (slice(0, rank_width // 2), slice(rank_width // 2, None))
        ]
    result_far = [dot(rows, down_rank) for rows in jnp.split(hidden_rows[1], 2)]
    across = settle((result_far[0], result_far[1].astype(bf16))).astype(bf16)
    grad_normed = plan.ordered(settle(rows_near) + arrived)
    key_parts, value_moved, qkv_kept, across, grad_normed = fence(
        key_parts, value_moved, qkv_kept, across, grad_normed
    )

    value_grad = plan.by_rep(plan.total(value_kept, value_moved))
    value_grad, qkv_moved, across = fence(value_grad, qkv_moved, across)
    value_parts = plan.reduce(value_grad)
    qkv_moved = plan.move(qkv_moved)
    result = settle_move(across)
    if plan.aligned:
        if hi_count == 2:
            out_kept, out_moved = out_halves[0].astype(f32), swap(out_halves[1], "hi")
        else:
            out_kept, out_moved = None, plan.move(jnp.concatenate(out_halves))
    result_near = [dot(rows, down_rank) for rows in jnp.split(hidden_rows[0], 2)]
    result = result + settle((result_near[0], result_near[1].astype(bf16)))
    result = result.reshape(item_count, item_len, D)
    layer_out = (middle + mlp_gate * result).astype(bf16).reshape(row_count, D)
    grad_mlp_gate = jnp.sum(grad_top * result, axis=1) * (1.0 - jnp.tanh(gate_mlp) ** 2)
    _, pull_attn_norm = jax.vjp(modulate, token_rows, gain_rows[0], scale_attn)
    grad_token_norm, grad_attn_gain, grad_scale_attn = pull_attn_norm(
        grad_normed.reshape(item_count, item_len, D)
    )
    tokens_grad = (grad_middle + grad_token_norm).reshape(row_count, D)
    qkv_grad = plan.by_rep(plan.total(qkv_kept, qkv_moved))
    if plan.aligned:
        out_grad = plan.total(out_kept, out_moved).reshape(rep_count, -1, 3 * rank_width)
        qkv_grad = jnp.concatenate([qkv_grad, out_grad], axis=1)
    else:
        at = (jnp.arange(RANKS) == plan.rank).astype(bf16)[:, None, None]
        out_grad = product(mixed_rows, branches, 0, rank_width, bf16)
        placed = (out_grad[None] * at).reshape(D, D)
        out_weight_grad = lax.psum_scatter(placed, AXES, scatter_dimension=0, tiled=True).astype(f32)
    value_parts, qkv_grad, grad_mlp_gate, grad_scale_attn, grad_attn_gain = fence(
        value_parts, qkv_grad, grad_mlp_gate, grad_scale_attn, grad_attn_gain
    )
    qkv_parts = plan.reduce(qkv_grad)
    if plan.aligned:
        out_weight_grad = qkv_parts[RANKS * rows :].reshape(-1, D).astype(f32)
        qkv_parts = qkv_parts[: RANKS * rows]

    grad_modulation = jnp.concatenate(
        [grad_scale_attn, grad_attn_gate, grad_scale_mlp, grad_mlp_gate], axis=1
    ).astype(bf16)
    gain_terms = gain_near + gain_far
    gain_terms = gain_terms.at[3].multiply(1.0 - cross_gate**2)
    gain_terms = [plan.place_lanes(row) for row in gain_terms]
    gains_grad = jnp.stack(
        [grad_attn_gain, gain_terms[0], gain_terms[1], gain_terms[2], grad_mlp_gain, gain_terms[3]]
    ).astype(bf16)
    gain_blocks = jnp.moveaxis(gains_grad.reshape(6, devices, -1), 1, 0).reshape(devices, -1)
    modulations = jnp.broadcast_to(grad_modulation.reshape(-1), (devices, grad_modulation.size))
    both = lax.all_to_all(
        jnp.concatenate([modulations, gain_blocks], axis=1), AXES, 0, 0, tiled=True
    )
    ada_weight_grad = dot_left(activated_mine, both[:, : modulations.shape[1]].reshape(-1, 4 * D))
    norm_gains_grad = jnp.sum(both[:, modulations.shape[1] :].astype(f32), axis=0).reshape(6, -1)

    def whole(parts, weight, sections, groups):
        blocks = trade_ranks(parts.reshape(RANKS, weight.shape[0], -1))
        return plan.from_ranks(blocks, sections, groups).astype(f32)

    gate_up_weight_grad = whole(
        jnp.concatenate([gate_parts, up_parts], axis=-1), gate_up_weight, 2, hi_count
    )
    text_weight_grad = whole(
        jnp.concatenate([key_parts, value_parts], axis=-1), text_weight, 2, plan.head_groups
    )
    qkv_weight_grad = whole(qkv_parts, qkv_weight, 3, plan.head_groups)
    down_weight_grad = down_parts.astype(f32)
    return (
        layer_out,
        tokens_grad,
        norm_gains_grad,
        ada_weight_grad,
        qkv_weight_grad,
        out_weight_grad,
        text_weight_grad,
        gate_up_weight_grad,
        down_weight_grad,
    )


def solution(mesh):
    grp, rep = mesh.devices.shape
    hi = grp // RANKS
    inner = Mesh(mesh.devices.reshape(hi, 2, 2, rep), AXES)
    rows = P(AXES, None)

    def step(*arrays):
        return local(hi, rep, *arrays)

    return jax.shard_map(
        step,
        mesh=inner,
        in_specs=(
            rows,
            rows,
            P(AXES, None, None),
            P(AXES),
            P(AXES),
            rows,
            P(None, AXES),
            rows,
            rows,
            rows,
            rows,
            rows,
            rows,
        ),
        out_specs=(rows, rows, P(None, AXES), rows, rows, rows, rows, rows, rows),
        check_vma=False,
    )
```

```python
import math

import jax
import jax.numpy as jnp
from jax import lax
from jax.experimental import pallas as pl
from jax.experimental.pallas import tpu as pltpu
from jax.sharding import Mesh
from jax.sharding import PartitionSpec as P

D = 1536
HEADS = 24
HEAD_DIM = 64
TEXT_DIM = 4096
FF = 4096
SIDE = 16
RANKS = 4
LANES = 128
MIB = 1 << 20
AXES = ("hi", "mid", "core", "rep")


EPSILON = 1e-06


def norm_rows(values, gain_row):
    return (
        values * lax.rsqrt(jnp.mean(values * values, axis=-1, keepdims=True) + EPSILON) * gain_row
    )


def rope_tables(item_kind, item_len):
    position = jnp.arange(item_len, dtype=jnp.int32)[None, :]
    half_side = SIDE // 2
    frame_index = position // (half_side * half_side)
    within = position % (half_side * half_side)
    is_clip = item_kind[:, None] == 1
    row_index = jnp.where(is_clip, frame_index * half_side + within // half_side, position // SIDE)
    columns = jnp.where(is_clip, within % half_side, position % SIDE)
    lane_index = jnp.arange(HEAD_DIM, dtype=jnp.int32)
    quarter = HEAD_DIM // 4
    frequency = jnp.exp(-(lane_index % quarter).astype(jnp.float32) * (math.log(10000.0) / quarter))
    coordinate = jnp.where(
        lane_index[None, None, :] < 2 * quarter, row_index[:, :, None], columns[:, :, None]
    ).astype(jnp.float32)
    angles = coordinate * frequency
    return (jnp.cos(angles), jnp.sin(angles))


def modulate(values, gain_row, scaling):
    return norm_rows(values, gain_row) * (1.0 + scaling[:, None, :])


def silu_product(gate_half, up_half):
    return jax.nn.silu(gate_half) * up_half


def dot(left, right):
    return jnp.dot(left, right, preferred_element_type=jnp.float32)


def dot_left(left, right):
    return lax.dot_general(left, right, (((0,), (0,)), ((), ())), preferred_element_type=jnp.float32)


def dot_right(left, right):
    return lax.dot_general(left, right, (((1,), (1,)), ((), ())), preferred_element_type=jnp.float32)


def lane_index(shape):
    return lax.broadcasted_iota(jnp.int32, shape, len(shape) - 1)

def head_sums(values):
    first = lane_index(values.shape) < HEAD_DIM
    low = jnp.sum(jnp.where(first, values, 0.0), axis=-1, keepdims=True)
    high = jnp.sum(jnp.where(first, 0.0, values), axis=-1, keepdims=True)
    return jnp.where(first, low, high)

def partner(values):
    quarter = HEAD_DIM // 4
    width = values.shape[-1]
    low = lane_index(values.shape) % (2 * quarter) < quarter
    return jnp.where(low, pltpu.roll(values, width - quarter, 1), pltpu.roll(values, quarter, 1))

def stack_heads(values):
    first = lane_index(values.shape) < HEAD_DIM
    zero = jnp.zeros_like(values)
    return jnp.concatenate([jnp.where(first, values, zero), jnp.where(first, zero, values)])

def join_heads(stacked):
    rows = stacked.shape[0] // 2
    first = lane_index((rows, stacked.shape[1])) < HEAD_DIM
    return jnp.where(first, stacked[:rows], stacked[rows:])

def inverse_rms(raw):
    return lax.rsqrt(head_sums(raw * raw) * (1.0 / HEAD_DIM) + EPSILON)

def dot_cut(rows, mine, other):
    half = mine.shape[0]
    return dot(rows[:, :half], mine[...]) + dot(rows[:, half:], other[...])


def attend_kernel(
    kind_ref,
    len_ref,
    rows_ref,
    core_rows_ref,
    caption_ref,
    core_caption_ref,
    qkv_mine_ref,
    qkv_other_ref,
    key_mine_ref,
    key_other_ref,
    value_mine_ref,
    value_other_ref,
    out_weight_ref,
    gain_ref,
    cos_ref,
    sin_ref,
    rows_out_ref,
    caption_out_ref,
    qkv_ref,
    text_ref,
    text_value_ref,
    q_ref,
    k_ref,
    tk_ref,
    mixed_ref,
    read_ref,
    branch_ref,
    core_branch_ref,
):
    item = pl.program_id(0)
    own = item < pl.num_programs(0) // 2
    kind, length = kind_ref[item], len_ref[item]
    width = q_ref.shape[1]
    cosine, sine = cos_ref[kind], sin_ref[kind]
    scaling = HEAD_DIM ** (-0.5)

    @pl.when(own)
    def _():
        rows_out_ref[...] = rows_ref[...]
        caption_out_ref[...] = caption_ref[...]

    @pl.when(jnp.logical_not(own))
    def _():
        rows_out_ref[...] = core_rows_ref[...]
        caption_out_ref[...] = core_caption_ref[...]

    qkv_ref[...] = dot_cut(rows_out_ref, qkv_mine_ref, qkv_other_ref)
    text_ref[...] = dot_cut(caption_out_ref, key_mine_ref, key_other_ref)
    text_value_ref[...] = dot_cut(caption_out_ref, value_mine_ref, value_other_ref)
    for at in range(0, width, LANES):
        lanes = slice(at, at + LANES)
        turned = []
        for part, out_ref in ((0, q_ref), (1, k_ref)):
            raw = qkv_ref[:, part * width + at : part * width + at + LANES]
            normal = raw * inverse_rms(raw) * gain_ref[part : part + 1, lanes]
            rows = (normal * cosine + partner(normal) * sine).astype(jnp.bfloat16)
            out_ref[:, lanes] = rows
            turned.append(rows)
        queries, keys = turned
        values = qkv_ref[:, 2 * width + at : 2 * width + at + LANES].astype(jnp.bfloat16)
        text_raw = text_ref[:, lanes]
        text_keys = (text_raw * inverse_rms(text_raw) * gain_ref[2:3, lanes]).astype(jnp.bfloat16)
        tk_ref[:, lanes] = text_keys
        text_values = text_value_ref[:, lanes].astype(jnp.bfloat16)
        stacked = stack_heads(queries)
        scores = dot_right(stacked, keys) * scaling
        scores = jnp.exp(scores - jnp.max(scores, axis=-1, keepdims=True))
        own_out = dot(scores.astype(jnp.bfloat16), values) / jnp.sum(scores, axis=-1, keepdims=True)
        text = dot_right(stacked, text_keys) * scaling
        text = jnp.where(lane_index(text.shape) < length, text, -1e30)
        text = jnp.exp(text - jnp.max(text, axis=-1, keepdims=True))
        text_out = dot(text.astype(jnp.bfloat16), text_values) / jnp.sum(text, axis=-1, keepdims=True)
        read = join_heads(text_out)
        read_ref[:, lanes] = read
        mixed_ref[:, lanes] = (join_heads(own_out) + gain_ref[3:4, lanes] * read).astype(jnp.bfloat16)

    branch = dot(mixed_ref[...], out_weight_ref[...])

    @pl.when(own)
    def _():
        branch_ref[...] = branch

    @pl.when(jnp.logical_not(own))
    def _():
        core_branch_ref[...] = branch.astype(jnp.bfloat16)


def head_norm_back(grad, raw, gain_row):
    inverse = inverse_rms(raw)
    scaled = grad * gain_row
    normal = raw * inverse
    inner = head_sums(scaled * normal) * (1.0 / HEAD_DIM)
    return inverse * (scaled - normal * inner), jnp.sum(grad * normal, axis=0, keepdims=True)

def attend_back_kernel(
    kind_ref,
    len_ref,
    branch_ref,
    core_branch_ref,
    qkv_ref,
    text_ref,
    text_value_ref,
    q_ref,
    k_ref,
    tk_ref,
    read_ref,
    qkv_mine_ref,
    qkv_other_ref,
    out_weight_ref,
    gain_ref,
    cos_ref,
    sin_ref,
    branch_out_ref,
    gqkv_ref,
    gtext_ref,
    grad_rows_ref,
    core_grad_rows_ref,
    gains_ref,
    mixed_ref,
):
    item = pl.program_id(0)
    own = item < pl.num_programs(0) // 2
    kind, length = kind_ref[item], len_ref[item]
    width = q_ref.shape[1]
    cosine, sine = cos_ref[kind], sin_ref[kind]
    scaling = HEAD_DIM ** (-0.5)

    @pl.when(own)
    def _():
        branch_out_ref[...] = branch_ref[...]

    @pl.when(jnp.logical_not(own))
    def _():
        branch_out_ref[...] = core_branch_ref[...]

    mixed_ref[...] = dot_right(branch_out_ref[...], out_weight_ref[...])

    @pl.when(item == 0)
    def _():
        gains_ref[...] = jnp.zeros_like(gains_ref)

    def one(stacked, keys, values, stacked_grad, valid):
        scores = dot_right(keys, stacked) * scaling
        if valid is not None:
            scores = jnp.where(valid(scores.shape), scores, -1e30)
        probs = jnp.exp(scores - jnp.max(scores, axis=0, keepdims=True))
        probs = probs * (1.0 / jnp.sum(probs, axis=0, keepdims=True))
        grad_values = dot(probs.astype(jnp.bfloat16), stacked_grad)
        grad_probs = dot_right(values, stacked_grad)
        inner = jnp.sum(probs * grad_probs, axis=0, keepdims=True)
        grad_scores = (probs * (grad_probs - inner)).astype(jnp.bfloat16)
        grad_keys = dot(grad_scores, stacked) * scaling
        grad_queries = dot_left(keys, grad_scores)
        return grad_queries, grad_keys, grad_values

    for at in range(0, width, LANES):
        lanes = slice(at, at + LANES)
        grad = mixed_ref[:, lanes]
        cross = gain_ref[3:4, lanes]
        values = qkv_ref[:, 2 * width + at : 2 * width + at + LANES].astype(jnp.bfloat16)
        text_values = text_value_ref[:, lanes].astype(jnp.bfloat16)
        stacked = stack_heads(q_ref[:, lanes])
        own_queries, own_keys, own_values = one(
            stacked, k_ref[:, lanes], values, stack_heads(grad.astype(jnp.bfloat16)), None
        )
        read_queries, read_keys, read_values = one(
            stacked, tk_ref[:, lanes], text_values, stack_heads((cross * grad).astype(jnp.bfloat16)),
            lambda shape: lax.broadcasted_iota(jnp.int32, shape, 0) < length,
        )
        grad_queries = join_heads((own_queries + read_queries).T) * scaling
        for part, turned in ((0, grad_queries), (1, own_keys)):
            raw = qkv_ref[:, part * width + at : part * width + at + LANES]
            back = turned * cosine + partner(turned * sine)
            grad_raw, gain = head_norm_back(back, raw, gain_ref[part : part + 1, lanes])
            gqkv_ref[:, part * width + at : part * width + at + LANES] = grad_raw.astype(jnp.bfloat16)
            gains_ref[part : part + 1, lanes] += gain
        gqkv_ref[:, 2 * width + at : 2 * width + at + LANES] = own_values.astype(jnp.bfloat16)
        grad_text, gain = head_norm_back(read_keys, text_ref[:, lanes], gain_ref[2:3, lanes])
        gtext_ref[:, lanes] = grad_text.astype(jnp.bfloat16)
        gains_ref[2:3, lanes] += gain
        gtext_ref[:, width + at : width + at + LANES] = read_values.astype(jnp.bfloat16)
        gains_ref[3:4, lanes] += jnp.sum(grad * read_ref[:, lanes], axis=0, keepdims=True)

    half = qkv_mine_ref.shape[0]
    low = dot_right(gqkv_ref[...], qkv_mine_ref[...])
    high = dot_right(gqkv_ref[...], qkv_other_ref[...])

    @pl.when(own)
    def _():
        grad_rows_ref[:, :half] = low
        grad_rows_ref[:, half:] = high

    @pl.when(jnp.logical_not(own))
    def _():
        core_grad_rows_ref[:, :half] = low.astype(jnp.bfloat16)
        core_grad_rows_ref[:, half:] = high.astype(jnp.bfloat16)


def whole_spec(array):
    zeros = (0,) * len(array.shape)
    return pl.BlockSpec(array.shape, lambda *_: zeros, pipeline_mode=pl.Buffered(1))


def mine_spec(array, steps):
    half = steps // 2
    return pl.BlockSpec(
        (array.shape[0] // half, array.shape[1]), lambda i, *_: (jnp.minimum(i, half - 1), 0)
    )


def core_spec(array, steps):
    half = steps // 2
    return pl.BlockSpec(
        (array.shape[0] // half, array.shape[1]), lambda i, *_: (jnp.maximum(i - half, 0), 0)
    )


def pair_specs(pair_of_arrays, steps):
    return [mine_spec(pair_of_arrays[0], steps), core_spec(pair_of_arrays[1], steps)]


def step_spec(array, steps):
    return pl.BlockSpec((array.shape[0] // steps, array.shape[1]), lambda i, *_: (i, 0))


def summed_spec(array):
    return pl.BlockSpec(array.shape, lambda i, *_: (0, 0))


def shaped(count, columns, dtype=jnp.bfloat16):
    return jax.ShapeDtypeStruct((count, columns), dtype)


def parameters():
    return pltpu.CompilerParams(dimension_semantics=("arbitrary",), vmem_limit_bytes=58 * MIB)


def attend(scalars, rows, captions, qkv_rank, key_rank, value_rank, out_rank, tables):
    items = scalars[0].shape[0]
    count, width = 2 * rows[0].shape[0], out_rank.shape[0]
    text_count = 2 * captions[0].shape[0]
    outs = [
        shaped(count, D),
        shaped(text_count, TEXT_DIM),
        shaped(count, 3 * width, jnp.float32),
        shaped(text_count, width, jnp.float32),
        shaped(text_count, width, jnp.float32),
        shaped(count, width),
        shaped(count, width),
        shaped(text_count, width),
        shaped(count, width),
        shaped(count, width, jnp.float32),
    ]
    branch = (shaped(count // 2, D, jnp.float32), shaped(count // 2, D))
    whole = [*qkv_rank, *key_rank, *value_rank, out_rank, *tables]
    rows, captions, *kept, branch_mine, branch_core = pl.pallas_call(
        attend_kernel,
        grid_spec=pltpu.PrefetchScalarGridSpec(
            num_scalar_prefetch=2,
            grid=(items,),
            in_specs=pair_specs(rows, items)
            + pair_specs(captions, items)
            + [whole_spec(array) for array in whole],
            out_specs=[step_spec(array, items) for array in outs] + pair_specs(branch, items),
        ),
        out_shape=[*outs, *branch],
        compiler_params=parameters(),
        name="attend",
    )(*scalars, *rows, *captions, *whole)
    return rows, captions, kept, (branch_mine, branch_core)


def attend_back(scalars, grad_branch, kept, qkv_rank, out_rank, tables):
    items = scalars[0].shape[0]
    qkv_raw, text_raw, text_value_raw, queries, keys, text_keys, _, read = kept
    count, width = queries.shape
    outs = [
        shaped(count, D),
        shaped(count, 3 * width),
        shaped(text_raw.shape[0], 2 * width),
    ]
    rows = (shaped(count // 2, D, jnp.float32), shaped(count // 2, D))
    gains = shaped(4, width, jnp.float32)
    by_item = [qkv_raw, text_raw, text_value_raw, queries, keys, text_keys, read]
    whole = [*qkv_rank, out_rank, *tables]
    branch, qkv, text, rows_mine, rows_core, gains = pl.pallas_call(
        attend_back_kernel,
        grid_spec=pltpu.PrefetchScalarGridSpec(
            num_scalar_prefetch=2,
            grid=(items,),
            in_specs=pair_specs(grad_branch, items)
            + [step_spec(array, items) for array in by_item]
            + [whole_spec(array) for array in whole],
            out_specs=[step_spec(array, items) for array in outs]
            + pair_specs(rows, items)
            + [summed_spec(gains)],
            scratch_shapes=[pltpu.VMEM((count // items, width), jnp.float32)],
        ),
        out_shape=[*outs, *rows, gains],
        compiler_params=parameters(),
        name="attend_back",
    )(*scalars, *grad_branch, *by_item, *whole)
    return branch, qkv, text, (rows_mine, rows_core), gains


def row_cuts(lefts, rights):
    cuts, left, right, left_row, right_row = [], 0, 0, 0, 0
    while left < len(lefts):
        count = min(lefts[left].shape[0] - left_row, rights[right].shape[0] - right_row)
        cuts.append((left, left_row, right, right_row, count))
        left_row, right_row = left_row + count, right_row + count
        if left_row == lefts[left].shape[0]:
            left, left_row = left + 1, 0
        if right_row == rights[right].shape[0]:
            right, right_row = right + 1, 0
    return cuts


def product(lefts, rights, first, lanes, dtype):
    columns = rights[0].shape[1]
    if lanes % LANES:
        block = lanes
    else:
        block = 384 if lanes % 384 == 0 else math.gcd(lanes, 512)
    cuts = row_cuts(lefts, rights)

    def kernel(first_ref, *refs):
        left_refs, right_refs, out_ref = refs[: len(lefts)], refs[len(lefts) : -1], refs[-1]
        total = None
        for left, left_row, right, right_row, count in cuts:
            term = dot_left(
                left_refs[left][left_row : left_row + count, :],
                right_refs[right][right_row : right_row + count, :],
            )
            total = term if total is None else total + term
        out_ref[...] = total.astype(out_ref.dtype)

    return pl.pallas_call(
        kernel,
        grid_spec=pltpu.PrefetchScalarGridSpec(
            num_scalar_prefetch=1,
            grid=(lanes // block,),
            in_specs=[
                pl.BlockSpec((array.shape[0], block), lambda i, first: (0, first[0] // block + i))
                for array in lefts
            ]
            + [whole_spec(array) for array in rights],
            out_specs=pl.BlockSpec((block, columns), lambda i, first: (i, 0)),
        ),
        out_shape=shaped(lanes, columns, dtype),
        compiler_params=parameters(),
        name="product",
    )(jnp.reshape(first, (1,)).astype(jnp.int32), *lefts, *rights)


def feed_kernel(
    rows_ref,
    core_rows_ref,
    result_ref,
    core_result_ref,
    gate_mine_ref,
    gate_other_ref,
    up_mine_ref,
    up_other_ref,
    down_ref,
    rows,
    result,
    hidden_ref,
    grad_gate_ref,
    grad_up_ref,
    grad_ref,
    core_grad_ref,
):
    own = pl.program_id(0) < pl.num_programs(0) // 2

    @pl.when(own)
    def _():
        rows[...] = rows_ref[...]
        result[...] = result_ref[...]

    @pl.when(jnp.logical_not(own))
    def _():
        rows[...] = core_rows_ref[...]
        result[...] = core_result_ref[...]

    gate = dot_cut(rows, gate_mine_ref, gate_other_ref)
    up = dot_cut(rows, up_mine_ref, up_other_ref)
    grad_hidden = dot_right(result[...], down_ref[...])
    sigmoid = 1.0 / (1.0 + jnp.exp(-gate))
    silu = gate * sigmoid
    hidden_ref[...] = (silu * up).astype(jnp.bfloat16)
    grad_gate = (grad_hidden * up * (sigmoid + silu * (1.0 - sigmoid))).astype(jnp.bfloat16)
    grad_up = (grad_hidden * silu).astype(jnp.bfloat16)
    grad_gate_ref[...] = grad_gate
    grad_up_ref[...] = grad_up
    half = gate_mine_ref.shape[0]
    low = dot_right(grad_gate, gate_mine_ref[...]) + dot_right(grad_up, up_mine_ref[...])
    high = dot_right(grad_gate, gate_other_ref[...]) + dot_right(grad_up, up_other_ref[...])

    @pl.when(own)
    def _():
        grad_ref[:, :half] = low
        grad_ref[:, half:] = high

    @pl.when(jnp.logical_not(own))
    def _():
        core_grad_ref[:, :half] = low.astype(jnp.bfloat16)
        core_grad_ref[:, half:] = high.astype(jnp.bfloat16)


def feed(rows, grad_result, gate_rank, up_rank, down_rank):
    count, width = 2 * rows[0].shape[0], down_rank.shape[0]
    block = 256
    steps = count // block
    outs = [shaped(count, D)] * 2 + [shaped(count, width)] * 3
    grads = (shaped(count // 2, D, jnp.float32), shaped(count // 2, D))
    whole = [*gate_rank, *up_rank, down_rank]
    *outs, grad_mine, grad_core = pl.pallas_call(
        feed_kernel,
        grid=(steps,),
        in_specs=pair_specs(rows, steps)
        + pair_specs(grad_result, steps)
        + [whole_spec(array) for array in whole],
        out_specs=[step_spec(array, steps) for array in outs] + pair_specs(grads, steps),
        out_shape=[*outs, *grads],
        compiler_params=parameters(),
        name="feed",
    )(*rows, *grad_result, *whole)
    return *outs, (grad_mine, grad_core)


def swap(block, axis, count=2, step=1):
    return lax.ppermute(block, axis, [(at, at ^ step) for at in range(count)])


def spread(block, axis, count):
    if count & (count - 1):
        return lax.all_gather(block, axis)
    block, step = block[None], 1
    while step < count:
        other = swap(block, axis, count, step)
        low = (lax.axis_index(axis) & step) == 0
        block = jnp.where(
            low, jnp.concatenate([block, other]), jnp.concatenate([other, block])
        )
        step *= 2
    return block


def fold(block, axis, count):
    if count & (count - 1):
        return lax.psum_scatter(block, axis, scatter_dimension=0)
    step = count // 2
    while step:
        half = block.shape[0] // 2
        low = (lax.axis_index(axis) & step) == 0
        lower, upper = block[:half], block[half:]
        block = jnp.where(low, lower, upper) + swap(
            jnp.where(low, upper, lower), axis, count, step
        )
        step //= 2
    return block[0]


def trade_ranks(block):
    return lax.all_to_all(block, ("mid", "core"), 0, 0, tiled=True)


def pick(stack, index):
    return lax.dynamic_index_in_dim(stack, index, 0, keepdims=False)


def pair(rows):
    return (rows, swap(rows, "core"))


def settle(partial):
    mine, core = partial
    return mine + swap(core, "core").astype(jnp.float32)


def settle_move(across):
    return swap(across, "mid").astype(jnp.float32)


class Layout:
    def __init__(self, hi, rep, out_rows):
        self.hi, self.rep = hi, rep
        self.aligned = (rep * out_rows) % HEAD_DIM == 0
        self.head_groups = hi if self.aligned else 1
        self.rank = lax.axis_index("mid") * 2 + lax.axis_index("core")

    def by_rank(self, weight, sections, groups):
        rows, columns = weight.shape
        width = columns // (sections * groups * RANKS)
        view = weight.reshape(rows, sections * groups, RANKS, width)
        view = jnp.transpose(view, (2, 0, 1, 3))
        return view.reshape(RANKS, rows, sections * groups * width)

    def from_ranks(self, blocks, sections, groups):
        _, rows, per_rank = blocks.shape
        width = per_rank // (sections * groups)
        view = blocks.reshape(RANKS, rows, sections * groups, width)
        return jnp.transpose(view, (1, 2, 0, 3)).reshape(rows, RANKS * per_rank)

    def ordered(self, values):
        if self.hi != 2:
            return values
        half = values.shape[-1] // 2
        turned = jnp.concatenate([values[..., half:], values[..., :half]], axis=-1)
        return jnp.where(lax.axis_index("hi") == 0, values, turned)

    def across_hi(self, block):
        if self.hi == 2:
            return (block, swap(block, "hi"))
        return spread(block, "hi", self.hi)

    def natural_hi(self, blocks):
        if self.hi != 2:
            return blocks
        mine, other = blocks
        low = lax.axis_index("hi") == 0
        return jnp.stack([jnp.where(low, mine, other), jnp.where(low, other, mine)])

    def halves(self, blocks):
        if self.hi == 2:
            return tuple(self.natural_rows(block[None]) for block in blocks)
        return tuple(jnp.split(self.natural_rows(blocks), 2))

    def natural_rows(self, stacked):
        view = stacked.reshape(stacked.shape[0], self.rep, RANKS, -1, stacked.shape[-1])
        return jnp.transpose(view, (0, 2, 1, 3, 4)).reshape(-1, stacked.shape[-1])

    def product_moved(self, lefts, rights, first=None):
        lanes = lefts[0].shape[1]
        if self.hi != 2:
            return product(lefts, rights, 0, lanes, jnp.bfloat16)
        return product(lefts, rights, lanes // 2 if first is None else first, lanes // 2, jnp.bfloat16)

    def move(self, moved):
        if self.hi == 2:
            return swap(moved, "hi")
        return fold(moved.reshape(self.hi, -1, moved.shape[1]), "hi", self.hi)

    def product_kept(self, lefts, rights, first=0):
        if self.hi != 2:
            return None
        return product(lefts, rights, first, lefts[0].shape[1] // 2, jnp.float32)

    def total(self, kept, arrived):
        if kept is None:
            return arrived
        return (kept + arrived.astype(jnp.float32)).astype(jnp.bfloat16)

    def by_rep(self, summed):
        view = summed.reshape(RANKS, self.rep, -1, summed.shape[1])
        return jnp.transpose(view, (1, 0, 2, 3)).reshape(self.rep, -1, summed.shape[1])

    def reduce(self, blocks):
        flat = blocks.reshape(-1, blocks.shape[-1])
        return lax.psum_scatter(flat, "rep", scatter_dimension=0, tiled=True)

    def rank_lanes(self, rows, groups):
        view = rows.reshape(rows.shape[0], groups, RANKS, -1)
        return lax.dynamic_index_in_dim(view, self.rank, 2, keepdims=False).reshape(rows.shape[0], -1)

    def place_lanes(self, row):
        view = row.reshape(self.head_groups, 1, -1)
        at = (jnp.arange(RANKS) == self.rank).astype(row.dtype)[None, :, None]
        return (view * at).reshape(-1)


def fence(*values):
    return lax.optimization_barrier(values)


def local(
    hi_count,
    rep_count,
    tokens,
    condition,
    caption,
    caption_len,
    item_kind,
    out_cotangent,
    norm_gains,
    ada_weight,
    qkv_weight,
    out_weight,
    text_weight,
    gate_up_weight,
    down_weight,
):
    bf16, f32 = jnp.bfloat16, jnp.float32
    item_count = condition.shape[0]
    item_len = tokens.shape[0] // item_count
    row_count = item_count * item_len
    rows = qkv_weight.shape[0]
    plan = Layout(hi_count, rep_count, out_weight.shape[0])
    rank_width = HEADS // RANKS * HEAD_DIM
    hi_at, mid_at, core_at, rep_at = [lax.axis_index(name) for name in AXES]
    device_shape = (hi_count, 2, 2, rep_count)

    feed_width = FF // RANKS
    devices = hi_count * RANKS * rep_count
    block_at = (hi_at * RANKS + plan.rank) * rep_count + rep_at

    def z_gather(block):
        return lax.all_gather(block.reshape(-1, block.shape[-1]), "rep", tiled=True)

    down_z = z_gather(down_weight)
    qkv_mine = trade_ranks(plan.by_rank(qkv_weight, 3, plan.head_groups))
    qkv_mine = qkv_mine.reshape(RANKS * rows, 3 * rank_width)
    if plan.aligned:
        qkv_mine = jnp.concatenate([qkv_mine, out_weight.reshape(-1, 3 * rank_width)])
    else:
        out_whole = lax.all_gather(out_weight, AXES, axis=0, tiled=True)
        out_rank = pick(out_whole.reshape(RANKS, rank_width, D), plan.rank)
    text_mine = trade_ranks(plan.by_rank(text_weight, 2, plan.head_groups))
    captions_near = pair(plan.ordered(caption.reshape(-1, TEXT_DIM)))

    head = condition.reshape(item_count, devices, rows)
    head = jnp.transpose(head, (1, 0, 2)).reshape(devices, -1)
    rest = jnp.concatenate(
        [norm_gains.reshape(-1), caption_len.astype(bf16), item_kind.astype(bf16)]
    )
    small = jnp.concatenate([head, jnp.broadcast_to(rest, (devices, rest.size))], axis=1)
    small = lax.all_to_all(small, AXES, 0, 0, tiled=True)
    cut = [head.shape[1], head.shape[1] + norm_gains.size]
    cut.append(cut[1] + item_count)
    conditions, gains, lengths, kinds = jnp.split(small, cut, axis=-1)
    activated_mine = jax.nn.silu(conditions.astype(f32)).astype(bf16).reshape(-1, rows)
    gain_rows = jnp.moveaxis(gains.astype(f32).reshape(devices, 6, -1), 1, 0).reshape(6, D)
    lengths, kinds = [
        values.reshape(device_shape + (item_count,)) for values in (lengths, kinds)
    ]

    def group_items(values):
        view = lax.dynamic_index_in_dim(pick(values, hi_at), rep_at, 2, keepdims=False)
        near, far = pick(view, mid_at), pick(view, 1 - mid_at)
        order = [core_at, 1 - core_at]
        return [
            jnp.concatenate([pick(side, at) for at in order]).astype(jnp.int32)
            for side in (near, far)
        ]

    lengths_sides = group_items(lengths)
    kinds_sides = group_items(kinds)
    cosine, sine = rope_tables(jnp.arange(2), item_len)
    signs = jnp.where(jnp.arange(HEAD_DIM) % (HEAD_DIM // 2) < HEAD_DIM // 4, -1.0, 1.0)
    cosine, sine = jnp.tile(cosine, (1, 1, 2)), jnp.tile(sine * signs, (1, 1, 2))
    head_gains = plan.rank_lanes(gain_rows, plan.head_groups)
    cross_gate = jnp.tanh(head_gains[5])
    head_gains = jnp.concatenate([head_gains[1:4], cross_gate[None]])
    tables = (head_gains, cosine, sine)
    scalars = list(zip(kinds_sides, lengths_sides, strict=True))

    partial = dot(activated_mine, ada_weight).astype(bf16).reshape(devices, item_count, 4 * D)
    text_key_mine, text_value_mine = text_mine[..., :rank_width], text_mine[..., rank_width:]
    down_z, qkv_mine, text_key_mine, text_value_mine, captions_near, partial = fence(
        down_z, qkv_mine, text_key_mine, text_value_mine, captions_near, partial
    )
    qkv_z = z_gather(qkv_mine)
    down_rank = plan.across_hi(down_z)
    gate_up_mine = trade_ranks(plan.by_rank(gate_up_weight, 2, hi_count))
    gate_mine, up_mine = gate_up_mine[..., :feed_width], gate_up_mine[..., feed_width:]
    modulation = jnp.sum(lax.all_to_all(partial, AXES, 0, 0, tiled=True).astype(f32), axis=0)
    qkv_z, down_rank, modulation, gate_mine, up_mine = fence(
        qkv_z, down_rank, modulation, gate_mine, up_mine
    )

    scale_attn, gate_attn, scale_mlp, gate_mlp = jnp.split(modulation, 4, axis=1)
    text_key_z = z_gather(text_key_mine)
    captions_far = swap(captions_near[0], "mid")
    qkv_rank = plan.across_hi(qkv_z)
    down_rank = plan.natural_hi(down_rank).reshape(feed_width, D)
    token_rows = tokens.astype(f32).reshape(item_count, item_len, D)
    normed = modulate(token_rows, gain_rows[0], scale_attn)
    normed = plan.ordered(normed.astype(bf16).reshape(row_count, D))
    mlp_gate = jnp.tanh(gate_mlp)[:, None, :]
    grad_top = out_cotangent.astype(f32).reshape(item_count, item_len, D)
    grad_result = (mlp_gate * grad_top).astype(bf16).reshape(row_count, D)
    normed_near, result_near = pair(normed), pair(grad_result)
    text_key_z, captions_far, qkv_rank, down_rank, normed_near, result_near = fence(
        text_key_z, captions_far, qkv_rank, down_rank, normed_near, result_near
    )

    text_value_z = z_gather(text_value_mine)
    text_key_rank = plan.across_hi(text_key_z)
    normed_far = swap(normed_near[0], "mid")
    captions_far = pair(captions_far)
    text_value_z, text_key_rank, normed_far, captions_far = fence(
        text_value_z, text_key_rank, normed_far, captions_far
    )

    gate_z = z_gather(gate_mine)
    text_value_rank = plan.across_hi(text_value_z)
    result_far = swap(result_near[0], "mid")
    normed_far = pair(normed_far)
    if plan.aligned:
        blocks = [block.reshape(rep_count, -1, 3 * rank_width) for block in qkv_rank]
        out_rank = plan.natural_hi([block[:, RANKS * rows :].reshape(-1, D) for block in blocks])
        out_rank = out_rank.reshape(rank_width, D)
        qkv_rank = [block[:, : RANKS * rows].reshape(-1, 3 * rank_width) for block in blocks]
        qkv_rank = qkv_rank if hi_count == 2 else jnp.stack(qkv_rank)
    qkv_rank, text_key_rank = plan.halves(qkv_rank), plan.halves(text_key_rank)
    gate_z, text_value_rank, result_far, normed_far, qkv_rank, out_rank, text_key_rank = fence(
        gate_z, text_value_rank, result_far, normed_far, qkv_rank, out_rank, text_key_rank
    )

    up_z = z_gather(up_mine)
    gate_rank = plan.across_hi(gate_z)
    attend_weights = (qkv_rank, text_key_rank, plan.halves(text_value_rank), out_rank, tables)
    normed_far, captions_far, kept_far, partial_far = attend(
        scalars[1], normed_far, captions_far, *attend_weights
    )
    up_z, gate_rank, normed_far, captions_far, kept_far, partial_far, attend_weights = fence(
        up_z, gate_rank, normed_far, captions_far, kept_far, partial_far, attend_weights
    )

    across = settle(partial_far).astype(bf16)
    across, normed_near, up_z = fence(across, normed_near, up_z)
    up_rank = plan.across_hi(up_z)
    arrived = settle_move(across)
    normed_near, captions_near, kept_near, partial_near = attend(
        scalars[0], normed_near, captions_near, *attend_weights
    )
    result_far = pair(result_far)
    gate_rank = plan.halves(gate_rank)
    up_rank, arrived, normed_near, captions_near, kept_near, partial_near, result_far, gate_rank = fence(
        up_rank, arrived, normed_near, captions_near, kept_near, partial_near, result_far, gate_rank
    )

    branch = (settle(partial_near) + arrived).reshape(item_count, item_len, D)
    attn_gate = jnp.tanh(gate_attn)[:, None, :]
    middle = token_rows + attn_gate * branch
    mlp_input = modulate(middle, gain_rows[4], scale_mlp)
    mlp_input = plan.ordered(mlp_input.astype(bf16).reshape(row_count, D))
    up_rank = plan.halves(up_rank)
    mlp_input, up_rank = fence(mlp_input, up_rank)

    feed_weights = (gate_rank, up_rank, down_rank)
    input_far = swap(mlp_input, "mid")
    input_near, result_near, hidden_near, gate_near, up_near, partial_near = feed(
        pair(mlp_input), result_near, *feed_weights
    )
    input_far, input_near, result_near, hidden_near, gate_near, up_near, partial_near = fence(
        input_far, input_near, result_near, hidden_near, gate_near, up_near, partial_near
    )
    input_far, result_far, hidden_far, gate_far, up_far, partial_far = feed(
        pair(input_far), result_far, *feed_weights
    )
    across = settle(partial_far).astype(bf16)
    inputs, results = (input_near, input_far), (result_near, result_far)
    gate_rows, up_rows, hidden_rows = (gate_near, gate_far), (up_near, up_far), (hidden_near, hidden_far)
    across, gate_rows, up_rows, hidden_rows = fence(across, gate_rows, up_rows, hidden_rows)
    arrived = settle_move(across)
    gate_moved = plan.product_moved(inputs, gate_rows)
    up_moved = plan.product_moved(inputs, up_rows)
    hidden_first = hi_at * (feed_width // 2)
    down_moved = plan.product_moved(hidden_rows, results, feed_width // 2 - hidden_first)
    gate_kept = plan.product_kept(inputs, gate_rows)
    arrived, gate_moved, up_moved, down_moved, gate_kept, partial_near = fence(
        arrived, gate_moved, up_moved, down_moved, gate_kept, partial_near
    )

    gate_moved, up_moved = plan.move(gate_moved), plan.move(up_moved)
    grad_mlp_input = plan.ordered(settle(partial_near) + arrived)
    _, pull_mlp_norm = jax.vjp(modulate, middle, gain_rows[4], scale_mlp)
    grad_middle_norm, grad_mlp_gain, grad_scale_mlp = pull_mlp_norm(
        grad_mlp_input.reshape(item_count, item_len, D)
    )
    grad_middle = grad_top + grad_middle_norm
    grad_attn_gate = jnp.sum(grad_middle * branch, axis=1) * (1.0 - jnp.tanh(gate_attn) ** 2)
    grad_branch = (attn_gate * grad_middle).astype(bf16).reshape(row_count, D)
    (grad_branch,) = fence(grad_branch)

    branch_far = swap(grad_branch, "mid")
    back_weights = (qkv_rank, out_rank, tables)
    branch_near, qkv_near, text_near, rows_near, gain_near = attend_back(
        scalars[0], pair(grad_branch), kept_near, *back_weights
    )
    up_kept = plan.product_kept(inputs, up_rows)
    branch_far, gate_moved, branch_near, qkv_near, text_near, rows_near, gain_near, up_kept = fence(
        branch_far, gate_moved, branch_near, qkv_near, text_near, rows_near, gain_near, up_kept
    )

    gate_grad = plan.by_rep(plan.total(gate_kept, gate_moved))
    gate_grad, branch_far, down_moved = fence(gate_grad, pair(branch_far), down_moved)
    gate_parts = plan.reduce(gate_grad)
    down_moved = plan.move(down_moved)
    branch_far, qkv_far, text_far, rows_far, gain_far = attend_back(
        scalars[1], branch_far, kept_far, *back_weights
    )
    down_kept = plan.product_kept(hidden_rows, results, hidden_first)
    captions, normed_rows = (captions_near, captions_far), (normed_near, normed_far)
    text_rows, qkv_rows, branches = (text_near, text_far), (qkv_near, qkv_far), (branch_near, branch_far)
    text_moved = plan.product_moved(captions, text_rows)
    gate_parts, up_moved, text_rows, qkv_rows, branches, rows_far, gain_far, down_kept, text_moved = fence(
        gate_parts, up_moved, text_rows, qkv_rows, branches, rows_far, gain_far, down_kept, text_moved
    )

    across = settle(rows_far).astype(bf16)
    up_grad = plan.by_rep(plan.total(up_kept, up_moved))
    across, up_grad, text_moved, text_rows, qkv_rows, hidden_rows = fence(
        across, up_grad, text_moved, text_rows, qkv_rows, hidden_rows
    )
    text_moved = plan.move(text_moved)
    up_parts = plan.reduce(up_grad)
    arrived = settle_move(across)
    down_grad = plan.total(down_kept, down_moved).reshape(rep_count, -1, D)
    down_parts = plan.reduce(down_grad)
    qkv_moved = plan.product_moved(normed_rows, qkv_rows)
    text_kept = plan.product_kept(captions, text_rows)
    qkv_kept = plan.product_kept(normed_rows, qkv_rows)
    mixed_rows = [plan.ordered(kept[6]) for kept in (kept_near, kept_far)]
    if plan.aligned:
        out_halves = [
            product([side[:, lanes] for side in mixed_rows], branches, 0, rank_width // 2, bf16)
            for lanes in (slice(0, rank_width // 2), slice(rank_width // 2, None))
        ]
    else:
        out_halves = []
    result_far = [dot(side, down_rank) for side in jnp.split(hidden_rows[1], 2)]
    result_across = settle((result_far[0], result_far[1].astype(bf16))).astype(bf16)
    grad_normed = plan.ordered(settle(rows_near) + arrived)
    text_moved, up_parts, down_parts, grad_normed, qkv_moved, text_kept, qkv_kept, out_halves, result_across = fence(
        text_moved, up_parts, down_parts, grad_normed, qkv_moved, text_kept, qkv_kept, out_halves, result_across
    )

    qkv_moved = plan.move(qkv_moved)
    result = settle_move(result_across)
    if plan.aligned:
        if hi_count == 2:
            out_kept, out_moved = out_halves[0].astype(f32), swap(out_halves[1], "hi")
        else:
            out_kept, out_moved = None, plan.move(jnp.concatenate(out_halves))
    text_grad = plan.by_rep(plan.total(text_kept, text_moved))
    text_parts = plan.reduce(text_grad)
    result_near = [dot(side, down_rank) for side in jnp.split(hidden_rows[0], 2)]
    result = result + settle((result_near[0], result_near[1].astype(bf16)))
    result = result.reshape(item_count, item_len, D)
    layer_out = (middle + mlp_gate * result).astype(bf16).reshape(row_count, D)
    grad_mlp_gate = jnp.sum(grad_top * result, axis=1) * (1.0 - jnp.tanh(gate_mlp) ** 2)
    _, pull_attn_norm = jax.vjp(modulate, token_rows, gain_rows[0], scale_attn)
    grad_token_norm, grad_attn_gain, grad_scale_attn = pull_attn_norm(
        grad_normed.reshape(item_count, item_len, D)
    )
    tokens_grad = (grad_middle + grad_token_norm).reshape(row_count, D)
    qkv_grad = plan.by_rep(plan.total(qkv_kept, qkv_moved))
    if plan.aligned:
        out_grad = plan.total(out_kept, out_moved).reshape(rep_count, -1, 3 * rank_width)
        qkv_grad = jnp.concatenate([qkv_grad, out_grad], axis=1)
    else:
        at = (jnp.arange(RANKS) == plan.rank).astype(bf16)[:, None, None]
        out_grad = product(mixed_rows, branches, 0, rank_width, bf16)
        placed = (out_grad[None] * at).reshape(D, D)
        out_weight_grad = lax.psum_scatter(placed, AXES, scatter_dimension=0, tiled=True).astype(f32)
    text_parts, qkv_grad, grad_mlp_gate, grad_scale_attn, grad_attn_gain = fence(
        text_parts, qkv_grad, grad_mlp_gate, grad_scale_attn, grad_attn_gain
    )
    qkv_parts = plan.reduce(qkv_grad)
    if plan.aligned:
        out_weight_grad = qkv_parts[RANKS * rows :].reshape(-1, D).astype(f32)
        qkv_parts = qkv_parts[: RANKS * rows]

    grad_modulation = jnp.concatenate(
        [grad_scale_attn, grad_attn_gate, grad_scale_mlp, grad_mlp_gate], axis=1
    ).astype(bf16)
    gain_terms = gain_near + gain_far
    gain_terms = gain_terms.at[3].multiply(1.0 - cross_gate**2)
    gain_terms = [plan.place_lanes(row) for row in gain_terms]
    gains_grad = jnp.stack(
        [grad_attn_gain, gain_terms[0], gain_terms[1], gain_terms[2], grad_mlp_gain, gain_terms[3]]
    ).astype(bf16)
    gain_blocks = jnp.moveaxis(gains_grad.reshape(6, devices, -1), 1, 0).reshape(devices, -1)
    modulations = jnp.broadcast_to(grad_modulation.reshape(-1), (devices, grad_modulation.size))
    both = lax.all_to_all(
        jnp.concatenate([modulations, gain_blocks], axis=1), AXES, 0, 0, tiled=True
    )
    ada_weight_grad = dot_left(activated_mine, both[:, : modulations.shape[1]].reshape(-1, 4 * D))
    norm_gains_grad = jnp.sum(both[:, modulations.shape[1] :].astype(f32), axis=0).reshape(6, -1)

    def whole(parts, weight, sections, groups):
        blocks = trade_ranks(parts.reshape(RANKS, weight.shape[0], -1))
        return plan.from_ranks(blocks, sections, groups).astype(f32)

    gate_up_weight_grad = whole(
        jnp.concatenate([gate_parts, up_parts], axis=-1), gate_up_weight, 2, hi_count
    )
    text_weight_grad = whole(text_parts, text_weight, 2, plan.head_groups)
    qkv_weight_grad = whole(qkv_parts, qkv_weight, 3, plan.head_groups)
    down_weight_grad = down_parts.astype(f32)
    return (
        layer_out,
        tokens_grad,
        norm_gains_grad,
        ada_weight_grad,
        qkv_weight_grad,
        out_weight_grad,
        text_weight_grad,
        gate_up_weight_grad,
        down_weight_grad,
    )


def solution(mesh):
    grp, rep = mesh.devices.shape
    hi = grp // RANKS
    inner = Mesh(mesh.devices.reshape(hi, 2, 2, rep), AXES)
    rows = P(AXES, None)

    def step(*arrays):
        return local(hi, rep, *arrays)

    return jax.shard_map(
        step,
        mesh=inner,
        in_specs=(
            rows,
            rows,
            P(AXES, None, None),
            P(AXES),
            P(AXES),
            rows,
            P(None, AXES),
            rows,
            rows,
            rows,
            rows,
            rows,
            rows,
        ),
        out_specs=(rows, rows, P(None, AXES), rows, rows, rows, rows, rows, rows),
        check_vma=False,
    )
```

```python
import math

import jax
import jax.numpy as jnp
from jax import lax
from jax.experimental import pallas as pl
from jax.experimental.pallas import tpu as pltpu
from jax.sharding import Mesh
from jax.sharding import PartitionSpec as P

D = 1536
HEADS = 24
HEAD_DIM = 64
TEXT_DIM = 4096
FF = 4096
SIDE = 16
RANKS = 4
LANES = 128
MIB = 1 << 20
AXES = ("hi", "mid", "core", "rep")


EPSILON = 1e-06


def norm_rows(values, gain_row):
    return (
        values * lax.rsqrt(jnp.mean(values * values, axis=-1, keepdims=True) + EPSILON) * gain_row
    )


def rope_tables(item_kind, item_len):
    position = jnp.arange(item_len, dtype=jnp.int32)[None, :]
    half_side = SIDE // 2
    frame_index = position // (half_side * half_side)
    within = position % (half_side * half_side)
    is_clip = item_kind[:, None] == 1
    row_index = jnp.where(is_clip, frame_index * half_side + within // half_side, position // SIDE)
    columns = jnp.where(is_clip, within % half_side, position % SIDE)
    lane_index = jnp.arange(HEAD_DIM, dtype=jnp.int32)
    quarter = HEAD_DIM // 4
    frequency = jnp.exp(-(lane_index % quarter).astype(jnp.float32) * (math.log(10000.0) / quarter))
    coordinate = jnp.where(
        lane_index[None, None, :] < 2 * quarter, row_index[:, :, None], columns[:, :, None]
    ).astype(jnp.float32)
    angles = coordinate * frequency
    return (jnp.cos(angles), jnp.sin(angles))


def modulate(values, gain_row, scaling):
    return norm_rows(values, gain_row) * (1.0 + scaling[:, None, :])


def silu_product(gate_half, up_half):
    return jax.nn.silu(gate_half) * up_half


def dot(left, right):
    return jnp.dot(left, right, preferred_element_type=jnp.float32)


def dot_left(left, right):
    return lax.dot_general(left, right, (((0,), (0,)), ((), ())), preferred_element_type=jnp.float32)


def dot_right(left, right):
    return lax.dot_general(left, right, (((1,), (1,)), ((), ())), preferred_element_type=jnp.float32)


def lane_index(shape):
    return lax.broadcasted_iota(jnp.int32, shape, len(shape) - 1)

def head_sums(values):
    first = lane_index(values.shape) < HEAD_DIM
    low = jnp.sum(jnp.where(first, values, 0.0), axis=-1, keepdims=True)
    high = jnp.sum(jnp.where(first, 0.0, values), axis=-1, keepdims=True)
    return jnp.where(first, low, high)

def partner(values):
    quarter = HEAD_DIM // 4
    width = values.shape[-1]
    low = lane_index(values.shape) % (2 * quarter) < quarter
    return jnp.where(low, pltpu.roll(values, width - quarter, 1), pltpu.roll(values, quarter, 1))

def stack_heads(values):
    first = lane_index(values.shape) < HEAD_DIM
    zero = jnp.zeros_like(values)
    return jnp.concatenate([jnp.where(first, values, zero), jnp.where(first, zero, values)])

def join_heads(stacked):
    rows = stacked.shape[0] // 2
    first = lane_index((rows, stacked.shape[1])) < HEAD_DIM
    return jnp.where(first, stacked[:rows], stacked[rows:])

def inverse_rms(raw):
    return lax.rsqrt(head_sums(raw * raw) * (1.0 / HEAD_DIM) + EPSILON)

def dot_cut(rows, mine, other):
    half = mine.shape[0]
    return dot(rows[:, :half], mine[...]) + dot(rows[:, half:], other[...])


def attend_kernel(
    kind_ref,
    len_ref,
    rows_ref,
    core_rows_ref,
    caption_ref,
    core_caption_ref,
    qkv_mine_ref,
    qkv_other_ref,
    key_mine_ref,
    key_other_ref,
    value_mine_ref,
    value_other_ref,
    out_weight_ref,
    gain_ref,
    cos_ref,
    sin_ref,
    rows_out_ref,
    caption_out_ref,
    qkv_ref,
    text_ref,
    text_value_ref,
    q_ref,
    k_ref,
    tk_ref,
    mixed_ref,
    read_ref,
    branch_ref,
    core_branch_ref,
):
    item = pl.program_id(0)
    own = item < pl.num_programs(0) // 2
    kind, length = kind_ref[item], len_ref[item]
    width = q_ref.shape[1]
    cosine, sine = cos_ref[kind], sin_ref[kind]
    scaling = HEAD_DIM ** (-0.5)

    @pl.when(own)
    def _():
        rows_out_ref[...] = rows_ref[...]
        caption_out_ref[...] = caption_ref[...]

    @pl.when(jnp.logical_not(own))
    def _():
        rows_out_ref[...] = core_rows_ref[...]
        caption_out_ref[...] = core_caption_ref[...]

    qkv_ref[...] = dot_cut(rows_out_ref, qkv_mine_ref, qkv_other_ref)
    text_ref[...] = dot_cut(caption_out_ref, key_mine_ref, key_other_ref)
    text_value_ref[...] = dot_cut(caption_out_ref, value_mine_ref, value_other_ref)
    for at in range(0, width, LANES):
        lanes = slice(at, at + LANES)
        turned = []
        for part, out_ref in ((0, q_ref), (1, k_ref)):
            raw = qkv_ref[:, part * width + at : part * width + at + LANES]
            normal = raw * inverse_rms(raw) * gain_ref[part : part + 1, lanes]
            rows = (normal * cosine + partner(normal) * sine).astype(jnp.bfloat16)
            out_ref[:, lanes] = rows
            turned.append(rows)
        queries, keys = turned
        values = qkv_ref[:, 2 * width + at : 2 * width + at + LANES].astype(jnp.bfloat16)
        text_raw = text_ref[:, lanes]
        text_keys = (text_raw * inverse_rms(text_raw) * gain_ref[2:3, lanes]).astype(jnp.bfloat16)
        tk_ref[:, lanes] = text_keys
        text_values = text_value_ref[:, lanes].astype(jnp.bfloat16)
        stacked = stack_heads(queries)
        scores = dot_right(stacked, keys) * scaling
        scores = jnp.exp(scores - jnp.max(scores, axis=-1, keepdims=True))
        own_out = dot(scores.astype(jnp.bfloat16), values) / jnp.sum(scores, axis=-1, keepdims=True)
        text = dot_right(stacked, text_keys) * scaling
        text = jnp.where(lane_index(text.shape) < length, text, -1e30)
        text = jnp.exp(text - jnp.max(text, axis=-1, keepdims=True))
        text_out = dot(text.astype(jnp.bfloat16), text_values) / jnp.sum(text, axis=-1, keepdims=True)
        read = join_heads(text_out)
        read_ref[:, lanes] = read
        mixed_ref[:, lanes] = (join_heads(own_out) + gain_ref[3:4, lanes] * read).astype(jnp.bfloat16)

    branch = dot(mixed_ref[...], out_weight_ref[...])

    @pl.when(own)
    def _():
        branch_ref[...] = branch

    @pl.when(jnp.logical_not(own))
    def _():
        core_branch_ref[...] = branch.astype(jnp.bfloat16)


def head_norm_back(grad, raw, gain_row):
    inverse = inverse_rms(raw)
    scaled = grad * gain_row
    normal = raw * inverse
    inner = head_sums(scaled * normal) * (1.0 / HEAD_DIM)
    return inverse * (scaled - normal * inner), jnp.sum(grad * normal, axis=0, keepdims=True)

def attend_back_kernel(
    kind_ref,
    len_ref,
    branch_ref,
    core_branch_ref,
    qkv_ref,
    text_ref,
    text_value_ref,
    q_ref,
    k_ref,
    tk_ref,
    read_ref,
    qkv_mine_ref,
    qkv_other_ref,
    out_weight_ref,
    gain_ref,
    cos_ref,
    sin_ref,
    branch_out_ref,
    gqkv_ref,
    gtext_ref,
    grad_rows_ref,
    core_grad_rows_ref,
    gains_ref,
    mixed_ref,
):
    item = pl.program_id(0)
    own = item < pl.num_programs(0) // 2
    kind, length = kind_ref[item], len_ref[item]
    width = q_ref.shape[1]
    cosine, sine = cos_ref[kind], sin_ref[kind]
    scaling = HEAD_DIM ** (-0.5)

    @pl.when(own)
    def _():
        branch_out_ref[...] = branch_ref[...]

    @pl.when(jnp.logical_not(own))
    def _():
        branch_out_ref[...] = core_branch_ref[...]

    mixed_ref[...] = dot_right(branch_out_ref[...], out_weight_ref[...])

    @pl.when(item == 0)
    def _():
        gains_ref[...] = jnp.zeros_like(gains_ref)

    def one(stacked, keys, values, stacked_grad, valid):
        scores = dot_right(keys, stacked) * scaling
        if valid is not None:
            scores = jnp.where(valid(scores.shape), scores, -1e30)
        probs = jnp.exp(scores - jnp.max(scores, axis=0, keepdims=True))
        probs = probs * (1.0 / jnp.sum(probs, axis=0, keepdims=True))
        grad_values = dot(probs.astype(jnp.bfloat16), stacked_grad)
        grad_probs = dot_right(values, stacked_grad)
        inner = jnp.sum(probs * grad_probs, axis=0, keepdims=True)
        grad_scores = (probs * (grad_probs - inner)).astype(jnp.bfloat16)
        grad_keys = dot(grad_scores, stacked) * scaling
        grad_queries = dot_left(keys, grad_scores)
        return grad_queries, grad_keys, grad_values

    for at in range(0, width, LANES):
        lanes = slice(at, at + LANES)
        grad = mixed_ref[:, lanes]
        cross = gain_ref[3:4, lanes]
        values = qkv_ref[:, 2 * width + at : 2 * width + at + LANES].astype(jnp.bfloat16)
        text_values = text_value_ref[:, lanes].astype(jnp.bfloat16)
        stacked = stack_heads(q_ref[:, lanes])
        own_queries, own_keys, own_values = one(
            stacked, k_ref[:, lanes], values, stack_heads(grad.astype(jnp.bfloat16)), None
        )
        read_queries, read_keys, read_values = one(
            stacked, tk_ref[:, lanes], text_values, stack_heads((cross * grad).astype(jnp.bfloat16)),
            lambda shape: lax.broadcasted_iota(jnp.int32, shape, 0) < length,
        )
        grad_queries = join_heads((own_queries + read_queries).T) * scaling
        for part, turned in ((0, grad_queries), (1, own_keys)):
            raw = qkv_ref[:, part * width + at : part * width + at + LANES]
            back = turned * cosine + partner(turned * sine)
            grad_raw, gain = head_norm_back(back, raw, gain_ref[part : part + 1, lanes])
            gqkv_ref[:, part * width + at : part * width + at + LANES] = grad_raw.astype(jnp.bfloat16)
            gains_ref[part : part + 1, lanes] += gain
        gqkv_ref[:, 2 * width + at : 2 * width + at + LANES] = own_values.astype(jnp.bfloat16)
        grad_text, gain = head_norm_back(read_keys, text_ref[:, lanes], gain_ref[2:3, lanes])
        gtext_ref[:, lanes] = grad_text.astype(jnp.bfloat16)
        gains_ref[2:3, lanes] += gain
        gtext_ref[:, width + at : width + at + LANES] = read_values.astype(jnp.bfloat16)
        gains_ref[3:4, lanes] += jnp.sum(grad * read_ref[:, lanes], axis=0, keepdims=True)

    half = qkv_mine_ref.shape[0]
    low = dot_right(gqkv_ref[...], qkv_mine_ref[...])
    high = dot_right(gqkv_ref[...], qkv_other_ref[...])

    @pl.when(own)
    def _():
        grad_rows_ref[:, :half] = low
        grad_rows_ref[:, half:] = high

    @pl.when(jnp.logical_not(own))
    def _():
        core_grad_rows_ref[:, :half] = low.astype(jnp.bfloat16)
        core_grad_rows_ref[:, half:] = high.astype(jnp.bfloat16)


def whole_spec(array):
    zeros = (0,) * len(array.shape)
    return pl.BlockSpec(array.shape, lambda *_: zeros, pipeline_mode=pl.Buffered(1))


def mine_spec(array, steps):
    half = steps // 2
    return pl.BlockSpec(
        (array.shape[0] // half, array.shape[1]), lambda i, *_: (jnp.minimum(i, half - 1), 0)
    )


def core_spec(array, steps):
    half = steps // 2
    return pl.BlockSpec(
        (array.shape[0] // half, array.shape[1]), lambda i, *_: (jnp.maximum(i - half, 0), 0)
    )


def pair_specs(pair_of_arrays, steps):
    return [mine_spec(pair_of_arrays[0], steps), core_spec(pair_of_arrays[1], steps)]


def step_spec(array, steps):
    return pl.BlockSpec((array.shape[0] // steps, array.shape[1]), lambda i, *_: (i, 0))


def summed_spec(array):
    return pl.BlockSpec(array.shape, lambda i, *_: (0, 0))


def shaped(count, columns, dtype=jnp.bfloat16):
    return jax.ShapeDtypeStruct((count, columns), dtype)


def parameters():
    return pltpu.CompilerParams(dimension_semantics=("arbitrary",), vmem_limit_bytes=58 * MIB)


def attend(scalars, rows, captions, qkv_rank, key_rank, value_rank, out_rank, tables):
    items = scalars[0].shape[0]
    count, width = 2 * rows[0].shape[0], out_rank.shape[0]
    text_count = 2 * captions[0].shape[0]
    outs = [
        shaped(count, D),
        shaped(text_count, TEXT_DIM),
        shaped(count, 3 * width, jnp.float32),
        shaped(text_count, width, jnp.float32),
        shaped(text_count, width, jnp.float32),
        shaped(count, width),
        shaped(count, width),
        shaped(text_count, width),
        shaped(count, width),
        shaped(count, width, jnp.float32),
    ]
    branch = (shaped(count // 2, D, jnp.float32), shaped(count // 2, D))
    whole = [*qkv_rank, *key_rank, *value_rank, out_rank, *tables]
    rows, captions, *kept, branch_mine, branch_core = pl.pallas_call(
        attend_kernel,
        grid_spec=pltpu.PrefetchScalarGridSpec(
            num_scalar_prefetch=2,
            grid=(items,),
            in_specs=pair_specs(rows, items)
            + pair_specs(captions, items)
            + [whole_spec(array) for array in whole],
            out_specs=[step_spec(array, items) for array in outs] + pair_specs(branch, items),
        ),
        out_shape=[*outs, *branch],
        compiler_params=parameters(),
        name="attend",
    )(*scalars, *rows, *captions, *whole)
    return rows, captions, kept, (branch_mine, branch_core)


def attend_back(scalars, grad_branch, kept, qkv_rank, out_rank, tables):
    items = scalars[0].shape[0]
    qkv_raw, text_raw, text_value_raw, queries, keys, text_keys, _, read = kept
    count, width = queries.shape
    outs = [
        shaped(count, D),
        shaped(count, 3 * width),
        shaped(text_raw.shape[0], 2 * width),
    ]
    rows = (shaped(count // 2, D, jnp.float32), shaped(count // 2, D))
    gains = shaped(4, width, jnp.float32)
    by_item = [qkv_raw, text_raw, text_value_raw, queries, keys, text_keys, read]
    whole = [*qkv_rank, out_rank, *tables]
    branch, qkv, text, rows_mine, rows_core, gains = pl.pallas_call(
        attend_back_kernel,
        grid_spec=pltpu.PrefetchScalarGridSpec(
            num_scalar_prefetch=2,
            grid=(items,),
            in_specs=pair_specs(grad_branch, items)
            + [step_spec(array, items) for array in by_item]
            + [whole_spec(array) for array in whole],
            out_specs=[step_spec(array, items) for array in outs]
            + pair_specs(rows, items)
            + [summed_spec(gains)],
            scratch_shapes=[pltpu.VMEM((count // items, width), jnp.float32)],
        ),
        out_shape=[*outs, *rows, gains],
        compiler_params=parameters(),
        name="attend_back",
    )(*scalars, *grad_branch, *by_item, *whole)
    return branch, qkv, text, (rows_mine, rows_core), gains


def row_cuts(lefts, rights):
    cuts, left, right, left_row, right_row = [], 0, 0, 0, 0
    while left < len(lefts):
        count = min(lefts[left].shape[0] - left_row, rights[right].shape[0] - right_row)
        cuts.append((left, left_row, right, right_row, count))
        left_row, right_row = left_row + count, right_row + count
        if left_row == lefts[left].shape[0]:
            left, left_row = left + 1, 0
        if right_row == rights[right].shape[0]:
            right, right_row = right + 1, 0
    return cuts


def product(lefts, rights, first, lanes, dtype):
    columns = rights[0].shape[1]
    if lanes % LANES:
        block = lanes
    else:
        block = 384 if lanes % 384 == 0 else math.gcd(lanes, 512)
    cuts = row_cuts(lefts, rights)

    def kernel(first_ref, *refs):
        left_refs, right_refs, out_ref = refs[: len(lefts)], refs[len(lefts) : -1], refs[-1]
        total = None
        for left, left_row, right, right_row, count in cuts:
            term = dot_left(
                left_refs[left][left_row : left_row + count, :],
                right_refs[right][right_row : right_row + count, :],
            )
            total = term if total is None else total + term
        out_ref[...] = total.astype(out_ref.dtype)

    return pl.pallas_call(
        kernel,
        grid_spec=pltpu.PrefetchScalarGridSpec(
            num_scalar_prefetch=1,
            grid=(lanes // block,),
            in_specs=[
                pl.BlockSpec((array.shape[0], block), lambda i, first: (0, first[0] // block + i))
                for array in lefts
            ]
            + [whole_spec(array) for array in rights],
            out_specs=pl.BlockSpec((block, columns), lambda i, first: (i, 0)),
        ),
        out_shape=shaped(lanes, columns, dtype),
        compiler_params=parameters(),
        name="product",
    )(jnp.reshape(first, (1,)).astype(jnp.int32), *lefts, *rights)


def feed_kernel(
    rows_ref,
    core_rows_ref,
    result_ref,
    core_result_ref,
    gate_mine_ref,
    gate_other_ref,
    up_mine_ref,
    up_other_ref,
    down_ref,
    rows,
    result,
    hidden_ref,
    grad_gate_ref,
    grad_up_ref,
    grad_ref,
    core_grad_ref,
):
    own = pl.program_id(0) < pl.num_programs(0) // 2

    @pl.when(own)
    def _():
        rows[...] = rows_ref[...]
        result[...] = result_ref[...]

    @pl.when(jnp.logical_not(own))
    def _():
        rows[...] = core_rows_ref[...]
        result[...] = core_result_ref[...]

    gate = dot_cut(rows, gate_mine_ref, gate_other_ref)
    up = dot_cut(rows, up_mine_ref, up_other_ref)
    grad_hidden = dot_right(result[...], down_ref[...])
    sigmoid = 1.0 / (1.0 + jnp.exp(-gate))
    silu = gate * sigmoid
    hidden_ref[...] = (silu * up).astype(jnp.bfloat16)
    grad_gate = (grad_hidden * up * (sigmoid + silu * (1.0 - sigmoid))).astype(jnp.bfloat16)
    grad_up = (grad_hidden * silu).astype(jnp.bfloat16)
    grad_gate_ref[...] = grad_gate
    grad_up_ref[...] = grad_up
    half = gate_mine_ref.shape[0]
    low = dot_right(grad_gate, gate_mine_ref[...]) + dot_right(grad_up, up_mine_ref[...])
    high = dot_right(grad_gate, gate_other_ref[...]) + dot_right(grad_up, up_other_ref[...])

    @pl.when(own)
    def _():
        grad_ref[:, :half] = low
        grad_ref[:, half:] = high

    @pl.when(jnp.logical_not(own))
    def _():
        core_grad_ref[:, :half] = low.astype(jnp.bfloat16)
        core_grad_ref[:, half:] = high.astype(jnp.bfloat16)


def feed(rows, grad_result, gate_rank, up_rank, down_rank):
    count, width = 2 * rows[0].shape[0], down_rank.shape[0]
    block = 256
    steps = count // block
    outs = [shaped(count, D)] * 2 + [shaped(count, width)] * 3
    grads = (shaped(count // 2, D, jnp.float32), shaped(count // 2, D))
    whole = [*gate_rank, *up_rank, down_rank]
    *outs, grad_mine, grad_core = pl.pallas_call(
        feed_kernel,
        grid=(steps,),
        in_specs=pair_specs(rows, steps)
        + pair_specs(grad_result, steps)
        + [whole_spec(array) for array in whole],
        out_specs=[step_spec(array, steps) for array in outs] + pair_specs(grads, steps),
        out_shape=[*outs, *grads],
        compiler_params=parameters(),
        name="feed",
    )(*rows, *grad_result, *whole)
    return *outs, (grad_mine, grad_core)


def swap(block, axis, count=2, step=1):
    return lax.ppermute(block, axis, [(at, at ^ step) for at in range(count)])


def spread(block, axis, count):
    if count & (count - 1):
        return lax.all_gather(block, axis)
    block, step = block[None], 1
    while step < count:
        other = swap(block, axis, count, step)
        low = (lax.axis_index(axis) & step) == 0
        block = jnp.where(
            low, jnp.concatenate([block, other]), jnp.concatenate([other, block])
        )
        step *= 2
    return block


def fold(block, axis, count):
    if count & (count - 1):
        return lax.psum_scatter(block, axis, scatter_dimension=0)
    step = count // 2
    while step:
        half = block.shape[0] // 2
        low = (lax.axis_index(axis) & step) == 0
        lower, upper = block[:half], block[half:]
        block = jnp.where(low, lower, upper) + swap(
            jnp.where(low, upper, lower), axis, count, step
        )
        step //= 2
    return block[0]


def trade_ranks(block):
    return lax.all_to_all(block, ("mid", "core"), 0, 0, tiled=True)


def pick(stack, index):
    return lax.dynamic_index_in_dim(stack, index, 0, keepdims=False)


def pair(rows):
    return (rows, swap(rows, "core"))


def settle(partial):
    mine, core = partial
    return mine + swap(core, "core").astype(jnp.float32)


def settle_move(across):
    return swap(across, "mid").astype(jnp.float32)


class Layout:
    def __init__(self, hi, rep, out_rows):
        self.hi, self.rep = hi, rep
        self.aligned = (rep * out_rows) % HEAD_DIM == 0
        self.head_groups = hi if self.aligned else 1
        self.rank = lax.axis_index("mid") * 2 + lax.axis_index("core")

    def by_rank(self, weight, sections, groups):
        rows, columns = weight.shape
        width = columns // (sections * groups * RANKS)
        view = weight.reshape(rows, sections * groups, RANKS, width)
        view = jnp.transpose(view, (2, 0, 1, 3))
        return view.reshape(RANKS, rows, sections * groups * width)

    def from_ranks(self, blocks, sections, groups):
        _, rows, per_rank = blocks.shape
        width = per_rank // (sections * groups)
        view = blocks.reshape(RANKS, rows, sections * groups, width)
        return jnp.transpose(view, (1, 2, 0, 3)).reshape(rows, RANKS * per_rank)

    def ordered(self, values):
        if self.hi != 2:
            return values
        half = values.shape[-1] // 2
        turned = jnp.concatenate([values[..., half:], values[..., :half]], axis=-1)
        return jnp.where(lax.axis_index("hi") == 0, values, turned)

    def across_hi(self, block):
        if self.hi == 2:
            return (block, swap(block, "hi"))
        return spread(block, "hi", self.hi)

    def natural_hi(self, blocks):
        if self.hi != 2:
            return blocks
        mine, other = blocks
        low = lax.axis_index("hi") == 0
        return jnp.stack([jnp.where(low, mine, other), jnp.where(low, other, mine)])

    def halves(self, blocks):
        if self.hi == 2:
            return tuple(self.natural_rows(block[None]) for block in blocks)
        return tuple(jnp.split(self.natural_rows(blocks), 2))

    def natural_rows(self, stacked):
        view = stacked.reshape(stacked.shape[0], self.rep, RANKS, -1, stacked.shape[-1])
        return jnp.transpose(view, (0, 2, 1, 3, 4)).reshape(-1, stacked.shape[-1])

    def product_moved(self, lefts, rights, first=None):
        lanes = lefts[0].shape[1]
        if self.hi != 2:
            return product(lefts, rights, 0, lanes, jnp.bfloat16)
        return product(lefts, rights, lanes // 2 if first is None else first, lanes // 2, jnp.bfloat16)

    def move(self, moved):
        if self.hi == 2:
            return swap(moved, "hi")
        return fold(moved.reshape(self.hi, -1, moved.shape[1]), "hi", self.hi)

    def product_kept(self, lefts, rights, first=0):
        if self.hi != 2:
            return None
        return product(lefts, rights, first, lefts[0].shape[1] // 2, jnp.float32)

    def total(self, kept, arrived):
        if kept is None:
            return arrived
        return (kept + arrived.astype(jnp.float32)).astype(jnp.bfloat16)

    def by_rep(self, summed):
        view = summed.reshape(RANKS, self.rep, -1, summed.shape[1])
        return jnp.transpose(view, (1, 0, 2, 3)).reshape(self.rep, -1, summed.shape[1])

    def reduce(self, blocks):
        flat = blocks.reshape(-1, blocks.shape[-1])
        return lax.psum_scatter(flat, "rep", scatter_dimension=0, tiled=True)

    def rank_lanes(self, rows, groups):
        view = rows.reshape(rows.shape[0], groups, RANKS, -1)
        return lax.dynamic_index_in_dim(view, self.rank, 2, keepdims=False).reshape(rows.shape[0], -1)

    def place_lanes(self, row):
        view = row.reshape(self.head_groups, 1, -1)
        at = (jnp.arange(RANKS) == self.rank).astype(row.dtype)[None, :, None]
        return (view * at).reshape(-1)


def fence(*values):
    return lax.optimization_barrier(values)


def local(
    hi_count,
    rep_count,
    tokens,
    condition,
    caption,
    caption_len,
    item_kind,
    out_cotangent,
    norm_gains,
    ada_weight,
    qkv_weight,
    out_weight,
    text_weight,
    gate_up_weight,
    down_weight,
):
    bf16, f32 = jnp.bfloat16, jnp.float32
    item_count = condition.shape[0]
    item_len = tokens.shape[0] // item_count
    row_count = item_count * item_len
    rows = qkv_weight.shape[0]
    plan = Layout(hi_count, rep_count, out_weight.shape[0])
    rank_width = HEADS // RANKS * HEAD_DIM
    hi_at, mid_at, core_at, rep_at = [lax.axis_index(name) for name in AXES]
    device_shape = (hi_count, 2, 2, rep_count)

    feed_width = FF // RANKS
    devices = hi_count * RANKS * rep_count
    block_at = (hi_at * RANKS + plan.rank) * rep_count + rep_at

    def z_gather(block):
        return lax.all_gather(block.reshape(-1, block.shape[-1]), "rep", tiled=True)

    down_z = z_gather(down_weight)
    qkv_mine = trade_ranks(plan.by_rank(qkv_weight, 3, plan.head_groups))
    qkv_mine = qkv_mine.reshape(RANKS * rows, 3 * rank_width)
    if plan.aligned:
        qkv_mine = jnp.concatenate([qkv_mine, out_weight.reshape(-1, 3 * rank_width)])
    else:
        out_whole = lax.all_gather(out_weight, AXES, axis=0, tiled=True)
        out_rank = pick(out_whole.reshape(RANKS, rank_width, D), plan.rank)

    head = condition.reshape(item_count, devices, rows)
    head = jnp.transpose(head, (1, 0, 2)).reshape(devices, -1)
    rest = jnp.concatenate(
        [norm_gains.reshape(-1), caption_len.astype(bf16), item_kind.astype(bf16)]
    )
    small = jnp.concatenate([head, jnp.broadcast_to(rest, (devices, rest.size))], axis=1)
    small = lax.all_to_all(small, AXES, 0, 0, tiled=True)
    cut = [head.shape[1], head.shape[1] + norm_gains.size]
    cut.append(cut[1] + item_count)
    conditions, gains, lengths, kinds = jnp.split(small, cut, axis=-1)
    activated_mine = jax.nn.silu(conditions.astype(f32)).astype(bf16).reshape(-1, rows)
    gain_rows = jnp.moveaxis(gains.astype(f32).reshape(devices, 6, -1), 1, 0).reshape(6, D)
    lengths, kinds = [
        values.reshape(device_shape + (item_count,)) for values in (lengths, kinds)
    ]

    def group_items(values):
        view = lax.dynamic_index_in_dim(pick(values, hi_at), rep_at, 2, keepdims=False)
        near, far = pick(view, mid_at), pick(view, 1 - mid_at)
        order = [core_at, 1 - core_at]
        return [
            jnp.concatenate([pick(side, at) for at in order]).astype(jnp.int32)
            for side in (near, far)
        ]

    lengths_sides = group_items(lengths)
    kinds_sides = group_items(kinds)
    cosine, sine = rope_tables(jnp.arange(2), item_len)
    signs = jnp.where(jnp.arange(HEAD_DIM) % (HEAD_DIM // 2) < HEAD_DIM // 4, -1.0, 1.0)
    cosine, sine = jnp.tile(cosine, (1, 1, 2)), jnp.tile(sine * signs, (1, 1, 2))
    head_gains = plan.rank_lanes(gain_rows, plan.head_groups)
    cross_gate = jnp.tanh(head_gains[5])
    head_gains = jnp.concatenate([head_gains[1:4], cross_gate[None]])
    tables = (head_gains, cosine, sine)
    scalars = list(zip(kinds_sides, lengths_sides, strict=True))

    down_z, qkv_mine, text_weight, activated_mine = fence(
        down_z, qkv_mine, text_weight, activated_mine
    )
    qkv_z = z_gather(qkv_mine)
    down_rank = plan.across_hi(down_z)
    text_mine = trade_ranks(plan.by_rank(text_weight, 2, plan.head_groups))
    captions_near = pair(plan.ordered(caption.reshape(-1, TEXT_DIM)))
    partial = dot(activated_mine, ada_weight).astype(bf16).reshape(devices, item_count, 4 * D)
    gate_up_mine = trade_ranks(plan.by_rank(gate_up_weight, 2, hi_count))
    modulation = jnp.sum(lax.all_to_all(partial, AXES, 0, 0, tiled=True).astype(f32), axis=0)
    text_key_mine, text_value_mine = text_mine[..., :rank_width], text_mine[..., rank_width:]
    gate_mine, up_mine = gate_up_mine[..., :feed_width], gate_up_mine[..., feed_width:]
    qkv_z, down_rank, modulation, text_key_mine, text_value_mine, gate_mine, up_mine, captions_near = fence(
        qkv_z, down_rank, modulation, text_key_mine, text_value_mine, gate_mine, up_mine, captions_near
    )

    scale_attn, gate_attn, scale_mlp, gate_mlp = jnp.split(modulation, 4, axis=1)
    text_key_z = z_gather(text_key_mine)
    captions_far = swap(captions_near[0], "mid")
    qkv_rank = plan.across_hi(qkv_z)
    down_rank = plan.natural_hi(down_rank).reshape(feed_width, D)
    token_rows = tokens.astype(f32).reshape(item_count, item_len, D)
    normed = modulate(token_rows, gain_rows[0], scale_attn)
    normed = plan.ordered(normed.astype(bf16).reshape(row_count, D))
    mlp_gate = jnp.tanh(gate_mlp)[:, None, :]
    grad_top = out_cotangent.astype(f32).reshape(item_count, item_len, D)
    grad_result = (mlp_gate * grad_top).astype(bf16).reshape(row_count, D)
    normed_near, result_near = pair(normed), pair(grad_result)
    text_key_z, captions_far, qkv_rank, down_rank, normed_near, result_near = fence(
        text_key_z, captions_far, qkv_rank, down_rank, normed_near, result_near
    )

    text_value_z = z_gather(text_value_mine)
    text_key_rank = plan.across_hi(text_key_z)
    normed_far = swap(normed_near[0], "mid")
    captions_far = pair(captions_far)
    text_value_z, text_key_rank, normed_far, captions_far = fence(
        text_value_z, text_key_rank, normed_far, captions_far
    )

    gate_z = z_gather(gate_mine)
    text_value_rank = plan.across_hi(text_value_z)
    result_far = swap(result_near[0], "mid")
    normed_far = pair(normed_far)
    if plan.aligned:
        blocks = [block.reshape(rep_count, -1, 3 * rank_width) for block in qkv_rank]
        out_rank = plan.natural_hi([block[:, RANKS * rows :].reshape(-1, D) for block in blocks])
        out_rank = out_rank.reshape(rank_width, D)
        qkv_rank = [block[:, : RANKS * rows].reshape(-1, 3 * rank_width) for block in blocks]
        qkv_rank = qkv_rank if hi_count == 2 else jnp.stack(qkv_rank)
    qkv_rank, text_key_rank = plan.halves(qkv_rank), plan.halves(text_key_rank)
    gate_z, text_value_rank, result_far, normed_far, qkv_rank, out_rank, text_key_rank = fence(
        gate_z, text_value_rank, result_far, normed_far, qkv_rank, out_rank, text_key_rank
    )

    up_z = z_gather(up_mine)
    gate_rank = plan.across_hi(gate_z)
    attend_weights = (qkv_rank, text_key_rank, plan.halves(text_value_rank), out_rank, tables)
    normed_far, captions_far, kept_far, partial_far = attend(
        scalars[1], normed_far, captions_far, *attend_weights
    )
    up_z, gate_rank, normed_far, captions_far, kept_far, partial_far, attend_weights = fence(
        up_z, gate_rank, normed_far, captions_far, kept_far, partial_far, attend_weights
    )

    across = settle(partial_far).astype(bf16)
    across, normed_near, up_z = fence(across, normed_near, up_z)
    up_rank = plan.across_hi(up_z)
    arrived = settle_move(across)
    normed_near, captions_near, kept_near, partial_near = attend(
        scalars[0], normed_near, captions_near, *attend_weights
    )
    result_far = pair(result_far)
    gate_rank = plan.halves(gate_rank)
    up_rank, arrived, normed_near, captions_near, kept_near, partial_near, result_far, gate_rank = fence(
        up_rank, arrived, normed_near, captions_near, kept_near, partial_near, result_far, gate_rank
    )

    branch = (settle(partial_near) + arrived).reshape(item_count, item_len, D)
    attn_gate = jnp.tanh(gate_attn)[:, None, :]
    middle = token_rows + attn_gate * branch
    mlp_input = modulate(middle, gain_rows[4], scale_mlp)
    mlp_input = plan.ordered(mlp_input.astype(bf16).reshape(row_count, D))
    up_rank = plan.halves(up_rank)
    mlp_input, up_rank = fence(mlp_input, up_rank)

    feed_weights = (gate_rank, up_rank, down_rank)
    input_far = swap(mlp_input, "mid")
    input_near, result_near, hidden_near, gate_near, up_near, partial_near = feed(
        pair(mlp_input), result_near, *feed_weights
    )
    input_far, input_near, result_near, hidden_near, gate_near, up_near, partial_near = fence(
        input_far, input_near, result_near, hidden_near, gate_near, up_near, partial_near
    )
    input_far, result_far, hidden_far, gate_far, up_far, partial_far = feed(
        pair(input_far), result_far, *feed_weights
    )
    inputs, results = (input_near, input_far), (result_near, result_far)
    gate_rows, up_rows, hidden_rows = (gate_near, gate_far), (up_near, up_far), (hidden_near, hidden_far)
    across = settle(partial_far).astype(bf16)
    gate_moved = plan.product_moved(inputs, gate_rows)
    across, gate_moved, gate_rows, up_rows, hidden_rows = fence(
        across, gate_moved, gate_rows, up_rows, hidden_rows
    )
    arrived = settle_move(across)
    gate_moved = plan.move(gate_moved)
    up_moved = plan.product_moved(inputs, up_rows)
    hidden_first = hi_at * (feed_width // 2)
    down_moved = plan.product_moved(hidden_rows, results, feed_width // 2 - hidden_first)
    gate_kept = plan.product_kept(inputs, gate_rows)
    arrived, gate_moved, up_moved, down_moved, gate_kept, partial_near = fence(
        arrived, gate_moved, up_moved, down_moved, gate_kept, partial_near
    )

    up_moved = plan.move(up_moved)
    gate_grad = plan.by_rep(plan.total(gate_kept, gate_moved))
    gate_parts = plan.reduce(gate_grad)
    grad_mlp_input = plan.ordered(settle(partial_near) + arrived)
    _, pull_mlp_norm = jax.vjp(modulate, middle, gain_rows[4], scale_mlp)
    grad_middle_norm, grad_mlp_gain, grad_scale_mlp = pull_mlp_norm(
        grad_mlp_input.reshape(item_count, item_len, D)
    )
    grad_middle = grad_top + grad_middle_norm
    grad_attn_gate = jnp.sum(grad_middle * branch, axis=1) * (1.0 - jnp.tanh(gate_attn) ** 2)
    grad_branch = (attn_gate * grad_middle).astype(bf16).reshape(row_count, D)
    grad_branch, up_rows = fence(grad_branch, up_rows)

    branch_far = swap(grad_branch, "mid")
    back_weights = (qkv_rank, out_rank, tables)
    branch_near, qkv_near, text_near, rows_near, gain_near = attend_back(
        scalars[0], pair(grad_branch), kept_near, *back_weights
    )
    up_kept = plan.product_kept(inputs, up_rows)
    branch_far, up_moved, gate_parts, branch_near, qkv_near, text_near, rows_near, gain_near, up_kept = fence(
        branch_far, up_moved, gate_parts, branch_near, qkv_near, text_near, rows_near, gain_near, up_kept
    )

    up_grad = plan.by_rep(plan.total(up_kept, up_moved))
    up_grad, branch_far, down_moved = fence(up_grad, pair(branch_far), down_moved)
    up_parts = plan.reduce(up_grad)
    down_moved = plan.move(down_moved)
    branch_far, qkv_far, text_far, rows_far, gain_far = attend_back(
        scalars[1], branch_far, kept_far, *back_weights
    )
    captions, normed_rows = (captions_near, captions_far), (normed_near, normed_far)
    text_rows, qkv_rows, branches = (text_near, text_far), (qkv_near, qkv_far), (branch_near, branch_far)
    text_moved = plan.product_moved(captions, text_rows)
    down_moved, up_parts, text_rows, qkv_rows, branches, rows_far, gain_far, text_moved, hidden_rows = fence(
        down_moved, up_parts, text_rows, qkv_rows, branches, rows_far, gain_far, text_moved, hidden_rows
    )

    text_moved = plan.move(text_moved)
    down_kept = plan.product_kept(hidden_rows, results, hidden_first)
    down_grad = plan.total(down_kept, down_moved).reshape(rep_count, -1, D)
    across = settle(rows_far).astype(bf16)
    across, down_grad, text_rows, qkv_rows, hidden_rows, branches = fence(
        across, down_grad, text_rows, qkv_rows, hidden_rows, branches
    )
    down_parts = plan.reduce(down_grad)
    arrived = settle_move(across)
    qkv_moved = plan.product_moved(normed_rows, qkv_rows)
    text_kept = plan.product_kept(captions, text_rows)
    qkv_kept = plan.product_kept(normed_rows, qkv_rows)
    mixed_rows = [plan.ordered(kept[6]) for kept in (kept_near, kept_far)]
    if plan.aligned:
        out_halves = [
            product([side[:, lanes] for side in mixed_rows], branches, 0, rank_width // 2, bf16)
            for lanes in (slice(0, rank_width // 2), slice(rank_width // 2, None))
        ]
    else:
        out_halves = []
    result_far = [dot(side, down_rank) for side in jnp.split(hidden_rows[1], 2)]
    result_across = settle((result_far[0], result_far[1].astype(bf16))).astype(bf16)
    grad_normed = plan.ordered(settle(rows_near) + arrived)
    text_moved, down_parts, grad_normed, qkv_moved, text_kept, qkv_kept, out_halves, result_across = fence(
        text_moved, down_parts, grad_normed, qkv_moved, text_kept, qkv_kept, out_halves, result_across
    )

    text_grad = plan.by_rep(plan.total(text_kept, text_moved))
    text_grad, qkv_moved, out_halves, result_across, hidden_rows = fence(
        text_grad, qkv_moved, out_halves, result_across, hidden_rows
    )
    text_parts = plan.reduce(text_grad)
    qkv_moved = plan.move(qkv_moved)
    result = settle_move(result_across)
    if plan.aligned:
        if hi_count == 2:
            out_kept, out_moved = out_halves[0].astype(f32), swap(out_halves[1], "hi")
        else:
            out_kept, out_moved = None, plan.move(jnp.concatenate(out_halves))
    result_near = [dot(side, down_rank) for side in jnp.split(hidden_rows[0], 2)]
    result = result + settle((result_near[0], result_near[1].astype(bf16)))
    result = result.reshape(item_count, item_len, D)
    layer_out = (middle + mlp_gate * result).astype(bf16).reshape(row_count, D)
    grad_mlp_gate = jnp.sum(grad_top * result, axis=1) * (1.0 - jnp.tanh(gate_mlp) ** 2)
    _, pull_attn_norm = jax.vjp(modulate, token_rows, gain_rows[0], scale_attn)
    grad_token_norm, grad_attn_gain, grad_scale_attn = pull_attn_norm(
        grad_normed.reshape(item_count, item_len, D)
    )
    tokens_grad = (grad_middle + grad_token_norm).reshape(row_count, D)
    qkv_grad = plan.by_rep(plan.total(qkv_kept, qkv_moved))
    if plan.aligned:
        out_grad = plan.total(out_kept, out_moved).reshape(rep_count, -1, 3 * rank_width)
        qkv_grad = jnp.concatenate([qkv_grad, out_grad], axis=1)
    else:
        at = (jnp.arange(RANKS) == plan.rank).astype(bf16)[:, None, None]
        out_grad = product(mixed_rows, branches, 0, rank_width, bf16)
        placed = (out_grad[None] * at).reshape(D, D)
        out_weight_grad = lax.psum_scatter(placed, AXES, scatter_dimension=0, tiled=True).astype(f32)
    text_parts, qkv_grad, grad_mlp_gate, grad_scale_attn, grad_attn_gain = fence(
        text_parts, qkv_grad, grad_mlp_gate, grad_scale_attn, grad_attn_gain
    )
    qkv_parts = plan.reduce(qkv_grad)
    if plan.aligned:
        out_weight_grad = qkv_parts[RANKS * rows :].reshape(-1, D).astype(f32)
        qkv_parts = qkv_parts[: RANKS * rows]

    grad_modulation = jnp.concatenate(
        [grad_scale_attn, grad_attn_gate, grad_scale_mlp, grad_mlp_gate], axis=1
    ).astype(bf16)
    gain_terms = gain_near + gain_far
    gain_terms = gain_terms.at[3].multiply(1.0 - cross_gate**2)
    gain_terms = [plan.place_lanes(row) for row in gain_terms]
    gains_grad = jnp.stack(
        [grad_attn_gain, gain_terms[0], gain_terms[1], gain_terms[2], grad_mlp_gain, gain_terms[3]]
    ).astype(bf16)
    gain_blocks = jnp.moveaxis(gains_grad.reshape(6, devices, -1), 1, 0).reshape(devices, -1)
    modulations = jnp.broadcast_to(grad_modulation.reshape(-1), (devices, grad_modulation.size))
    both = lax.all_to_all(
        jnp.concatenate([modulations, gain_blocks], axis=1), AXES, 0, 0, tiled=True
    )
    ada_weight_grad = dot_left(activated_mine, both[:, : modulations.shape[1]].reshape(-1, 4 * D))
    norm_gains_grad = jnp.sum(both[:, modulations.shape[1] :].astype(f32), axis=0).reshape(6, -1)

    def whole(parts, weight, sections, groups):
        blocks = trade_ranks(parts.reshape(RANKS, weight.shape[0], -1))
        return plan.from_ranks(blocks, sections, groups).astype(f32)

    gate_up_weight_grad = whole(
        jnp.concatenate([gate_parts, up_parts], axis=-1), gate_up_weight, 2, hi_count
    )
    text_weight_grad = whole(text_parts, text_weight, 2, plan.head_groups)
    qkv_weight_grad = whole(qkv_parts, qkv_weight, 3, plan.head_groups)
    down_weight_grad = down_parts.astype(f32)
    return (
        layer_out,
        tokens_grad,
        norm_gains_grad,
        ada_weight_grad,
        qkv_weight_grad,
        out_weight_grad,
        text_weight_grad,
        gate_up_weight_grad,
        down_weight_grad,
    )


def solution(mesh):
    grp, rep = mesh.devices.shape
    hi = grp // RANKS
    inner = Mesh(mesh.devices.reshape(hi, 2, 2, rep), AXES)
    rows = P(AXES, None)

    def step(*arrays):
        return local(hi, rep, *arrays)

    return jax.shard_map(
        step,
        mesh=inner,
        in_specs=(
            rows,
            rows,
            P(AXES, None, None),
            P(AXES),
            P(AXES),
            rows,
            P(None, AXES),
            rows,
            rows,
            rows,
            rows,
            rows,
            rows,
        ),
        out_specs=(rows, rows, P(None, AXES), rows, rows, rows, rows, rows, rows),
        check_vma=False,
    )
```

```python
import math

import jax
import jax.numpy as jnp
from jax import lax
from jax.experimental import pallas as pl
from jax.experimental.pallas import tpu as pltpu
from jax.sharding import Mesh
from jax.sharding import PartitionSpec as P

D = 1536
HEADS = 24
HEAD_DIM = 64
TEXT_DIM = 4096
FF = 4096
SIDE = 16
RANKS = 4
LANES = 128
MIB = 1 << 20
AXES = ("hi", "mid", "core", "rep")


EPSILON = 1e-06


def norm_rows(values, gain_row):
    return (
        values * lax.rsqrt(jnp.mean(values * values, axis=-1, keepdims=True) + EPSILON) * gain_row
    )


def rope_tables(item_kind, item_len):
    position = jnp.arange(item_len, dtype=jnp.int32)[None, :]
    half_side = SIDE // 2
    frame_index = position // (half_side * half_side)
    within = position % (half_side * half_side)
    is_clip = item_kind[:, None] == 1
    row_index = jnp.where(is_clip, frame_index * half_side + within // half_side, position // SIDE)
    columns = jnp.where(is_clip, within % half_side, position % SIDE)
    lane_index = jnp.arange(HEAD_DIM, dtype=jnp.int32)
    quarter = HEAD_DIM // 4
    frequency = jnp.exp(-(lane_index % quarter).astype(jnp.float32) * (math.log(10000.0) / quarter))
    coordinate = jnp.where(
        lane_index[None, None, :] < 2 * quarter, row_index[:, :, None], columns[:, :, None]
    ).astype(jnp.float32)
    angles = coordinate * frequency
    return (jnp.cos(angles), jnp.sin(angles))


def modulate(values, gain_row, scaling):
    return norm_rows(values, gain_row) * (1.0 + scaling[:, None, :])


def silu_product(gate_half, up_half):
    return jax.nn.silu(gate_half) * up_half


def dot(left, right):
    return jnp.dot(left, right, preferred_element_type=jnp.float32)


def dot_left(left, right):
    return lax.dot_general(left, right, (((0,), (0,)), ((), ())), preferred_element_type=jnp.float32)


def dot_right(left, right):
    return lax.dot_general(left, right, (((1,), (1,)), ((), ())), preferred_element_type=jnp.float32)


def lane_index(shape):
    return lax.broadcasted_iota(jnp.int32, shape, len(shape) - 1)

def head_sums(values):
    first = lane_index(values.shape) < HEAD_DIM
    low = jnp.sum(jnp.where(first, values, 0.0), axis=-1, keepdims=True)
    high = jnp.sum(jnp.where(first, 0.0, values), axis=-1, keepdims=True)
    return jnp.where(first, low, high)

def partner(values):
    quarter = HEAD_DIM // 4
    width = values.shape[-1]
    low = lane_index(values.shape) % (2 * quarter) < quarter
    return jnp.where(low, pltpu.roll(values, width - quarter, 1), pltpu.roll(values, quarter, 1))

def stack_heads(values):
    first = lane_index(values.shape) < HEAD_DIM
    zero = jnp.zeros_like(values)
    return jnp.concatenate([jnp.where(first, values, zero), jnp.where(first, zero, values)])

def join_heads(stacked):
    rows = stacked.shape[0] // 2
    first = lane_index((rows, stacked.shape[1])) < HEAD_DIM
    return jnp.where(first, stacked[:rows], stacked[rows:])

def inverse_rms(raw):
    return lax.rsqrt(head_sums(raw * raw) * (1.0 / HEAD_DIM) + EPSILON)

def dot_cut(rows, mine, other):
    half = mine.shape[0]
    return dot(rows[:, :half], mine[...]) + dot(rows[:, half:], other[...])


def attend_kernel(
    kind_ref,
    len_ref,
    rows_ref,
    core_rows_ref,
    caption_ref,
    core_caption_ref,
    qkv_mine_ref,
    qkv_other_ref,
    key_mine_ref,
    key_other_ref,
    value_mine_ref,
    value_other_ref,
    out_weight_ref,
    gain_ref,
    cos_ref,
    sin_ref,
    rows_out_ref,
    caption_out_ref,
    qkv_ref,
    text_ref,
    text_value_ref,
    q_ref,
    k_ref,
    tk_ref,
    mixed_ref,
    read_ref,
    branch_ref,
    core_branch_ref,
):
    item = pl.program_id(0)
    own = item < pl.num_programs(0) // 2
    kind, length = kind_ref[item], len_ref[item]
    width = q_ref.shape[1]
    cosine, sine = cos_ref[kind], sin_ref[kind]
    scaling = HEAD_DIM ** (-0.5)

    @pl.when(own)
    def _():
        rows_out_ref[...] = rows_ref[...]
        caption_out_ref[...] = caption_ref[...]

    @pl.when(jnp.logical_not(own))
    def _():
        rows_out_ref[...] = core_rows_ref[...]
        caption_out_ref[...] = core_caption_ref[...]

    qkv_ref[...] = dot_cut(rows_out_ref, qkv_mine_ref, qkv_other_ref)
    text_ref[...] = dot_cut(caption_out_ref, key_mine_ref, key_other_ref)
    text_value_ref[...] = dot_cut(caption_out_ref, value_mine_ref, value_other_ref)
    for at in range(0, width, LANES):
        lanes = slice(at, at + LANES)
        turned = []
        for part, out_ref in ((0, q_ref), (1, k_ref)):
            raw = qkv_ref[:, part * width + at : part * width + at + LANES]
            normal = raw * inverse_rms(raw) * gain_ref[part : part + 1, lanes]
            rows = (normal * cosine + partner(normal) * sine).astype(jnp.bfloat16)
            out_ref[:, lanes] = rows
            turned.append(rows)
        queries, keys = turned
        values = qkv_ref[:, 2 * width + at : 2 * width + at + LANES].astype(jnp.bfloat16)
        text_raw = text_ref[:, lanes]
        text_keys = (text_raw * inverse_rms(text_raw) * gain_ref[2:3, lanes]).astype(jnp.bfloat16)
        tk_ref[:, lanes] = text_keys
        text_values = text_value_ref[:, lanes].astype(jnp.bfloat16)
        stacked = stack_heads(queries)
        scores = dot_right(stacked, keys) * scaling
        scores = jnp.exp(scores - jnp.max(scores, axis=-1, keepdims=True))
        own_out = dot(scores.astype(jnp.bfloat16), values) / jnp.sum(scores, axis=-1, keepdims=True)
        text = dot_right(stacked, text_keys) * scaling
        text = jnp.where(lane_index(text.shape) < length, text, -1e30)
        text = jnp.exp(text - jnp.max(text, axis=-1, keepdims=True))
        text_out = dot(text.astype(jnp.bfloat16), text_values) / jnp.sum(text, axis=-1, keepdims=True)
        read = join_heads(text_out)
        read_ref[:, lanes] = read
        mixed_ref[:, lanes] = (join_heads(own_out) + gain_ref[3:4, lanes] * read).astype(jnp.bfloat16)

    branch = dot(mixed_ref[...], out_weight_ref[...])

    @pl.when(own)
    def _():
        branch_ref[...] = branch

    @pl.when(jnp.logical_not(own))
    def _():
        core_branch_ref[...] = branch.astype(jnp.bfloat16)


def head_norm_back(grad, raw, gain_row):
    inverse = inverse_rms(raw)
    scaled = grad * gain_row
    normal = raw * inverse
    inner = head_sums(scaled * normal) * (1.0 / HEAD_DIM)
    return inverse * (scaled - normal * inner), jnp.sum(grad * normal, axis=0, keepdims=True)

def attend_back_kernel(
    kind_ref,
    len_ref,
    branch_ref,
    core_branch_ref,
    qkv_ref,
    text_ref,
    text_value_ref,
    q_ref,
    k_ref,
    tk_ref,
    read_ref,
    qkv_mine_ref,
    qkv_other_ref,
    out_weight_ref,
    gain_ref,
    cos_ref,
    sin_ref,
    branch_out_ref,
    gqkv_ref,
    gtext_ref,
    grad_rows_ref,
    core_grad_rows_ref,
    gains_ref,
    mixed_ref,
):
    item = pl.program_id(0)
    own = item < pl.num_programs(0) // 2
    kind, length = kind_ref[item], len_ref[item]
    width = q_ref.shape[1]
    cosine, sine = cos_ref[kind], sin_ref[kind]
    scaling = HEAD_DIM ** (-0.5)

    @pl.when(own)
    def _():
        branch_out_ref[...] = branch_ref[...]

    @pl.when(jnp.logical_not(own))
    def _():
        branch_out_ref[...] = core_branch_ref[...]

    mixed_ref[...] = dot_right(branch_out_ref[...], out_weight_ref[...])

    @pl.when(item == 0)
    def _():
        gains_ref[...] = jnp.zeros_like(gains_ref)

    def one(stacked, keys, values, stacked_grad, valid):
        scores = dot_right(keys, stacked) * scaling
        if valid is not None:
            scores = jnp.where(valid(scores.shape), scores, -1e30)
        probs = jnp.exp(scores - jnp.max(scores, axis=0, keepdims=True))
        probs = probs * (1.0 / jnp.sum(probs, axis=0, keepdims=True))
        grad_values = dot(probs.astype(jnp.bfloat16), stacked_grad)
        grad_probs = dot_right(values, stacked_grad)
        inner = jnp.sum(probs * grad_probs, axis=0, keepdims=True)
        grad_scores = (probs * (grad_probs - inner)).astype(jnp.bfloat16)
        grad_keys = dot(grad_scores, stacked) * scaling
        grad_queries = dot_left(keys, grad_scores)
        return grad_queries, grad_keys, grad_values

    for at in range(0, width, LANES):
        lanes = slice(at, at + LANES)
        grad = mixed_ref[:, lanes]
        cross = gain_ref[3:4, lanes]
        values = qkv_ref[:, 2 * width + at : 2 * width + at + LANES].astype(jnp.bfloat16)
        text_values = text_value_ref[:, lanes].astype(jnp.bfloat16)
        stacked = stack_heads(q_ref[:, lanes])
        own_queries, own_keys, own_values = one(
            stacked, k_ref[:, lanes], values, stack_heads(grad.astype(jnp.bfloat16)), None
        )
        read_queries, read_keys, read_values = one(
            stacked, tk_ref[:, lanes], text_values, stack_heads((cross * grad).astype(jnp.bfloat16)),
            lambda shape: lax.broadcasted_iota(jnp.int32, shape, 0) < length,
        )
        grad_queries = join_heads((own_queries + read_queries).T) * scaling
        for part, turned in ((0, grad_queries), (1, own_keys)):
            raw = qkv_ref[:, part * width + at : part * width + at + LANES]
            back = turned * cosine + partner(turned * sine)
            grad_raw, gain = head_norm_back(back, raw, gain_ref[part : part + 1, lanes])
            gqkv_ref[:, part * width + at : part * width + at + LANES] = grad_raw.astype(jnp.bfloat16)
            gains_ref[part : part + 1, lanes] += gain
        gqkv_ref[:, 2 * width + at : 2 * width + at + LANES] = own_values.astype(jnp.bfloat16)
        grad_text, gain = head_norm_back(read_keys, text_ref[:, lanes], gain_ref[2:3, lanes])
        gtext_ref[:, lanes] = grad_text.astype(jnp.bfloat16)
        gains_ref[2:3, lanes] += gain
        gtext_ref[:, width + at : width + at + LANES] = read_values.astype(jnp.bfloat16)
        gains_ref[3:4, lanes] += jnp.sum(grad * read_ref[:, lanes], axis=0, keepdims=True)

    half = qkv_mine_ref.shape[0]
    low = dot_right(gqkv_ref[...], qkv_mine_ref[...])
    high = dot_right(gqkv_ref[...], qkv_other_ref[...])

    @pl.when(own)
    def _():
        grad_rows_ref[:, :half] = low
        grad_rows_ref[:, half:] = high

    @pl.when(jnp.logical_not(own))
    def _():
        core_grad_rows_ref[:, :half] = low.astype(jnp.bfloat16)
        core_grad_rows_ref[:, half:] = high.astype(jnp.bfloat16)


def whole_spec(array):
    zeros = (0,) * len(array.shape)
    return pl.BlockSpec(array.shape, lambda *_: zeros, pipeline_mode=pl.Buffered(1))


def mine_spec(array, steps):
    half = steps // 2
    return pl.BlockSpec(
        (array.shape[0] // half, array.shape[1]), lambda i, *_: (jnp.minimum(i, half - 1), 0)
    )


def core_spec(array, steps):
    half = steps // 2
    return pl.BlockSpec(
        (array.shape[0] // half, array.shape[1]), lambda i, *_: (jnp.maximum(i - half, 0), 0)
    )


def pair_specs(pair_of_arrays, steps):
    return [mine_spec(pair_of_arrays[0], steps), core_spec(pair_of_arrays[1], steps)]


def step_spec(array, steps):
    return pl.BlockSpec((array.shape[0] // steps, array.shape[1]), lambda i, *_: (i, 0))


def summed_spec(array):
    return pl.BlockSpec(array.shape, lambda i, *_: (0, 0))


def shaped(count, columns, dtype=jnp.bfloat16):
    return jax.ShapeDtypeStruct((count, columns), dtype)


def parameters():
    return pltpu.CompilerParams(dimension_semantics=("arbitrary",), vmem_limit_bytes=58 * MIB)


def attend(scalars, rows, captions, qkv_rank, key_rank, value_rank, out_rank, tables):
    items = scalars[0].shape[0]
    count, width = 2 * rows[0].shape[0], out_rank.shape[0]
    text_count = 2 * captions[0].shape[0]
    outs = [
        shaped(count, D),
        shaped(text_count, TEXT_DIM),
        shaped(count, 3 * width, jnp.float32),
        shaped(text_count, width, jnp.float32),
        shaped(text_count, width, jnp.float32),
        shaped(count, width),
        shaped(count, width),
        shaped(text_count, width),
        shaped(count, width),
        shaped(count, width, jnp.float32),
    ]
    branch = (shaped(count // 2, D, jnp.float32), shaped(count // 2, D))
    whole = [*qkv_rank, *key_rank, *value_rank, out_rank, *tables]
    rows, captions, *kept, branch_mine, branch_core = pl.pallas_call(
        attend_kernel,
        grid_spec=pltpu.PrefetchScalarGridSpec(
            num_scalar_prefetch=2,
            grid=(items,),
            in_specs=pair_specs(rows, items)
            + pair_specs(captions, items)
            + [whole_spec(array) for array in whole],
            out_specs=[step_spec(array, items) for array in outs] + pair_specs(branch, items),
        ),
        out_shape=[*outs, *branch],
        compiler_params=parameters(),
        name="attend",
    )(*scalars, *rows, *captions, *whole)
    return rows, captions, kept, (branch_mine, branch_core)


def attend_back(scalars, grad_branch, kept, qkv_rank, out_rank, tables):
    items = scalars[0].shape[0]
    qkv_raw, text_raw, text_value_raw, queries, keys, text_keys, _, read = kept
    count, width = queries.shape
    outs = [
        shaped(count, D),
        shaped(count, 3 * width),
        shaped(text_raw.shape[0], 2 * width),
    ]
    rows = (shaped(count // 2, D, jnp.float32), shaped(count // 2, D))
    gains = shaped(4, width, jnp.float32)
    by_item = [qkv_raw, text_raw, text_value_raw, queries, keys, text_keys, read]
    whole = [*qkv_rank, out_rank, *tables]
    branch, qkv, text, rows_mine, rows_core, gains = pl.pallas_call(
        attend_back_kernel,
        grid_spec=pltpu.PrefetchScalarGridSpec(
            num_scalar_prefetch=2,
            grid=(items,),
            in_specs=pair_specs(grad_branch, items)
            + [step_spec(array, items) for array in by_item]
            + [whole_spec(array) for array in whole],
            out_specs=[step_spec(array, items) for array in outs]
            + pair_specs(rows, items)
            + [summed_spec(gains)],
            scratch_shapes=[pltpu.VMEM((count // items, width), jnp.float32)],
        ),
        out_shape=[*outs, *rows, gains],
        compiler_params=parameters(),
        name="attend_back",
    )(*scalars, *grad_branch, *by_item, *whole)
    return branch, qkv, text, (rows_mine, rows_core), gains


def row_cuts(lefts, rights):
    cuts, left, right, left_row, right_row = [], 0, 0, 0, 0
    while left < len(lefts):
        count = min(lefts[left].shape[0] - left_row, rights[right].shape[0] - right_row)
        cuts.append((left, left_row, right, right_row, count))
        left_row, right_row = left_row + count, right_row + count
        if left_row == lefts[left].shape[0]:
            left, left_row = left + 1, 0
        if right_row == rights[right].shape[0]:
            right, right_row = right + 1, 0
    return cuts


def product(lefts, rights, first, lanes, dtype):
    columns = rights[0].shape[1]
    if lanes % LANES:
        block = lanes
    else:
        block = 384 if lanes % 384 == 0 else math.gcd(lanes, 512)
    cuts = row_cuts(lefts, rights)

    def kernel(first_ref, *refs):
        left_refs, right_refs, out_ref = refs[: len(lefts)], refs[len(lefts) : -1], refs[-1]
        total = None
        for left, left_row, right, right_row, count in cuts:
            term = dot_left(
                left_refs[left][left_row : left_row + count, :],
                right_refs[right][right_row : right_row + count, :],
            )
            total = term if total is None else total + term
        out_ref[...] = total.astype(out_ref.dtype)

    return pl.pallas_call(
        kernel,
        grid_spec=pltpu.PrefetchScalarGridSpec(
            num_scalar_prefetch=1,
            grid=(lanes // block,),
            in_specs=[
                pl.BlockSpec((array.shape[0], block), lambda i, first: (0, first[0] // block + i))
                for array in lefts
            ]
            + [whole_spec(array) for array in rights],
            out_specs=pl.BlockSpec((block, columns), lambda i, first: (i, 0)),
        ),
        out_shape=shaped(lanes, columns, dtype),
        compiler_params=parameters(),
        name="product",
    )(jnp.reshape(first, (1,)).astype(jnp.int32), *lefts, *rights)


def feed_kernel(
    rows_ref,
    core_rows_ref,
    result_ref,
    core_result_ref,
    gate_mine_ref,
    gate_other_ref,
    up_mine_ref,
    up_other_ref,
    down_ref,
    rows,
    result,
    hidden_ref,
    grad_gate_ref,
    grad_up_ref,
    grad_ref,
    core_grad_ref,
):
    own = pl.program_id(0) < pl.num_programs(0) // 2

    @pl.when(own)
    def _():
        rows[...] = rows_ref[...]
        result[...] = result_ref[...]

    @pl.when(jnp.logical_not(own))
    def _():
        rows[...] = core_rows_ref[...]
        result[...] = core_result_ref[...]

    gate = dot_cut(rows, gate_mine_ref, gate_other_ref)
    up = dot_cut(rows, up_mine_ref, up_other_ref)
    grad_hidden = dot_right(result[...], down_ref[...])
    sigmoid = 1.0 / (1.0 + jnp.exp(-gate))
    silu = gate * sigmoid
    hidden_ref[...] = (silu * up).astype(jnp.bfloat16)
    grad_gate = (grad_hidden * up * (sigmoid + silu * (1.0 - sigmoid))).astype(jnp.bfloat16)
    grad_up = (grad_hidden * silu).astype(jnp.bfloat16)
    grad_gate_ref[...] = grad_gate
    grad_up_ref[...] = grad_up
    half = gate_mine_ref.shape[0]
    low = dot_right(grad_gate, gate_mine_ref[...]) + dot_right(grad_up, up_mine_ref[...])
    high = dot_right(grad_gate, gate_other_ref[...]) + dot_right(grad_up, up_other_ref[...])

    @pl.when(own)
    def _():
        grad_ref[:, :half] = low
        grad_ref[:, half:] = high

    @pl.when(jnp.logical_not(own))
    def _():
        core_grad_ref[:, :half] = low.astype(jnp.bfloat16)
        core_grad_ref[:, half:] = high.astype(jnp.bfloat16)


def feed(rows, grad_result, gate_rank, up_rank, down_rank):
    count, width = 2 * rows[0].shape[0], down_rank.shape[0]
    block = 256
    steps = count // block
    outs = [shaped(count, D)] * 2 + [shaped(count, width)] * 3
    grads = (shaped(count // 2, D, jnp.float32), shaped(count // 2, D))
    whole = [*gate_rank, *up_rank, down_rank]
    *outs, grad_mine, grad_core = pl.pallas_call(
        feed_kernel,
        grid=(steps,),
        in_specs=pair_specs(rows, steps)
        + pair_specs(grad_result, steps)
        + [whole_spec(array) for array in whole],
        out_specs=[step_spec(array, steps) for array in outs] + pair_specs(grads, steps),
        out_shape=[*outs, *grads],
        compiler_params=parameters(),
        name="feed",
    )(*rows, *grad_result, *whole)
    return *outs, (grad_mine, grad_core)


def result_kernel(hidden_ref, down_ref, result_ref, core_result_ref):
    own = pl.program_id(0) < pl.num_programs(0) // 2
    rows = dot(hidden_ref[...], down_ref[...])

    @pl.when(own)
    def _():
        result_ref[...] = rows

    @pl.when(jnp.logical_not(own))
    def _():
        core_result_ref[...] = rows.astype(jnp.bfloat16)


def result_part(hidden, down_rank):
    count = hidden.shape[0]
    steps = count // 256
    outs = (shaped(count // 2, D, jnp.float32), shaped(count // 2, D))
    return pl.pallas_call(
        result_kernel,
        grid=(steps,),
        in_specs=[step_spec(hidden, steps), whole_spec(down_rank)],
        out_specs=pair_specs(outs, steps),
        out_shape=outs,
        compiler_params=parameters(),
        name="result",
    )(hidden, down_rank)


def swap(block, axis, count=2, step=1):
    return lax.ppermute(block, axis, [(at, at ^ step) for at in range(count)])


def spread(block, axis, count):
    if count & (count - 1):
        return lax.all_gather(block, axis)
    block, step = block[None], 1
    while step < count:
        other = swap(block, axis, count, step)
        low = (lax.axis_index(axis) & step) == 0
        block = jnp.where(
            low, jnp.concatenate([block, other]), jnp.concatenate([other, block])
        )
        step *= 2
    return block


def fold(block, axis, count):
    if count & (count - 1):
        return lax.psum_scatter(block, axis, scatter_dimension=0)
    step = count // 2
    while step:
        half = block.shape[0] // 2
        low = (lax.axis_index(axis) & step) == 0
        lower, upper = block[:half], block[half:]
        block = jnp.where(low, lower, upper) + swap(
            jnp.where(low, upper, lower), axis, count, step
        )
        step //= 2
    return block[0]


def trade_ranks(block):
    return lax.all_to_all(block, ("mid", "core"), 0, 0, tiled=True)


def pick(stack, index):
    return lax.dynamic_index_in_dim(stack, index, 0, keepdims=False)


def pair(rows):
    return (rows, swap(rows, "core"))


def settle(partial):
    mine, core = partial
    return mine + swap(core, "core").astype(jnp.float32)


def settle_move(across):
    return swap(across, "mid")


class Layout:
    def __init__(self, hi, rep, out_rows):
        self.hi, self.rep = hi, rep
        self.aligned = (rep * out_rows) % HEAD_DIM == 0
        self.head_groups = hi if self.aligned else 1
        self.rank = lax.axis_index("mid") * 2 + lax.axis_index("core")

    def by_rank(self, weight, sections, groups):
        rows, columns = weight.shape
        width = columns // (sections * groups * RANKS)
        view = weight.reshape(rows, sections * groups, RANKS, width)
        view = jnp.transpose(view, (2, 0, 1, 3))
        return view.reshape(RANKS, rows, sections * groups * width)

    def from_ranks(self, blocks, sections, groups):
        _, rows, per_rank = blocks.shape
        width = per_rank // (sections * groups)
        view = blocks.reshape(RANKS, rows, sections * groups, width)
        return jnp.transpose(view, (1, 2, 0, 3)).reshape(rows, RANKS * per_rank)

    def ordered(self, values):
        if self.hi != 2:
            return values
        half = values.shape[-1] // 2
        turned = jnp.concatenate([values[..., half:], values[..., :half]], axis=-1)
        return jnp.where(lax.axis_index("hi") == 0, values, turned)

    def ordered_text(self, values):
        if self.hi != 2:
            return values
        view = values.reshape(values.shape[0], self.hi, RANKS, self.rep, -1)
        return self.ordered(jnp.swapaxes(view, 2, 3).reshape(values.shape))

    def text_halves(self, blocks):
        return tuple(blocks) if self.hi == 2 else self.halves(blocks)

    def text_by_rep(self, summed):
        return summed.reshape(self.rep, -1, summed.shape[1]) if self.hi == 2 else self.by_rep(summed)

    def across_hi(self, block):
        if self.hi == 2:
            return (block, swap(block, "hi"))
        return spread(block, "hi", self.hi)

    def natural_hi(self, blocks):
        if self.hi != 2:
            return blocks
        mine, other = blocks
        low = lax.axis_index("hi") == 0
        return jnp.stack([jnp.where(low, mine, other), jnp.where(low, other, mine)])

    def halves(self, blocks):
        if self.hi == 2:
            return tuple(self.natural_rows(block[None]) for block in blocks)
        return tuple(jnp.split(self.natural_rows(blocks), 2))

    def natural_rows(self, stacked):
        view = stacked.reshape(stacked.shape[0], self.rep, RANKS, -1, stacked.shape[-1])
        return jnp.transpose(view, (0, 2, 1, 3, 4)).reshape(-1, stacked.shape[-1])

    def product_moved(self, lefts, rights, first=None):
        lanes = lefts[0].shape[1]
        if self.hi != 2:
            return product(lefts, rights, 0, lanes, jnp.bfloat16)
        return product(lefts, rights, lanes // 2 if first is None else first, lanes // 2, jnp.bfloat16)

    def move(self, moved):
        if self.hi == 2:
            return swap(moved, "hi")
        return fold(moved.reshape(self.hi, -1, moved.shape[1]), "hi", self.hi)

    def product_kept(self, lefts, rights, first=0):
        if self.hi != 2:
            return None
        return product(lefts, rights, first, lefts[0].shape[1] // 2, jnp.float32)

    def total(self, kept, arrived):
        if kept is None:
            return arrived
        return (kept + arrived.astype(jnp.float32)).astype(jnp.bfloat16)

    def by_rep(self, summed):
        view = summed.reshape(RANKS, self.rep, -1, summed.shape[1])
        return jnp.transpose(view, (1, 0, 2, 3)).reshape(self.rep, -1, summed.shape[1])

    def reduce(self, blocks):
        flat = blocks.reshape(-1, blocks.shape[-1])
        return lax.psum_scatter(flat, "rep", scatter_dimension=0, tiled=True)

    def rank_lanes(self, rows, groups):
        view = rows.reshape(rows.shape[0], groups, RANKS, -1)
        return lax.dynamic_index_in_dim(view, self.rank, 2, keepdims=False).reshape(rows.shape[0], -1)

    def place_lanes(self, row):
        view = row.reshape(self.head_groups, 1, -1)
        at = (jnp.arange(RANKS) == self.rank).astype(row.dtype)[None, :, None]
        return (view * at).reshape(-1)


def fence(*values):
    return lax.optimization_barrier(values)


def local(
    hi_count,
    rep_count,
    tokens,
    condition,
    caption,
    caption_len,
    item_kind,
    out_cotangent,
    norm_gains,
    ada_weight,
    qkv_weight,
    out_weight,
    text_weight,
    gate_up_weight,
    down_weight,
):
    bf16, f32 = jnp.bfloat16, jnp.float32
    item_count = condition.shape[0]
    item_len = tokens.shape[0] // item_count
    row_count = item_count * item_len
    rows = qkv_weight.shape[0]
    plan = Layout(hi_count, rep_count, out_weight.shape[0])
    rank_width = HEADS // RANKS * HEAD_DIM
    hi_at, mid_at, core_at, rep_at = [lax.axis_index(name) for name in AXES]
    device_shape = (hi_count, 2, 2, rep_count)

    feed_width = FF // RANKS
    devices = hi_count * RANKS * rep_count
    block_at = (hi_at * RANKS + plan.rank) * rep_count + rep_at

    def z_gather(block):
        return lax.all_gather(block.reshape(-1, block.shape[-1]), "rep", tiled=True)

    down_z = z_gather(down_weight)
    qkv_mine = trade_ranks(plan.by_rank(qkv_weight, 3, plan.head_groups))
    qkv_mine = qkv_mine.reshape(RANKS * rows, 3 * rank_width)
    if plan.aligned:
        qkv_mine = jnp.concatenate([qkv_mine, out_weight.reshape(-1, 3 * rank_width)])
    else:
        out_whole = lax.all_gather(out_weight, AXES, axis=0, tiled=True)
        out_rank = pick(out_whole.reshape(RANKS, rank_width, D), plan.rank)

    head = condition.reshape(item_count, devices, rows)
    head = jnp.transpose(head, (1, 0, 2)).reshape(devices, -1)
    rest = jnp.concatenate(
        [norm_gains.reshape(-1), caption_len.astype(bf16), item_kind.astype(bf16)]
    )
    small = jnp.concatenate([head, jnp.broadcast_to(rest, (devices, rest.size))], axis=1)
    small = lax.all_to_all(small, AXES, 0, 0, tiled=True)
    cut = [head.shape[1], head.shape[1] + norm_gains.size]
    cut.append(cut[1] + item_count)
    conditions, gains, lengths, kinds = jnp.split(small, cut, axis=-1)
    activated_mine = jax.nn.silu(conditions.astype(f32)).astype(bf16).reshape(-1, rows)
    gain_rows = jnp.moveaxis(gains.astype(f32).reshape(devices, 6, -1), 1, 0).reshape(6, D)
    lengths, kinds = [
        values.reshape(device_shape + (item_count,)) for values in (lengths, kinds)
    ]

    def group_items(values):
        view = lax.dynamic_index_in_dim(pick(values, hi_at), rep_at, 2, keepdims=False)
        near, far = pick(view, mid_at), pick(view, 1 - mid_at)
        order = [core_at, 1 - core_at]
        return [
            jnp.concatenate([pick(side, at) for at in order]).astype(jnp.int32)
            for side in (near, far)
        ]

    lengths_sides = group_items(lengths)
    kinds_sides = group_items(kinds)
    cosine, sine = rope_tables(jnp.arange(2), item_len)
    signs = jnp.where(jnp.arange(HEAD_DIM) % (HEAD_DIM // 2) < HEAD_DIM // 4, -1.0, 1.0)
    cosine, sine = jnp.tile(cosine, (1, 1, 2)), jnp.tile(sine * signs, (1, 1, 2))
    head_gains = plan.rank_lanes(gain_rows, plan.head_groups)
    cross_gate = jnp.tanh(head_gains[5])
    head_gains = jnp.concatenate([head_gains[1:4], cross_gate[None]])
    tables = (head_gains, cosine, sine)
    scalars = list(zip(kinds_sides, lengths_sides, strict=True))

    down_z, qkv_mine, text_weight, activated_mine = fence(
        down_z, qkv_mine, text_weight, activated_mine
    )
    qkv_z = z_gather(qkv_mine)
    down_rank = plan.across_hi(down_z)
    text_mine = trade_ranks(plan.by_rank(text_weight, 2, plan.head_groups))
    captions_near = pair(plan.ordered_text(caption.reshape(-1, TEXT_DIM)))
    partial = dot(activated_mine, ada_weight).astype(bf16).reshape(devices, item_count, 4 * D)
    gate_up_mine = trade_ranks(plan.by_rank(gate_up_weight, 2, hi_count))
    modulation = jnp.sum(lax.all_to_all(partial, AXES, 0, 0, tiled=True).astype(f32), axis=0)
    text_key_mine, text_value_mine = text_mine[..., :rank_width], text_mine[..., rank_width:]
    gate_mine, up_mine = gate_up_mine[..., :feed_width], gate_up_mine[..., feed_width:]
    qkv_z, down_rank, modulation, text_key_mine, text_value_mine, gate_mine, up_mine, captions_near = fence(
        qkv_z, down_rank, modulation, text_key_mine, text_value_mine, gate_mine, up_mine, captions_near
    )

    scale_attn, gate_attn, scale_mlp, gate_mlp = jnp.split(modulation, 4, axis=1)
    text_key_z = z_gather(text_key_mine)
    captions_far = swap(captions_near[0], "mid")
    qkv_rank = plan.across_hi(qkv_z)
    down_rank = plan.natural_hi(down_rank).reshape(feed_width, D)
    token_rows = tokens.astype(f32).reshape(item_count, item_len, D)
    normed = modulate(token_rows, gain_rows[0], scale_attn)
    normed = plan.ordered(normed.astype(bf16).reshape(row_count, D))
    mlp_gate = jnp.tanh(gate_mlp)[:, None, :]
    grad_top = out_cotangent.astype(f32).reshape(item_count, item_len, D)
    grad_result = (mlp_gate * grad_top).astype(bf16).reshape(row_count, D)
    normed_near, result_near = pair(normed), pair(grad_result)
    text_key_z, captions_far, qkv_rank, down_rank, normed_near, result_near = fence(
        text_key_z, captions_far, qkv_rank, down_rank, normed_near, result_near
    )

    text_value_z = z_gather(text_value_mine)
    text_key_rank = plan.across_hi(text_key_z)
    normed_far = swap(normed_near[0], "mid")
    captions_far = pair(captions_far)
    text_value_z, text_key_rank, normed_far, captions_far = fence(
        text_value_z, text_key_rank, normed_far, captions_far
    )

    gate_z = z_gather(gate_mine)
    text_value_rank = plan.across_hi(text_value_z)
    result_far = swap(result_near[0], "mid")
    normed_far = pair(normed_far)
    if plan.aligned:
        blocks = [block.reshape(rep_count, -1, 3 * rank_width) for block in qkv_rank]
        out_rank = plan.natural_hi([block[:, RANKS * rows :].reshape(-1, D) for block in blocks])
        out_rank = out_rank.reshape(rank_width, D)
        qkv_rank = [block[:, : RANKS * rows].reshape(-1, 3 * rank_width) for block in blocks]
        qkv_rank = qkv_rank if hi_count == 2 else jnp.stack(qkv_rank)
    qkv_rank, text_key_rank = plan.halves(qkv_rank), plan.text_halves(text_key_rank)
    gate_z, text_value_rank, result_far, normed_far, qkv_rank, out_rank, text_key_rank = fence(
        gate_z, text_value_rank, result_far, normed_far, qkv_rank, out_rank, text_key_rank
    )

    up_z = z_gather(up_mine)
    gate_rank = plan.across_hi(gate_z)
    attend_weights = (qkv_rank, text_key_rank, plan.text_halves(text_value_rank), out_rank, tables)
    normed_far, captions_far, kept_far, partial_far = attend(
        scalars[1], normed_far, captions_far, *attend_weights
    )
    up_z, gate_rank, normed_far, captions_far, kept_far, partial_far, attend_weights = fence(
        up_z, gate_rank, normed_far, captions_far, kept_far, partial_far, attend_weights
    )

    across = settle(partial_far).astype(bf16)
    across, normed_near, up_z = fence(across, normed_near, up_z)
    up_rank = plan.across_hi(up_z)
    arrived = settle_move(across)
    normed_near, captions_near, kept_near, partial_near = attend(
        scalars[0], normed_near, captions_near, *attend_weights
    )
    result_far = pair(result_far)
    gate_rank = plan.halves(gate_rank)
    up_rank, arrived, normed_near, captions_near, kept_near, partial_near, result_far, gate_rank = fence(
        up_rank, arrived, normed_near, captions_near, kept_near, partial_near, result_far, gate_rank
    )

    branch = (settle(partial_near) + arrived.astype(f32)).reshape(item_count, item_len, D)
    attn_gate = jnp.tanh(gate_attn)[:, None, :]
    middle = token_rows + attn_gate * branch
    mlp_input = modulate(middle, gain_rows[4], scale_mlp)
    mlp_input = plan.ordered(mlp_input.astype(bf16).reshape(row_count, D))
    up_rank = plan.halves(up_rank)
    mlp_input, up_rank = fence(mlp_input, up_rank)

    feed_weights = (gate_rank, up_rank, down_rank)
    input_far = swap(mlp_input, "mid")
    input_near, result_near, hidden_near, gate_near, up_near, partial_near = feed(
        pair(mlp_input), result_near, *feed_weights
    )
    result_part_near = result_part(hidden_near, down_rank)
    input_far, input_near, result_near, hidden_near, gate_near, up_near, partial_near, result_part_near = fence(
        input_far, input_near, result_near, hidden_near, gate_near, up_near, partial_near, result_part_near
    )
    input_far, result_far, hidden_far, gate_far, up_far, partial_far = feed(
        pair(input_far), result_far, *feed_weights
    )
    inputs, results = (input_near, input_far), (result_near, result_far)
    gate_rows, up_rows, hidden_rows = (gate_near, gate_far), (up_near, up_far), (hidden_near, hidden_far)
    across = settle(partial_far).astype(bf16)
    gate_moved = plan.product_moved(inputs, gate_rows)
    across, gate_moved, gate_rows, up_rows, hidden_rows = fence(
        across, gate_moved, gate_rows, up_rows, hidden_rows
    )
    arrived = settle_move(across)
    gate_moved = plan.move(gate_moved)
    up_moved = plan.product_moved(inputs, up_rows)
    hidden_first = hi_at * (feed_width // 2)
    down_moved = plan.product_moved(hidden_rows, results, feed_width // 2 - hidden_first)
    gate_kept = plan.product_kept(inputs, gate_rows)
    up_kept = plan.product_kept(inputs, up_rows)
    result_part_far = result_part(hidden_rows[1], down_rank)
    arrived, gate_moved, up_moved, down_moved, gate_kept, up_kept, result_part_far, partial_near = fence(
        arrived, gate_moved, up_moved, down_moved, gate_kept, up_kept, result_part_far, partial_near
    )

    up_moved = plan.move(up_moved)
    gate_grad = plan.by_rep(plan.total(gate_kept, gate_moved))
    gate_parts = plan.reduce(gate_grad)
    grad_mlp_input = plan.ordered(settle(partial_near) + arrived.astype(f32))
    _, pull_mlp_norm = jax.vjp(modulate, middle, gain_rows[4], scale_mlp)
    grad_middle_norm, grad_mlp_gain, grad_scale_mlp = pull_mlp_norm(
        grad_mlp_input.reshape(item_count, item_len, D)
    )
    grad_middle = grad_top + grad_middle_norm
    grad_attn_gate = jnp.sum(grad_middle * branch, axis=1) * (1.0 - jnp.tanh(gate_attn) ** 2)
    grad_branch = (attn_gate * grad_middle).astype(bf16).reshape(row_count, D)
    grad_branch, result_part_far = fence(grad_branch, result_part_far)

    branch_far = swap(grad_branch, "mid")
    back_weights = (qkv_rank, out_rank, tables)
    branch_near, qkv_near, text_near, rows_near, gain_near = attend_back(
        scalars[0], pair(grad_branch), kept_near, *back_weights
    )
    result_across = settle(result_part_far).astype(bf16)
    branch_far, up_moved, gate_parts, branch_near, qkv_near, text_near, rows_near, gain_near, result_across = fence(
        branch_far, up_moved, gate_parts, branch_near, qkv_near, text_near, rows_near, gain_near, result_across
    )

    up_grad = plan.by_rep(plan.total(up_kept, up_moved))
    up_grad, branch_far, down_moved, result_across = fence(
        up_grad, pair(branch_far), down_moved, result_across
    )
    up_parts = plan.reduce(up_grad)
    down_moved = plan.move(down_moved)
    result_arrived = settle_move(result_across)
    branch_far, qkv_far, text_far, rows_far, gain_far = attend_back(
        scalars[1], branch_far, kept_far, *back_weights
    )
    captions, normed_rows = (captions_near, captions_far), (normed_near, normed_far)
    text_rows, qkv_rows, branches = (text_near, text_far), (qkv_near, qkv_far), (branch_near, branch_far)
    text_moved = plan.product_moved(captions, text_rows)
    down_moved, up_parts, result_arrived, text_rows, qkv_rows, branches, rows_far, gain_far, text_moved = fence(
        down_moved, up_parts, result_arrived, text_rows, qkv_rows, branches, rows_far, gain_far, text_moved
    )

    text_moved = plan.move(text_moved)
    down_kept = plan.product_kept(hidden_rows, results, hidden_first)
    down_grad = plan.total(down_kept, down_moved).reshape(rep_count, -1, D)
    across = settle(rows_far).astype(bf16)
    across, down_grad, text_rows, qkv_rows, branches = fence(
        across, down_grad, text_rows, qkv_rows, branches
    )
    down_parts = plan.reduce(down_grad)
    arrived = settle_move(across)
    qkv_moved = plan.product_moved(normed_rows, qkv_rows)
    mixed_rows = [plan.ordered(kept[6]) for kept in (kept_near, kept_far)]
    if plan.aligned:
        out_halves = [
            product([side[:, lanes] for side in mixed_rows], branches, 0, rank_width // 2, bf16)
            for lanes in (slice(0, rank_width // 2), slice(rank_width // 2, None))
        ]
    else:
        out_halves = []
    text_kept = plan.product_kept(captions, text_rows)
    qkv_kept = plan.product_kept(normed_rows, qkv_rows)
    text_moved, down_parts, arrived, qkv_moved, text_kept, qkv_kept, out_halves = fence(
        text_moved, down_parts, arrived, qkv_moved, text_kept, qkv_kept, out_halves
    )

    qkv_moved = plan.move(qkv_moved)
    if plan.aligned:
        if hi_count == 2:
            out_kept, out_moved = out_halves[0].astype(f32), swap(out_halves[1], "hi")
        else:
            out_kept, out_moved = None, plan.move(jnp.concatenate(out_halves))
    else:
        out_moved = ()
    text_grad = plan.text_by_rep(plan.total(text_kept, text_moved))
    text_parts = plan.reduce(text_grad)
    grad_normed = plan.ordered(settle(rows_near) + arrived.astype(f32))
    _, pull_attn_norm = jax.vjp(modulate, token_rows, gain_rows[0], scale_attn)
    grad_token_norm, grad_attn_gain, grad_scale_attn = pull_attn_norm(
        grad_normed.reshape(item_count, item_len, D)
    )
    result = settle(result_part_near) + result_arrived.astype(f32)
    result = result.reshape(item_count, item_len, D)
    grad_mlp_gate = jnp.sum(grad_top * result, axis=1) * (1.0 - jnp.tanh(gate_mlp) ** 2)
    gate_up_parts = jnp.concatenate([gate_parts, up_parts], axis=-1)
    gate_up_parts = trade_ranks(gate_up_parts.reshape(RANKS, rows, -1))
    text_parts, qkv_moved, out_moved, grad_mlp_gate, grad_scale_attn, grad_attn_gain, gate_up_parts = fence(
        text_parts, qkv_moved, out_moved, grad_mlp_gate, grad_scale_attn, grad_attn_gain, gate_up_parts
    )
    layer_out = (middle + mlp_gate * result).astype(bf16).reshape(row_count, D)
    tokens_grad = (grad_middle + grad_token_norm).reshape(row_count, D)
    qkv_grad = plan.by_rep(plan.total(qkv_kept, qkv_moved))
    if plan.aligned:
        out_grad = plan.total(out_kept, out_moved).reshape(rep_count, -1, 3 * rank_width)
        qkv_grad = jnp.concatenate([qkv_grad, out_grad], axis=1)
    else:
        at = (jnp.arange(RANKS) == plan.rank).astype(bf16)[:, None, None]
        out_grad = product(mixed_rows, branches, 0, rank_width, bf16)
        placed = (out_grad[None] * at).reshape(D, D)
        out_weight_grad = lax.psum_scatter(placed, AXES, scatter_dimension=0, tiled=True).astype(f32)
    qkv_grad, grad_mlp_gate, text_parts = fence(qkv_grad, grad_mlp_gate, text_parts)
    qkv_parts = plan.reduce(qkv_grad)
    if plan.aligned:
        out_weight_grad = qkv_parts[RANKS * rows :].reshape(-1, D).astype(f32)
        qkv_parts = qkv_parts[: RANKS * rows]

    grad_modulation = jnp.concatenate(
        [grad_scale_attn, grad_attn_gate, grad_scale_mlp, grad_mlp_gate], axis=1
    ).astype(bf16)
    gain_terms = gain_near + gain_far
    gain_terms = gain_terms.at[3].multiply(1.0 - cross_gate**2)
    gain_terms = [plan.place_lanes(row) for row in gain_terms]
    gains_grad = jnp.stack(
        [grad_attn_gain, gain_terms[0], gain_terms[1], gain_terms[2], grad_mlp_gain, gain_terms[3]]
    ).astype(bf16)
    gain_blocks = jnp.moveaxis(gains_grad.reshape(6, devices, -1), 1, 0)
    gain_blocks = gain_blocks.reshape(devices, item_count, -1)
    modulations = jnp.broadcast_to(grad_modulation, (devices,) + grad_modulation.shape)
    both = lax.all_to_all(
        jnp.concatenate([modulations, gain_blocks], axis=2), AXES, 0, 0, tiled=True
    )
    ada_weight_grad = lax.dot_general(
        activated_mine.reshape(devices, item_count, rows),
        both[:, :, : 4 * D],
        (((0, 1), (0, 1)), ((), ())),
        preferred_element_type=f32,
    )
    norm_gains_grad = jnp.sum(both[:, :, 4 * D :].astype(f32), axis=0).reshape(6, -1)

    def whole(parts, weight, sections, groups):
        blocks = trade_ranks(parts.reshape(RANKS, weight.shape[0], -1))
        return plan.from_ranks(blocks, sections, groups).astype(f32)

    gate_up_weight_grad = plan.from_ranks(gate_up_parts, 2, hi_count).astype(f32)
    text_weight_grad = whole(text_parts, text_weight, 2, plan.head_groups)
    qkv_weight_grad = whole(qkv_parts, qkv_weight, 3, plan.head_groups)
    down_weight_grad = down_parts.astype(f32)
    return (
        layer_out,
        tokens_grad,
        norm_gains_grad,
        ada_weight_grad,
        qkv_weight_grad,
        out_weight_grad,
        text_weight_grad,
        gate_up_weight_grad,
        down_weight_grad,
    )


def solution(mesh):
    grp, rep = mesh.devices.shape
    hi = grp // RANKS
    inner = Mesh(mesh.devices.reshape(hi, 2, 2, rep), AXES)
    rows = P(AXES, None)

    def step(*arrays):
        return local(hi, rep, *arrays)

    return jax.shard_map(
        step,
        mesh=inner,
        in_specs=(
            rows,
            rows,
            P(AXES, None, None),
            P(AXES),
            P(AXES),
            rows,
            P(None, AXES),
            rows,
            rows,
            rows,
            rows,
            rows,
            rows,
        ),
        out_specs=(rows, rows, P(None, AXES), rows, rows, rows, rows, rows, rows),
        check_vma=False,
    )
```

```python
import math

import jax
import jax.numpy as jnp
from jax import lax
from jax.experimental import pallas as pl
from jax.experimental.pallas import tpu as pltpu
from jax.sharding import Mesh
from jax.sharding import PartitionSpec as P

D = 1536
HEADS = 24
HEAD_DIM = 64
TEXT_DIM = 4096
FF = 4096
SIDE = 16
RANKS = 4
LANES = 128
MIB = 1 << 20
AXES = ("hi", "mid", "core", "rep")


EPSILON = 1e-06


def norm_rows(values, gain_row):
    return (
        values * lax.rsqrt(jnp.mean(values * values, axis=-1, keepdims=True) + EPSILON) * gain_row
    )


def rope_tables(item_kind, item_len):
    position = jnp.arange(item_len, dtype=jnp.int32)[None, :]
    half_side = SIDE // 2
    frame_index = position // (half_side * half_side)
    within = position % (half_side * half_side)
    is_clip = item_kind[:, None] == 1
    row_index = jnp.where(is_clip, frame_index * half_side + within // half_side, position // SIDE)
    columns = jnp.where(is_clip, within % half_side, position % SIDE)
    lane_index = jnp.arange(HEAD_DIM, dtype=jnp.int32)
    quarter = HEAD_DIM // 4
    frequency = jnp.exp(-(lane_index % quarter).astype(jnp.float32) * (math.log(10000.0) / quarter))
    coordinate = jnp.where(
        lane_index[None, None, :] < 2 * quarter, row_index[:, :, None], columns[:, :, None]
    ).astype(jnp.float32)
    angles = coordinate * frequency
    return (jnp.cos(angles), jnp.sin(angles))


def modulate(values, gain_row, scaling):
    return norm_rows(values, gain_row) * (1.0 + scaling[:, None, :])


def silu_product(gate_half, up_half):
    return jax.nn.silu(gate_half) * up_half


def dot(left, right):
    return jnp.dot(left, right, preferred_element_type=jnp.float32)


def dot_left(left, right):
    return lax.dot_general(left, right, (((0,), (0,)), ((), ())), preferred_element_type=jnp.float32)


def dot_right(left, right):
    return lax.dot_general(left, right, (((1,), (1,)), ((), ())), preferred_element_type=jnp.float32)


def lane_index(shape):
    return lax.broadcasted_iota(jnp.int32, shape, len(shape) - 1)

def head_sums(values):
    first = lane_index(values.shape) < HEAD_DIM
    low = jnp.sum(jnp.where(first, values, 0.0), axis=-1, keepdims=True)
    high = jnp.sum(jnp.where(first, 0.0, values), axis=-1, keepdims=True)
    return jnp.where(first, low, high)

def partner(values):
    quarter = HEAD_DIM // 4
    width = values.shape[-1]
    low = lane_index(values.shape) % (2 * quarter) < quarter
    return jnp.where(low, pltpu.roll(values, width - quarter, 1), pltpu.roll(values, quarter, 1))

def stack_heads(values):
    first = lane_index(values.shape) < HEAD_DIM
    zero = jnp.zeros_like(values)
    return jnp.concatenate([jnp.where(first, values, zero), jnp.where(first, zero, values)])

def join_heads(stacked):
    rows = stacked.shape[0] // 2
    first = lane_index((rows, stacked.shape[1])) < HEAD_DIM
    return jnp.where(first, stacked[:rows], stacked[rows:])

def inverse_rms(raw):
    return lax.rsqrt(head_sums(raw * raw) * (1.0 / HEAD_DIM) + EPSILON)

def rows_of(ref):
    return ref.shape[0]


def dot_cut(rows, mine, other):
    half = mine.shape[0]
    return dot(rows[:, :half], mine[...]) + dot(rows[:, half:], other[...])


def attend_kernel(
    kind_ref,
    len_ref,
    rows_ref,
    core_rows_ref,
    caption_ref,
    core_caption_ref,
    qkv_mine_ref,
    qkv_other_ref,
    key_mine_ref,
    key_other_ref,
    value_mine_ref,
    value_other_ref,
    out_weight_ref,
    gain_ref,
    cos_ref,
    sin_ref,
    rows_out_ref,
    caption_out_ref,
    qkv_ref,
    text_ref,
    text_value_ref,
    q_ref,
    k_ref,
    tk_ref,
    mixed_ref,
    read_ref,
    branch_ref,
    core_branch_ref,
):
    item = pl.program_id(0)
    own = item < pl.num_programs(0) // 2
    kind, length = kind_ref[item], len_ref[item]
    width = q_ref.shape[1]
    positions = pl.ds(kind * rows_of(q_ref), rows_of(q_ref))
    cosine, sine = cos_ref[positions, :], sin_ref[positions, :]
    scaling = HEAD_DIM ** (-0.5)

    @pl.when(own)
    def _():
        rows_out_ref[...] = rows_ref[...]
        caption_out_ref[...] = caption_ref[...]

    @pl.when(jnp.logical_not(own))
    def _():
        rows_out_ref[...] = core_rows_ref[...]
        caption_out_ref[...] = core_caption_ref[...]

    qkv_ref[...] = dot_cut(rows_out_ref, qkv_mine_ref, qkv_other_ref)
    text_ref[...] = dot_cut(caption_out_ref, key_mine_ref, key_other_ref)
    text_value_ref[...] = dot_cut(caption_out_ref, value_mine_ref, value_other_ref)
    for at in range(0, width, LANES):
        lanes = slice(at, at + LANES)
        turned = []
        for part, out_ref in ((0, q_ref), (1, k_ref)):
            raw = qkv_ref[:, part * width + at : part * width + at + LANES]
            normal = raw * inverse_rms(raw) * gain_ref[part : part + 1, lanes]
            rows = (normal * cosine + partner(normal) * sine).astype(jnp.bfloat16)
            out_ref[:, lanes] = rows
            turned.append(rows)
        queries, keys = turned
        values = qkv_ref[:, 2 * width + at : 2 * width + at + LANES].astype(jnp.bfloat16)
        text_raw = text_ref[:, lanes]
        text_keys = (text_raw * inverse_rms(text_raw) * gain_ref[2:3, lanes]).astype(jnp.bfloat16)
        tk_ref[:, lanes] = text_keys
        text_values = text_value_ref[:, lanes].astype(jnp.bfloat16)
        stacked = stack_heads(queries)
        scores = dot_right(stacked, keys) * scaling
        scores = jnp.exp(scores - jnp.max(scores, axis=-1, keepdims=True))
        own_out = dot(scores.astype(jnp.bfloat16), values) / jnp.sum(scores, axis=-1, keepdims=True)
        text = dot_right(stacked, text_keys) * scaling
        text = jnp.where(lane_index(text.shape) < length, text, -1e30)
        text = jnp.exp(text - jnp.max(text, axis=-1, keepdims=True))
        text_out = dot(text.astype(jnp.bfloat16), text_values) / jnp.sum(text, axis=-1, keepdims=True)
        read = join_heads(text_out)
        read_ref[:, lanes] = read
        mixed_ref[:, lanes] = (join_heads(own_out) + gain_ref[3:4, lanes] * read).astype(jnp.bfloat16)

    branch = dot(mixed_ref[...], out_weight_ref[...])

    @pl.when(own)
    def _():
        branch_ref[...] = branch

    @pl.when(jnp.logical_not(own))
    def _():
        core_branch_ref[...] = branch.astype(jnp.bfloat16)


def head_norm_back(grad, raw, gain_row):
    inverse = inverse_rms(raw)
    scaled = grad * gain_row
    normal = raw * inverse
    inner = head_sums(scaled * normal) * (1.0 / HEAD_DIM)
    return inverse * (scaled - normal * inner), jnp.sum(grad * normal, axis=0, keepdims=True)

def attend_back_kernel(
    kind_ref,
    len_ref,
    branch_ref,
    core_branch_ref,
    qkv_ref,
    text_ref,
    text_value_ref,
    q_ref,
    k_ref,
    tk_ref,
    read_ref,
    qkv_mine_ref,
    qkv_other_ref,
    out_weight_ref,
    gain_ref,
    cos_ref,
    sin_ref,
    branch_out_ref,
    gqkv_ref,
    gtext_ref,
    grad_rows_ref,
    core_grad_rows_ref,
    gains_ref,
    mixed_ref,
):
    item = pl.program_id(0)
    own = item < pl.num_programs(0) // 2
    kind, length = kind_ref[item], len_ref[item]
    width = q_ref.shape[1]
    positions = pl.ds(kind * rows_of(q_ref), rows_of(q_ref))
    cosine, sine = cos_ref[positions, :], sin_ref[positions, :]
    scaling = HEAD_DIM ** (-0.5)

    @pl.when(own)
    def _():
        branch_out_ref[...] = branch_ref[...]

    @pl.when(jnp.logical_not(own))
    def _():
        branch_out_ref[...] = core_branch_ref[...]

    mixed_ref[...] = dot_right(branch_out_ref[...], out_weight_ref[...])

    @pl.when(item == 0)
    def _():
        gains_ref[...] = jnp.zeros_like(gains_ref)

    def one(stacked, keys, values, stacked_grad, valid):
        scores = dot_right(keys, stacked) * scaling
        if valid is not None:
            scores = jnp.where(valid(scores.shape), scores, -1e30)
        probs = jnp.exp(scores - jnp.max(scores, axis=0, keepdims=True))
        probs = probs * (1.0 / jnp.sum(probs, axis=0, keepdims=True))
        grad_values = dot(probs.astype(jnp.bfloat16), stacked_grad)
        grad_probs = dot_right(values, stacked_grad)
        inner = jnp.sum(probs * grad_probs, axis=0, keepdims=True)
        grad_scores = (probs * (grad_probs - inner)).astype(jnp.bfloat16)
        grad_keys = dot(grad_scores, stacked) * scaling
        grad_queries = dot_left(keys, grad_scores)
        return grad_queries, grad_keys, grad_values

    for at in range(0, width, LANES):
        lanes = slice(at, at + LANES)
        grad = mixed_ref[:, lanes]
        cross = gain_ref[3:4, lanes]
        values = qkv_ref[:, 2 * width + at : 2 * width + at + LANES].astype(jnp.bfloat16)
        text_values = text_value_ref[:, lanes].astype(jnp.bfloat16)
        stacked = stack_heads(q_ref[:, lanes])
        own_queries, own_keys, own_values = one(
            stacked, k_ref[:, lanes], values, stack_heads(grad.astype(jnp.bfloat16)), None
        )
        read_queries, read_keys, read_values = one(
            stacked, tk_ref[:, lanes], text_values, stack_heads((cross * grad).astype(jnp.bfloat16)),
            lambda shape: lax.broadcasted_iota(jnp.int32, shape, 0) < length,
        )
        grad_queries = join_heads((own_queries + read_queries).T) * scaling
        for part, turned in ((0, grad_queries), (1, own_keys)):
            raw = qkv_ref[:, part * width + at : part * width + at + LANES]
            back = turned * cosine + partner(turned * sine)
            grad_raw, gain = head_norm_back(back, raw, gain_ref[part : part + 1, lanes])
            gqkv_ref[:, part * width + at : part * width + at + LANES] = grad_raw.astype(jnp.bfloat16)
            gains_ref[part : part + 1, lanes] += gain
        gqkv_ref[:, 2 * width + at : 2 * width + at + LANES] = own_values.astype(jnp.bfloat16)
        grad_text, gain = head_norm_back(read_keys, text_ref[:, lanes], gain_ref[2:3, lanes])
        gtext_ref[:, lanes] = grad_text.astype(jnp.bfloat16)
        gains_ref[2:3, lanes] += gain
        gtext_ref[:, width + at : width + at + LANES] = read_values.astype(jnp.bfloat16)
        gains_ref[3:4, lanes] += jnp.sum(grad * read_ref[:, lanes], axis=0, keepdims=True)

    half = qkv_mine_ref.shape[0]
    low = dot_right(gqkv_ref[...], qkv_mine_ref[...])
    high = dot_right(gqkv_ref[...], qkv_other_ref[...])

    @pl.when(own)
    def _():
        grad_rows_ref[:, :half] = low
        grad_rows_ref[:, half:] = high

    @pl.when(jnp.logical_not(own))
    def _():
        core_grad_rows_ref[:, :half] = low.astype(jnp.bfloat16)
        core_grad_rows_ref[:, half:] = high.astype(jnp.bfloat16)


def whole_spec(array):
    zeros = (0,) * len(array.shape)
    return pl.BlockSpec(array.shape, lambda *_: zeros, pipeline_mode=pl.Buffered(1))


def mine_spec(array, steps):
    half = steps // 2
    return pl.BlockSpec(
        (array.shape[0] // half, array.shape[1]), lambda i, *_: (jnp.minimum(i, half - 1), 0)
    )


def core_spec(array, steps):
    half = steps // 2
    return pl.BlockSpec(
        (array.shape[0] // half, array.shape[1]), lambda i, *_: (jnp.maximum(i - half, 0), 0)
    )


def pair_specs(pair_of_arrays, steps):
    return [mine_spec(pair_of_arrays[0], steps), core_spec(pair_of_arrays[1], steps)]


def step_spec(array, steps):
    return pl.BlockSpec((array.shape[0] // steps, array.shape[1]), lambda i, *_: (i, 0))


def summed_spec(array):
    return pl.BlockSpec(array.shape, lambda i, *_: (0, 0))


def shaped(count, columns, dtype=jnp.bfloat16):
    return jax.ShapeDtypeStruct((count, columns), dtype)


def parameters():
    return pltpu.CompilerParams(dimension_semantics=("arbitrary",), vmem_limit_bytes=58 * MIB)


def attend(scalars, rows, captions, qkv_rank, key_rank, value_rank, out_rank, tables):
    items = scalars[0].shape[0]
    count, width = 2 * rows[0].shape[0], out_rank.shape[0]
    text_count = 2 * captions[0].shape[0]
    outs = [
        shaped(count, D),
        shaped(text_count, TEXT_DIM),
        shaped(count, 3 * width, jnp.float32),
        shaped(text_count, width, jnp.float32),
        shaped(text_count, width, jnp.float32),
        shaped(count, width),
        shaped(count, width),
        shaped(text_count, width),
        shaped(count, width),
        shaped(count, width, jnp.float32),
    ]
    branch = (shaped(count // 2, D, jnp.float32), shaped(count // 2, D))
    whole = [*qkv_rank, *key_rank, *value_rank, out_rank, *tables]
    rows, captions, *kept, branch_mine, branch_core = pl.pallas_call(
        attend_kernel,
        grid_spec=pltpu.PrefetchScalarGridSpec(
            num_scalar_prefetch=2,
            grid=(items,),
            in_specs=pair_specs(rows, items)
            + pair_specs(captions, items)
            + [whole_spec(array) for array in whole],
            out_specs=[step_spec(array, items) for array in outs] + pair_specs(branch, items),
        ),
        out_shape=[*outs, *branch],
        compiler_params=parameters(),
        name="attend",
    )(*scalars, *rows, *captions, *whole)
    return rows, captions, kept, (branch_mine, branch_core)


def attend_back(scalars, grad_branch, kept, qkv_rank, out_rank, tables):
    items = scalars[0].shape[0]
    qkv_raw, text_raw, text_value_raw, queries, keys, text_keys, _, read = kept
    count, width = queries.shape
    outs = [
        shaped(count, D),
        shaped(count, 3 * width),
        shaped(text_raw.shape[0], 2 * width),
    ]
    rows = (shaped(count // 2, D, jnp.float32), shaped(count // 2, D))
    gains = shaped(4, width, jnp.float32)
    by_item = [qkv_raw, text_raw, text_value_raw, queries, keys, text_keys, read]
    whole = [*qkv_rank, out_rank, *tables]
    branch, qkv, text, rows_mine, rows_core, gains = pl.pallas_call(
        attend_back_kernel,
        grid_spec=pltpu.PrefetchScalarGridSpec(
            num_scalar_prefetch=2,
            grid=(items,),
            in_specs=pair_specs(grad_branch, items)
            + [step_spec(array, items) for array in by_item]
            + [whole_spec(array) for array in whole],
            out_specs=[step_spec(array, items) for array in outs]
            + pair_specs(rows, items)
            + [summed_spec(gains)],
            scratch_shapes=[pltpu.VMEM((count // items, width), jnp.float32)],
        ),
        out_shape=[*outs, *rows, gains],
        compiler_params=parameters(),
        name="attend_back",
    )(*scalars, *grad_branch, *by_item, *whole)
    return branch, qkv, text, (rows_mine, rows_core), gains


def row_cuts(lefts, rights):
    cuts, left, right, left_row, right_row = [], 0, 0, 0, 0
    while left < len(lefts):
        count = min(lefts[left].shape[0] - left_row, rights[right].shape[0] - right_row)
        cuts.append((left, left_row, right, right_row, count))
        left_row, right_row = left_row + count, right_row + count
        if left_row == lefts[left].shape[0]:
            left, left_row = left + 1, 0
        if right_row == rights[right].shape[0]:
            right, right_row = right + 1, 0
    return cuts


def product(lefts, rights, first, lanes, dtype):
    columns = rights[0].shape[1]
    if lanes % LANES:
        block = lanes
    else:
        block = 384 if lanes % 384 == 0 else math.gcd(lanes, 512)
    cuts = row_cuts(lefts, rights)

    def kernel(first_ref, *refs):
        left_refs, right_refs, out_ref = refs[: len(lefts)], refs[len(lefts) : -1], refs[-1]
        total = None
        for left, left_row, right, right_row, count in cuts:
            term = dot_left(
                left_refs[left][left_row : left_row + count, :],
                right_refs[right][right_row : right_row + count, :],
            )
            total = term if total is None else total + term
        out_ref[...] = total.astype(out_ref.dtype)

    return pl.pallas_call(
        kernel,
        grid_spec=pltpu.PrefetchScalarGridSpec(
            num_scalar_prefetch=1,
            grid=(lanes // block,),
            in_specs=[
                pl.BlockSpec((array.shape[0], block), lambda i, first: (0, first[0] // block + i))
                for array in lefts
            ]
            + [whole_spec(array) for array in rights],
            out_specs=pl.BlockSpec((block, columns), lambda i, first: (i, 0)),
        ),
        out_shape=shaped(lanes, columns, dtype),
        compiler_params=parameters(),
        name="product",
    )(jnp.reshape(first, (1,)).astype(jnp.int32), *lefts, *rights)


def feed_kernel(
    rows_ref,
    core_rows_ref,
    result_ref,
    core_result_ref,
    gate_mine_ref,
    gate_other_ref,
    up_mine_ref,
    up_other_ref,
    down_ref,
    rows,
    result,
    hidden_ref,
    grad_gate_ref,
    grad_up_ref,
    grad_ref,
    core_grad_ref,
):
    own = pl.program_id(0) < pl.num_programs(0) // 2

    @pl.when(own)
    def _():
        rows[...] = rows_ref[...]
        result[...] = result_ref[...]

    @pl.when(jnp.logical_not(own))
    def _():
        rows[...] = core_rows_ref[...]
        result[...] = core_result_ref[...]

    gate = dot_cut(rows, gate_mine_ref, gate_other_ref)
    up = dot_cut(rows, up_mine_ref, up_other_ref)
    grad_hidden = dot_right(result[...], down_ref[...])
    sigmoid = 1.0 / (1.0 + jnp.exp(-gate))
    silu = gate * sigmoid
    hidden_ref[...] = (silu * up).astype(jnp.bfloat16)
    grad_gate = (grad_hidden * up * (sigmoid + silu * (1.0 - sigmoid))).astype(jnp.bfloat16)
    grad_up = (grad_hidden * silu).astype(jnp.bfloat16)
    grad_gate_ref[...] = grad_gate
    grad_up_ref[...] = grad_up
    half = gate_mine_ref.shape[0]
    low = dot_right(grad_gate, gate_mine_ref[...]) + dot_right(grad_up, up_mine_ref[...])
    high = dot_right(grad_gate, gate_other_ref[...]) + dot_right(grad_up, up_other_ref[...])

    @pl.when(own)
    def _():
        grad_ref[:, :half] = low
        grad_ref[:, half:] = high

    @pl.when(jnp.logical_not(own))
    def _():
        core_grad_ref[:, :half] = low.astype(jnp.bfloat16)
        core_grad_ref[:, half:] = high.astype(jnp.bfloat16)


def feed(rows, grad_result, gate_rank, up_rank, down_rank):
    count, width = 2 * rows[0].shape[0], down_rank.shape[0]
    block = 256
    steps = count // block
    outs = [shaped(count, D)] * 2 + [shaped(count, width)] * 3
    grads = (shaped(count // 2, D, jnp.float32), shaped(count // 2, D))
    whole = [*gate_rank, *up_rank, down_rank]
    *outs, grad_mine, grad_core = pl.pallas_call(
        feed_kernel,
        grid=(steps,),
        in_specs=pair_specs(rows, steps)
        + pair_specs(grad_result, steps)
        + [whole_spec(array) for array in whole],
        out_specs=[step_spec(array, steps) for array in outs] + pair_specs(grads, steps),
        out_shape=[*outs, *grads],
        compiler_params=parameters(),
        name="feed",
    )(*rows, *grad_result, *whole)
    return *outs, (grad_mine, grad_core)


def result_kernel(hidden_ref, down_ref, result_ref, core_result_ref):
    own = pl.program_id(0) < pl.num_programs(0) // 2
    rows = dot(hidden_ref[...], down_ref[...])

    @pl.when(own)
    def _():
        result_ref[...] = rows

    @pl.when(jnp.logical_not(own))
    def _():
        core_result_ref[...] = rows.astype(jnp.bfloat16)


def result_part(hidden, down_rank):
    count = hidden.shape[0]
    steps = count // 256
    outs = (shaped(count // 2, D, jnp.float32), shaped(count // 2, D))
    return pl.pallas_call(
        result_kernel,
        grid=(steps,),
        in_specs=[step_spec(hidden, steps), whole_spec(down_rank)],
        out_specs=pair_specs(outs, steps),
        out_shape=outs,
        compiler_params=parameters(),
        name="result",
    )(hidden, down_rank)


def swap(block, axis, count=2, step=1):
    return lax.ppermute(block, axis, [(at, at ^ step) for at in range(count)])


def spread(block, axis, count):
    if count & (count - 1):
        return lax.all_gather(block, axis)
    block, step = block[None], 1
    while step < count:
        other = swap(block, axis, count, step)
        low = (lax.axis_index(axis) & step) == 0
        block = jnp.where(
            low, jnp.concatenate([block, other]), jnp.concatenate([other, block])
        )
        step *= 2
    return block


def fold(block, axis, count):
    if count & (count - 1):
        return lax.psum_scatter(block, axis, scatter_dimension=0)
    step = count // 2
    while step:
        half = block.shape[0] // 2
        low = (lax.axis_index(axis) & step) == 0
        lower, upper = block[:half], block[half:]
        block = jnp.where(low, lower, upper) + swap(
            jnp.where(low, upper, lower), axis, count, step
        )
        step //= 2
    return block[0]


def trade_ranks(block):
    return lax.all_to_all(block, ("mid", "core"), 0, 0, tiled=True)


def pick(stack, index):
    return lax.dynamic_index_in_dim(stack, index, 0, keepdims=False)


def pair(rows):
    return (rows, swap(rows, "core"))


def settle(partial):
    mine, core = partial
    return mine + swap(core, "core").astype(jnp.float32)


def settle_move(across):
    return swap(across, "mid")


class Layout:
    def __init__(self, hi, rep, out_rows):
        self.hi, self.rep = hi, rep
        self.aligned = (rep * out_rows) % HEAD_DIM == 0
        self.head_groups = hi if self.aligned else 1
        self.rank = lax.axis_index("mid") * 2 + lax.axis_index("core")

    def by_rank(self, weight, sections, groups):
        rows, columns = weight.shape
        width = columns // (sections * groups * RANKS)
        view = weight.reshape(rows, sections * groups, RANKS, width)
        view = jnp.transpose(view, (2, 0, 1, 3))
        return view.reshape(RANKS, rows, sections * groups * width)

    def from_ranks(self, blocks, sections, groups):
        _, rows, per_rank = blocks.shape
        width = per_rank // (sections * groups)
        view = blocks.reshape(RANKS, rows, sections * groups, width)
        return jnp.transpose(view, (1, 2, 0, 3)).reshape(rows, RANKS * per_rank)

    def ordered(self, values):
        if self.hi != 2:
            return values
        half = values.shape[-1] // 2
        turned = jnp.concatenate([values[..., half:], values[..., :half]], axis=-1)
        return jnp.where(lax.axis_index("hi") == 0, values, turned)

    def ordered_text(self, values):
        if self.hi != 2:
            return values
        view = values.reshape(values.shape[0], self.hi, RANKS, self.rep, -1)
        return self.ordered(jnp.swapaxes(view, 2, 3).reshape(values.shape))

    def text_halves(self, blocks):
        return tuple(blocks) if self.hi == 2 else self.halves(blocks)

    def text_by_rep(self, summed):
        return summed.reshape(self.rep, -1, summed.shape[1]) if self.hi == 2 else self.by_rep(summed)

    def across_hi(self, block):
        if self.hi == 2:
            return (block, swap(block, "hi"))
        return spread(block, "hi", self.hi)

    def natural_hi(self, blocks):
        if self.hi != 2:
            return blocks
        mine, other = blocks
        low = lax.axis_index("hi") == 0
        return jnp.stack([jnp.where(low, mine, other), jnp.where(low, other, mine)])

    def halves(self, blocks):
        if self.hi == 2:
            return tuple(self.natural_rows(block[None]) for block in blocks)
        return tuple(jnp.split(self.natural_rows(blocks), 2))

    def natural_rows(self, stacked):
        view = stacked.reshape(stacked.shape[0], self.rep, RANKS, -1, stacked.shape[-1])
        return jnp.transpose(view, (0, 2, 1, 3, 4)).reshape(-1, stacked.shape[-1])

    def product_moved(self, lefts, rights, first=None):
        lanes = lefts[0].shape[1]
        if self.hi != 2:
            return product(lefts, rights, 0, lanes, jnp.bfloat16)
        return product(lefts, rights, lanes // 2 if first is None else first, lanes // 2, jnp.bfloat16)

    def move(self, moved):
        if self.hi == 2:
            return swap(moved, "hi")
        return fold(moved.reshape(self.hi, -1, moved.shape[1]), "hi", self.hi)

    def product_kept(self, lefts, rights, first=0):
        if self.hi != 2:
            return None
        return product(lefts, rights, first, lefts[0].shape[1] // 2, jnp.float32)

    def total(self, kept, arrived):
        if kept is None:
            return arrived
        return (kept + arrived.astype(jnp.float32)).astype(jnp.bfloat16)

    def by_rep(self, summed):
        view = summed.reshape(RANKS, self.rep, -1, summed.shape[1])
        return jnp.transpose(view, (1, 0, 2, 3)).reshape(self.rep, -1, summed.shape[1])

    def reduce(self, blocks):
        flat = blocks.reshape(-1, blocks.shape[-1])
        return lax.psum_scatter(flat, "rep", scatter_dimension=0, tiled=True)

    def rank_lanes(self, rows, groups):
        view = rows.reshape(rows.shape[0], groups, RANKS, -1)
        return lax.dynamic_index_in_dim(view, self.rank, 2, keepdims=False).reshape(rows.shape[0], -1)

    def place_lanes(self, row):
        view = row.reshape(self.head_groups, 1, -1)
        at = (jnp.arange(RANKS) == self.rank).astype(row.dtype)[None, :, None]
        return (view * at).reshape(-1)


def fence(*values):
    return lax.optimization_barrier(values)


def local(
    hi_count,
    rep_count,
    tokens,
    condition,
    caption,
    caption_len,
    item_kind,
    out_cotangent,
    norm_gains,
    ada_weight,
    qkv_weight,
    out_weight,
    text_weight,
    gate_up_weight,
    down_weight,
):
    bf16, f32 = jnp.bfloat16, jnp.float32
    item_count = condition.shape[0]
    item_len = tokens.shape[0] // item_count
    row_count = item_count * item_len
    rows = qkv_weight.shape[0]
    plan = Layout(hi_count, rep_count, out_weight.shape[0])
    rank_width = HEADS // RANKS * HEAD_DIM
    hi_at, mid_at, core_at, rep_at = [lax.axis_index(name) for name in AXES]
    device_shape = (hi_count, 2, 2, rep_count)

    feed_width = FF // RANKS
    devices = hi_count * RANKS * rep_count
    block_at = (hi_at * RANKS + plan.rank) * rep_count + rep_at

    def z_gather(block):
        return lax.all_gather(block.reshape(-1, block.shape[-1]), "rep", tiled=True)

    down_z = z_gather(down_weight)
    qkv_mine = trade_ranks(plan.by_rank(qkv_weight, 3, plan.head_groups))
    qkv_mine = qkv_mine.reshape(RANKS * rows, 3 * rank_width)
    if plan.aligned:
        qkv_mine = jnp.concatenate([qkv_mine, out_weight.reshape(-1, 3 * rank_width)])
    else:
        out_whole = lax.all_gather(out_weight, AXES, axis=0, tiled=True)
        out_rank = pick(out_whole.reshape(RANKS, rank_width, D), plan.rank)

    head = condition.reshape(item_count, devices, rows)
    head = jnp.transpose(head, (1, 0, 2)).reshape(devices, -1)
    rest = jnp.concatenate(
        [norm_gains.reshape(-1), caption_len.astype(bf16), item_kind.astype(bf16)]
    )
    small = jnp.concatenate([head, jnp.broadcast_to(rest, (devices, rest.size))], axis=1)
    small = lax.all_to_all(small, AXES, 0, 0, tiled=True)
    cut = [head.shape[1], head.shape[1] + norm_gains.size]
    cut.append(cut[1] + item_count)
    conditions, gains, lengths, kinds = jnp.split(small, cut, axis=-1)
    activated_mine = jax.nn.silu(conditions.astype(f32)).astype(bf16).reshape(-1, rows)
    gain_rows = jnp.moveaxis(gains.astype(f32).reshape(devices, 6, -1), 1, 0).reshape(6, D)
    lengths, kinds = [
        values.reshape(device_shape + (item_count,)) for values in (lengths, kinds)
    ]

    def group_items(values):
        view = lax.dynamic_index_in_dim(pick(values, hi_at), rep_at, 2, keepdims=False)
        near, far = pick(view, mid_at), pick(view, 1 - mid_at)
        order = [core_at, 1 - core_at]
        return [
            jnp.concatenate([pick(side, at) for at in order]).astype(jnp.int32)
            for side in (near, far)
        ]

    lengths_sides = group_items(lengths)
    kinds_sides = group_items(kinds)
    cosine, sine = rope_tables(jnp.arange(2), item_len)
    signs = jnp.where(jnp.arange(HEAD_DIM) % (HEAD_DIM // 2) < HEAD_DIM // 4, -1.0, 1.0)
    cosine, sine = [
        jnp.tile(table, (1, 1, LANES // HEAD_DIM)).reshape(-1, LANES) for table in (cosine, sine * signs)
    ]
    head_gains = plan.rank_lanes(gain_rows, plan.head_groups)
    cross_gate = jnp.tanh(head_gains[5])
    head_gains = jnp.concatenate([head_gains[1:4], cross_gate[None]])
    tables = (head_gains, cosine, sine)
    scalars = list(zip(kinds_sides, lengths_sides, strict=True))
    tables, scalars = fence(tables, scalars)

    down_z, qkv_mine, text_weight, activated_mine = fence(
        down_z, qkv_mine, text_weight, activated_mine
    )
    qkv_z = z_gather(qkv_mine)
    down_rank = plan.across_hi(down_z)
    text_mine = trade_ranks(plan.by_rank(text_weight, 2, plan.head_groups))
    captions_near = pair(plan.ordered_text(caption.reshape(-1, TEXT_DIM)))
    partial = dot(activated_mine, ada_weight).astype(bf16).reshape(devices, item_count, 4 * D)
    gate_up_mine = trade_ranks(plan.by_rank(gate_up_weight, 2, hi_count))
    modulation = jnp.sum(lax.all_to_all(partial, AXES, 0, 0, tiled=True).astype(f32), axis=0)
    text_key_mine, text_value_mine = text_mine[..., :rank_width], text_mine[..., rank_width:]
    gate_mine, up_mine = gate_up_mine[..., :feed_width], gate_up_mine[..., feed_width:]
    qkv_z, down_rank, modulation, text_key_mine, text_value_mine, gate_mine, up_mine, captions_near = fence(
        qkv_z, down_rank, modulation, text_key_mine, text_value_mine, gate_mine, up_mine, captions_near
    )

    scale_attn, gate_attn, scale_mlp, gate_mlp = jnp.split(modulation, 4, axis=1)
    text_key_z = z_gather(text_key_mine)
    captions_far = swap(captions_near[0], "mid")
    qkv_rank = plan.across_hi(qkv_z)
    down_rank = plan.natural_hi(down_rank).reshape(feed_width, D)
    token_rows = tokens.astype(f32).reshape(item_count, item_len, D)
    normed = modulate(token_rows, gain_rows[0], scale_attn)
    normed = plan.ordered(normed.astype(bf16).reshape(row_count, D))
    mlp_gate = jnp.tanh(gate_mlp)[:, None, :]
    grad_top = out_cotangent.astype(f32).reshape(item_count, item_len, D)
    grad_result = (mlp_gate * grad_top).astype(bf16).reshape(row_count, D)
    normed_near, result_near = pair(normed), pair(grad_result)
    text_key_z, captions_far, qkv_rank, down_rank, normed_near, result_near = fence(
        text_key_z, captions_far, qkv_rank, down_rank, normed_near, result_near
    )

    text_value_z = z_gather(text_value_mine)
    text_key_rank = plan.across_hi(text_key_z)
    normed_far = swap(normed_near[0], "mid")
    captions_far = pair(captions_far)
    text_value_z, text_key_rank, normed_far, captions_far = fence(
        text_value_z, text_key_rank, normed_far, captions_far
    )

    gate_z = z_gather(gate_mine)
    text_value_rank = plan.across_hi(text_value_z)
    result_far = swap(result_near[0], "mid")
    normed_far = pair(normed_far)
    if plan.aligned:
        blocks = [block.reshape(rep_count, -1, 3 * rank_width) for block in qkv_rank]
        out_rank = plan.natural_hi([block[:, RANKS * rows :].reshape(-1, D) for block in blocks])
        out_rank = out_rank.reshape(rank_width, D)
        qkv_rank = [block[:, : RANKS * rows].reshape(-1, 3 * rank_width) for block in blocks]
        qkv_rank = qkv_rank if hi_count == 2 else jnp.stack(qkv_rank)
    qkv_rank, text_key_rank = plan.halves(qkv_rank), plan.text_halves(text_key_rank)
    gate_z, text_value_rank, result_far, normed_far, qkv_rank, out_rank, text_key_rank = fence(
        gate_z, text_value_rank, result_far, normed_far, qkv_rank, out_rank, text_key_rank
    )

    up_z = z_gather(up_mine)
    gate_rank = plan.across_hi(gate_z)
    attend_weights = (qkv_rank, text_key_rank, plan.text_halves(text_value_rank), out_rank)
    normed_far, captions_far, kept_far, partial_far = attend(
        scalars[1], normed_far, captions_far, *attend_weights, tables
    )
    up_z, gate_rank, normed_far, captions_far, kept_far, partial_far, attend_weights = fence(
        up_z, gate_rank, normed_far, captions_far, kept_far, partial_far, attend_weights
    )

    across = settle(partial_far).astype(bf16)
    across, normed_near, up_z = fence(across, normed_near, up_z)
    up_rank = plan.across_hi(up_z)
    arrived = settle_move(across)
    normed_near, captions_near, kept_near, partial_near = attend(
        scalars[0], normed_near, captions_near, *attend_weights, tables
    )
    result_far = pair(result_far)
    gate_rank = plan.halves(gate_rank)
    up_rank, arrived, normed_near, captions_near, kept_near, partial_near, result_far, gate_rank = fence(
        up_rank, arrived, normed_near, captions_near, kept_near, partial_near, result_far, gate_rank
    )

    branch = (settle(partial_near) + arrived.astype(f32)).reshape(item_count, item_len, D)
    attn_gate = jnp.tanh(gate_attn)[:, None, :]
    middle = token_rows + attn_gate * branch
    mlp_input = modulate(middle, gain_rows[4], scale_mlp)
    mlp_input = plan.ordered(mlp_input.astype(bf16).reshape(row_count, D))
    up_rank = plan.halves(up_rank)
    mlp_input, up_rank = fence(mlp_input, up_rank)

    feed_weights = (gate_rank, up_rank, down_rank)
    input_far = swap(mlp_input, "mid")
    input_near, result_near, hidden_near, gate_near, up_near, partial_near = feed(
        pair(mlp_input), result_near, *feed_weights
    )
    input_far, input_near, result_near, hidden_near, gate_near, up_near, partial_near = fence(
        input_far, input_near, result_near, hidden_near, gate_near, up_near, partial_near
    )
    input_far, result_far, hidden_far, gate_far, up_far, partial_far = feed(
        pair(input_far), result_far, *feed_weights
    )
    inputs, results = (input_near, input_far), (result_near, result_far)
    gate_rows, up_rows, hidden_rows = (gate_near, gate_far), (up_near, up_far), (hidden_near, hidden_far)
    across = settle(partial_far).astype(bf16)
    gate_moved = plan.product_moved(inputs, gate_rows)
    across, gate_moved, gate_rows, up_rows, hidden_rows = fence(
        across, gate_moved, gate_rows, up_rows, hidden_rows
    )
    arrived = settle_move(across)
    gate_moved = plan.move(gate_moved)
    up_moved = plan.product_moved(inputs, up_rows)
    hidden_first = hi_at * (feed_width // 2)
    down_moved = plan.product_moved(hidden_rows, results, feed_width // 2 - hidden_first)
    gate_kept = plan.product_kept(inputs, gate_rows)
    up_kept = plan.product_kept(inputs, up_rows)
    down_kept = plan.product_kept(hidden_rows, results, hidden_first)
    near = settle(partial_near)
    arrived, gate_moved, up_moved, down_moved, gate_kept, up_kept, down_kept, near = fence(
        arrived, gate_moved, up_moved, down_moved, gate_kept, up_kept, down_kept, near
    )

    up_moved = plan.move(up_moved)
    gate_grad = plan.by_rep(plan.total(gate_kept, gate_moved))
    gate_parts = plan.reduce(gate_grad)
    grad_mlp_input = plan.ordered(near + arrived.astype(f32))
    _, pull_mlp_norm = jax.vjp(modulate, middle, gain_rows[4], scale_mlp)
    grad_middle_norm, grad_mlp_gain, grad_scale_mlp = pull_mlp_norm(
        grad_mlp_input.reshape(item_count, item_len, D)
    )
    grad_middle = grad_top + grad_middle_norm
    grad_attn_gate = jnp.sum(grad_middle * branch, axis=1) * (1.0 - jnp.tanh(gate_attn) ** 2)
    grad_branch = (attn_gate * grad_middle).astype(bf16).reshape(row_count, D)
    (grad_branch,) = fence(grad_branch)

    branch_far = swap(grad_branch, "mid")
    back_weights = (qkv_rank, out_rank, tables)
    branch_near, qkv_near, text_near, rows_near, gain_near = attend_back(
        scalars[0], pair(grad_branch), kept_near, *back_weights
    )
    branch_far, up_moved, gate_parts, branch_near, qkv_near, text_near, rows_near, gain_near = fence(
        branch_far, up_moved, gate_parts, branch_near, qkv_near, text_near, rows_near, gain_near
    )

    up_grad = plan.by_rep(plan.total(up_kept, up_moved))
    up_grad, branch_far, down_moved = fence(up_grad, pair(branch_far), down_moved)
    up_parts = plan.reduce(up_grad)
    down_moved = plan.move(down_moved)
    branch_far, qkv_far, text_far, rows_far, gain_far = attend_back(
        scalars[1], branch_far, kept_far, *back_weights
    )
    captions, normed_rows = (captions_near, captions_far), (normed_near, normed_far)
    text_rows, qkv_rows, branches = (text_near, text_far), (qkv_near, qkv_far), (branch_near, branch_far)
    text_moved = plan.product_moved(captions, text_rows)
    down_moved, up_parts, text_rows, qkv_rows, branches, rows_far, gain_far, text_moved = fence(
        down_moved, up_parts, text_rows, qkv_rows, branches, rows_far, gain_far, text_moved
    )

    text_moved = plan.move(text_moved)
    down_grad = plan.total(down_kept, down_moved).reshape(rep_count, -1, D)
    across = settle(rows_far).astype(bf16)
    mixed_rows = [plan.ordered(kept[6]) for kept in (kept_near, kept_far)]
    if plan.aligned:
        halves = [slice(0, rank_width // 2), slice(rank_width // 2, None)]
        out_kept, out_moved = [
            product([side[:, lanes] for side in mixed_rows], branches, 0, rank_width // 2, bf16)
            for lanes in halves
        ]
    else:
        out_kept, out_moved = (), ()
    across, down_grad, text_rows, qkv_rows, out_kept, out_moved, hidden_rows = fence(
        across, down_grad, text_rows, qkv_rows, out_kept, out_moved, hidden_rows
    )
    down_parts = plan.reduce(down_grad)
    arrived = settle_move(across)
    if plan.aligned:
        if hi_count == 2:
            out_grad = plan.total(out_kept.astype(f32), swap(out_moved, "hi"))
        else:
            out_grad = plan.move(jnp.concatenate([out_kept, out_moved]))
        out_parts = plan.reduce(out_grad.reshape(rep_count, -1, D))
    else:
        at = (jnp.arange(RANKS) == plan.rank).astype(bf16)[:, None, None]
        out_grad = product(mixed_rows, branches, 0, rank_width, bf16)
        placed = (out_grad[None] * at).reshape(D, D)
        out_parts = lax.psum_scatter(placed, AXES, scatter_dimension=0, tiled=True)
    qkv_moved = plan.product_moved(normed_rows, qkv_rows)
    text_kept = plan.product_kept(captions, text_rows)
    qkv_kept = plan.product_kept(normed_rows, qkv_rows)
    result_far = result_part(hidden_rows[1], down_rank)
    result_near = result_part(hidden_rows[0], down_rank)
    text_moved, down_parts, out_parts, arrived, qkv_moved, text_kept, qkv_kept, result_far, result_near = fence(
        text_moved, down_parts, out_parts, arrived, qkv_moved, text_kept, qkv_kept, result_far, result_near
    )

    qkv_moved = plan.move(qkv_moved)
    text_grad = plan.text_by_rep(plan.total(text_kept, text_moved))
    text_parts = plan.reduce(text_grad)
    result_arrived = settle_move(settle(result_far).astype(bf16))
    grad_normed = plan.ordered(settle(rows_near) + arrived.astype(f32))
    _, pull_attn_norm = jax.vjp(modulate, token_rows, gain_rows[0], scale_attn)
    grad_token_norm, grad_attn_gain, grad_scale_attn = pull_attn_norm(
        grad_normed.reshape(item_count, item_len, D)
    )
    result_near = settle(result_near)
    gate_up_parts = jnp.concatenate([gate_parts, up_parts], axis=-1)
    gate_up_parts = trade_ranks(gate_up_parts.reshape(RANKS, rows, -1))
    text_parts, qkv_moved, result_arrived, result_near, grad_scale_attn, grad_attn_gain, gate_up_parts = fence(
        text_parts, qkv_moved, result_arrived, result_near, grad_scale_attn, grad_attn_gain, gate_up_parts
    )

    qkv_grad = plan.by_rep(plan.total(qkv_kept, qkv_moved))
    qkv_grad, result_near, text_parts = fence(qkv_grad, result_near, text_parts)
    qkv_parts = plan.reduce(qkv_grad)
    result = (result_near + result_arrived.astype(f32)).reshape(item_count, item_len, D)
    grad_mlp_gate = jnp.sum(grad_top * result, axis=1) * (1.0 - jnp.tanh(gate_mlp) ** 2)
    layer_out = (middle + mlp_gate * result).astype(bf16).reshape(row_count, D)
    tokens_grad = (grad_middle + grad_token_norm).reshape(row_count, D)

    grad_modulation = jnp.concatenate(
        [grad_scale_attn, grad_attn_gate, grad_scale_mlp, grad_mlp_gate], axis=1
    ).astype(bf16)
    gain_terms = gain_near + gain_far
    gain_terms = gain_terms.at[3].multiply(1.0 - cross_gate**2)
    gain_terms = [plan.place_lanes(row) for row in gain_terms]
    gains_grad = jnp.stack(
        [grad_attn_gain, gain_terms[0], gain_terms[1], gain_terms[2], grad_mlp_gain, gain_terms[3]]
    ).astype(bf16)
    gain_blocks = jnp.moveaxis(gains_grad.reshape(6, devices, -1), 1, 0)
    gain_blocks = gain_blocks.reshape(devices, item_count, -1)
    modulations = jnp.broadcast_to(grad_modulation, (devices,) + grad_modulation.shape)
    both = lax.all_to_all(
        jnp.concatenate([modulations, gain_blocks], axis=2), AXES, 0, 0, tiled=True
    )
    ada_weight_grad = lax.dot_general(
        activated_mine.reshape(devices, item_count, rows),
        both[:, :, : 4 * D],
        (((0, 1), (0, 1)), ((), ())),
        preferred_element_type=f32,
    )
    norm_gains_grad = jnp.sum(both[:, :, 4 * D :].astype(f32), axis=0).reshape(6, -1)

    def whole(parts, weight, sections, groups):
        blocks = trade_ranks(parts.reshape(RANKS, weight.shape[0], -1))
        return plan.from_ranks(blocks, sections, groups).astype(f32)

    gate_up_weight_grad = plan.from_ranks(gate_up_parts, 2, hi_count).astype(f32)
    text_weight_grad = whole(text_parts, text_weight, 2, plan.head_groups)
    qkv_weight_grad = whole(qkv_parts, qkv_weight, 3, plan.head_groups)
    down_weight_grad, out_weight_grad = down_parts.astype(f32), out_parts.astype(f32)
    return (
        layer_out,
        tokens_grad,
        norm_gains_grad,
        ada_weight_grad,
        qkv_weight_grad,
        out_weight_grad,
        text_weight_grad,
        gate_up_weight_grad,
        down_weight_grad,
    )


def solution(mesh):
    grp, rep = mesh.devices.shape
    hi = grp // RANKS
    inner = Mesh(mesh.devices.reshape(hi, 2, 2, rep), AXES)
    rows = P(AXES, None)

    def step(*arrays):
        return local(hi, rep, *arrays)

    return jax.shard_map(
        step,
        mesh=inner,
        in_specs=(
            rows,
            rows,
            P(AXES, None, None),
            P(AXES),
            P(AXES),
            rows,
            P(None, AXES),
            rows,
            rows,
            rows,
            rows,
            rows,
            rows,
        ),
        out_specs=(rows, rows, P(None, AXES), rows, rows, rows, rows, rows, rows),
        check_vma=False,
    )
```

```python
import math

import jax
import jax.numpy as jnp
from jax import lax
from jax.experimental import pallas as pl
from jax.experimental.pallas import tpu as pltpu
from jax.sharding import Mesh
from jax.sharding import PartitionSpec as P

D = 1536
HEADS = 24
HEAD_DIM = 64
TEXT_DIM = 4096
FF = 4096
SIDE = 16
RANKS = 4
LANES = 128
MIB = 1 << 20
AXES = ("hi", "mid", "core", "rep")


EPSILON = 1e-06


def norm_rows(values, gain_row):
    return (
        values * lax.rsqrt(jnp.mean(values * values, axis=-1, keepdims=True) + EPSILON) * gain_row
    )


def rope_tables(item_kind, item_len):
    position = jnp.arange(item_len, dtype=jnp.int32)[None, :]
    half_side = SIDE // 2
    frame_index = position // (half_side * half_side)
    within = position % (half_side * half_side)
    is_clip = item_kind[:, None] == 1
    row_index = jnp.where(is_clip, frame_index * half_side + within // half_side, position // SIDE)
    columns = jnp.where(is_clip, within % half_side, position % SIDE)
    lane_index = jnp.arange(HEAD_DIM, dtype=jnp.int32)
    quarter = HEAD_DIM // 4
    frequency = jnp.exp(-(lane_index % quarter).astype(jnp.float32) * (math.log(10000.0) / quarter))
    coordinate = jnp.where(
        lane_index[None, None, :] < 2 * quarter, row_index[:, :, None], columns[:, :, None]
    ).astype(jnp.float32)
    angles = coordinate * frequency
    return (jnp.cos(angles), jnp.sin(angles))


def modulate(values, gain_row, scaling):
    return norm_rows(values, gain_row) * (1.0 + scaling[:, None, :])


def silu_product(gate_half, up_half):
    return jax.nn.silu(gate_half) * up_half


def dot(left, right):
    return jnp.dot(left, right, preferred_element_type=jnp.float32)


def dot_left(left, right):
    return lax.dot_general(left, right, (((0,), (0,)), ((), ())), preferred_element_type=jnp.float32)


def dot_right(left, right):
    return lax.dot_general(left, right, (((1,), (1,)), ((), ())), preferred_element_type=jnp.float32)


def lane_index(shape):
    return lax.broadcasted_iota(jnp.int32, shape, len(shape) - 1)

def head_sums(values):
    first = lane_index(values.shape) < HEAD_DIM
    low = jnp.sum(jnp.where(first, values, 0.0), axis=-1, keepdims=True)
    high = jnp.sum(jnp.where(first, 0.0, values), axis=-1, keepdims=True)
    return jnp.where(first, low, high)

def partner(values):
    quarter = HEAD_DIM // 4
    width = values.shape[-1]
    low = lane_index(values.shape) % (2 * quarter) < quarter
    return jnp.where(low, pltpu.roll(values, width - quarter, 1), pltpu.roll(values, quarter, 1))

def stack_heads(values):
    first = lane_index(values.shape) < HEAD_DIM
    zero = jnp.zeros_like(values)
    return jnp.concatenate([jnp.where(first, values, zero), jnp.where(first, zero, values)])

def join_heads(stacked):
    rows = stacked.shape[0] // 2
    first = lane_index((rows, stacked.shape[1])) < HEAD_DIM
    return jnp.where(first, stacked[:rows], stacked[rows:])

def inverse_rms(raw):
    return lax.rsqrt(head_sums(raw * raw) * (1.0 / HEAD_DIM) + EPSILON)

def rows_of(ref):
    return ref.shape[0]


def dot_cut(rows, mine, other):
    half = mine.shape[0]
    return dot(rows[:, :half], mine[...]) + dot(rows[:, half:], other[...])


def attend_kernel(
    kind_ref,
    len_ref,
    rows_ref,
    core_rows_ref,
    caption_ref,
    core_caption_ref,
    qkv_mine_ref,
    qkv_other_ref,
    key_mine_ref,
    key_other_ref,
    value_mine_ref,
    value_other_ref,
    out_weight_ref,
    gain_ref,
    cos_ref,
    sin_ref,
    rows_out_ref,
    caption_out_ref,
    qkv_ref,
    text_ref,
    text_value_ref,
    q_ref,
    k_ref,
    tk_ref,
    mixed_ref,
    read_ref,
    branch_ref,
    core_branch_ref,
):
    item = pl.program_id(0)
    own = item < pl.num_programs(0) // 2
    kind, length = kind_ref[item], len_ref[item]
    width = q_ref.shape[1]
    positions = pl.ds(kind * rows_of(q_ref), rows_of(q_ref))
    cosine, sine = cos_ref[positions, :], sin_ref[positions, :]
    scaling = HEAD_DIM ** (-0.5)

    @pl.when(own)
    def _():
        rows_out_ref[...] = rows_ref[...]
        caption_out_ref[...] = caption_ref[...]

    @pl.when(jnp.logical_not(own))
    def _():
        rows_out_ref[...] = core_rows_ref[...]
        caption_out_ref[...] = core_caption_ref[...]

    qkv_ref[...] = dot_cut(rows_out_ref, qkv_mine_ref, qkv_other_ref)
    text_ref[...] = dot_cut(caption_out_ref, key_mine_ref, key_other_ref)
    text_value_ref[...] = dot_cut(caption_out_ref, value_mine_ref, value_other_ref)
    for at in range(0, width, LANES):
        lanes = slice(at, at + LANES)
        turned = []
        for part, out_ref in ((0, q_ref), (1, k_ref)):
            raw = qkv_ref[:, part * width + at : part * width + at + LANES]
            normal = raw * inverse_rms(raw) * gain_ref[part : part + 1, lanes]
            rows = (normal * cosine + partner(normal) * sine).astype(jnp.bfloat16)
            out_ref[:, lanes] = rows
            turned.append(rows)
        queries, keys = turned
        values = qkv_ref[:, 2 * width + at : 2 * width + at + LANES].astype(jnp.bfloat16)
        text_raw = text_ref[:, lanes]
        text_keys = (text_raw * inverse_rms(text_raw) * gain_ref[2:3, lanes]).astype(jnp.bfloat16)
        tk_ref[:, lanes] = text_keys
        text_values = text_value_ref[:, lanes].astype(jnp.bfloat16)
        stacked = stack_heads(queries)
        scores = dot_right(stacked, keys) * scaling
        scores = jnp.exp(scores - jnp.max(scores, axis=-1, keepdims=True))
        own_out = dot(scores.astype(jnp.bfloat16), values) / jnp.sum(scores, axis=-1, keepdims=True)
        text = dot_right(stacked, text_keys) * scaling
        text = jnp.where(lane_index(text.shape) < length, text, -1e30)
        text = jnp.exp(text - jnp.max(text, axis=-1, keepdims=True))
        text_out = dot(text.astype(jnp.bfloat16), text_values) / jnp.sum(text, axis=-1, keepdims=True)
        read = join_heads(text_out)
        read_ref[:, lanes] = read
        mixed_ref[:, lanes] = (join_heads(own_out) + gain_ref[3:4, lanes] * read).astype(jnp.bfloat16)

    branch = dot(mixed_ref[...], out_weight_ref[...])

    @pl.when(own)
    def _():
        branch_ref[...] = branch

    @pl.when(jnp.logical_not(own))
    def _():
        core_branch_ref[...] = branch.astype(jnp.bfloat16)


def head_norm_back(grad, raw, gain_row):
    inverse = inverse_rms(raw)
    scaled = grad * gain_row
    normal = raw * inverse
    inner = head_sums(scaled * normal) * (1.0 / HEAD_DIM)
    return inverse * (scaled - normal * inner), jnp.sum(grad * normal, axis=0, keepdims=True)

def attend_back_kernel(
    kind_ref,
    len_ref,
    branch_ref,
    core_branch_ref,
    qkv_ref,
    text_ref,
    text_value_ref,
    q_ref,
    k_ref,
    tk_ref,
    read_ref,
    qkv_mine_ref,
    qkv_other_ref,
    out_weight_ref,
    gain_ref,
    cos_ref,
    sin_ref,
    branch_out_ref,
    gqkv_ref,
    gtext_ref,
    grad_rows_ref,
    core_grad_rows_ref,
    gains_ref,
    mixed_ref,
):
    item = pl.program_id(0)
    own = item < pl.num_programs(0) // 2
    kind, length = kind_ref[item], len_ref[item]
    width = q_ref.shape[1]
    positions = pl.ds(kind * rows_of(q_ref), rows_of(q_ref))
    cosine, sine = cos_ref[positions, :], sin_ref[positions, :]
    scaling = HEAD_DIM ** (-0.5)

    @pl.when(own)
    def _():
        branch_out_ref[...] = branch_ref[...]

    @pl.when(jnp.logical_not(own))
    def _():
        branch_out_ref[...] = core_branch_ref[...]

    mixed_ref[...] = dot_right(branch_out_ref[...], out_weight_ref[...])

    @pl.when(item == 0)
    def _():
        gains_ref[...] = jnp.zeros_like(gains_ref)

    def one(stacked, keys, values, stacked_grad, valid):
        scores = dot_right(keys, stacked) * scaling
        if valid is not None:
            scores = jnp.where(valid(scores.shape), scores, -1e30)
        probs = jnp.exp(scores - jnp.max(scores, axis=0, keepdims=True))
        probs = probs * (1.0 / jnp.sum(probs, axis=0, keepdims=True))
        grad_values = dot(probs.astype(jnp.bfloat16), stacked_grad)
        grad_probs = dot_right(values, stacked_grad)
        inner = jnp.sum(probs * grad_probs, axis=0, keepdims=True)
        grad_scores = (probs * (grad_probs - inner)).astype(jnp.bfloat16)
        grad_keys = dot(grad_scores, stacked) * scaling
        grad_queries = dot_left(keys, grad_scores)
        return grad_queries, grad_keys, grad_values

    for at in range(0, width, LANES):
        lanes = slice(at, at + LANES)
        grad = mixed_ref[:, lanes]
        cross = gain_ref[3:4, lanes]
        values = qkv_ref[:, 2 * width + at : 2 * width + at + LANES].astype(jnp.bfloat16)
        text_values = text_value_ref[:, lanes].astype(jnp.bfloat16)
        stacked = stack_heads(q_ref[:, lanes])
        own_queries, own_keys, own_values = one(
            stacked, k_ref[:, lanes], values, stack_heads(grad.astype(jnp.bfloat16)), None
        )
        read_queries, read_keys, read_values = one(
            stacked, tk_ref[:, lanes], text_values, stack_heads((cross * grad).astype(jnp.bfloat16)),
            lambda shape: lax.broadcasted_iota(jnp.int32, shape, 0) < length,
        )
        grad_queries = join_heads((own_queries + read_queries).T) * scaling
        for part, turned in ((0, grad_queries), (1, own_keys)):
            raw = qkv_ref[:, part * width + at : part * width + at + LANES]
            back = turned * cosine + partner(turned * sine)
            grad_raw, gain = head_norm_back(back, raw, gain_ref[part : part + 1, lanes])
            gqkv_ref[:, part * width + at : part * width + at + LANES] = grad_raw.astype(jnp.bfloat16)
            gains_ref[part : part + 1, lanes] += gain
        gqkv_ref[:, 2 * width + at : 2 * width + at + LANES] = own_values.astype(jnp.bfloat16)
        grad_text, gain = head_norm_back(read_keys, text_ref[:, lanes], gain_ref[2:3, lanes])
        gtext_ref[:, lanes] = grad_text.astype(jnp.bfloat16)
        gains_ref[2:3, lanes] += gain
        gtext_ref[:, width + at : width + at + LANES] = read_values.astype(jnp.bfloat16)
        gains_ref[3:4, lanes] += jnp.sum(grad * read_ref[:, lanes], axis=0, keepdims=True)

    half = qkv_mine_ref.shape[0]
    low = dot_right(gqkv_ref[...], qkv_mine_ref[...])
    high = dot_right(gqkv_ref[...], qkv_other_ref[...])

    @pl.when(own)
    def _():
        grad_rows_ref[:, :half] = low
        grad_rows_ref[:, half:] = high

    @pl.when(jnp.logical_not(own))
    def _():
        core_grad_rows_ref[:, :half] = low.astype(jnp.bfloat16)
        core_grad_rows_ref[:, half:] = high.astype(jnp.bfloat16)


def whole_spec(array):
    zeros = (0,) * len(array.shape)
    return pl.BlockSpec(array.shape, lambda *_: zeros, pipeline_mode=pl.Buffered(1))


def mine_spec(array, steps):
    half = steps // 2
    return pl.BlockSpec(
        (array.shape[0] // half, array.shape[1]), lambda i, *_: (jnp.minimum(i, half - 1), 0)
    )


def core_spec(array, steps):
    half = steps // 2
    return pl.BlockSpec(
        (array.shape[0] // half, array.shape[1]), lambda i, *_: (jnp.maximum(i - half, 0), 0)
    )


def pair_specs(pair_of_arrays, steps):
    return [mine_spec(pair_of_arrays[0], steps), core_spec(pair_of_arrays[1], steps)]


def step_spec(array, steps):
    return pl.BlockSpec((array.shape[0] // steps, array.shape[1]), lambda i, *_: (i, 0))


def summed_spec(array):
    return pl.BlockSpec(array.shape, lambda i, *_: (0, 0))


def shaped(count, columns, dtype=jnp.bfloat16):
    return jax.ShapeDtypeStruct((count, columns), dtype)


def parameters():
    return pltpu.CompilerParams(dimension_semantics=("arbitrary",), vmem_limit_bytes=58 * MIB)


def attend(scalars, rows, captions, qkv_rank, key_rank, value_rank, out_rank, tables):
    items = scalars[0].shape[0]
    count, width = 2 * rows[0].shape[0], out_rank.shape[0]
    text_count = 2 * captions[0].shape[0]
    outs = [
        shaped(count, D),
        shaped(text_count, TEXT_DIM),
        shaped(count, 3 * width, jnp.float32),
        shaped(text_count, width, jnp.float32),
        shaped(text_count, width, jnp.float32),
        shaped(count, width),
        shaped(count, width),
        shaped(text_count, width),
        shaped(count, width),
        shaped(count, width, jnp.float32),
    ]
    branch = (shaped(count // 2, D, jnp.float32), shaped(count // 2, D))
    whole = [*qkv_rank, *key_rank, *value_rank, out_rank, *tables]
    rows, captions, *kept, branch_mine, branch_core = pl.pallas_call(
        attend_kernel,
        grid_spec=pltpu.PrefetchScalarGridSpec(
            num_scalar_prefetch=2,
            grid=(items,),
            in_specs=pair_specs(rows, items)
            + pair_specs(captions, items)
            + [whole_spec(array) for array in whole],
            out_specs=[step_spec(array, items) for array in outs] + pair_specs(branch, items),
        ),
        out_shape=[*outs, *branch],
        compiler_params=parameters(),
        name="attend",
    )(*scalars, *rows, *captions, *whole)
    return rows, captions, kept, (branch_mine, branch_core)


def attend_back(scalars, grad_branch, kept, qkv_rank, out_rank, tables):
    items = scalars[0].shape[0]
    qkv_raw, text_raw, text_value_raw, queries, keys, text_keys, _, read = kept
    count, width = queries.shape
    outs = [
        shaped(count, D),
        shaped(count, 3 * width),
        shaped(text_raw.shape[0], 2 * width),
    ]
    rows = (shaped(count // 2, D, jnp.float32), shaped(count // 2, D))
    gains = shaped(4, width, jnp.float32)
    by_item = [qkv_raw, text_raw, text_value_raw, queries, keys, text_keys, read]
    whole = [*qkv_rank, out_rank, *tables]
    branch, qkv, text, rows_mine, rows_core, gains = pl.pallas_call(
        attend_back_kernel,
        grid_spec=pltpu.PrefetchScalarGridSpec(
            num_scalar_prefetch=2,
            grid=(items,),
            in_specs=pair_specs(grad_branch, items)
            + [step_spec(array, items) for array in by_item]
            + [whole_spec(array) for array in whole],
            out_specs=[step_spec(array, items) for array in outs]
            + pair_specs(rows, items)
            + [summed_spec(gains)],
            scratch_shapes=[pltpu.VMEM((count // items, width), jnp.float32)],
        ),
        out_shape=[*outs, *rows, gains],
        compiler_params=parameters(),
        name="attend_back",
    )(*scalars, *grad_branch, *by_item, *whole)
    return branch, qkv, text, (rows_mine, rows_core), gains


def row_cuts(lefts, rights):
    cuts, left, right, left_row, right_row = [], 0, 0, 0, 0
    while left < len(lefts):
        count = min(lefts[left].shape[0] - left_row, rights[right].shape[0] - right_row)
        cuts.append((left, left_row, right, right_row, count))
        left_row, right_row = left_row + count, right_row + count
        if left_row == lefts[left].shape[0]:
            left, left_row = left + 1, 0
        if right_row == rights[right].shape[0]:
            right, right_row = right + 1, 0
    return cuts


def product(lefts, rights, first, lanes, dtype):
    columns = rights[0].shape[1]
    if lanes % LANES:
        block = lanes
    else:
        block = 384 if lanes % 384 == 0 else math.gcd(lanes, 512)
    cuts = row_cuts(lefts, rights)

    def kernel(first_ref, *refs):
        left_refs, right_refs, out_ref = refs[: len(lefts)], refs[len(lefts) : -1], refs[-1]
        total = None
        for left, left_row, right, right_row, count in cuts:
            term = dot_left(
                left_refs[left][left_row : left_row + count, :],
                right_refs[right][right_row : right_row + count, :],
            )
            total = term if total is None else total + term
        out_ref[...] = total.astype(out_ref.dtype)

    return pl.pallas_call(
        kernel,
        grid_spec=pltpu.PrefetchScalarGridSpec(
            num_scalar_prefetch=1,
            grid=(lanes // block,),
            in_specs=[
                pl.BlockSpec((array.shape[0], block), lambda i, first: (0, first[0] // block + i))
                for array in lefts
            ]
            + [whole_spec(array) for array in rights],
            out_specs=pl.BlockSpec((block, columns), lambda i, first: (i, 0)),
        ),
        out_shape=shaped(lanes, columns, dtype),
        compiler_params=parameters(),
        name="product",
    )(jnp.reshape(first, (1,)).astype(jnp.int32), *lefts, *rights)


def feed_kernel(
    rows_ref,
    core_rows_ref,
    result_ref,
    core_result_ref,
    gate_mine_ref,
    gate_other_ref,
    up_mine_ref,
    up_other_ref,
    down_ref,
    rows,
    result,
    hidden_ref,
    grad_gate_ref,
    grad_up_ref,
    grad_ref,
    core_grad_ref,
):
    own = pl.program_id(0) < pl.num_programs(0) // 2

    @pl.when(own)
    def _():
        rows[...] = rows_ref[...]
        result[...] = result_ref[...]

    @pl.when(jnp.logical_not(own))
    def _():
        rows[...] = core_rows_ref[...]
        result[...] = core_result_ref[...]

    gate = dot_cut(rows, gate_mine_ref, gate_other_ref)
    up = dot_cut(rows, up_mine_ref, up_other_ref)
    grad_hidden = dot_right(result[...], down_ref[...])
    sigmoid = 1.0 / (1.0 + jnp.exp(-gate))
    silu = gate * sigmoid
    hidden_ref[...] = (silu * up).astype(jnp.bfloat16)
    grad_gate = (grad_hidden * up * (sigmoid + silu * (1.0 - sigmoid))).astype(jnp.bfloat16)
    grad_up = (grad_hidden * silu).astype(jnp.bfloat16)
    grad_gate_ref[...] = grad_gate
    grad_up_ref[...] = grad_up
    half = gate_mine_ref.shape[0]
    low = dot_right(grad_gate, gate_mine_ref[...]) + dot_right(grad_up, up_mine_ref[...])
    high = dot_right(grad_gate, gate_other_ref[...]) + dot_right(grad_up, up_other_ref[...])

    @pl.when(own)
    def _():
        grad_ref[:, :half] = low
        grad_ref[:, half:] = high

    @pl.when(jnp.logical_not(own))
    def _():
        core_grad_ref[:, :half] = low.astype(jnp.bfloat16)
        core_grad_ref[:, half:] = high.astype(jnp.bfloat16)


def feed(rows, grad_result, gate_rank, up_rank, down_rank):
    count, width = 2 * rows[0].shape[0], down_rank.shape[0]
    block = 256
    steps = count // block
    outs = [shaped(count, D)] * 2 + [shaped(count, width)] * 3
    grads = (shaped(count // 2, D, jnp.float32), shaped(count // 2, D))
    whole = [*gate_rank, *up_rank, down_rank]
    *outs, grad_mine, grad_core = pl.pallas_call(
        feed_kernel,
        grid=(steps,),
        in_specs=pair_specs(rows, steps)
        + pair_specs(grad_result, steps)
        + [whole_spec(array) for array in whole],
        out_specs=[step_spec(array, steps) for array in outs] + pair_specs(grads, steps),
        out_shape=[*outs, *grads],
        compiler_params=parameters(),
        name="feed",
    )(*rows, *grad_result, *whole)
    return *outs, (grad_mine, grad_core)


def result_kernel(hidden_ref, down_ref, result_ref, core_result_ref):
    own = pl.program_id(0) < pl.num_programs(0) // 2
    rows = dot(hidden_ref[...], down_ref[...])

    @pl.when(own)
    def _():
        result_ref[...] = rows

    @pl.when(jnp.logical_not(own))
    def _():
        core_result_ref[...] = rows.astype(jnp.bfloat16)


def result_part(hidden, down_rank):
    count = hidden.shape[0]
    steps = count // 256
    outs = (shaped(count // 2, D, jnp.float32), shaped(count // 2, D))
    return pl.pallas_call(
        result_kernel,
        grid=(steps,),
        in_specs=[step_spec(hidden, steps), whole_spec(down_rank)],
        out_specs=pair_specs(outs, steps),
        out_shape=outs,
        compiler_params=parameters(),
        name="result",
    )(hidden, down_rank)


def swap(block, axis, count=2, step=1):
    return lax.ppermute(block, axis, [(at, at ^ step) for at in range(count)])


def spread(block, axis, count):
    if count & (count - 1):
        return lax.all_gather(block, axis)
    block, step = block[None], 1
    while step < count:
        other = swap(block, axis, count, step)
        low = (lax.axis_index(axis) & step) == 0
        block = jnp.where(
            low, jnp.concatenate([block, other]), jnp.concatenate([other, block])
        )
        step *= 2
    return block


def fold(block, axis, count):
    if count & (count - 1):
        return lax.psum_scatter(block, axis, scatter_dimension=0)
    step = count // 2
    while step:
        half = block.shape[0] // 2
        low = (lax.axis_index(axis) & step) == 0
        lower, upper = block[:half], block[half:]
        block = jnp.where(low, lower, upper) + swap(
            jnp.where(low, upper, lower), axis, count, step
        )
        step //= 2
    return block[0]


def trade_ranks(block):
    return lax.all_to_all(block, ("mid", "core"), 0, 0, tiled=True)


def pick(stack, index):
    return lax.dynamic_index_in_dim(stack, index, 0, keepdims=False)


def pair(rows):
    return (rows, swap(rows, "core"))


def settle(partial):
    mine, core = partial
    return mine + swap(core, "core").astype(jnp.float32)


def settle_move(across):
    return swap(across, "mid")


class Layout:
    def __init__(self, hi, rep, out_rows):
        self.hi, self.rep = hi, rep
        self.aligned = (rep * out_rows) % HEAD_DIM == 0
        self.head_groups = hi if self.aligned else 1
        self.rank = lax.axis_index("mid") * 2 + lax.axis_index("core")

    def by_rank(self, weight, sections, groups):
        rows, columns = weight.shape
        width = columns // (sections * groups * RANKS)
        view = weight.reshape(rows, sections * groups, RANKS, width)
        view = jnp.transpose(view, (2, 0, 1, 3))
        return view.reshape(RANKS, rows, sections * groups * width)

    def from_ranks(self, blocks, sections, groups):
        _, rows, per_rank = blocks.shape
        width = per_rank // (sections * groups)
        view = blocks.reshape(RANKS, rows, sections * groups, width)
        return jnp.transpose(view, (1, 2, 0, 3)).reshape(rows, RANKS * per_rank)

    def ordered(self, values):
        if self.hi != 2:
            return values
        half = values.shape[-1] // 2
        turned = jnp.concatenate([values[..., half:], values[..., :half]], axis=-1)
        return jnp.where(lax.axis_index("hi") == 0, values, turned)

    def ordered_text(self, values):
        if self.hi != 2:
            return values
        view = values.reshape(values.shape[0], self.hi, RANKS, self.rep, -1)
        return self.ordered(jnp.swapaxes(view, 2, 3).reshape(values.shape))

    def text_halves(self, blocks):
        return tuple(blocks) if self.hi == 2 else self.halves(blocks)

    def text_by_rep(self, summed):
        return summed.reshape(self.rep, -1, summed.shape[1]) if self.hi == 2 else self.by_rep(summed)

    def across_hi(self, block):
        if self.hi == 2:
            return (block, swap(block, "hi"))
        return spread(block, "hi", self.hi)

    def natural_hi(self, blocks):
        if self.hi != 2:
            return blocks
        mine, other = blocks
        low = lax.axis_index("hi") == 0
        return jnp.stack([jnp.where(low, mine, other), jnp.where(low, other, mine)])

    def halves(self, blocks):
        if self.hi == 2:
            return tuple(self.natural_rows(block[None]) for block in blocks)
        return tuple(jnp.split(self.natural_rows(blocks), 2))

    def natural_rows(self, stacked):
        view = stacked.reshape(stacked.shape[0], self.rep, RANKS, -1, stacked.shape[-1])
        return jnp.transpose(view, (0, 2, 1, 3, 4)).reshape(-1, stacked.shape[-1])

    def product_moved(self, lefts, rights, first=None):
        lanes = lefts[0].shape[1]
        if self.hi != 2:
            return product(lefts, rights, 0, lanes, jnp.bfloat16)
        return product(lefts, rights, lanes // 2 if first is None else first, lanes // 2, jnp.bfloat16)

    def move(self, moved):
        if self.hi == 2:
            return swap(moved, "hi")
        return fold(moved.reshape(self.hi, -1, moved.shape[1]), "hi", self.hi)

    def product_kept(self, lefts, rights, first=0):
        if self.hi != 2:
            return None
        return product(lefts, rights, first, lefts[0].shape[1] // 2, jnp.float32)

    def total(self, kept, arrived):
        if kept is None:
            return arrived
        return (kept + arrived.astype(jnp.float32)).astype(jnp.bfloat16)

    def by_rep(self, summed):
        view = summed.reshape(RANKS, self.rep, -1, summed.shape[1])
        return jnp.transpose(view, (1, 0, 2, 3)).reshape(self.rep, -1, summed.shape[1])

    def reduce(self, blocks):
        flat = blocks.reshape(-1, blocks.shape[-1])
        return lax.psum_scatter(flat, "rep", scatter_dimension=0, tiled=True)

    def rank_lanes(self, rows, groups):
        view = rows.reshape(rows.shape[0], groups, RANKS, -1)
        return lax.dynamic_index_in_dim(view, self.rank, 2, keepdims=False).reshape(rows.shape[0], -1)

    def place_lanes(self, row):
        view = row.reshape(self.head_groups, 1, -1)
        at = (jnp.arange(RANKS) == self.rank).astype(row.dtype)[None, :, None]
        return (view * at).reshape(-1)


def fence(*values):
    return lax.optimization_barrier(values)


def local(
    hi_count,
    rep_count,
    tokens,
    condition,
    caption,
    caption_len,
    item_kind,
    out_cotangent,
    norm_gains,
    ada_weight,
    qkv_weight,
    out_weight,
    text_weight,
    gate_up_weight,
    down_weight,
):
    bf16, f32 = jnp.bfloat16, jnp.float32
    item_count = condition.shape[0]
    item_len = tokens.shape[0] // item_count
    row_count = item_count * item_len
    rows = qkv_weight.shape[0]
    plan = Layout(hi_count, rep_count, out_weight.shape[0])
    rank_width = HEADS // RANKS * HEAD_DIM
    hi_at, mid_at, core_at, rep_at = [lax.axis_index(name) for name in AXES]
    device_shape = (hi_count, 2, 2, rep_count)

    feed_width = FF // RANKS
    devices = hi_count * RANKS * rep_count
    block_at = (hi_at * RANKS + plan.rank) * rep_count + rep_at

    def z_gather(block):
        return lax.all_gather(block.reshape(-1, block.shape[-1]), "rep", tiled=True)

    down_z = z_gather(down_weight)
    qkv_mine = trade_ranks(plan.by_rank(qkv_weight, 3, plan.head_groups))
    qkv_mine = qkv_mine.reshape(RANKS * rows, 3 * rank_width)
    if plan.aligned:
        qkv_mine = jnp.concatenate([qkv_mine, out_weight.reshape(-1, 3 * rank_width)])
    else:
        out_whole = lax.all_gather(out_weight, AXES, axis=0, tiled=True)
        out_rank = pick(out_whole.reshape(RANKS, rank_width, D), plan.rank)

    head = condition.reshape(item_count, devices, rows)
    head = jnp.transpose(head, (1, 0, 2)).reshape(devices, -1)
    rest = jnp.concatenate(
        [norm_gains.reshape(-1), caption_len.astype(bf16), item_kind.astype(bf16)]
    )
    small = jnp.concatenate([head, jnp.broadcast_to(rest, (devices, rest.size))], axis=1)
    small = lax.all_to_all(small, AXES, 0, 0, tiled=True)
    cut = [head.shape[1], head.shape[1] + norm_gains.size]
    cut.append(cut[1] + item_count)
    conditions, gains, lengths, kinds = jnp.split(small, cut, axis=-1)
    activated_mine = jax.nn.silu(conditions.astype(f32)).astype(bf16).reshape(-1, rows)
    gain_rows = jnp.moveaxis(gains.astype(f32).reshape(devices, 6, -1), 1, 0).reshape(6, D)
    lengths, kinds = [
        values.reshape(device_shape + (item_count,)) for values in (lengths, kinds)
    ]

    def group_items(values):
        view = lax.dynamic_index_in_dim(pick(values, hi_at), rep_at, 2, keepdims=False)
        near, far = pick(view, mid_at), pick(view, 1 - mid_at)
        order = [core_at, 1 - core_at]
        return [
            jnp.concatenate([pick(side, at) for at in order]).astype(jnp.int32)
            for side in (near, far)
        ]

    lengths_sides = group_items(lengths)
    kinds_sides = group_items(kinds)
    cosine, sine = rope_tables(jnp.arange(2), item_len)
    signs = jnp.where(jnp.arange(HEAD_DIM) % (HEAD_DIM // 2) < HEAD_DIM // 4, -1.0, 1.0)
    cosine, sine = [
        jnp.tile(table, (1, 1, LANES // HEAD_DIM)).reshape(-1, LANES) for table in (cosine, sine * signs)
    ]
    head_gains = plan.rank_lanes(gain_rows, plan.head_groups)
    cross_gate = jnp.tanh(head_gains[5])
    head_gains = jnp.concatenate([head_gains[1:4], cross_gate[None]])
    tables = (head_gains, cosine, sine)
    scalars = list(zip(kinds_sides, lengths_sides, strict=True))

    down_z, qkv_mine, text_weight, activated_mine = fence(
        down_z, qkv_mine, text_weight, activated_mine
    )
    qkv_z = z_gather(qkv_mine)
    down_rank = plan.across_hi(down_z)
    text_mine = trade_ranks(plan.by_rank(text_weight, 2, plan.head_groups))
    captions_near = pair(plan.ordered_text(caption.reshape(-1, TEXT_DIM)))
    partial = dot(activated_mine, ada_weight).astype(bf16).reshape(devices, item_count, 4 * D)
    gate_up_mine = trade_ranks(plan.by_rank(gate_up_weight, 2, hi_count))
    modulation = jnp.sum(lax.all_to_all(partial, AXES, 0, 0, tiled=True).astype(f32), axis=0)
    text_key_mine, text_value_mine = text_mine[..., :rank_width], text_mine[..., rank_width:]
    gate_mine, up_mine = gate_up_mine[..., :feed_width], gate_up_mine[..., feed_width:]
    qkv_z, down_rank, modulation, text_key_mine, text_value_mine, gate_mine, up_mine, captions_near = fence(
        qkv_z, down_rank, modulation, text_key_mine, text_value_mine, gate_mine, up_mine, captions_near
    )

    scale_attn, gate_attn, scale_mlp, gate_mlp = jnp.split(modulation, 4, axis=1)
    text_key_z = z_gather(text_key_mine)
    captions_far = swap(captions_near[0], "mid")
    qkv_rank = plan.across_hi(qkv_z)
    down_rank = plan.natural_hi(down_rank).reshape(feed_width, D)
    token_rows = tokens.astype(f32).reshape(item_count, item_len, D)
    normed = modulate(token_rows, gain_rows[0], scale_attn)
    normed = plan.ordered(normed.astype(bf16).reshape(row_count, D))
    mlp_gate = jnp.tanh(gate_mlp)[:, None, :]
    grad_top = out_cotangent.astype(f32).reshape(item_count, item_len, D)
    grad_result = (mlp_gate * grad_top).astype(bf16).reshape(row_count, D)
    normed_near, result_near = pair(normed), pair(grad_result)
    text_key_z, captions_far, qkv_rank, down_rank, normed_near, result_near, tables, scalars = fence(
        text_key_z, captions_far, qkv_rank, down_rank, normed_near, result_near, tables, scalars
    )

    text_value_z = z_gather(text_value_mine)
    text_key_rank = plan.across_hi(text_key_z)
    normed_far = swap(normed_near[0], "mid")
    captions_far = pair(captions_far)
    text_value_z, text_key_rank, normed_far, captions_far = fence(
        text_value_z, text_key_rank, normed_far, captions_far
    )

    gate_z = z_gather(gate_mine)
    text_value_rank = plan.across_hi(text_value_z)
    result_far = swap(result_near[0], "mid")
    normed_far = pair(normed_far)
    if plan.aligned:
        blocks = [block.reshape(rep_count, -1, 3 * rank_width) for block in qkv_rank]
        out_rank = plan.natural_hi([block[:, RANKS * rows :].reshape(-1, D) for block in blocks])
        out_rank = out_rank.reshape(rank_width, D)
        qkv_rank = [block[:, : RANKS * rows].reshape(-1, 3 * rank_width) for block in blocks]
        qkv_rank = qkv_rank if hi_count == 2 else jnp.stack(qkv_rank)
    qkv_rank, text_key_rank = plan.halves(qkv_rank), plan.text_halves(text_key_rank)
    gate_z, text_value_rank, result_far, normed_far, qkv_rank, out_rank, text_key_rank = fence(
        gate_z, text_value_rank, result_far, normed_far, qkv_rank, out_rank, text_key_rank
    )

    up_z = z_gather(up_mine)
    gate_rank = plan.across_hi(gate_z)
    attend_weights = (qkv_rank, text_key_rank, plan.text_halves(text_value_rank), out_rank)
    normed_far, captions_far, kept_far, partial_far = attend(
        scalars[1], normed_far, captions_far, *attend_weights, tables
    )
    up_z, gate_rank, normed_far, captions_far, kept_far, partial_far, attend_weights = fence(
        up_z, gate_rank, normed_far, captions_far, kept_far, partial_far, attend_weights
    )

    across = settle(partial_far).astype(bf16)
    across, normed_near, up_z = fence(across, normed_near, up_z)
    up_rank = plan.across_hi(up_z)
    arrived = settle_move(across)
    normed_near, captions_near, kept_near, partial_near = attend(
        scalars[0], normed_near, captions_near, *attend_weights, tables
    )
    result_far = pair(result_far)
    gate_rank = plan.halves(gate_rank)
    up_rank, arrived, normed_near, captions_near, kept_near, partial_near, result_far, gate_rank = fence(
        up_rank, arrived, normed_near, captions_near, kept_near, partial_near, result_far, gate_rank
    )

    branch = (settle(partial_near) + arrived.astype(f32)).reshape(item_count, item_len, D)
    attn_gate = jnp.tanh(gate_attn)[:, None, :]
    middle = token_rows + attn_gate * branch
    mlp_input = modulate(middle, gain_rows[4], scale_mlp)
    mlp_input = plan.ordered(mlp_input.astype(bf16).reshape(row_count, D))
    up_rank = plan.halves(up_rank)
    mlp_input, up_rank = fence(mlp_input, up_rank)

    feed_weights = (gate_rank, up_rank, down_rank)
    input_far = swap(mlp_input, "mid")
    input_near, result_near, hidden_near, gate_near, up_near, partial_near = feed(
        pair(mlp_input), result_near, *feed_weights
    )
    input_far, input_near, result_near, hidden_near, gate_near, up_near, partial_near = fence(
        input_far, input_near, result_near, hidden_near, gate_near, up_near, partial_near
    )
    input_far, result_far, hidden_far, gate_far, up_far, partial_far = feed(
        pair(input_far), result_far, *feed_weights
    )
    inputs, results = (input_near, input_far), (result_near, result_far)
    gate_rows, up_rows, hidden_rows = (gate_near, gate_far), (up_near, up_far), (hidden_near, hidden_far)
    across = settle(partial_far).astype(bf16)
    gate_moved = plan.product_moved(inputs, gate_rows)
    across, gate_moved, gate_rows, up_rows, hidden_rows = fence(
        across, gate_moved, gate_rows, up_rows, hidden_rows
    )
    arrived = settle_move(across)
    gate_moved = plan.move(gate_moved)
    up_moved = plan.product_moved(inputs, up_rows)
    hidden_first = hi_at * (feed_width // 2)
    down_moved = plan.product_moved(hidden_rows, results, feed_width // 2 - hidden_first)
    gate_kept = plan.product_kept(inputs, gate_rows)
    up_kept = plan.product_kept(inputs, up_rows)
    down_kept = plan.product_kept(hidden_rows, results, hidden_first)
    near = settle(partial_near)
    arrived, gate_moved, up_moved, down_moved, gate_kept, up_kept, down_kept, near = fence(
        arrived, gate_moved, up_moved, down_moved, gate_kept, up_kept, down_kept, near
    )

    up_moved = plan.move(up_moved)
    gate_grad = plan.by_rep(plan.total(gate_kept, gate_moved))
    gate_parts = plan.reduce(gate_grad)
    grad_mlp_input = plan.ordered(near + arrived.astype(f32))
    _, pull_mlp_norm = jax.vjp(modulate, middle, gain_rows[4], scale_mlp)
    grad_middle_norm, grad_mlp_gain, grad_scale_mlp = pull_mlp_norm(
        grad_mlp_input.reshape(item_count, item_len, D)
    )
    grad_middle = grad_top + grad_middle_norm
    grad_attn_gate = jnp.sum(grad_middle * branch, axis=1) * (1.0 - jnp.tanh(gate_attn) ** 2)
    grad_branch = (attn_gate * grad_middle).astype(bf16).reshape(row_count, D)
    (grad_branch,) = fence(grad_branch)

    branch_far = swap(grad_branch, "mid")
    back_weights = (qkv_rank, out_rank, tables)
    branch_near, qkv_near, text_near, rows_near, gain_near = attend_back(
        scalars[0], pair(grad_branch), kept_near, *back_weights
    )
    branch_far, up_moved, gate_parts, branch_near, qkv_near, text_near, rows_near, gain_near = fence(
        branch_far, up_moved, gate_parts, branch_near, qkv_near, text_near, rows_near, gain_near
    )

    up_grad = plan.by_rep(plan.total(up_kept, up_moved))
    up_grad, branch_far, down_moved = fence(up_grad, pair(branch_far), down_moved)
    up_parts = plan.reduce(up_grad)
    down_moved = plan.move(down_moved)
    branch_far, qkv_far, text_far, rows_far, gain_far = attend_back(
        scalars[1], branch_far, kept_far, *back_weights
    )
    captions, normed_rows = (captions_near, captions_far), (normed_near, normed_far)
    text_rows, qkv_rows, branches = (text_near, text_far), (qkv_near, qkv_far), (branch_near, branch_far)
    text_moved = plan.product_moved(captions, text_rows)
    down_grad = plan.total(down_kept, down_moved).reshape(rep_count, -1, D)
    across = settle(rows_far).astype(bf16)
    down_grad, up_parts, across, text_rows, qkv_rows, branches, gain_far, text_moved, hidden_rows = fence(
        down_grad, up_parts, across, text_rows, qkv_rows, branches, gain_far, text_moved, hidden_rows
    )

    text_moved = plan.move(text_moved)
    down_parts = plan.reduce(down_grad)
    arrived = settle_move(across)
    result_far = result_part(hidden_rows[1], down_rank)
    result_arrived = settle_move(settle(result_far).astype(bf16))
    result_near = result_part(hidden_rows[0], down_rank)
    qkv_moved = plan.product_moved(normed_rows, qkv_rows)
    text_kept = plan.product_kept(captions, text_rows)
    qkv_kept = plan.product_kept(normed_rows, qkv_rows)
    mixed_rows = [plan.ordered(kept[6]) for kept in (kept_near, kept_far)]
    if plan.aligned:
        halves = [slice(0, rank_width // 2), slice(rank_width // 2, None)]
        out_kept, out_moved = [
            product([side[:, lanes] for side in mixed_rows], branches, 0, rank_width // 2, bf16)
            for lanes in halves
        ]
    else:
        out_kept, out_moved = (), ()
    (
        text_moved,
        down_parts,
        arrived,
        result_arrived,
        result_near,
        qkv_moved,
        text_kept,
        qkv_kept,
        out_kept,
        out_moved,
    ) = fence(
        text_moved,
        down_parts,
        arrived,
        result_arrived,
        result_near,
        qkv_moved,
        text_kept,
        qkv_kept,
        out_kept,
        out_moved,
    )

    qkv_moved = plan.move(qkv_moved)
    if plan.aligned:
        if hi_count == 2:
            out_moved = swap(out_moved, "hi")
        else:
            out_moved = plan.move(jnp.concatenate([out_kept, out_moved]))
    text_grad = plan.text_by_rep(plan.total(text_kept, text_moved))
    text_parts = plan.reduce(text_grad)
    grad_normed = plan.ordered(settle(rows_near) + arrived.astype(f32))
    _, pull_attn_norm = jax.vjp(modulate, token_rows, gain_rows[0], scale_attn)
    grad_token_norm, grad_attn_gain, grad_scale_attn = pull_attn_norm(
        grad_normed.reshape(item_count, item_len, D)
    )
    result = (settle(result_near) + result_arrived.astype(f32)).reshape(item_count, item_len, D)
    grad_mlp_gate = jnp.sum(grad_top * result, axis=1) * (1.0 - jnp.tanh(gate_mlp) ** 2)
    text_parts, qkv_moved, out_moved, grad_mlp_gate, grad_scale_attn, grad_attn_gain = fence(
        text_parts, qkv_moved, out_moved, grad_mlp_gate, grad_scale_attn, grad_attn_gain
    )

    qkv_grad = plan.by_rep(plan.total(qkv_kept, qkv_moved))
    if plan.aligned:
        out_grad = plan.total(out_kept.astype(f32), out_moved) if hi_count == 2 else out_moved
        out_grad = out_grad.reshape(rep_count, -1, D)
    else:
        at = (jnp.arange(RANKS) == plan.rank).astype(bf16)[:, None, None]
        out_grad = product(mixed_rows, branches, 0, rank_width, bf16)
        out_grad = (out_grad[None] * at).reshape(D, D)
    qkv_grad, out_grad, grad_mlp_gate, text_parts = fence(
        qkv_grad, out_grad, grad_mlp_gate, text_parts
    )
    qkv_parts = plan.reduce(qkv_grad)
    if plan.aligned:
        out_parts = plan.reduce(out_grad)
    else:
        out_parts = lax.psum_scatter(out_grad, AXES, scatter_dimension=0, tiled=True)
    layer_out = (middle + mlp_gate * result).astype(bf16).reshape(row_count, D)
    tokens_grad = (grad_middle + grad_token_norm).reshape(row_count, D)

    grad_modulation = jnp.concatenate(
        [grad_scale_attn, grad_attn_gate, grad_scale_mlp, grad_mlp_gate], axis=1
    ).astype(bf16)
    gain_terms = gain_near + gain_far
    gain_terms = gain_terms.at[3].multiply(1.0 - cross_gate**2)
    gain_terms = [plan.place_lanes(row) for row in gain_terms]
    gains_grad = jnp.stack(
        [grad_attn_gain, gain_terms[0], gain_terms[1], gain_terms[2], grad_mlp_gain, gain_terms[3]]
    ).astype(bf16)
    gain_blocks = jnp.moveaxis(gains_grad.reshape(6, devices, -1), 1, 0)
    gain_blocks = gain_blocks.reshape(devices, item_count, -1)
    modulations = jnp.broadcast_to(grad_modulation, (devices,) + grad_modulation.shape)
    both = lax.all_to_all(
        jnp.concatenate([modulations, gain_blocks], axis=2), AXES, 0, 0, tiled=True
    )
    ada_weight_grad = lax.dot_general(
        activated_mine.reshape(devices, item_count, rows),
        both[:, :, : 4 * D],
        (((0, 1), (0, 1)), ((), ())),
        preferred_element_type=f32,
    )
    norm_gains_grad = jnp.sum(both[:, :, 4 * D :].astype(f32), axis=0).reshape(6, -1)

    def whole(parts, weight, sections, groups):
        blocks = trade_ranks(parts.reshape(RANKS, weight.shape[0], -1))
        return plan.from_ranks(blocks, sections, groups).astype(f32)

    gate_up_weight_grad = whole(
        jnp.concatenate([gate_parts, up_parts], axis=-1), gate_up_weight, 2, hi_count
    )
    text_weight_grad = whole(text_parts, text_weight, 2, plan.head_groups)
    qkv_weight_grad = whole(qkv_parts, qkv_weight, 3, plan.head_groups)
    down_weight_grad, out_weight_grad = down_parts.astype(f32), out_parts.astype(f32)
    return (
        layer_out,
        tokens_grad,
        norm_gains_grad,
        ada_weight_grad,
        qkv_weight_grad,
        out_weight_grad,
        text_weight_grad,
        gate_up_weight_grad,
        down_weight_grad,
    )


def solution(mesh):
    grp, rep = mesh.devices.shape
    hi = grp // RANKS
    inner = Mesh(mesh.devices.reshape(hi, 2, 2, rep), AXES)
    rows = P(AXES, None)

    def step(*arrays):
        return local(hi, rep, *arrays)

    return jax.shard_map(
        step,
        mesh=inner,
        in_specs=(
            rows,
            rows,
            P(AXES, None, None),
            P(AXES),
            P(AXES),
            rows,
            P(None, AXES),
            rows,
            rows,
            rows,
            rows,
            rows,
            rows,
        ),
        out_specs=(rows, rows, P(None, AXES), rows, rows, rows, rows, rows, rows),
        check_vma=False,
    )
```

```python
import math

import jax
import jax.numpy as jnp
from jax import lax
from jax.experimental import pallas as pl
from jax.experimental.pallas import tpu as pltpu
from jax.sharding import Mesh
from jax.sharding import PartitionSpec as P

D = 1536
HEADS = 24
HEAD_DIM = 64
TEXT_DIM = 4096
FF = 4096
SIDE = 16
RANKS = 4
LANES = 128
MIB = 1 << 20
AXES = ("hi", "mid", "core", "rep")


EPSILON = 1e-06


def norm_rows(values, gain_row):
    return (
        values * lax.rsqrt(jnp.mean(values * values, axis=-1, keepdims=True) + EPSILON) * gain_row
    )


def rope_tables(item_kind, item_len):
    position = jnp.arange(item_len, dtype=jnp.int32)[None, :]
    half_side = SIDE // 2
    frame_index = position // (half_side * half_side)
    within = position % (half_side * half_side)
    is_clip = item_kind[:, None] == 1
    row_index = jnp.where(is_clip, frame_index * half_side + within // half_side, position // SIDE)
    columns = jnp.where(is_clip, within % half_side, position % SIDE)
    lane_index = jnp.arange(HEAD_DIM, dtype=jnp.int32)
    quarter = HEAD_DIM // 4
    frequency = jnp.exp(-(lane_index % quarter).astype(jnp.float32) * (math.log(10000.0) / quarter))
    coordinate = jnp.where(
        lane_index[None, None, :] < 2 * quarter, row_index[:, :, None], columns[:, :, None]
    ).astype(jnp.float32)
    angles = coordinate * frequency
    return (jnp.cos(angles), jnp.sin(angles))


def modulate(values, gain_row, scaling):
    return norm_rows(values, gain_row) * (1.0 + scaling[:, None, :])


def silu_product(gate_half, up_half):
    return jax.nn.silu(gate_half) * up_half


def dot(left, right):
    return jnp.dot(left, right, preferred_element_type=jnp.float32)


def dot_left(left, right):
    return lax.dot_general(left, right, (((0,), (0,)), ((), ())), preferred_element_type=jnp.float32)


def dot_right(left, right):
    return lax.dot_general(left, right, (((1,), (1,)), ((), ())), preferred_element_type=jnp.float32)


def lane_index(shape):
    return lax.broadcasted_iota(jnp.int32, shape, len(shape) - 1)

def head_sums(values):
    first = lane_index(values.shape) < HEAD_DIM
    low = jnp.sum(jnp.where(first, values, 0.0), axis=-1, keepdims=True)
    high = jnp.sum(jnp.where(first, 0.0, values), axis=-1, keepdims=True)
    return jnp.where(first, low, high)

def partner(values):
    quarter = HEAD_DIM // 4
    width = values.shape[-1]
    low = lane_index(values.shape) % (2 * quarter) < quarter
    return jnp.where(low, pltpu.roll(values, width - quarter, 1), pltpu.roll(values, quarter, 1))

def stack_heads(values):
    first = lane_index(values.shape) < HEAD_DIM
    zero = jnp.zeros_like(values)
    return jnp.concatenate([jnp.where(first, values, zero), jnp.where(first, zero, values)])

def join_heads(stacked):
    rows = stacked.shape[0] // 2
    first = lane_index((rows, stacked.shape[1])) < HEAD_DIM
    return jnp.where(first, stacked[:rows], stacked[rows:])

def inverse_rms(raw):
    return lax.rsqrt(head_sums(raw * raw) * (1.0 / HEAD_DIM) + EPSILON)

def rows_of(ref):
    return ref.shape[0]


def dot_cut(rows, mine, other):
    half = mine.shape[0]
    return dot(rows[:, :half], mine[...]) + dot(rows[:, half:], other[...])


def attend_kernel(
    kind_ref,
    len_ref,
    rows_ref,
    core_rows_ref,
    caption_ref,
    core_caption_ref,
    qkv_mine_ref,
    qkv_other_ref,
    key_mine_ref,
    key_other_ref,
    value_mine_ref,
    value_other_ref,
    out_weight_ref,
    gain_ref,
    cos_ref,
    sin_ref,
    rows_out_ref,
    caption_out_ref,
    qkv_ref,
    text_ref,
    text_value_ref,
    q_ref,
    k_ref,
    tk_ref,
    mixed_ref,
    read_ref,
    branch_ref,
    core_branch_ref,
):
    item = pl.program_id(0)
    own = item < pl.num_programs(0) // 2
    kind, length = kind_ref[item], len_ref[item]
    width = q_ref.shape[1]
    positions = pl.ds(kind * rows_of(q_ref), rows_of(q_ref))
    cosine, sine = cos_ref[positions, :], sin_ref[positions, :]
    scaling = HEAD_DIM ** (-0.5)

    @pl.when(own)
    def _():
        rows_out_ref[...] = rows_ref[...]
        caption_out_ref[...] = caption_ref[...]

    @pl.when(jnp.logical_not(own))
    def _():
        rows_out_ref[...] = core_rows_ref[...]
        caption_out_ref[...] = core_caption_ref[...]

    qkv_ref[...] = dot_cut(rows_out_ref, qkv_mine_ref, qkv_other_ref)
    text_ref[...] = dot_cut(caption_out_ref, key_mine_ref, key_other_ref)
    text_value_ref[...] = dot_cut(caption_out_ref, value_mine_ref, value_other_ref)
    for at in range(0, width, LANES):
        lanes = slice(at, at + LANES)
        turned = []
        for part, out_ref in ((0, q_ref), (1, k_ref)):
            raw = qkv_ref[:, part * width + at : part * width + at + LANES]
            normal = raw * inverse_rms(raw) * gain_ref[part : part + 1, lanes]
            rows = (normal * cosine + partner(normal) * sine).astype(jnp.bfloat16)
            out_ref[:, lanes] = rows
            turned.append(rows)
        queries, keys = turned
        values = qkv_ref[:, 2 * width + at : 2 * width + at + LANES].astype(jnp.bfloat16)
        text_raw = text_ref[:, lanes]
        text_keys = (text_raw * inverse_rms(text_raw) * gain_ref[2:3, lanes]).astype(jnp.bfloat16)
        tk_ref[:, lanes] = text_keys
        text_values = text_value_ref[:, lanes].astype(jnp.bfloat16)
        stacked = stack_heads(queries)
        scores = dot_right(stacked, keys) * scaling
        scores = jnp.exp(scores - jnp.max(scores, axis=-1, keepdims=True))
        own_out = dot(scores.astype(jnp.bfloat16), values) / jnp.sum(scores, axis=-1, keepdims=True)
        text = dot_right(stacked, text_keys) * scaling
        text = jnp.where(lane_index(text.shape) < length, text, -1e30)
        text = jnp.exp(text - jnp.max(text, axis=-1, keepdims=True))
        text_out = dot(text.astype(jnp.bfloat16), text_values) / jnp.sum(text, axis=-1, keepdims=True)
        read = join_heads(text_out)
        read_ref[:, lanes] = read
        mixed_ref[:, lanes] = (join_heads(own_out) + gain_ref[3:4, lanes] * read).astype(jnp.bfloat16)

    branch = dot(mixed_ref[...], out_weight_ref[...])

    @pl.when(own)
    def _():
        branch_ref[...] = branch

    @pl.when(jnp.logical_not(own))
    def _():
        core_branch_ref[...] = branch.astype(jnp.bfloat16)


def head_norm_back(grad, raw, gain_row):
    inverse = inverse_rms(raw)
    scaled = grad * gain_row
    normal = raw * inverse
    inner = head_sums(scaled * normal) * (1.0 / HEAD_DIM)
    return inverse * (scaled - normal * inner), jnp.sum(grad * normal, axis=0, keepdims=True)

def attend_back_kernel(
    kind_ref,
    len_ref,
    branch_ref,
    core_branch_ref,
    qkv_ref,
    text_ref,
    text_value_ref,
    q_ref,
    k_ref,
    tk_ref,
    read_ref,
    qkv_mine_ref,
    qkv_other_ref,
    out_weight_ref,
    gain_ref,
    cos_ref,
    sin_ref,
    branch_out_ref,
    gqkv_ref,
    gtext_ref,
    grad_rows_ref,
    core_grad_rows_ref,
    gains_ref,
    mixed_ref,
):
    item = pl.program_id(0)
    own = item < pl.num_programs(0) // 2
    kind, length = kind_ref[item], len_ref[item]
    width = q_ref.shape[1]
    positions = pl.ds(kind * rows_of(q_ref), rows_of(q_ref))
    cosine, sine = cos_ref[positions, :], sin_ref[positions, :]
    scaling = HEAD_DIM ** (-0.5)

    @pl.when(own)
    def _():
        branch_out_ref[...] = branch_ref[...]

    @pl.when(jnp.logical_not(own))
    def _():
        branch_out_ref[...] = core_branch_ref[...]

    mixed_ref[...] = dot_right(branch_out_ref[...], out_weight_ref[...])

    @pl.when(item == 0)
    def _():
        gains_ref[...] = jnp.zeros_like(gains_ref)

    def one(stacked, keys, values, stacked_grad, valid):
        scores = dot_right(keys, stacked) * scaling
        if valid is not None:
            scores = jnp.where(valid(scores.shape), scores, -1e30)
        probs = jnp.exp(scores - jnp.max(scores, axis=0, keepdims=True))
        probs = probs * (1.0 / jnp.sum(probs, axis=0, keepdims=True))
        grad_values = dot(probs.astype(jnp.bfloat16), stacked_grad)
        grad_probs = dot_right(values, stacked_grad)
        inner = jnp.sum(probs * grad_probs, axis=0, keepdims=True)
        grad_scores = (probs * (grad_probs - inner)).astype(jnp.bfloat16)
        grad_keys = dot(grad_scores, stacked) * scaling
        grad_queries = dot_left(keys, grad_scores)
        return grad_queries, grad_keys, grad_values

    for at in range(0, width, LANES):
        lanes = slice(at, at + LANES)
        grad = mixed_ref[:, lanes]
        cross = gain_ref[3:4, lanes]
        values = qkv_ref[:, 2 * width + at : 2 * width + at + LANES].astype(jnp.bfloat16)
        text_values = text_value_ref[:, lanes].astype(jnp.bfloat16)
        stacked = stack_heads(q_ref[:, lanes])
        own_queries, own_keys, own_values = one(
            stacked, k_ref[:, lanes], values, stack_heads(grad.astype(jnp.bfloat16)), None
        )
        read_queries, read_keys, read_values = one(
            stacked, tk_ref[:, lanes], text_values, stack_heads((cross * grad).astype(jnp.bfloat16)),
            lambda shape: lax.broadcasted_iota(jnp.int32, shape, 0) < length,
        )
        grad_queries = join_heads((own_queries + read_queries).T) * scaling
        for part, turned in ((0, grad_queries), (1, own_keys)):
            raw = qkv_ref[:, part * width + at : part * width + at + LANES]
            back = turned * cosine + partner(turned * sine)
            grad_raw, gain = head_norm_back(back, raw, gain_ref[part : part + 1, lanes])
            gqkv_ref[:, part * width + at : part * width + at + LANES] = grad_raw.astype(jnp.bfloat16)
            gains_ref[part : part + 1, lanes] += gain
        gqkv_ref[:, 2 * width + at : 2 * width + at + LANES] = own_values.astype(jnp.bfloat16)
        grad_text, gain = head_norm_back(read_keys, text_ref[:, lanes], gain_ref[2:3, lanes])
        gtext_ref[:, lanes] = grad_text.astype(jnp.bfloat16)
        gains_ref[2:3, lanes] += gain
        gtext_ref[:, width + at : width + at + LANES] = read_values.astype(jnp.bfloat16)
        gains_ref[3:4, lanes] += jnp.sum(grad * read_ref[:, lanes], axis=0, keepdims=True)

    half = qkv_mine_ref.shape[0]
    low = dot_right(gqkv_ref[...], qkv_mine_ref[...])
    high = dot_right(gqkv_ref[...], qkv_other_ref[...])

    @pl.when(own)
    def _():
        grad_rows_ref[:, :half] = low
        grad_rows_ref[:, half:] = high

    @pl.when(jnp.logical_not(own))
    def _():
        core_grad_rows_ref[:, :half] = low.astype(jnp.bfloat16)
        core_grad_rows_ref[:, half:] = high.astype(jnp.bfloat16)


def whole_spec(array):
    zeros = (0,) * len(array.shape)
    return pl.BlockSpec(array.shape, lambda *_: zeros, pipeline_mode=pl.Buffered(1))


def mine_spec(array, steps):
    half = steps // 2
    return pl.BlockSpec(
        (array.shape[0] // half, array.shape[1]), lambda i, *_: (jnp.minimum(i, half - 1), 0)
    )


def core_spec(array, steps):
    half = steps // 2
    return pl.BlockSpec(
        (array.shape[0] // half, array.shape[1]), lambda i, *_: (jnp.maximum(i - half, 0), 0)
    )


def pair_specs(pair_of_arrays, steps):
    return [mine_spec(pair_of_arrays[0], steps), core_spec(pair_of_arrays[1], steps)]


def step_spec(array, steps):
    return pl.BlockSpec((array.shape[0] // steps, array.shape[1]), lambda i, *_: (i, 0))


def summed_spec(array):
    return pl.BlockSpec(array.shape, lambda i, *_: (0, 0))


def shaped(count, columns, dtype=jnp.bfloat16):
    return jax.ShapeDtypeStruct((count, columns), dtype)


def parameters():
    return pltpu.CompilerParams(dimension_semantics=("arbitrary",), vmem_limit_bytes=58 * MIB)


def attend(scalars, rows, captions, qkv_rank, key_rank, value_rank, out_rank, tables):
    items = scalars[0].shape[0]
    count, width = 2 * rows[0].shape[0], out_rank.shape[0]
    text_count = 2 * captions[0].shape[0]
    outs = [
        shaped(count, D),
        shaped(text_count, TEXT_DIM),
        shaped(count, 3 * width, jnp.float32),
        shaped(text_count, width, jnp.float32),
        shaped(text_count, width, jnp.float32),
        shaped(count, width),
        shaped(count, width),
        shaped(text_count, width),
        shaped(count, width),
        shaped(count, width, jnp.float32),
    ]
    branch = (shaped(count // 2, D, jnp.float32), shaped(count // 2, D))
    whole = [*qkv_rank, *key_rank, *value_rank, out_rank, *tables]
    rows, captions, *kept, branch_mine, branch_core = pl.pallas_call(
        attend_kernel,
        grid_spec=pltpu.PrefetchScalarGridSpec(
            num_scalar_prefetch=2,
            grid=(items,),
            in_specs=pair_specs(rows, items)
            + pair_specs(captions, items)
            + [whole_spec(array) for array in whole],
            out_specs=[step_spec(array, items) for array in outs] + pair_specs(branch, items),
        ),
        out_shape=[*outs, *branch],
        compiler_params=parameters(),
        name="attend",
    )(*scalars, *rows, *captions, *whole)
    return rows, captions, kept, (branch_mine, branch_core)


def attend_back(scalars, grad_branch, kept, qkv_rank, out_rank, tables):
    items = scalars[0].shape[0]
    qkv_raw, text_raw, text_value_raw, queries, keys, text_keys, _, read = kept
    count, width = queries.shape
    outs = [
        shaped(count, D),
        shaped(count, 3 * width),
        shaped(text_raw.shape[0], 2 * width),
    ]
    rows = (shaped(count // 2, D, jnp.float32), shaped(count // 2, D))
    gains = shaped(4, width, jnp.float32)
    by_item = [qkv_raw, text_raw, text_value_raw, queries, keys, text_keys, read]
    whole = [*qkv_rank, out_rank, *tables]
    branch, qkv, text, rows_mine, rows_core, gains = pl.pallas_call(
        attend_back_kernel,
        grid_spec=pltpu.PrefetchScalarGridSpec(
            num_scalar_prefetch=2,
            grid=(items,),
            in_specs=pair_specs(grad_branch, items)
            + [step_spec(array, items) for array in by_item]
            + [whole_spec(array) for array in whole],
            out_specs=[step_spec(array, items) for array in outs]
            + pair_specs(rows, items)
            + [summed_spec(gains)],
            scratch_shapes=[pltpu.VMEM((count // items, width), jnp.float32)],
        ),
        out_shape=[*outs, *rows, gains],
        compiler_params=parameters(),
        name="attend_back",
    )(*scalars, *grad_branch, *by_item, *whole)
    return branch, qkv, text, (rows_mine, rows_core), gains


def row_cuts(lefts, rights):
    cuts, left, right, left_row, right_row = [], 0, 0, 0, 0
    while left < len(lefts):
        count = min(lefts[left].shape[0] - left_row, rights[right].shape[0] - right_row)
        cuts.append((left, left_row, right, right_row, count))
        left_row, right_row = left_row + count, right_row + count
        if left_row == lefts[left].shape[0]:
            left, left_row = left + 1, 0
        if right_row == rights[right].shape[0]:
            right, right_row = right + 1, 0
    return cuts


def product(lefts, rights, first, lanes, dtype):
    columns = rights[0].shape[1]
    if lanes % LANES:
        block = lanes
    else:
        block = 384 if lanes % 384 == 0 else math.gcd(lanes, 512)
    cuts = row_cuts(lefts, rights)

    def kernel(first_ref, *refs):
        left_refs, right_refs, out_ref = refs[: len(lefts)], refs[len(lefts) : -1], refs[-1]
        total = None
        for left, left_row, right, right_row, count in cuts:
            term = dot_left(
                left_refs[left][left_row : left_row + count, :],
                right_refs[right][right_row : right_row + count, :],
            )
            total = term if total is None else total + term
        out_ref[...] = total.astype(out_ref.dtype)

    return pl.pallas_call(
        kernel,
        grid_spec=pltpu.PrefetchScalarGridSpec(
            num_scalar_prefetch=1,
            grid=(lanes // block,),
            in_specs=[
                pl.BlockSpec((array.shape[0], block), lambda i, first: (0, first[0] // block + i))
                for array in lefts
            ]
            + [whole_spec(array) for array in rights],
            out_specs=pl.BlockSpec((block, columns), lambda i, first: (i, 0)),
        ),
        out_shape=shaped(lanes, columns, dtype),
        compiler_params=parameters(),
        name="product",
    )(jnp.reshape(first, (1,)).astype(jnp.int32), *lefts, *rights)


def feed_kernel(
    rows_ref,
    core_rows_ref,
    result_ref,
    core_result_ref,
    gate_mine_ref,
    gate_other_ref,
    up_mine_ref,
    up_other_ref,
    down_ref,
    rows,
    result,
    hidden_ref,
    grad_gate_ref,
    grad_up_ref,
    grad_ref,
    core_grad_ref,
):
    own = pl.program_id(0) < pl.num_programs(0) // 2

    @pl.when(own)
    def _():
        rows[...] = rows_ref[...]
        result[...] = result_ref[...]

    @pl.when(jnp.logical_not(own))
    def _():
        rows[...] = core_rows_ref[...]
        result[...] = core_result_ref[...]

    gate = dot_cut(rows, gate_mine_ref, gate_other_ref)
    up = dot_cut(rows, up_mine_ref, up_other_ref)
    grad_hidden = dot_right(result[...], down_ref[...])
    sigmoid = 1.0 / (1.0 + jnp.exp(-gate))
    silu = gate * sigmoid
    hidden_ref[...] = (silu * up).astype(jnp.bfloat16)
    grad_gate = (grad_hidden * up * (sigmoid + silu * (1.0 - sigmoid))).astype(jnp.bfloat16)
    grad_up = (grad_hidden * silu).astype(jnp.bfloat16)
    grad_gate_ref[...] = grad_gate
    grad_up_ref[...] = grad_up
    half = gate_mine_ref.shape[0]
    low = dot_right(grad_gate, gate_mine_ref[...]) + dot_right(grad_up, up_mine_ref[...])
    high = dot_right(grad_gate, gate_other_ref[...]) + dot_right(grad_up, up_other_ref[...])

    @pl.when(own)
    def _():
        grad_ref[:, :half] = low
        grad_ref[:, half:] = high

    @pl.when(jnp.logical_not(own))
    def _():
        core_grad_ref[:, :half] = low.astype(jnp.bfloat16)
        core_grad_ref[:, half:] = high.astype(jnp.bfloat16)


def feed(rows, grad_result, gate_rank, up_rank, down_rank):
    count, width = 2 * rows[0].shape[0], down_rank.shape[0]
    block = 256
    steps = count // block
    outs = [shaped(count, D)] * 2 + [shaped(count, width)] * 3
    grads = (shaped(count // 2, D, jnp.float32), shaped(count // 2, D))
    whole = [*gate_rank, *up_rank, down_rank]
    *outs, grad_mine, grad_core = pl.pallas_call(
        feed_kernel,
        grid=(steps,),
        in_specs=pair_specs(rows, steps)
        + pair_specs(grad_result, steps)
        + [whole_spec(array) for array in whole],
        out_specs=[step_spec(array, steps) for array in outs] + pair_specs(grads, steps),
        out_shape=[*outs, *grads],
        compiler_params=parameters(),
        name="feed",
    )(*rows, *grad_result, *whole)
    return *outs, (grad_mine, grad_core)


def result_kernel(hidden_ref, down_ref, result_ref, core_result_ref):
    own = pl.program_id(0) < pl.num_programs(0) // 2
    rows = dot(hidden_ref[...], down_ref[...])

    @pl.when(own)
    def _():
        result_ref[...] = rows

    @pl.when(jnp.logical_not(own))
    def _():
        core_result_ref[...] = rows.astype(jnp.bfloat16)


def result_part(hidden, down_rank):
    count = hidden.shape[0]
    steps = count // 256
    outs = (shaped(count // 2, D, jnp.float32), shaped(count // 2, D))
    return pl.pallas_call(
        result_kernel,
        grid=(steps,),
        in_specs=[step_spec(hidden, steps), whole_spec(down_rank)],
        out_specs=pair_specs(outs, steps),
        out_shape=outs,
        compiler_params=parameters(),
        name="result",
    )(hidden, down_rank)


def swap(block, axis, count=2, step=1):
    return lax.ppermute(block, axis, [(at, at ^ step) for at in range(count)])


def spread(block, axis, count):
    if count & (count - 1):
        return lax.all_gather(block, axis)
    block, step = block[None], 1
    while step < count:
        other = swap(block, axis, count, step)
        low = (lax.axis_index(axis) & step) == 0
        block = jnp.where(
            low, jnp.concatenate([block, other]), jnp.concatenate([other, block])
        )
        step *= 2
    return block


def fold(block, axis, count):
    if count & (count - 1):
        return lax.psum_scatter(block, axis, scatter_dimension=0)
    step = count // 2
    while step:
        half = block.shape[0] // 2
        low = (lax.axis_index(axis) & step) == 0
        lower, upper = block[:half], block[half:]
        block = jnp.where(low, lower, upper) + swap(
            jnp.where(low, upper, lower), axis, count, step
        )
        step //= 2
    return block[0]


def trade_ranks(block):
    return lax.all_to_all(block, ("mid", "core"), 0, 0, tiled=True)


def pick(stack, index):
    return lax.dynamic_index_in_dim(stack, index, 0, keepdims=False)


def pair(rows):
    return (rows, swap(rows, "core"))


def settle(partial):
    mine, core = partial
    return mine + swap(core, "core").astype(jnp.float32)


def settle_move(across):
    return swap(across, "mid")


class Layout:
    def __init__(self, hi, rep, out_rows):
        self.hi, self.rep = hi, rep
        self.aligned = (rep * out_rows) % HEAD_DIM == 0
        self.head_groups = hi if self.aligned else 1
        self.rank = lax.axis_index("mid") * 2 + lax.axis_index("core")

    def by_rank(self, weight, sections, groups):
        rows, columns = weight.shape
        width = columns // (sections * groups * RANKS)
        view = weight.reshape(rows, sections * groups, RANKS, width)
        view = jnp.transpose(view, (2, 0, 1, 3))
        return view.reshape(RANKS, rows, sections * groups * width)

    def from_ranks(self, blocks, sections, groups):
        _, rows, per_rank = blocks.shape
        width = per_rank // (sections * groups)
        view = blocks.reshape(RANKS, rows, sections * groups, width)
        return jnp.transpose(view, (1, 2, 0, 3)).reshape(rows, RANKS * per_rank)

    def ordered(self, values):
        if self.hi != 2:
            return values
        half = values.shape[-1] // 2
        turned = jnp.concatenate([values[..., half:], values[..., :half]], axis=-1)
        return jnp.where(lax.axis_index("hi") == 0, values, turned)

    def ordered_text(self, values):
        if self.hi != 2:
            return values
        view = values.reshape(values.shape[0], self.hi, RANKS, self.rep, -1)
        return self.ordered(jnp.swapaxes(view, 2, 3).reshape(values.shape))

    def text_halves(self, blocks):
        return tuple(blocks) if self.hi == 2 else self.halves(blocks)

    def text_by_rep(self, summed):
        return summed.reshape(self.rep, -1, summed.shape[1]) if self.hi == 2 else self.by_rep(summed)

    def across_hi(self, block):
        if self.hi == 2:
            return (block, swap(block, "hi"))
        return spread(block, "hi", self.hi)

    def natural_hi(self, blocks):
        if self.hi != 2:
            return blocks
        mine, other = blocks
        low = lax.axis_index("hi") == 0
        return jnp.stack([jnp.where(low, mine, other), jnp.where(low, other, mine)])

    def halves(self, blocks):
        if self.hi == 2:
            return tuple(self.natural_rows(block[None]) for block in blocks)
        return tuple(jnp.split(self.natural_rows(blocks), 2))

    def natural_rows(self, stacked):
        view = stacked.reshape(stacked.shape[0], self.rep, RANKS, -1, stacked.shape[-1])
        return jnp.transpose(view, (0, 2, 1, 3, 4)).reshape(-1, stacked.shape[-1])

    def product_moved(self, lefts, rights, first=None):
        lanes = lefts[0].shape[1]
        if self.hi != 2:
            return product(lefts, rights, 0, lanes, jnp.bfloat16)
        return product(lefts, rights, lanes // 2 if first is None else first, lanes // 2, jnp.bfloat16)

    def move(self, moved):
        if self.hi == 2:
            return swap(moved, "hi")
        return fold(moved.reshape(self.hi, -1, moved.shape[1]), "hi", self.hi)

    def product_kept(self, lefts, rights, first=0):
        if self.hi != 2:
            return None
        return product(lefts, rights, first, lefts[0].shape[1] // 2, jnp.float32)

    def total(self, kept, arrived):
        if kept is None:
            return arrived
        return (kept + arrived.astype(jnp.float32)).astype(jnp.bfloat16)

    def by_rep(self, summed):
        view = summed.reshape(RANKS, self.rep, -1, summed.shape[1])
        return jnp.transpose(view, (1, 0, 2, 3)).reshape(self.rep, -1, summed.shape[1])

    def reduce(self, blocks):
        flat = blocks.reshape(-1, blocks.shape[-1])
        return lax.psum_scatter(flat, "rep", scatter_dimension=0, tiled=True)

    def rank_lanes(self, rows, groups):
        view = rows.reshape(rows.shape[0], groups, RANKS, -1)
        return lax.dynamic_index_in_dim(view, self.rank, 2, keepdims=False).reshape(rows.shape[0], -1)

    def place_lanes(self, row):
        view = row.reshape(self.head_groups, 1, -1)
        at = (jnp.arange(RANKS) == self.rank).astype(row.dtype)[None, :, None]
        return (view * at).reshape(-1)


def fence(*values):
    return lax.optimization_barrier(values)


def local(
    hi_count,
    rep_count,
    tokens,
    condition,
    caption,
    caption_len,
    item_kind,
    out_cotangent,
    norm_gains,
    ada_weight,
    qkv_weight,
    out_weight,
    text_weight,
    gate_up_weight,
    down_weight,
):
    bf16, f32 = jnp.bfloat16, jnp.float32
    item_count = condition.shape[0]
    item_len = tokens.shape[0] // item_count
    row_count = item_count * item_len
    rows = qkv_weight.shape[0]
    plan = Layout(hi_count, rep_count, out_weight.shape[0])
    rank_width = HEADS // RANKS * HEAD_DIM
    hi_at, mid_at, core_at, rep_at = [lax.axis_index(name) for name in AXES]
    device_shape = (hi_count, 2, 2, rep_count)

    feed_width = FF // RANKS
    devices = hi_count * RANKS * rep_count
    block_at = (hi_at * RANKS + plan.rank) * rep_count + rep_at

    def z_gather(block):
        return lax.all_gather(block.reshape(-1, block.shape[-1]), "rep", tiled=True)

    down_z = z_gather(down_weight)
    qkv_mine = trade_ranks(plan.by_rank(qkv_weight, 3, plan.head_groups))
    qkv_mine = qkv_mine.reshape(RANKS * rows, 3 * rank_width)
    if plan.aligned:
        qkv_mine = jnp.concatenate([qkv_mine, out_weight.reshape(-1, 3 * rank_width)])
    else:
        out_whole = lax.all_gather(out_weight, AXES, axis=0, tiled=True)
        out_rank = pick(out_whole.reshape(RANKS, rank_width, D), plan.rank)

    head = condition.reshape(item_count, devices, rows)
    head = jnp.transpose(head, (1, 0, 2)).reshape(devices, -1)
    rest = jnp.concatenate(
        [norm_gains.reshape(-1), caption_len.astype(bf16), item_kind.astype(bf16)]
    )
    small = jnp.concatenate([head, jnp.broadcast_to(rest, (devices, rest.size))], axis=1)
    small = lax.all_to_all(small, AXES, 0, 0, tiled=True)
    cut = [head.shape[1], head.shape[1] + norm_gains.size]
    cut.append(cut[1] + item_count)
    conditions, gains, lengths, kinds = jnp.split(small, cut, axis=-1)
    activated_mine = jax.nn.silu(conditions.astype(f32)).astype(bf16).reshape(-1, rows)
    gain_rows = jnp.moveaxis(gains.astype(f32).reshape(devices, 6, -1), 1, 0).reshape(6, D)
    lengths, kinds = [
        values.reshape(device_shape + (item_count,)) for values in (lengths, kinds)
    ]

    def group_items(values):
        view = lax.dynamic_index_in_dim(pick(values, hi_at), rep_at, 2, keepdims=False)
        near, far = pick(view, mid_at), pick(view, 1 - mid_at)
        order = [core_at, 1 - core_at]
        return [
            jnp.concatenate([pick(side, at) for at in order]).astype(jnp.int32)
            for side in (near, far)
        ]

    lengths_sides = group_items(lengths)
    kinds_sides = group_items(kinds)
    cosine, sine = rope_tables(jnp.arange(2), item_len)
    signs = jnp.where(jnp.arange(HEAD_DIM) % (HEAD_DIM // 2) < HEAD_DIM // 4, -1.0, 1.0)
    cosine, sine = [
        jnp.tile(table, (1, 1, LANES // HEAD_DIM)).reshape(-1, LANES) for table in (cosine, sine * signs)
    ]
    head_gains = plan.rank_lanes(gain_rows, plan.head_groups)
    cross_gate = jnp.tanh(head_gains[5])
    head_gains = jnp.concatenate([head_gains[1:4], cross_gate[None]])
    tables = (head_gains, cosine, sine)
    scalars = list(zip(kinds_sides, lengths_sides, strict=True))

    down_z, qkv_mine, text_weight, activated_mine = fence(
        down_z, qkv_mine, text_weight, activated_mine
    )
    qkv_z = z_gather(qkv_mine)
    down_rank = plan.across_hi(down_z)
    text_mine = trade_ranks(plan.by_rank(text_weight, 2, plan.head_groups))
    captions_near = pair(plan.ordered_text(caption.reshape(-1, TEXT_DIM)))
    partial = dot(activated_mine, ada_weight).astype(bf16).reshape(devices, item_count, 4 * D)
    gate_up_mine = trade_ranks(plan.by_rank(gate_up_weight, 2, hi_count))
    modulation = jnp.sum(lax.all_to_all(partial, AXES, 0, 0, tiled=True).astype(f32), axis=0)
    text_key_mine, text_value_mine = text_mine[..., :rank_width], text_mine[..., rank_width:]
    gate_mine, up_mine = gate_up_mine[..., :feed_width], gate_up_mine[..., feed_width:]
    qkv_z, down_rank, modulation, text_key_mine, text_value_mine, gate_mine, up_mine, captions_near = fence(
        qkv_z, down_rank, modulation, text_key_mine, text_value_mine, gate_mine, up_mine, captions_near
    )

    scale_attn, gate_attn, scale_mlp, gate_mlp = jnp.split(modulation, 4, axis=1)
    text_key_z = z_gather(text_key_mine)
    captions_far = swap(captions_near[0], "mid")
    qkv_rank = plan.across_hi(qkv_z)
    down_rank = plan.natural_hi(down_rank).reshape(feed_width, D)
    token_rows = tokens.astype(f32).reshape(item_count, item_len, D)
    normed = modulate(token_rows, gain_rows[0], scale_attn)
    normed = plan.ordered(normed.astype(bf16).reshape(row_count, D))
    mlp_gate = jnp.tanh(gate_mlp)[:, None, :]
    grad_top = out_cotangent.astype(f32).reshape(item_count, item_len, D)
    grad_result = (mlp_gate * grad_top).astype(bf16).reshape(row_count, D)
    normed_near, result_near = pair(normed), pair(grad_result)
    text_key_z, captions_far, qkv_rank, down_rank, normed_near, result_near, tables, scalars = fence(
        text_key_z, captions_far, qkv_rank, down_rank, normed_near, result_near, tables, scalars
    )

    text_value_z = z_gather(text_value_mine)
    text_key_rank = plan.across_hi(text_key_z)
    normed_far = swap(normed_near[0], "mid")
    captions_far = pair(captions_far)
    text_value_z, text_key_rank, normed_far, captions_far = fence(
        text_value_z, text_key_rank, normed_far, captions_far
    )

    gate_z = z_gather(gate_mine)
    text_value_rank = plan.across_hi(text_value_z)
    normed_far = pair(normed_far)
    if plan.aligned:
        blocks = [block.reshape(rep_count, -1, 3 * rank_width) for block in qkv_rank]
        out_rank = plan.natural_hi([block[:, RANKS * rows :].reshape(-1, D) for block in blocks])
        out_rank = out_rank.reshape(rank_width, D)
        qkv_rank = [block[:, : RANKS * rows].reshape(-1, 3 * rank_width) for block in blocks]
        qkv_rank = qkv_rank if hi_count == 2 else jnp.stack(qkv_rank)
    qkv_rank, text_key_rank = plan.halves(qkv_rank), plan.text_halves(text_key_rank)
    gate_z, text_value_rank, normed_far, qkv_rank, out_rank, text_key_rank = fence(
        gate_z, text_value_rank, normed_far, qkv_rank, out_rank, text_key_rank
    )

    up_z = z_gather(up_mine)
    gate_rank = plan.across_hi(gate_z)
    attend_weights = (qkv_rank, text_key_rank, plan.text_halves(text_value_rank), out_rank)
    normed_far, captions_far, kept_far, partial_far = attend(
        scalars[1], normed_far, captions_far, *attend_weights, tables
    )
    result_far = swap(result_near[0], "mid")
    up_z, gate_rank, result_far, normed_far, captions_far, kept_far, partial_far, attend_weights = fence(
        up_z, gate_rank, result_far, normed_far, captions_far, kept_far, partial_far, attend_weights
    )

    across = settle(partial_far).astype(bf16)
    across, normed_near, up_z = fence(across, normed_near, up_z)
    up_rank = plan.across_hi(up_z)
    arrived = settle_move(across)
    normed_near, captions_near, kept_near, partial_near = attend(
        scalars[0], normed_near, captions_near, *attend_weights, tables
    )
    result_far = pair(result_far)
    gate_rank = plan.halves(gate_rank)
    up_rank, arrived, normed_near, captions_near, kept_near, partial_near, result_far, gate_rank = fence(
        up_rank, arrived, normed_near, captions_near, kept_near, partial_near, result_far, gate_rank
    )

    branch = (settle(partial_near) + arrived.astype(f32)).reshape(item_count, item_len, D)
    attn_gate = jnp.tanh(gate_attn)[:, None, :]
    middle = token_rows + attn_gate * branch
    mlp_input = modulate(middle, gain_rows[4], scale_mlp)
    mlp_input = plan.ordered(mlp_input.astype(bf16).reshape(row_count, D))
    up_rank = plan.halves(up_rank)
    mlp_input, up_rank = fence(mlp_input, up_rank)

    feed_weights = (gate_rank, up_rank, down_rank)
    input_far = swap(mlp_input, "mid")
    input_near, result_near, hidden_near, gate_near, up_near, partial_near = feed(
        pair(mlp_input), result_near, *feed_weights
    )
    input_far, input_near, result_near, hidden_near, gate_near, up_near, partial_near = fence(
        input_far, input_near, result_near, hidden_near, gate_near, up_near, partial_near
    )
    input_far, result_far, hidden_far, gate_far, up_far, partial_far = feed(
        pair(input_far), result_far, *feed_weights
    )
    inputs, results = (input_near, input_far), (result_near, result_far)
    gate_rows, up_rows, hidden_rows = (gate_near, gate_far), (up_near, up_far), (hidden_near, hidden_far)
    across = settle(partial_far).astype(bf16)
    gate_moved = plan.product_moved(inputs, gate_rows)
    across, gate_moved, gate_rows, up_rows, hidden_rows = fence(
        across, gate_moved, gate_rows, up_rows, hidden_rows
    )
    arrived = settle_move(across)
    gate_moved = plan.move(gate_moved)
    up_moved = plan.product_moved(inputs, up_rows)
    hidden_first = hi_at * (feed_width // 2)
    down_moved = plan.product_moved(hidden_rows, results, feed_width // 2 - hidden_first)
    gate_kept = plan.product_kept(inputs, gate_rows)
    up_kept = plan.product_kept(inputs, up_rows)
    down_kept = plan.product_kept(hidden_rows, results, hidden_first)
    near = settle(partial_near)
    arrived, gate_moved, up_moved, down_moved, gate_kept, up_kept, down_kept, near = fence(
        arrived, gate_moved, up_moved, down_moved, gate_kept, up_kept, down_kept, near
    )

    up_moved = plan.move(up_moved)
    gate_grad = plan.by_rep(plan.total(gate_kept, gate_moved))
    gate_parts = plan.reduce(gate_grad)
    grad_mlp_input = plan.ordered(near + arrived.astype(f32))
    _, pull_mlp_norm = jax.vjp(modulate, middle, gain_rows[4], scale_mlp)
    grad_middle_norm, grad_mlp_gain, grad_scale_mlp = pull_mlp_norm(
        grad_mlp_input.reshape(item_count, item_len, D)
    )
    grad_middle = grad_top + grad_middle_norm
    grad_attn_gate = jnp.sum(grad_middle * branch, axis=1) * (1.0 - jnp.tanh(gate_attn) ** 2)
    grad_branch = (attn_gate * grad_middle).astype(bf16).reshape(row_count, D)
    (grad_branch,) = fence(grad_branch)

    branch_far = swap(grad_branch, "mid")
    back_weights = (qkv_rank, out_rank, tables)
    branch_near, qkv_near, text_near, rows_near, gain_near = attend_back(
        scalars[0], pair(grad_branch), kept_near, *back_weights
    )
    branch_far, up_moved, gate_parts, branch_near, qkv_near, text_near, rows_near, gain_near = fence(
        branch_far, up_moved, gate_parts, branch_near, qkv_near, text_near, rows_near, gain_near
    )

    up_grad = plan.by_rep(plan.total(up_kept, up_moved))
    up_grad, branch_far, down_moved = fence(up_grad, pair(branch_far), down_moved)
    up_parts = plan.reduce(up_grad)
    down_moved = plan.move(down_moved)
    branch_far, qkv_far, text_far, rows_far, gain_far = attend_back(
        scalars[1], branch_far, kept_far, *back_weights
    )
    captions, normed_rows = (captions_near, captions_far), (normed_near, normed_far)
    text_rows, qkv_rows, branches = (text_near, text_far), (qkv_near, qkv_far), (branch_near, branch_far)
    qkv_moved = plan.product_moved(normed_rows, qkv_rows)
    down_moved, up_parts, text_rows, qkv_rows, branches, rows_far, gain_far, qkv_moved, hidden_rows = fence(
        down_moved, up_parts, text_rows, qkv_rows, branches, rows_far, gain_far, qkv_moved, hidden_rows
    )

    qkv_moved = plan.move(qkv_moved)
    down_grad = plan.total(down_kept, down_moved).reshape(rep_count, -1, D)
    across = settle(rows_far).astype(bf16)
    mixed_rows = (kept_near[6], kept_far[6])
    across, down_grad, text_rows, qkv_rows, branches, hidden_rows, mixed_rows = fence(
        across, down_grad, text_rows, qkv_rows, branches, hidden_rows, mixed_rows
    )
    down_parts = plan.reduce(down_grad)
    arrived = settle_move(across)
    mixed_rows = [plan.ordered(rows) for rows in mixed_rows]
    if plan.aligned:
        halves = [slice(0, rank_width // 2), slice(rank_width // 2, None)]
        out_kept, out_moved = [
            product([side[:, lanes] for side in mixed_rows], branches, 0, rank_width // 2, bf16)
            for lanes in halves
        ]
        if hi_count == 2:
            out_moved = swap(out_moved, "hi")
        else:
            out_moved = plan.move(jnp.concatenate([out_kept, out_moved]))
    else:
        out_kept, out_moved = (), ()
    text_moved = plan.product_moved(captions, text_rows)
    text_kept = plan.product_kept(captions, text_rows)
    qkv_kept = plan.product_kept(normed_rows, qkv_rows)
    result_far = result_part(hidden_rows[1], down_rank)
    result_near = result_part(hidden_rows[0], down_rank)
    qkv_moved, down_parts, arrived, text_moved, out_kept, out_moved, text_kept, qkv_kept, result_far, result_near = fence(
        qkv_moved, down_parts, arrived, text_moved, out_kept, out_moved, text_kept, qkv_kept, result_far, result_near
    )

    text_moved = plan.move(text_moved)
    qkv_grad = plan.by_rep(plan.total(qkv_kept, qkv_moved))
    if plan.aligned:
        out_grad = plan.total(out_kept.astype(f32), out_moved) if hi_count == 2 else out_moved
        out_grad = out_grad.reshape(rep_count, -1, 3 * rank_width)
        qkv_grad = jnp.concatenate([qkv_grad, out_grad], axis=1)
    else:
        at = (jnp.arange(RANKS) == plan.rank).astype(bf16)[:, None, None]
        out_grad = product(mixed_rows, branches, 0, rank_width, bf16)
        out_grad = (out_grad[None] * at).reshape(D, D)
    qkv_parts = plan.reduce(qkv_grad)
    result_arrived = settle_move(settle(result_far).astype(bf16))
    grad_normed = plan.ordered(settle(rows_near) + arrived.astype(f32))
    _, pull_attn_norm = jax.vjp(modulate, token_rows, gain_rows[0], scale_attn)
    grad_token_norm, grad_attn_gain, grad_scale_attn = pull_attn_norm(
        grad_normed.reshape(item_count, item_len, D)
    )
    gate_up_parts = jnp.concatenate([gate_parts, up_parts], axis=-1)
    gate_up_parts = trade_ranks(gate_up_parts.reshape(RANKS, rows, -1))
    gain_terms = gain_near + gain_far
    gain_terms = gain_terms.at[3].multiply(1.0 - cross_gate**2)
    gain_terms = [plan.place_lanes(row) for row in gain_terms]
    (
        text_moved,
        qkv_parts,
        result_arrived,
        result_near,
        grad_scale_attn,
        grad_attn_gain,
        gate_up_parts,
        gain_terms,
    ) = fence(
        text_moved,
        qkv_parts,
        result_arrived,
        result_near,
        grad_scale_attn,
        grad_attn_gain,
        gate_up_parts,
        gain_terms,
    )

    text_grad = plan.text_by_rep(plan.total(text_kept, text_moved))
    text_grad, result_near, result_arrived, qkv_parts, gate_up_parts = fence(
        text_grad, result_near, result_arrived, qkv_parts, gate_up_parts
    )
    text_parts = plan.reduce(text_grad)
    if plan.aligned:
        out_parts = qkv_parts[RANKS * rows :].reshape(-1, D)
        qkv_parts = qkv_parts[: RANKS * rows]
    else:
        out_parts = lax.psum_scatter(out_grad, AXES, scatter_dimension=0, tiled=True)
    result = (settle(result_near) + result_arrived.astype(f32)).reshape(item_count, item_len, D)
    grad_mlp_gate = jnp.sum(grad_top * result, axis=1) * (1.0 - jnp.tanh(gate_mlp) ** 2)
    layer_out = (middle + mlp_gate * result).astype(bf16).reshape(row_count, D)
    tokens_grad = (grad_middle + grad_token_norm).reshape(row_count, D)

    grad_modulation = jnp.concatenate(
        [grad_scale_attn, grad_attn_gate, grad_scale_mlp, grad_mlp_gate], axis=1
    ).astype(bf16)
    gains_grad = jnp.stack(
        [grad_attn_gain, gain_terms[0], gain_terms[1], gain_terms[2], grad_mlp_gain, gain_terms[3]]
    ).astype(bf16)
    gain_blocks = jnp.moveaxis(gains_grad.reshape(6, devices, -1), 1, 0)
    gain_blocks = gain_blocks.reshape(devices, item_count, -1)
    modulations = jnp.broadcast_to(grad_modulation, (devices,) + grad_modulation.shape)
    both = lax.all_to_all(
        jnp.concatenate([modulations, gain_blocks], axis=2), AXES, 0, 0, tiled=True
    )
    ada_weight_grad = lax.dot_general(
        activated_mine.reshape(devices, item_count, rows),
        both[:, :, : 4 * D],
        (((0, 1), (0, 1)), ((), ())),
        preferred_element_type=f32,
    )
    norm_gains_grad = jnp.sum(both[:, :, 4 * D :].astype(f32), axis=0).reshape(6, -1)

    def whole(parts, weight, sections, groups):
        blocks = trade_ranks(parts.reshape(RANKS, weight.shape[0], -1))
        return plan.from_ranks(blocks, sections, groups).astype(f32)

    gate_up_weight_grad = plan.from_ranks(gate_up_parts, 2, hi_count).astype(f32)
    both, qkv_parts = fence(both, qkv_parts)
    qkv_weight_grad = whole(qkv_parts, qkv_weight, 3, plan.head_groups)
    qkv_weight_grad, text_parts = fence(qkv_weight_grad, text_parts)
    text_weight_grad = whole(text_parts, text_weight, 2, plan.head_groups)
    down_weight_grad, out_weight_grad = down_parts.astype(f32), out_parts.astype(f32)
    return (
        layer_out,
        tokens_grad,
        norm_gains_grad,
        ada_weight_grad,
        qkv_weight_grad,
        out_weight_grad,
        text_weight_grad,
        gate_up_weight_grad,
        down_weight_grad,
    )


def solution(mesh):
    grp, rep = mesh.devices.shape
    hi = grp // RANKS
    inner = Mesh(mesh.devices.reshape(hi, 2, 2, rep), AXES)
    rows = P(AXES, None)

    def step(*arrays):
        return local(hi, rep, *arrays)

    return jax.shard_map(
        step,
        mesh=inner,
        in_specs=(
            rows,
            rows,
            P(AXES, None, None),
            P(AXES),
            P(AXES),
            rows,
            P(None, AXES),
            rows,
            rows,
            rows,
            rows,
            rows,
            rows,
        ),
        out_specs=(rows, rows, P(None, AXES), rows, rows, rows, rows, rows, rows),
        check_vma=False,
    )
```

```python
import math

import jax
import jax.numpy as jnp
from jax import lax
from jax.experimental import pallas as pl
from jax.experimental.pallas import tpu as pltpu
from jax.sharding import Mesh
from jax.sharding import PartitionSpec as P

D = 1536
HEADS = 24
HEAD_DIM = 64
TEXT_DIM = 4096
FF = 4096
SIDE = 16
RANKS = 4
LANES = 128
MIB = 1 << 20
AXES = ("hi", "mid", "core", "rep")


EPSILON = 1e-06


def norm_rows(values, gain_row):
    return (
        values * lax.rsqrt(jnp.mean(values * values, axis=-1, keepdims=True) + EPSILON) * gain_row
    )


def rope_tables(item_kind, item_len):
    position = jnp.arange(item_len, dtype=jnp.int32)[None, :]
    half_side = SIDE // 2
    frame_index = position // (half_side * half_side)
    within = position % (half_side * half_side)
    is_clip = item_kind[:, None] == 1
    row_index = jnp.where(is_clip, frame_index * half_side + within // half_side, position // SIDE)
    columns = jnp.where(is_clip, within % half_side, position % SIDE)
    lane_index = jnp.arange(HEAD_DIM, dtype=jnp.int32)
    quarter = HEAD_DIM // 4
    frequency = jnp.exp(-(lane_index % quarter).astype(jnp.float32) * (math.log(10000.0) / quarter))
    coordinate = jnp.where(
        lane_index[None, None, :] < 2 * quarter, row_index[:, :, None], columns[:, :, None]
    ).astype(jnp.float32)
    angles = coordinate * frequency
    return (jnp.cos(angles), jnp.sin(angles))


def modulate(values, gain_row, scaling):
    return norm_rows(values, gain_row) * (1.0 + scaling[:, None, :])


def silu_product(gate_half, up_half):
    return jax.nn.silu(gate_half) * up_half


def dot(left, right):
    return jnp.dot(left, right, preferred_element_type=jnp.float32)


def dot_left(left, right):
    return lax.dot_general(left, right, (((0,), (0,)), ((), ())), preferred_element_type=jnp.float32)


def dot_right(left, right):
    return lax.dot_general(left, right, (((1,), (1,)), ((), ())), preferred_element_type=jnp.float32)


def lane_index(shape):
    return lax.broadcasted_iota(jnp.int32, shape, len(shape) - 1)

def head_sums(values):
    first = lane_index(values.shape) < HEAD_DIM
    low = jnp.sum(jnp.where(first, values, 0.0), axis=-1, keepdims=True)
    high = jnp.sum(jnp.where(first, 0.0, values), axis=-1, keepdims=True)
    return jnp.where(first, low, high)

def partner(values):
    quarter = HEAD_DIM // 4
    width = values.shape[-1]
    low = lane_index(values.shape) % (2 * quarter) < quarter
    return jnp.where(low, pltpu.roll(values, width - quarter, 1), pltpu.roll(values, quarter, 1))

def stack_heads(values):
    first = lane_index(values.shape) < HEAD_DIM
    zero = jnp.zeros_like(values)
    return jnp.concatenate([jnp.where(first, values, zero), jnp.where(first, zero, values)])

def join_heads(stacked):
    rows = stacked.shape[0] // 2
    first = lane_index((rows, stacked.shape[1])) < HEAD_DIM
    return jnp.where(first, stacked[:rows], stacked[rows:])

def inverse_rms(raw):
    return lax.rsqrt(head_sums(raw * raw) * (1.0 / HEAD_DIM) + EPSILON)

def rows_of(ref):
    return ref.shape[0]


def dot_cut(rows, mine, other):
    half = mine.shape[0]
    return dot(rows[:, :half], mine[...]) + dot(rows[:, half:], other[...])


def attend_kernel(
    kind_ref,
    len_ref,
    rows_ref,
    core_rows_ref,
    caption_ref,
    core_caption_ref,
    qkv_mine_ref,
    qkv_other_ref,
    key_mine_ref,
    key_other_ref,
    value_mine_ref,
    value_other_ref,
    out_weight_ref,
    gain_ref,
    cos_ref,
    sin_ref,
    rows_out_ref,
    caption_out_ref,
    qkv_ref,
    text_ref,
    text_value_ref,
    q_ref,
    k_ref,
    tk_ref,
    mixed_ref,
    read_ref,
    branch_ref,
    core_branch_ref,
):
    item = pl.program_id(0)
    own = item < pl.num_programs(0) // 2
    kind, length = kind_ref[item], len_ref[item]
    width = q_ref.shape[1]
    positions = pl.ds(kind * rows_of(q_ref), rows_of(q_ref))
    cosine, sine = cos_ref[positions, :], sin_ref[positions, :]
    scaling = HEAD_DIM ** (-0.5)

    @pl.when(own)
    def _():
        rows_out_ref[...] = rows_ref[...]
        caption_out_ref[...] = caption_ref[...]

    @pl.when(jnp.logical_not(own))
    def _():
        rows_out_ref[...] = core_rows_ref[...]
        caption_out_ref[...] = core_caption_ref[...]

    qkv_ref[...] = dot_cut(rows_out_ref, qkv_mine_ref, qkv_other_ref)
    text_ref[...] = dot_cut(caption_out_ref, key_mine_ref, key_other_ref)
    text_value_ref[...] = dot_cut(caption_out_ref, value_mine_ref, value_other_ref)
    for at in range(0, width, LANES):
        lanes = slice(at, at + LANES)
        turned = []
        for part, out_ref in ((0, q_ref), (1, k_ref)):
            raw = qkv_ref[:, part * width + at : part * width + at + LANES]
            normal = raw * inverse_rms(raw) * gain_ref[part : part + 1, lanes]
            rows = (normal * cosine + partner(normal) * sine).astype(jnp.bfloat16)
            out_ref[:, lanes] = rows
            turned.append(rows)
        queries, keys = turned
        values = qkv_ref[:, 2 * width + at : 2 * width + at + LANES].astype(jnp.bfloat16)
        text_raw = text_ref[:, lanes]
        text_keys = (text_raw * inverse_rms(text_raw) * gain_ref[2:3, lanes]).astype(jnp.bfloat16)
        tk_ref[:, lanes] = text_keys
        text_values = text_value_ref[:, lanes].astype(jnp.bfloat16)
        stacked = stack_heads(queries)
        scores = dot_right(stacked, keys) * scaling
        scores = jnp.exp(scores - jnp.max(scores, axis=-1, keepdims=True))
        own_out = dot(scores.astype(jnp.bfloat16), values) / jnp.sum(scores, axis=-1, keepdims=True)
        text = dot_right(stacked, text_keys) * scaling
        text = jnp.where(lane_index(text.shape) < length, text, -1e30)
        text = jnp.exp(text - jnp.max(text, axis=-1, keepdims=True))
        text_out = dot(text.astype(jnp.bfloat16), text_values) / jnp.sum(text, axis=-1, keepdims=True)
        read = join_heads(text_out)
        read_ref[:, lanes] = read
        mixed_ref[:, lanes] = (join_heads(own_out) + gain_ref[3:4, lanes] * read).astype(jnp.bfloat16)

    branch = dot(mixed_ref[...], out_weight_ref[...])

    @pl.when(own)
    def _():
        branch_ref[...] = branch

    @pl.when(jnp.logical_not(own))
    def _():
        core_branch_ref[...] = branch.astype(jnp.bfloat16)


def head_norm_back(grad, raw, gain_row):
    inverse = inverse_rms(raw)
    scaled = grad * gain_row
    normal = raw * inverse
    inner = head_sums(scaled * normal) * (1.0 / HEAD_DIM)
    return inverse * (scaled - normal * inner), jnp.sum(grad * normal, axis=0, keepdims=True)

def attend_back_kernel(
    kind_ref,
    len_ref,
    branch_ref,
    core_branch_ref,
    qkv_ref,
    text_ref,
    text_value_ref,
    q_ref,
    k_ref,
    tk_ref,
    read_ref,
    qkv_mine_ref,
    qkv_other_ref,
    out_weight_ref,
    gain_ref,
    cos_ref,
    sin_ref,
    branch_out_ref,
    gqkv_ref,
    gtext_ref,
    grad_rows_ref,
    core_grad_rows_ref,
    gains_ref,
    mixed_ref,
):
    item = pl.program_id(0)
    own = item < pl.num_programs(0) // 2
    kind, length = kind_ref[item], len_ref[item]
    width = q_ref.shape[1]
    positions = pl.ds(kind * rows_of(q_ref), rows_of(q_ref))
    cosine, sine = cos_ref[positions, :], sin_ref[positions, :]
    scaling = HEAD_DIM ** (-0.5)

    @pl.when(own)
    def _():
        branch_out_ref[...] = branch_ref[...]

    @pl.when(jnp.logical_not(own))
    def _():
        branch_out_ref[...] = core_branch_ref[...]

    mixed_ref[...] = dot_right(branch_out_ref[...], out_weight_ref[...])

    @pl.when(item == 0)
    def _():
        gains_ref[...] = jnp.zeros_like(gains_ref)

    def one(stacked, keys, values, stacked_grad, valid):
        scores = dot_right(keys, stacked) * scaling
        if valid is not None:
            scores = jnp.where(valid(scores.shape), scores, -1e30)
        probs = jnp.exp(scores - jnp.max(scores, axis=0, keepdims=True))
        probs = probs * (1.0 / jnp.sum(probs, axis=0, keepdims=True))
        grad_values = dot(probs.astype(jnp.bfloat16), stacked_grad)
        grad_probs = dot_right(values, stacked_grad)
        inner = jnp.sum(probs * grad_probs, axis=0, keepdims=True)
        grad_scores = (probs * (grad_probs - inner)).astype(jnp.bfloat16)
        grad_keys = dot(grad_scores, stacked) * scaling
        grad_queries = dot_left(keys, grad_scores)
        return grad_queries, grad_keys, grad_values

    for at in range(0, width, LANES):
        lanes = slice(at, at + LANES)
        grad = mixed_ref[:, lanes]
        cross = gain_ref[3:4, lanes]
        values = qkv_ref[:, 2 * width + at : 2 * width + at + LANES].astype(jnp.bfloat16)
        text_values = text_value_ref[:, lanes].astype(jnp.bfloat16)
        stacked = stack_heads(q_ref[:, lanes])
        own_queries, own_keys, own_values = one(
            stacked, k_ref[:, lanes], values, stack_heads(grad.astype(jnp.bfloat16)), None
        )
        read_queries, read_keys, read_values = one(
            stacked, tk_ref[:, lanes], text_values, stack_heads((cross * grad).astype(jnp.bfloat16)),
            lambda shape: lax.broadcasted_iota(jnp.int32, shape, 0) < length,
        )
        grad_queries = join_heads((own_queries + read_queries).T) * scaling
        for part, turned in ((0, grad_queries), (1, own_keys)):
            raw = qkv_ref[:, part * width + at : part * width + at + LANES]
            back = turned * cosine + partner(turned * sine)
            grad_raw, gain = head_norm_back(back, raw, gain_ref[part : part + 1, lanes])
            gqkv_ref[:, part * width + at : part * width + at + LANES] = grad_raw.astype(jnp.bfloat16)
            gains_ref[part : part + 1, lanes] += gain
        gqkv_ref[:, 2 * width + at : 2 * width + at + LANES] = own_values.astype(jnp.bfloat16)
        grad_text, gain = head_norm_back(read_keys, text_ref[:, lanes], gain_ref[2:3, lanes])
        gtext_ref[:, lanes] = grad_text.astype(jnp.bfloat16)
        gains_ref[2:3, lanes] += gain
        gtext_ref[:, width + at : width + at + LANES] = read_values.astype(jnp.bfloat16)
        gains_ref[3:4, lanes] += jnp.sum(grad * read_ref[:, lanes], axis=0, keepdims=True)

    half = qkv_mine_ref.shape[0]
    low = dot_right(gqkv_ref[...], qkv_mine_ref[...])
    high = dot_right(gqkv_ref[...], qkv_other_ref[...])

    @pl.when(own)
    def _():
        grad_rows_ref[:, :half] = low
        grad_rows_ref[:, half:] = high

    @pl.when(jnp.logical_not(own))
    def _():
        core_grad_rows_ref[:, :half] = low.astype(jnp.bfloat16)
        core_grad_rows_ref[:, half:] = high.astype(jnp.bfloat16)


def whole_spec(array):
    zeros = (0,) * len(array.shape)
    return pl.BlockSpec(array.shape, lambda *_: zeros, pipeline_mode=pl.Buffered(1))


def mine_spec(array, steps):
    half = steps // 2
    return pl.BlockSpec(
        (array.shape[0] // half, array.shape[1]), lambda i, *_: (jnp.minimum(i, half - 1), 0)
    )


def core_spec(array, steps):
    half = steps // 2
    return pl.BlockSpec(
        (array.shape[0] // half, array.shape[1]), lambda i, *_: (jnp.maximum(i - half, 0), 0)
    )


def pair_specs(pair_of_arrays, steps):
    return [mine_spec(pair_of_arrays[0], steps), core_spec(pair_of_arrays[1], steps)]


def step_spec(array, steps):
    return pl.BlockSpec((array.shape[0] // steps, array.shape[1]), lambda i, *_: (i, 0))


def summed_spec(array):
    return pl.BlockSpec(array.shape, lambda i, *_: (0, 0))


def shaped(count, columns, dtype=jnp.bfloat16):
    return jax.ShapeDtypeStruct((count, columns), dtype)


def parameters():
    return pltpu.CompilerParams(dimension_semantics=("arbitrary",), vmem_limit_bytes=58 * MIB)


def attend(scalars, rows, captions, qkv_rank, key_rank, value_rank, out_rank, tables):
    items = scalars[0].shape[0]
    count, width = 2 * rows[0].shape[0], out_rank.shape[0]
    text_count = 2 * captions[0].shape[0]
    outs = [
        shaped(count, D),
        shaped(text_count, TEXT_DIM),
        shaped(count, 3 * width, jnp.float32),
        shaped(text_count, width, jnp.float32),
        shaped(text_count, width, jnp.float32),
        shaped(count, width),
        shaped(count, width),
        shaped(text_count, width),
        shaped(count, width),
        shaped(count, width, jnp.float32),
    ]
    branch = (shaped(count // 2, D, jnp.float32), shaped(count // 2, D))
    whole = [*qkv_rank, *key_rank, *value_rank, out_rank, *tables]
    rows, captions, *kept, branch_mine, branch_core = pl.pallas_call(
        attend_kernel,
        grid_spec=pltpu.PrefetchScalarGridSpec(
            num_scalar_prefetch=2,
            grid=(items,),
            in_specs=pair_specs(rows, items)
            + pair_specs(captions, items)
            + [whole_spec(array) for array in whole],
            out_specs=[step_spec(array, items) for array in outs] + pair_specs(branch, items),
        ),
        out_shape=[*outs, *branch],
        compiler_params=parameters(),
        name="attend",
    )(*scalars, *rows, *captions, *whole)
    return rows, captions, kept, (branch_mine, branch_core)


def attend_back(scalars, grad_branch, kept, qkv_rank, out_rank, tables):
    items = scalars[0].shape[0]
    qkv_raw, text_raw, text_value_raw, queries, keys, text_keys, _, read = kept
    count, width = queries.shape
    outs = [
        shaped(count, D),
        shaped(count, 3 * width),
        shaped(text_raw.shape[0], 2 * width),
    ]
    rows = (shaped(count // 2, D, jnp.float32), shaped(count // 2, D))
    gains = shaped(4, width, jnp.float32)
    by_item = [qkv_raw, text_raw, text_value_raw, queries, keys, text_keys, read]
    whole = [*qkv_rank, out_rank, *tables]
    branch, qkv, text, rows_mine, rows_core, gains = pl.pallas_call(
        attend_back_kernel,
        grid_spec=pltpu.PrefetchScalarGridSpec(
            num_scalar_prefetch=2,
            grid=(items,),
            in_specs=pair_specs(grad_branch, items)
            + [step_spec(array, items) for array in by_item]
            + [whole_spec(array) for array in whole],
            out_specs=[step_spec(array, items) for array in outs]
            + pair_specs(rows, items)
            + [summed_spec(gains)],
            scratch_shapes=[pltpu.VMEM((count // items, width), jnp.float32)],
        ),
        out_shape=[*outs, *rows, gains],
        compiler_params=parameters(),
        name="attend_back",
    )(*scalars, *grad_branch, *by_item, *whole)
    return branch, qkv, text, (rows_mine, rows_core), gains


def row_cuts(lefts, rights):
    cuts, left, right, left_row, right_row = [], 0, 0, 0, 0
    while left < len(lefts):
        count = min(lefts[left].shape[0] - left_row, rights[right].shape[0] - right_row)
        cuts.append((left, left_row, right, right_row, count))
        left_row, right_row = left_row + count, right_row + count
        if left_row == lefts[left].shape[0]:
            left, left_row = left + 1, 0
        if right_row == rights[right].shape[0]:
            right, right_row = right + 1, 0
    return cuts


def product(lefts, rights, first, lanes, dtype):
    columns = rights[0].shape[1]
    if lanes % LANES:
        block = lanes
    else:
        block = 384 if lanes % 384 == 0 else math.gcd(lanes, 512)
    cuts = row_cuts(lefts, rights)

    def kernel(first_ref, *refs):
        left_refs, right_refs, out_ref = refs[: len(lefts)], refs[len(lefts) : -1], refs[-1]
        total = None
        for left, left_row, right, right_row, count in cuts:
            term = dot_left(
                left_refs[left][left_row : left_row + count, :],
                right_refs[right][right_row : right_row + count, :],
            )
            total = term if total is None else total + term
        out_ref[...] = total.astype(out_ref.dtype)

    return pl.pallas_call(
        kernel,
        grid_spec=pltpu.PrefetchScalarGridSpec(
            num_scalar_prefetch=1,
            grid=(lanes // block,),
            in_specs=[
                pl.BlockSpec((array.shape[0], block), lambda i, first: (0, first[0] // block + i))
                for array in lefts
            ]
            + [whole_spec(array) for array in rights],
            out_specs=pl.BlockSpec((block, columns), lambda i, first: (i, 0)),
        ),
        out_shape=shaped(lanes, columns, dtype),
        compiler_params=parameters(),
        name="product",
    )(jnp.reshape(first, (1,)).astype(jnp.int32), *lefts, *rights)


def feed_kernel(
    rows_ref,
    core_rows_ref,
    result_ref,
    core_result_ref,
    gate_mine_ref,
    gate_other_ref,
    up_mine_ref,
    up_other_ref,
    down_ref,
    rows,
    result,
    hidden_ref,
    grad_gate_ref,
    grad_up_ref,
    grad_ref,
    core_grad_ref,
):
    own = pl.program_id(0) < pl.num_programs(0) // 2

    @pl.when(own)
    def _():
        rows[...] = rows_ref[...]
        result[...] = result_ref[...]

    @pl.when(jnp.logical_not(own))
    def _():
        rows[...] = core_rows_ref[...]
        result[...] = core_result_ref[...]

    gate = dot_cut(rows, gate_mine_ref, gate_other_ref)
    up = dot_cut(rows, up_mine_ref, up_other_ref)
    grad_hidden = dot_right(result[...], down_ref[...])
    sigmoid = 1.0 / (1.0 + jnp.exp(-gate))
    silu = gate * sigmoid
    hidden_ref[...] = (silu * up).astype(jnp.bfloat16)
    grad_gate = (grad_hidden * up * (sigmoid + silu * (1.0 - sigmoid))).astype(jnp.bfloat16)
    grad_up = (grad_hidden * silu).astype(jnp.bfloat16)
    grad_gate_ref[...] = grad_gate
    grad_up_ref[...] = grad_up
    half = gate_mine_ref.shape[0]
    low = dot_right(grad_gate, gate_mine_ref[...]) + dot_right(grad_up, up_mine_ref[...])
    high = dot_right(grad_gate, gate_other_ref[...]) + dot_right(grad_up, up_other_ref[...])

    @pl.when(own)
    def _():
        grad_ref[:, :half] = low
        grad_ref[:, half:] = high

    @pl.when(jnp.logical_not(own))
    def _():
        core_grad_ref[:, :half] = low.astype(jnp.bfloat16)
        core_grad_ref[:, half:] = high.astype(jnp.bfloat16)


def feed(rows, grad_result, gate_rank, up_rank, down_rank):
    count, width = 2 * rows[0].shape[0], down_rank.shape[0]
    block = 256
    steps = count // block
    outs = [shaped(count, D)] * 2 + [shaped(count, width)] * 3
    grads = (shaped(count // 2, D, jnp.float32), shaped(count // 2, D))
    whole = [*gate_rank, *up_rank, down_rank]
    *outs, grad_mine, grad_core = pl.pallas_call(
        feed_kernel,
        grid=(steps,),
        in_specs=pair_specs(rows, steps)
        + pair_specs(grad_result, steps)
        + [whole_spec(array) for array in whole],
        out_specs=[step_spec(array, steps) for array in outs] + pair_specs(grads, steps),
        out_shape=[*outs, *grads],
        compiler_params=parameters(),
        name="feed",
    )(*rows, *grad_result, *whole)
    return *outs, (grad_mine, grad_core)


def result_kernel(hidden_ref, down_ref, result_ref, core_result_ref):
    own = pl.program_id(0) < pl.num_programs(0) // 2
    rows = dot(hidden_ref[...], down_ref[...])

    @pl.when(own)
    def _():
        result_ref[...] = rows

    @pl.when(jnp.logical_not(own))
    def _():
        core_result_ref[...] = rows.astype(jnp.bfloat16)


def result_part(hidden, down_rank):
    count = hidden.shape[0]
    steps = count // 256
    outs = (shaped(count // 2, D, jnp.float32), shaped(count // 2, D))
    return pl.pallas_call(
        result_kernel,
        grid=(steps,),
        in_specs=[step_spec(hidden, steps), whole_spec(down_rank)],
        out_specs=pair_specs(outs, steps),
        out_shape=outs,
        compiler_params=parameters(),
        name="result",
    )(hidden, down_rank)


def swap(block, axis, count=2, step=1):
    return lax.ppermute(block, axis, [(at, at ^ step) for at in range(count)])


def spread(block, axis, count):
    if count & (count - 1):
        return lax.all_gather(block, axis)
    block, step = block[None], 1
    while step < count:
        other = swap(block, axis, count, step)
        low = (lax.axis_index(axis) & step) == 0
        block = jnp.where(
            low, jnp.concatenate([block, other]), jnp.concatenate([other, block])
        )
        step *= 2
    return block


def fold(block, axis, count):
    if count & (count - 1):
        return lax.psum_scatter(block, axis, scatter_dimension=0)
    step = count // 2
    while step:
        half = block.shape[0] // 2
        low = (lax.axis_index(axis) & step) == 0
        lower, upper = block[:half], block[half:]
        block = jnp.where(low, lower, upper) + swap(
            jnp.where(low, upper, lower), axis, count, step
        )
        step //= 2
    return block[0]


def trade_ranks(block):
    return lax.all_to_all(block, ("mid", "core"), 0, 0, tiled=True)


def pick(stack, index):
    return lax.dynamic_index_in_dim(stack, index, 0, keepdims=False)


def pair(rows):
    return (rows, swap(rows, "core"))


def settle(partial):
    mine, core = partial
    return mine + swap(core, "core").astype(jnp.float32)


def settle_move(across):
    return swap(across, "mid")


class Layout:
    def __init__(self, hi, rep, out_rows):
        self.hi, self.rep = hi, rep
        self.aligned = (rep * out_rows) % HEAD_DIM == 0
        self.head_groups = hi if self.aligned else 1
        self.rank = lax.axis_index("mid") * 2 + lax.axis_index("core")

    def by_rank(self, weight, sections, groups):
        rows, columns = weight.shape
        width = columns // (sections * groups * RANKS)
        view = weight.reshape(rows, sections * groups, RANKS, width)
        view = jnp.transpose(view, (2, 0, 1, 3))
        return view.reshape(RANKS, rows, sections * groups * width)

    def from_ranks(self, blocks, sections, groups):
        _, rows, per_rank = blocks.shape
        width = per_rank // (sections * groups)
        view = blocks.reshape(RANKS, rows, sections * groups, width)
        return jnp.transpose(view, (1, 2, 0, 3)).reshape(rows, RANKS * per_rank)

    def ordered(self, values):
        if self.hi != 2:
            return values
        half = values.shape[-1] // 2
        turned = jnp.concatenate([values[..., half:], values[..., :half]], axis=-1)
        return jnp.where(lax.axis_index("hi") == 0, values, turned)

    def ordered_text(self, values):
        if self.hi != 2:
            return values
        view = values.reshape(values.shape[0], self.hi, RANKS, self.rep, -1)
        return self.ordered(jnp.swapaxes(view, 2, 3).reshape(values.shape))

    def text_halves(self, blocks):
        return tuple(blocks) if self.hi == 2 else self.halves(blocks)

    def text_by_rep(self, summed):
        return summed.reshape(self.rep, -1, summed.shape[1]) if self.hi == 2 else self.by_rep(summed)

    def across_hi(self, block):
        if self.hi == 2:
            return (block, swap(block, "hi"))
        return spread(block, "hi", self.hi)

    def natural_hi(self, blocks):
        if self.hi != 2:
            return blocks
        mine, other = blocks
        low = lax.axis_index("hi") == 0
        return jnp.stack([jnp.where(low, mine, other), jnp.where(low, other, mine)])

    def halves(self, blocks):
        if self.hi == 2:
            return tuple(self.natural_rows(block[None]) for block in blocks)
        return tuple(jnp.split(self.natural_rows(blocks), 2))

    def natural_rows(self, stacked):
        view = stacked.reshape(stacked.shape[0], self.rep, RANKS, -1, stacked.shape[-1])
        return jnp.transpose(view, (0, 2, 1, 3, 4)).reshape(-1, stacked.shape[-1])

    def product_moved(self, lefts, rights, first=None):
        lanes = lefts[0].shape[1]
        if self.hi != 2:
            return product(lefts, rights, 0, lanes, jnp.bfloat16)
        return product(lefts, rights, lanes // 2 if first is None else first, lanes // 2, jnp.bfloat16)

    def move(self, moved):
        if self.hi == 2:
            return swap(moved, "hi")
        return fold(moved.reshape(self.hi, -1, moved.shape[1]), "hi", self.hi)

    def product_kept(self, lefts, rights, first=0):
        if self.hi != 2:
            return None
        return product(lefts, rights, first, lefts[0].shape[1] // 2, jnp.float32)

    def total(self, kept, arrived):
        if kept is None:
            return arrived
        return (kept + arrived.astype(jnp.float32)).astype(jnp.bfloat16)

    def by_rep(self, summed):
        view = summed.reshape(RANKS, self.rep, -1, summed.shape[1])
        return jnp.transpose(view, (1, 0, 2, 3)).reshape(self.rep, -1, summed.shape[1])

    def reduce(self, blocks):
        flat = blocks.reshape(-1, blocks.shape[-1])
        return lax.psum_scatter(flat, "rep", scatter_dimension=0, tiled=True)

    def rank_lanes(self, rows, groups):
        view = rows.reshape(rows.shape[0], groups, RANKS, -1)
        return lax.dynamic_index_in_dim(view, self.rank, 2, keepdims=False).reshape(rows.shape[0], -1)

    def place_lanes(self, row):
        view = row.reshape(self.head_groups, 1, -1)
        at = (jnp.arange(RANKS) == self.rank).astype(row.dtype)[None, :, None]
        return (view * at).reshape(-1)


def fence(*values):
    return lax.optimization_barrier(values)


def local(
    hi_count,
    rep_count,
    tokens,
    condition,
    caption,
    caption_len,
    item_kind,
    out_cotangent,
    norm_gains,
    ada_weight,
    qkv_weight,
    out_weight,
    text_weight,
    gate_up_weight,
    down_weight,
):
    bf16, f32 = jnp.bfloat16, jnp.float32
    item_count = condition.shape[0]
    item_len = tokens.shape[0] // item_count
    row_count = item_count * item_len
    rows = qkv_weight.shape[0]
    plan = Layout(hi_count, rep_count, out_weight.shape[0])
    rank_width = HEADS // RANKS * HEAD_DIM
    hi_at, mid_at, core_at, rep_at = [lax.axis_index(name) for name in AXES]
    device_shape = (hi_count, 2, 2, rep_count)

    feed_width = FF // RANKS
    devices = hi_count * RANKS * rep_count
    block_at = (hi_at * RANKS + plan.rank) * rep_count + rep_at

    def z_gather(block):
        return lax.all_gather(block.reshape(-1, block.shape[-1]), "rep", tiled=True)

    down_z = z_gather(down_weight)
    qkv_mine = trade_ranks(plan.by_rank(qkv_weight, 3, plan.head_groups))
    qkv_mine = qkv_mine.reshape(RANKS * rows, 3 * rank_width)
    if plan.aligned:
        qkv_mine = jnp.concatenate([qkv_mine, out_weight.reshape(-1, 3 * rank_width)])
    else:
        out_whole = lax.all_gather(out_weight, AXES, axis=0, tiled=True)
        out_rank = pick(out_whole.reshape(RANKS, rank_width, D), plan.rank)

    head = condition.reshape(item_count, devices, rows)
    head = jnp.transpose(head, (1, 0, 2)).reshape(devices, -1)
    rest = jnp.concatenate(
        [norm_gains.reshape(-1), caption_len.astype(bf16), item_kind.astype(bf16)]
    )
    small = jnp.concatenate([head, jnp.broadcast_to(rest, (devices, rest.size))], axis=1)
    small = lax.all_to_all(small, AXES, 0, 0, tiled=True)
    cut = [head.shape[1], head.shape[1] + norm_gains.size]
    cut.append(cut[1] + item_count)
    conditions, gains, lengths, kinds = jnp.split(small, cut, axis=-1)
    activated_mine = jax.nn.silu(conditions.astype(f32)).astype(bf16).reshape(-1, rows)
    gain_rows = jnp.moveaxis(gains.astype(f32).reshape(devices, 6, -1), 1, 0).reshape(6, D)
    lengths, kinds = [
        values.reshape(device_shape + (item_count,)) for values in (lengths, kinds)
    ]

    def group_items(values):
        view = lax.dynamic_index_in_dim(pick(values, hi_at), rep_at, 2, keepdims=False)
        near, far = pick(view, mid_at), pick(view, 1 - mid_at)
        order = [core_at, 1 - core_at]
        return [
            jnp.concatenate([pick(side, at) for at in order]).astype(jnp.int32)
            for side in (near, far)
        ]

    lengths_sides = group_items(lengths)
    kinds_sides = group_items(kinds)
    cosine, sine = rope_tables(jnp.arange(2), item_len)
    signs = jnp.where(jnp.arange(HEAD_DIM) % (HEAD_DIM // 2) < HEAD_DIM // 4, -1.0, 1.0)
    cosine, sine = [
        jnp.tile(table, (1, 1, LANES // HEAD_DIM)).reshape(-1, LANES) for table in (cosine, sine * signs)
    ]
    head_gains = plan.rank_lanes(gain_rows, plan.head_groups)
    cross_gate = jnp.tanh(head_gains[5])
    head_gains = jnp.concatenate([head_gains[1:4], cross_gate[None]])
    tables = (head_gains, cosine, sine)
    scalars = list(zip(kinds_sides, lengths_sides, strict=True))

    down_z, qkv_mine, text_weight, activated_mine = fence(
        down_z, qkv_mine, text_weight, activated_mine
    )
    qkv_z = z_gather(qkv_mine)
    down_rank = plan.across_hi(down_z)
    text_mine = trade_ranks(plan.by_rank(text_weight, 2, plan.head_groups))
    captions_near = pair(plan.ordered_text(caption.reshape(-1, TEXT_DIM)))
    partial = dot(activated_mine, ada_weight).astype(bf16).reshape(devices, item_count, 4 * D)
    gate_up_mine = trade_ranks(plan.by_rank(gate_up_weight, 2, hi_count))
    modulation = jnp.sum(lax.all_to_all(partial, AXES, 0, 0, tiled=True).astype(f32), axis=0)
    text_key_mine, text_value_mine = text_mine[..., :rank_width], text_mine[..., rank_width:]
    gate_mine, up_mine = gate_up_mine[..., :feed_width], gate_up_mine[..., feed_width:]
    qkv_z, down_rank, modulation, text_key_mine, text_value_mine, gate_mine, up_mine, captions_near = fence(
        qkv_z, down_rank, modulation, text_key_mine, text_value_mine, gate_mine, up_mine, captions_near
    )

    scale_attn, gate_attn, scale_mlp, gate_mlp = jnp.split(modulation, 4, axis=1)
    text_key_z = z_gather(text_key_mine)
    captions_far = swap(captions_near[0], "mid")
    qkv_rank = plan.across_hi(qkv_z)
    down_rank = plan.natural_hi(down_rank).reshape(feed_width, D)
    token_rows = tokens.astype(f32).reshape(item_count, item_len, D)
    normed = modulate(token_rows, gain_rows[0], scale_attn)
    normed = plan.ordered(normed.astype(bf16).reshape(row_count, D))
    mlp_gate = jnp.tanh(gate_mlp)[:, None, :]
    grad_top = out_cotangent.astype(f32).reshape(item_count, item_len, D)
    grad_result = (mlp_gate * grad_top).astype(bf16).reshape(row_count, D)
    normed_near, result_near = pair(normed), pair(grad_result)
    text_key_z, captions_far, qkv_rank, down_rank, normed_near, result_near, tables, scalars = fence(
        text_key_z, captions_far, qkv_rank, down_rank, normed_near, result_near, tables, scalars
    )

    text_value_z = z_gather(text_value_mine)
    text_key_rank = plan.across_hi(text_key_z)
    normed_far = swap(normed_near[0], "mid")
    captions_far = pair(captions_far)
    text_value_z, text_key_rank, normed_far, captions_far = fence(
        text_value_z, text_key_rank, normed_far, captions_far
    )

    gate_z = z_gather(gate_mine)
    text_value_rank = plan.across_hi(text_value_z)
    normed_far = pair(normed_far)
    if plan.aligned:
        blocks = [block.reshape(rep_count, -1, 3 * rank_width) for block in qkv_rank]
        out_rank = plan.natural_hi([block[:, RANKS * rows :].reshape(-1, D) for block in blocks])
        out_rank = out_rank.reshape(rank_width, D)
        qkv_rank = [block[:, : RANKS * rows].reshape(-1, 3 * rank_width) for block in blocks]
        qkv_rank = qkv_rank if hi_count == 2 else jnp.stack(qkv_rank)
    qkv_rank, text_key_rank = plan.halves(qkv_rank), plan.text_halves(text_key_rank)
    gate_z, text_value_rank, normed_far, qkv_rank, out_rank, text_key_rank = fence(
        gate_z, text_value_rank, normed_far, qkv_rank, out_rank, text_key_rank
    )

    up_z = z_gather(up_mine)
    gate_rank = plan.across_hi(gate_z)
    attend_weights = (qkv_rank, text_key_rank, plan.text_halves(text_value_rank), out_rank)
    normed_far, captions_far, kept_far, partial_far = attend(
        scalars[1], normed_far, captions_far, *attend_weights, tables
    )
    result_far = swap(result_near[0], "mid")
    up_z, gate_rank, result_far, normed_far, captions_far, kept_far, partial_far, attend_weights = fence(
        up_z, gate_rank, result_far, normed_far, captions_far, kept_far, partial_far, attend_weights
    )

    across = settle(partial_far).astype(bf16)
    across, normed_near, up_z = fence(across, normed_near, up_z)
    up_rank = plan.across_hi(up_z)
    arrived = settle_move(across)
    normed_near, captions_near, kept_near, partial_near = attend(
        scalars[0], normed_near, captions_near, *attend_weights, tables
    )
    result_far = pair(result_far)
    gate_rank = plan.halves(gate_rank)
    up_rank, arrived, normed_near, captions_near, kept_near, partial_near, result_far, gate_rank = fence(
        up_rank, arrived, normed_near, captions_near, kept_near, partial_near, result_far, gate_rank
    )

    branch = (settle(partial_near) + arrived.astype(f32)).reshape(item_count, item_len, D)
    attn_gate = jnp.tanh(gate_attn)[:, None, :]
    middle = token_rows + attn_gate * branch
    mlp_input = modulate(middle, gain_rows[4], scale_mlp)
    mlp_input = plan.ordered(mlp_input.astype(bf16).reshape(row_count, D))
    up_rank = plan.halves(up_rank)
    mlp_input, up_rank = fence(mlp_input, up_rank)

    feed_weights = (gate_rank, up_rank, down_rank)
    input_far = swap(mlp_input, "mid")
    input_near, result_near, hidden_near, gate_near, up_near, partial_near = feed(
        pair(mlp_input), result_near, *feed_weights
    )
    input_far, input_near, result_near, hidden_near, gate_near, up_near, partial_near = fence(
        input_far, input_near, result_near, hidden_near, gate_near, up_near, partial_near
    )
    input_far, result_far, hidden_far, gate_far, up_far, partial_far = feed(
        pair(input_far), result_far, *feed_weights
    )
    inputs, results = (input_near, input_far), (result_near, result_far)
    gate_rows, up_rows, hidden_rows = (gate_near, gate_far), (up_near, up_far), (hidden_near, hidden_far)
    across = settle(partial_far).astype(bf16)
    gate_moved = plan.product_moved(inputs, gate_rows)
    across, gate_moved, gate_rows, up_rows, hidden_rows = fence(
        across, gate_moved, gate_rows, up_rows, hidden_rows
    )
    arrived = settle_move(across)
    gate_moved = plan.move(gate_moved)
    up_moved = plan.product_moved(inputs, up_rows)
    hidden_first = hi_at * (feed_width // 2)
    down_moved = plan.product_moved(hidden_rows, results, feed_width // 2 - hidden_first)
    gate_kept = plan.product_kept(inputs, gate_rows)
    up_kept = plan.product_kept(inputs, up_rows)
    down_kept = plan.product_kept(hidden_rows, results, hidden_first)
    near = settle(partial_near)
    arrived, gate_moved, up_moved, down_moved, gate_kept, up_kept, down_kept, near = fence(
        arrived, gate_moved, up_moved, down_moved, gate_kept, up_kept, down_kept, near
    )

    up_moved = plan.move(up_moved)
    gate_grad = plan.by_rep(plan.total(gate_kept, gate_moved))
    gate_parts = plan.reduce(gate_grad)
    grad_mlp_input = plan.ordered(near + arrived.astype(f32))
    _, pull_mlp_norm = jax.vjp(modulate, middle, gain_rows[4], scale_mlp)
    grad_middle_norm, grad_mlp_gain, grad_scale_mlp = pull_mlp_norm(
        grad_mlp_input.reshape(item_count, item_len, D)
    )
    grad_middle = grad_top + grad_middle_norm
    grad_attn_gate = jnp.sum(grad_middle * branch, axis=1) * (1.0 - jnp.tanh(gate_attn) ** 2)
    grad_branch = (attn_gate * grad_middle).astype(bf16).reshape(row_count, D)
    (grad_branch,) = fence(grad_branch)

    branch_far = swap(grad_branch, "mid")
    back_weights = (qkv_rank, out_rank, tables)
    branch_near, qkv_near, text_near, rows_near, gain_near = attend_back(
        scalars[0], pair(grad_branch), kept_near, *back_weights
    )
    branch_far, up_moved, gate_parts, branch_near, qkv_near, text_near, rows_near, gain_near = fence(
        branch_far, up_moved, gate_parts, branch_near, qkv_near, text_near, rows_near, gain_near
    )

    up_grad = plan.by_rep(plan.total(up_kept, up_moved))
    up_grad, branch_far, down_moved = fence(up_grad, pair(branch_far), down_moved)
    up_parts = plan.reduce(up_grad)
    down_moved = plan.move(down_moved)
    branch_far, qkv_far, text_far, rows_far, gain_far = attend_back(
        scalars[1], branch_far, kept_far, *back_weights
    )
    captions, normed_rows = (captions_near, captions_far), (normed_near, normed_far)
    text_rows, qkv_rows, branches = (text_near, text_far), (qkv_near, qkv_far), (branch_near, branch_far)
    qkv_moved = plan.product_moved(normed_rows, qkv_rows)
    down_moved, up_parts, text_rows, qkv_rows, branches, rows_far, gain_far, qkv_moved, hidden_rows = fence(
        down_moved, up_parts, text_rows, qkv_rows, branches, rows_far, gain_far, qkv_moved, hidden_rows
    )

    qkv_moved = plan.move(qkv_moved)
    down_grad = plan.total(down_kept, down_moved).reshape(rep_count, -1, D)
    across = settle(rows_far).astype(bf16)
    mixed_rows = (kept_near[6], kept_far[6])
    across, down_grad, text_rows, qkv_rows, branches, hidden_rows, mixed_rows = fence(
        across, down_grad, text_rows, qkv_rows, branches, hidden_rows, mixed_rows
    )
    down_parts = plan.reduce(down_grad)
    arrived = settle_move(across)
    mixed_rows = [plan.ordered(rows) for rows in mixed_rows]
    if plan.aligned:
        halves = [slice(0, rank_width // 2), slice(rank_width // 2, None)]
        out_kept, out_moved = [
            product([side[:, lanes] for side in mixed_rows], branches, 0, rank_width // 2, bf16)
            for lanes in halves
        ]
        if hi_count == 2:
            out_moved = swap(out_moved, "hi")
        else:
            out_moved = plan.move(jnp.concatenate([out_kept, out_moved]))
    else:
        out_kept, out_moved = (), ()
    text_moved = plan.product_moved(captions, text_rows)
    qkv_kept = plan.product_kept(normed_rows, qkv_rows)
    qkv_moved, arrived, text_moved, out_kept, out_moved, qkv_kept, text_rows, hidden_rows = fence(
        qkv_moved, arrived, text_moved, out_kept, out_moved, qkv_kept, text_rows, hidden_rows
    )

    text_moved = plan.move(text_moved)
    qkv_grad = plan.by_rep(plan.total(qkv_kept, qkv_moved))
    if plan.aligned:
        out_grad = plan.total(out_kept.astype(f32), out_moved) if hi_count == 2 else out_moved
        out_grad = out_grad.reshape(rep_count, -1, 3 * rank_width)
        qkv_grad = jnp.concatenate([qkv_grad, out_grad], axis=1)
    else:
        at = (jnp.arange(RANKS) == plan.rank).astype(bf16)[:, None, None]
        out_grad = product(mixed_rows, branches, 0, rank_width, bf16)
        out_grad = (out_grad[None] * at).reshape(D, D)
    qkv_grad, text_rows, hidden_rows, rows_near = fence(qkv_grad, text_rows, hidden_rows, rows_near)
    qkv_parts = plan.reduce(qkv_grad)
    result_far = result_part(hidden_rows[1], down_rank)
    result_near = result_part(hidden_rows[0], down_rank)
    text_kept = plan.product_kept(captions, text_rows)
    result_arrived = settle_move(settle(result_far).astype(bf16))
    grad_normed = plan.ordered(settle(rows_near) + arrived.astype(f32))
    _, pull_attn_norm = jax.vjp(modulate, token_rows, gain_rows[0], scale_attn)
    grad_token_norm, grad_attn_gain, grad_scale_attn = pull_attn_norm(
        grad_normed.reshape(item_count, item_len, D)
    )
    gain_terms = gain_near + gain_far
    gain_terms = gain_terms.at[3].multiply(1.0 - cross_gate**2)
    gain_terms = [plan.place_lanes(row) for row in gain_terms]
    (
        text_moved,
        down_parts,
        text_kept,
        qkv_parts,
        result_arrived,
        result_near,
        grad_scale_attn,
        grad_attn_gain,
        gain_terms,
    ) = fence(
        text_moved,
        down_parts,
        text_kept,
        qkv_parts,
        result_arrived,
        result_near,
        grad_scale_attn,
        grad_attn_gain,
        gain_terms,
    )

    text_grad = plan.text_by_rep(plan.total(text_kept, text_moved))
    text_grad, result_near, result_arrived, qkv_parts = fence(
        text_grad, result_near, result_arrived, qkv_parts
    )
    text_parts = plan.reduce(text_grad)
    if plan.aligned:
        out_parts = qkv_parts[RANKS * rows :].reshape(-1, D)
        qkv_parts = qkv_parts[: RANKS * rows]
    else:
        out_parts = lax.psum_scatter(out_grad, AXES, scatter_dimension=0, tiled=True)
    result = (settle(result_near) + result_arrived.astype(f32)).reshape(item_count, item_len, D)
    grad_mlp_gate = jnp.sum(grad_top * result, axis=1) * (1.0 - jnp.tanh(gate_mlp) ** 2)
    layer_out = (middle + mlp_gate * result).astype(bf16).reshape(row_count, D)
    tokens_grad = (grad_middle + grad_token_norm).reshape(row_count, D)

    grad_modulation = jnp.concatenate(
        [grad_scale_attn, grad_attn_gate, grad_scale_mlp, grad_mlp_gate], axis=1
    ).astype(bf16)
    gains_grad = jnp.stack(
        [grad_attn_gain, gain_terms[0], gain_terms[1], gain_terms[2], grad_mlp_gain, gain_terms[3]]
    ).astype(bf16)
    gain_blocks = jnp.moveaxis(gains_grad.reshape(6, devices, -1), 1, 0)
    gain_blocks = gain_blocks.reshape(devices, item_count, -1)
    modulations = jnp.broadcast_to(grad_modulation, (devices,) + grad_modulation.shape)
    both = lax.all_to_all(
        jnp.concatenate([modulations, gain_blocks], axis=2), AXES, 0, 0, tiled=True
    )
    def whole(parts, weight, sections, groups):
        blocks = trade_ranks(parts.reshape(RANKS, weight.shape[0], -1))
        return plan.from_ranks(blocks, sections, groups).astype(f32)

    both, qkv_parts, gate_parts, up_parts, layer_out, tokens_grad = fence(
        both, qkv_parts, gate_parts, up_parts, layer_out, tokens_grad
    )
    gate_up_weight_grad = whole(
        jnp.concatenate([gate_parts, up_parts], axis=-1), gate_up_weight, 2, hi_count
    )
    ada_weight_grad = lax.dot_general(
        activated_mine.reshape(devices, item_count, rows),
        both[:, :, : 4 * D],
        (((0, 1), (0, 1)), ((), ())),
        preferred_element_type=f32,
    )
    norm_gains_grad = jnp.sum(both[:, :, 4 * D :].astype(f32), axis=0).reshape(6, -1)
    qkv_weight_grad = whole(qkv_parts, qkv_weight, 3, plan.head_groups)
    gate_up_weight_grad, qkv_weight_grad, text_parts = fence(
        gate_up_weight_grad, qkv_weight_grad, text_parts
    )
    text_weight_grad = whole(text_parts, text_weight, 2, plan.head_groups)
    down_weight_grad, out_weight_grad = down_parts.astype(f32), out_parts.astype(f32)
    return (
        layer_out,
        tokens_grad,
        norm_gains_grad,
        ada_weight_grad,
        qkv_weight_grad,
        out_weight_grad,
        text_weight_grad,
        gate_up_weight_grad,
        down_weight_grad,
    )


def solution(mesh):
    grp, rep = mesh.devices.shape
    hi = grp // RANKS
    inner = Mesh(mesh.devices.reshape(hi, 2, 2, rep), AXES)
    rows = P(AXES, None)

    def step(*arrays):
        return local(hi, rep, *arrays)

    return jax.shard_map(
        step,
        mesh=inner,
        in_specs=(
            rows,
            rows,
            P(AXES, None, None),
            P(AXES),
            P(AXES),
            rows,
            P(None, AXES),
            rows,
            rows,
            rows,
            rows,
            rows,
            rows,
        ),
        out_specs=(rows, rows, P(None, AXES), rows, rows, rows, rows, rows, rows),
        check_vma=False,
    )
```

```python
import math

import jax
import jax.numpy as jnp
from jax import lax
from jax.experimental import pallas as pl
from jax.experimental.pallas import tpu as pltpu
from jax.sharding import Mesh
from jax.sharding import PartitionSpec as P

D = 1536
HEADS = 24
HEAD_DIM = 64
TEXT_DIM = 4096
FF = 4096
SIDE = 16
RANKS = 4
LANES = 128
MIB = 1 << 20
AXES = ("hi", "mid", "core", "rep")


EPSILON = 1e-06


def norm_rows(values, gain_row):
    return (
        values * lax.rsqrt(jnp.mean(values * values, axis=-1, keepdims=True) + EPSILON) * gain_row
    )


def rope_tables(item_kind, item_len):
    position = jnp.arange(item_len, dtype=jnp.int32)[None, :]
    half_side = SIDE // 2
    frame_index = position // (half_side * half_side)
    within = position % (half_side * half_side)
    is_clip = item_kind[:, None] == 1
    row_index = jnp.where(is_clip, frame_index * half_side + within // half_side, position // SIDE)
    columns = jnp.where(is_clip, within % half_side, position % SIDE)
    lane_index = jnp.arange(HEAD_DIM, dtype=jnp.int32)
    quarter = HEAD_DIM // 4
    frequency = jnp.exp(-(lane_index % quarter).astype(jnp.float32) * (math.log(10000.0) / quarter))
    coordinate = jnp.where(
        lane_index[None, None, :] < 2 * quarter, row_index[:, :, None], columns[:, :, None]
    ).astype(jnp.float32)
    angles = coordinate * frequency
    return (jnp.cos(angles), jnp.sin(angles))


def modulate(values, gain_row, scaling):
    return norm_rows(values, gain_row) * (1.0 + scaling[:, None, :])


def silu_product(gate_half, up_half):
    return jax.nn.silu(gate_half) * up_half


def dot(left, right):
    return jnp.dot(left, right, preferred_element_type=jnp.float32)


def dot_left(left, right):
    return lax.dot_general(left, right, (((0,), (0,)), ((), ())), preferred_element_type=jnp.float32)


def dot_right(left, right):
    return lax.dot_general(left, right, (((1,), (1,)), ((), ())), preferred_element_type=jnp.float32)


def lane_index(shape):
    return lax.broadcasted_iota(jnp.int32, shape, len(shape) - 1)

def head_sums(values):
    first = lane_index(values.shape) < HEAD_DIM
    low = jnp.sum(jnp.where(first, values, 0.0), axis=-1, keepdims=True)
    high = jnp.sum(jnp.where(first, 0.0, values), axis=-1, keepdims=True)
    return jnp.where(first, low, high)

def partner(values):
    quarter = HEAD_DIM // 4
    width = values.shape[-1]
    low = lane_index(values.shape) % (2 * quarter) < quarter
    return jnp.where(low, pltpu.roll(values, width - quarter, 1), pltpu.roll(values, quarter, 1))

def stack_heads(values):
    first = lane_index(values.shape) < HEAD_DIM
    zero = jnp.zeros_like(values)
    return jnp.concatenate([jnp.where(first, values, zero), jnp.where(first, zero, values)])

def join_heads(stacked):
    rows = stacked.shape[0] // 2
    first = lane_index((rows, stacked.shape[1])) < HEAD_DIM
    return jnp.where(first, stacked[:rows], stacked[rows:])

def inverse_rms(raw):
    return lax.rsqrt(head_sums(raw * raw) * (1.0 / HEAD_DIM) + EPSILON)

def rows_of(ref):
    return ref.shape[0]


def dot_cut(rows, mine, other):
    half = mine.shape[0]
    return dot(rows[:, :half], mine[...]) + dot(rows[:, half:], other[...])


def attend_kernel(
    kind_ref,
    len_ref,
    rows_ref,
    core_rows_ref,
    caption_ref,
    core_caption_ref,
    qkv_mine_ref,
    qkv_other_ref,
    key_mine_ref,
    key_other_ref,
    value_mine_ref,
    value_other_ref,
    out_weight_ref,
    gain_ref,
    cos_ref,
    sin_ref,
    rows_out_ref,
    caption_out_ref,
    qkv_ref,
    text_ref,
    text_value_ref,
    q_ref,
    k_ref,
    tk_ref,
    mixed_ref,
    read_ref,
    branch_ref,
    core_branch_ref,
):
    item = pl.program_id(0)
    own = item < pl.num_programs(0) // 2
    kind, length = kind_ref[item], len_ref[item]
    width = q_ref.shape[1]
    positions = pl.ds(kind * rows_of(q_ref), rows_of(q_ref))
    cosine, sine = cos_ref[positions, :], sin_ref[positions, :]
    scaling = HEAD_DIM ** (-0.5)

    @pl.when(own)
    def _():
        rows_out_ref[...] = rows_ref[...]
        caption_out_ref[...] = caption_ref[...]

    @pl.when(jnp.logical_not(own))
    def _():
        rows_out_ref[...] = core_rows_ref[...]
        caption_out_ref[...] = core_caption_ref[...]

    qkv_ref[...] = dot_cut(rows_out_ref, qkv_mine_ref, qkv_other_ref)
    text_ref[...] = dot_cut(caption_out_ref, key_mine_ref, key_other_ref)
    text_value_ref[...] = dot_cut(caption_out_ref, value_mine_ref, value_other_ref)
    for at in range(0, width, LANES):
        lanes = slice(at, at + LANES)
        turned = []
        for part, out_ref in ((0, q_ref), (1, k_ref)):
            raw = qkv_ref[:, part * width + at : part * width + at + LANES]
            normal = raw * inverse_rms(raw) * gain_ref[part : part + 1, lanes]
            rows = (normal * cosine + partner(normal) * sine).astype(jnp.bfloat16)
            out_ref[:, lanes] = rows
            turned.append(rows)
        queries, keys = turned
        values = qkv_ref[:, 2 * width + at : 2 * width + at + LANES].astype(jnp.bfloat16)
        text_raw = text_ref[:, lanes]
        text_keys = (text_raw * inverse_rms(text_raw) * gain_ref[2:3, lanes]).astype(jnp.bfloat16)
        tk_ref[:, lanes] = text_keys
        text_values = text_value_ref[:, lanes].astype(jnp.bfloat16)
        stacked = stack_heads(queries)
        scores = dot_right(stacked, keys) * scaling
        scores = jnp.exp(scores - jnp.max(scores, axis=-1, keepdims=True))
        own_out = dot(scores.astype(jnp.bfloat16), values) / jnp.sum(scores, axis=-1, keepdims=True)
        text = dot_right(stacked, text_keys) * scaling
        text = jnp.where(lane_index(text.shape) < length, text, -1e30)
        text = jnp.exp(text - jnp.max(text, axis=-1, keepdims=True))
        text_out = dot(text.astype(jnp.bfloat16), text_values) / jnp.sum(text, axis=-1, keepdims=True)
        read = join_heads(text_out)
        read_ref[:, lanes] = read
        mixed_ref[:, lanes] = (join_heads(own_out) + gain_ref[3:4, lanes] * read).astype(jnp.bfloat16)

    branch = dot(mixed_ref[...], out_weight_ref[...])

    @pl.when(own)
    def _():
        branch_ref[...] = branch

    @pl.when(jnp.logical_not(own))
    def _():
        core_branch_ref[...] = branch.astype(jnp.bfloat16)


def head_norm_back(grad, raw, gain_row):
    inverse = inverse_rms(raw)
    scaled = grad * gain_row
    normal = raw * inverse
    inner = head_sums(scaled * normal) * (1.0 / HEAD_DIM)
    return inverse * (scaled - normal * inner), jnp.sum(grad * normal, axis=0, keepdims=True)

def attend_back_kernel(
    kind_ref,
    len_ref,
    branch_ref,
    core_branch_ref,
    qkv_ref,
    text_ref,
    text_value_ref,
    q_ref,
    k_ref,
    tk_ref,
    read_ref,
    qkv_mine_ref,
    qkv_other_ref,
    out_weight_ref,
    gain_ref,
    cos_ref,
    sin_ref,
    branch_out_ref,
    gqkv_ref,
    gtext_ref,
    grad_rows_ref,
    core_grad_rows_ref,
    gains_ref,
    mixed_ref,
):
    item = pl.program_id(0)
    own = item < pl.num_programs(0) // 2
    kind, length = kind_ref[item], len_ref[item]
    width = q_ref.shape[1]
    positions = pl.ds(kind * rows_of(q_ref), rows_of(q_ref))
    cosine, sine = cos_ref[positions, :], sin_ref[positions, :]
    scaling = HEAD_DIM ** (-0.5)

    @pl.when(own)
    def _():
        branch_out_ref[...] = branch_ref[...]

    @pl.when(jnp.logical_not(own))
    def _():
        branch_out_ref[...] = core_branch_ref[...]

    mixed_ref[...] = dot_right(branch_out_ref[...], out_weight_ref[...])

    @pl.when(item == 0)
    def _():
        gains_ref[...] = jnp.zeros_like(gains_ref)

    def one(stacked, keys, values, stacked_grad, valid):
        scores = dot_right(keys, stacked) * scaling
        if valid is not None:
            scores = jnp.where(valid(scores.shape), scores, -1e30)
        probs = jnp.exp(scores - jnp.max(scores, axis=0, keepdims=True))
        probs = probs * (1.0 / jnp.sum(probs, axis=0, keepdims=True))
        grad_values = dot(probs.astype(jnp.bfloat16), stacked_grad)
        grad_probs = dot_right(values, stacked_grad)
        inner = jnp.sum(probs * grad_probs, axis=0, keepdims=True)
        grad_scores = (probs * (grad_probs - inner)).astype(jnp.bfloat16)
        grad_keys = dot(grad_scores, stacked) * scaling
        grad_queries = dot_left(keys, grad_scores)
        return grad_queries, grad_keys, grad_values

    for at in range(0, width, LANES):
        lanes = slice(at, at + LANES)
        grad = mixed_ref[:, lanes]
        cross = gain_ref[3:4, lanes]
        values = qkv_ref[:, 2 * width + at : 2 * width + at + LANES].astype(jnp.bfloat16)
        text_values = text_value_ref[:, lanes].astype(jnp.bfloat16)
        stacked = stack_heads(q_ref[:, lanes])
        own_queries, own_keys, own_values = one(
            stacked, k_ref[:, lanes], values, stack_heads(grad.astype(jnp.bfloat16)), None
        )
        read_queries, read_keys, read_values = one(
            stacked, tk_ref[:, lanes], text_values, stack_heads((cross * grad).astype(jnp.bfloat16)),
            lambda shape: lax.broadcasted_iota(jnp.int32, shape, 0) < length,
        )
        grad_queries = join_heads((own_queries + read_queries).T) * scaling
        for part, turned in ((0, grad_queries), (1, own_keys)):
            raw = qkv_ref[:, part * width + at : part * width + at + LANES]
            back = turned * cosine + partner(turned * sine)
            grad_raw, gain = head_norm_back(back, raw, gain_ref[part : part + 1, lanes])
            gqkv_ref[:, part * width + at : part * width + at + LANES] = grad_raw.astype(jnp.bfloat16)
            gains_ref[part : part + 1, lanes] += gain
        gqkv_ref[:, 2 * width + at : 2 * width + at + LANES] = own_values.astype(jnp.bfloat16)
        grad_text, gain = head_norm_back(read_keys, text_ref[:, lanes], gain_ref[2:3, lanes])
        gtext_ref[:, lanes] = grad_text.astype(jnp.bfloat16)
        gains_ref[2:3, lanes] += gain
        gtext_ref[:, width + at : width + at + LANES] = read_values.astype(jnp.bfloat16)
        gains_ref[3:4, lanes] += jnp.sum(grad * read_ref[:, lanes], axis=0, keepdims=True)

    half = qkv_mine_ref.shape[0]
    low = dot_right(gqkv_ref[...], qkv_mine_ref[...])
    high = dot_right(gqkv_ref[...], qkv_other_ref[...])

    @pl.when(own)
    def _():
        grad_rows_ref[:, :half] = low
        grad_rows_ref[:, half:] = high

    @pl.when(jnp.logical_not(own))
    def _():
        core_grad_rows_ref[:, :half] = low.astype(jnp.bfloat16)
        core_grad_rows_ref[:, half:] = high.astype(jnp.bfloat16)


def whole_spec(array):
    zeros = (0,) * len(array.shape)
    return pl.BlockSpec(array.shape, lambda *_: zeros, pipeline_mode=pl.Buffered(1))


def mine_spec(array, steps):
    half = steps // 2
    return pl.BlockSpec(
        (array.shape[0] // half, array.shape[1]), lambda i, *_: (jnp.minimum(i, half - 1), 0)
    )


def core_spec(array, steps):
    half = steps // 2
    return pl.BlockSpec(
        (array.shape[0] // half, array.shape[1]), lambda i, *_: (jnp.maximum(i - half, 0), 0)
    )


def pair_specs(pair_of_arrays, steps):
    return [mine_spec(pair_of_arrays[0], steps), core_spec(pair_of_arrays[1], steps)]


def step_spec(array, steps):
    return pl.BlockSpec((array.shape[0] // steps, array.shape[1]), lambda i, *_: (i, 0))


def summed_spec(array):
    return pl.BlockSpec(array.shape, lambda i, *_: (0, 0))


def shaped(count, columns, dtype=jnp.bfloat16):
    return jax.ShapeDtypeStruct((count, columns), dtype)


def parameters():
    return pltpu.CompilerParams(dimension_semantics=("arbitrary",), vmem_limit_bytes=58 * MIB)


def attend(scalars, rows, captions, qkv_rank, key_rank, value_rank, out_rank, tables):
    items = scalars[0].shape[0]
    count, width = 2 * rows[0].shape[0], out_rank.shape[0]
    text_count = 2 * captions[0].shape[0]
    outs = [
        shaped(count, D),
        shaped(text_count, TEXT_DIM),
        shaped(count, 3 * width, jnp.float32),
        shaped(text_count, width, jnp.float32),
        shaped(text_count, width, jnp.float32),
        shaped(count, width),
        shaped(count, width),
        shaped(text_count, width),
        shaped(count, width),
        shaped(count, width, jnp.float32),
    ]
    branch = (shaped(count // 2, D, jnp.float32), shaped(count // 2, D))
    whole = [*qkv_rank, *key_rank, *value_rank, out_rank, *tables]
    rows, captions, *kept, branch_mine, branch_core = pl.pallas_call(
        attend_kernel,
        grid_spec=pltpu.PrefetchScalarGridSpec(
            num_scalar_prefetch=2,
            grid=(items,),
            in_specs=pair_specs(rows, items)
            + pair_specs(captions, items)
            + [whole_spec(array) for array in whole],
            out_specs=[step_spec(array, items) for array in outs] + pair_specs(branch, items),
        ),
        out_shape=[*outs, *branch],
        compiler_params=parameters(),
        name="attend",
    )(*scalars, *rows, *captions, *whole)
    return rows, captions, kept, (branch_mine, branch_core)


def attend_back(scalars, grad_branch, kept, qkv_rank, out_rank, tables):
    items = scalars[0].shape[0]
    qkv_raw, text_raw, text_value_raw, queries, keys, text_keys, _, read = kept
    count, width = queries.shape
    outs = [
        shaped(count, D),
        shaped(count, 3 * width),
        shaped(text_raw.shape[0], 2 * width),
    ]
    rows = (shaped(count // 2, D, jnp.float32), shaped(count // 2, D))
    gains = shaped(4, width, jnp.float32)
    by_item = [qkv_raw, text_raw, text_value_raw, queries, keys, text_keys, read]
    whole = [*qkv_rank, out_rank, *tables]
    branch, qkv, text, rows_mine, rows_core, gains = pl.pallas_call(
        attend_back_kernel,
        grid_spec=pltpu.PrefetchScalarGridSpec(
            num_scalar_prefetch=2,
            grid=(items,),
            in_specs=pair_specs(grad_branch, items)
            + [step_spec(array, items) for array in by_item]
            + [whole_spec(array) for array in whole],
            out_specs=[step_spec(array, items) for array in outs]
            + pair_specs(rows, items)
            + [summed_spec(gains)],
            scratch_shapes=[pltpu.VMEM((count // items, width), jnp.float32)],
        ),
        out_shape=[*outs, *rows, gains],
        compiler_params=parameters(),
        name="attend_back",
    )(*scalars, *grad_branch, *by_item, *whole)
    return branch, qkv, text, (rows_mine, rows_core), gains


def row_cuts(lefts, rights):
    cuts, left, right, left_row, right_row = [], 0, 0, 0, 0
    while left < len(lefts):
        count = min(lefts[left].shape[0] - left_row, rights[right].shape[0] - right_row)
        cuts.append((left, left_row, right, right_row, count))
        left_row, right_row = left_row + count, right_row + count
        if left_row == lefts[left].shape[0]:
            left, left_row = left + 1, 0
        if right_row == rights[right].shape[0]:
            right, right_row = right + 1, 0
    return cuts


def product(lefts, rights, first, lanes, dtype):
    columns = rights[0].shape[1]
    if lanes % LANES:
        block = lanes
    else:
        block = 384 if lanes % 384 == 0 else math.gcd(lanes, 512)
    cuts = row_cuts(lefts, rights)

    def kernel(first_ref, *refs):
        left_refs, right_refs, out_ref = refs[: len(lefts)], refs[len(lefts) : -1], refs[-1]
        total = None
        for left, left_row, right, right_row, count in cuts:
            term = dot_left(
                left_refs[left][left_row : left_row + count, :],
                right_refs[right][right_row : right_row + count, :],
            )
            total = term if total is None else total + term
        out_ref[...] = total.astype(out_ref.dtype)

    return pl.pallas_call(
        kernel,
        grid_spec=pltpu.PrefetchScalarGridSpec(
            num_scalar_prefetch=1,
            grid=(lanes // block,),
            in_specs=[
                pl.BlockSpec((array.shape[0], block), lambda i, first: (0, first[0] // block + i))
                for array in lefts
            ]
            + [whole_spec(array) for array in rights],
            out_specs=pl.BlockSpec((block, columns), lambda i, first: (i, 0)),
        ),
        out_shape=shaped(lanes, columns, dtype),
        compiler_params=parameters(),
        name="product",
    )(jnp.reshape(first, (1,)).astype(jnp.int32), *lefts, *rights)


def feed_kernel(
    rows_ref,
    core_rows_ref,
    result_ref,
    core_result_ref,
    gate_mine_ref,
    gate_other_ref,
    up_mine_ref,
    up_other_ref,
    down_ref,
    rows,
    result,
    hidden_ref,
    grad_gate_ref,
    grad_up_ref,
    grad_ref,
    core_grad_ref,
):
    own = pl.program_id(0) < pl.num_programs(0) // 2

    @pl.when(own)
    def _():
        rows[...] = rows_ref[...]
        result[...] = result_ref[...]

    @pl.when(jnp.logical_not(own))
    def _():
        rows[...] = core_rows_ref[...]
        result[...] = core_result_ref[...]

    gate = dot_cut(rows, gate_mine_ref, gate_other_ref)
    up = dot_cut(rows, up_mine_ref, up_other_ref)
    grad_hidden = dot_right(result[...], down_ref[...])
    sigmoid = 1.0 / (1.0 + jnp.exp(-gate))
    silu = gate * sigmoid
    hidden_ref[...] = (silu * up).astype(jnp.bfloat16)
    grad_gate = (grad_hidden * up * (sigmoid + silu * (1.0 - sigmoid))).astype(jnp.bfloat16)
    grad_up = (grad_hidden * silu).astype(jnp.bfloat16)
    grad_gate_ref[...] = grad_gate
    grad_up_ref[...] = grad_up
    half = gate_mine_ref.shape[0]
    low = dot_right(grad_gate, gate_mine_ref[...]) + dot_right(grad_up, up_mine_ref[...])
    high = dot_right(grad_gate, gate_other_ref[...]) + dot_right(grad_up, up_other_ref[...])

    @pl.when(own)
    def _():
        grad_ref[:, :half] = low
        grad_ref[:, half:] = high

    @pl.when(jnp.logical_not(own))
    def _():
        core_grad_ref[:, :half] = low.astype(jnp.bfloat16)
        core_grad_ref[:, half:] = high.astype(jnp.bfloat16)


def feed(rows, grad_result, gate_rank, up_rank, down_rank):
    count, width = 2 * rows[0].shape[0], down_rank.shape[0]
    block = 256
    steps = count // block
    outs = [shaped(count, D)] * 2 + [shaped(count, width)] * 3
    grads = (shaped(count // 2, D, jnp.float32), shaped(count // 2, D))
    whole = [*gate_rank, *up_rank, down_rank]
    *outs, grad_mine, grad_core = pl.pallas_call(
        feed_kernel,
        grid=(steps,),
        in_specs=pair_specs(rows, steps)
        + pair_specs(grad_result, steps)
        + [whole_spec(array) for array in whole],
        out_specs=[step_spec(array, steps) for array in outs] + pair_specs(grads, steps),
        out_shape=[*outs, *grads],
        compiler_params=parameters(),
        name="feed",
    )(*rows, *grad_result, *whole)
    return *outs, (grad_mine, grad_core)


def result_kernel(hidden_ref, down_ref, result_ref, core_result_ref):
    own = pl.program_id(0) < pl.num_programs(0) // 2
    rows = dot(hidden_ref[...], down_ref[...])

    @pl.when(own)
    def _():
        result_ref[...] = rows

    @pl.when(jnp.logical_not(own))
    def _():
        core_result_ref[...] = rows.astype(jnp.bfloat16)


def result_part(hidden, down_rank):
    count = hidden.shape[0]
    steps = count // 256
    outs = (shaped(count // 2, D, jnp.float32), shaped(count // 2, D))
    return pl.pallas_call(
        result_kernel,
        grid=(steps,),
        in_specs=[step_spec(hidden, steps), whole_spec(down_rank)],
        out_specs=pair_specs(outs, steps),
        out_shape=outs,
        compiler_params=parameters(),
        name="result",
    )(hidden, down_rank)


def swap(block, axis, count=2, step=1):
    return lax.ppermute(block, axis, [(at, at ^ step) for at in range(count)])


def spread(block, axis, count):
    if count & (count - 1):
        return lax.all_gather(block, axis)
    block, step = block[None], 1
    while step < count:
        other = swap(block, axis, count, step)
        low = (lax.axis_index(axis) & step) == 0
        block = jnp.where(
            low, jnp.concatenate([block, other]), jnp.concatenate([other, block])
        )
        step *= 2
    return block


def fold(block, axis, count):
    if count & (count - 1):
        return lax.psum_scatter(block, axis, scatter_dimension=0)
    step = count // 2
    while step:
        half = block.shape[0] // 2
        low = (lax.axis_index(axis) & step) == 0
        lower, upper = block[:half], block[half:]
        block = jnp.where(low, lower, upper) + swap(
            jnp.where(low, upper, lower), axis, count, step
        )
        step //= 2
    return block[0]


def trade_ranks(block):
    return lax.all_to_all(block, ("mid", "core"), 0, 0, tiled=True)


def pick(stack, index):
    return lax.dynamic_index_in_dim(stack, index, 0, keepdims=False)


def pair(rows):
    return (rows, swap(rows, "core"))


def settle(partial):
    mine, core = partial
    return mine + swap(core, "core").astype(jnp.float32)


def settle_move(across):
    return swap(across, "mid")


class Layout:
    def __init__(self, hi, rep, out_rows):
        self.hi, self.rep = hi, rep
        self.aligned = (rep * out_rows) % HEAD_DIM == 0
        self.head_groups = hi if self.aligned else 1
        self.rank = lax.axis_index("mid") * 2 + lax.axis_index("core")

    def by_rank(self, weight, sections, groups):
        rows, columns = weight.shape
        width = columns // (sections * groups * RANKS)
        view = weight.reshape(rows, sections * groups, RANKS, width)
        view = jnp.transpose(view, (2, 0, 1, 3))
        return view.reshape(RANKS, rows, sections * groups * width)

    def from_ranks(self, blocks, sections, groups):
        _, rows, per_rank = blocks.shape
        width = per_rank // (sections * groups)
        view = blocks.reshape(RANKS, rows, sections * groups, width)
        return jnp.transpose(view, (1, 2, 0, 3)).reshape(rows, RANKS * per_rank)

    def ordered(self, values):
        if self.hi != 2:
            return values
        half = values.shape[-1] // 2
        turned = jnp.concatenate([values[..., half:], values[..., :half]], axis=-1)
        return jnp.where(lax.axis_index("hi") == 0, values, turned)

    def ordered_text(self, values):
        if self.hi != 2:
            return values
        view = values.reshape(values.shape[0], self.hi, RANKS, self.rep, -1)
        return self.ordered(jnp.swapaxes(view, 2, 3).reshape(values.shape))

    def text_halves(self, blocks):
        return tuple(blocks) if self.hi == 2 else self.halves(blocks)

    def text_by_rep(self, summed):
        return summed.reshape(self.rep, -1, summed.shape[1]) if self.hi == 2 else self.by_rep(summed)

    def across_hi(self, block):
        if self.hi == 2:
            return (block, swap(block, "hi"))
        return spread(block, "hi", self.hi)

    def natural_hi(self, blocks):
        if self.hi != 2:
            return blocks
        mine, other = blocks
        low = lax.axis_index("hi") == 0
        return jnp.stack([jnp.where(low, mine, other), jnp.where(low, other, mine)])

    def halves(self, blocks):
        if self.hi == 2:
            return tuple(self.natural_rows(block[None]) for block in blocks)
        return tuple(jnp.split(self.natural_rows(blocks), 2))

    def natural_rows(self, stacked):
        view = stacked.reshape(stacked.shape[0], self.rep, RANKS, -1, stacked.shape[-1])
        return jnp.transpose(view, (0, 2, 1, 3, 4)).reshape(-1, stacked.shape[-1])

    def product_moved(self, lefts, rights, first=None):
        lanes = lefts[0].shape[1]
        if self.hi != 2:
            return product(lefts, rights, 0, lanes, jnp.bfloat16)
        return product(lefts, rights, lanes // 2 if first is None else first, lanes // 2, jnp.bfloat16)

    def move(self, moved):
        if self.hi == 2:
            return swap(moved, "hi")
        return fold(moved.reshape(self.hi, -1, moved.shape[1]), "hi", self.hi)

    def product_kept(self, lefts, rights, first=0):
        if self.hi != 2:
            return None
        return product(lefts, rights, first, lefts[0].shape[1] // 2, jnp.float32)

    def total(self, kept, arrived):
        if kept is None:
            return arrived
        return (kept + arrived.astype(jnp.float32)).astype(jnp.bfloat16)

    def by_rep(self, summed):
        view = summed.reshape(RANKS, self.rep, -1, summed.shape[1])
        return jnp.transpose(view, (1, 0, 2, 3)).reshape(self.rep, -1, summed.shape[1])

    def reduce(self, blocks):
        flat = blocks.reshape(-1, blocks.shape[-1])
        return lax.psum_scatter(flat, "rep", scatter_dimension=0, tiled=True)

    def rank_lanes(self, rows, groups):
        view = rows.reshape(rows.shape[0], groups, RANKS, -1)
        return lax.dynamic_index_in_dim(view, self.rank, 2, keepdims=False).reshape(rows.shape[0], -1)

    def place_lanes(self, row):
        view = row.reshape(self.head_groups, 1, -1)
        at = (jnp.arange(RANKS) == self.rank).astype(row.dtype)[None, :, None]
        return (view * at).reshape(-1)


def fence(*values):
    return lax.optimization_barrier(values)


def local(
    hi_count,
    rep_count,
    tokens,
    condition,
    caption,
    caption_len,
    item_kind,
    out_cotangent,
    norm_gains,
    ada_weight,
    qkv_weight,
    out_weight,
    text_weight,
    gate_up_weight,
    down_weight,
):
    bf16, f32 = jnp.bfloat16, jnp.float32
    item_count = condition.shape[0]
    item_len = tokens.shape[0] // item_count
    row_count = item_count * item_len
    rows = qkv_weight.shape[0]
    plan = Layout(hi_count, rep_count, out_weight.shape[0])
    rank_width = HEADS // RANKS * HEAD_DIM
    hi_at, mid_at, core_at, rep_at = [lax.axis_index(name) for name in AXES]
    device_shape = (hi_count, 2, 2, rep_count)

    feed_width = FF // RANKS
    devices = hi_count * RANKS * rep_count
    block_at = (hi_at * RANKS + plan.rank) * rep_count + rep_at

    def z_gather(block):
        return lax.all_gather(block.reshape(-1, block.shape[-1]), "rep", tiled=True)

    down_z = z_gather(down_weight)
    qkv_mine = trade_ranks(plan.by_rank(qkv_weight, 3, plan.head_groups))
    qkv_mine = qkv_mine.reshape(RANKS * rows, 3 * rank_width)
    if plan.aligned:
        qkv_mine = jnp.concatenate([qkv_mine, out_weight.reshape(-1, 3 * rank_width)])
    else:
        out_whole = lax.all_gather(out_weight, AXES, axis=0, tiled=True)
        out_rank = pick(out_whole.reshape(RANKS, rank_width, D), plan.rank)

    head = condition.reshape(item_count, devices, rows)
    head = jnp.transpose(head, (1, 0, 2)).reshape(devices, -1)
    rest = jnp.concatenate(
        [norm_gains.reshape(-1), caption_len.astype(bf16), item_kind.astype(bf16)]
    )
    small = jnp.concatenate([head, jnp.broadcast_to(rest, (devices, rest.size))], axis=1)
    small = lax.all_to_all(small, AXES, 0, 0, tiled=True)
    cut = [head.shape[1], head.shape[1] + norm_gains.size]
    cut.append(cut[1] + item_count)
    conditions, gains, lengths, kinds = jnp.split(small, cut, axis=-1)
    activated_mine = jax.nn.silu(conditions.astype(f32)).astype(bf16).reshape(-1, rows)
    gain_rows = jnp.moveaxis(gains.astype(f32).reshape(devices, 6, -1), 1, 0).reshape(6, D)
    lengths, kinds = [
        values.reshape(device_shape + (item_count,)) for values in (lengths, kinds)
    ]

    def group_items(values):
        view = lax.dynamic_index_in_dim(pick(values, hi_at), rep_at, 2, keepdims=False)
        near, far = pick(view, mid_at), pick(view, 1 - mid_at)
        order = [core_at, 1 - core_at]
        return [
            jnp.concatenate([pick(side, at) for at in order]).astype(jnp.int32)
            for side in (near, far)
        ]

    lengths_sides = group_items(lengths)
    kinds_sides = group_items(kinds)
    cosine, sine = rope_tables(jnp.arange(2), item_len)
    signs = jnp.where(jnp.arange(HEAD_DIM) % (HEAD_DIM // 2) < HEAD_DIM // 4, -1.0, 1.0)
    cosine, sine = [
        jnp.tile(table, (1, 1, LANES // HEAD_DIM)).reshape(-1, LANES) for table in (cosine, sine * signs)
    ]
    head_gains = plan.rank_lanes(gain_rows, plan.head_groups)
    cross_gate = jnp.tanh(head_gains[5])
    head_gains = jnp.concatenate([head_gains[1:4], cross_gate[None]])
    tables = (head_gains, cosine, sine)
    scalars = list(zip(kinds_sides, lengths_sides, strict=True))

    down_z, qkv_mine, text_weight, activated_mine = fence(
        down_z, qkv_mine, text_weight, activated_mine
    )
    qkv_z = z_gather(qkv_mine)
    down_rank = plan.across_hi(down_z)
    text_mine = trade_ranks(plan.by_rank(text_weight, 2, plan.head_groups))
    captions_near = pair(plan.ordered_text(caption.reshape(-1, TEXT_DIM)))
    partial = dot(activated_mine, ada_weight).astype(bf16).reshape(devices, item_count, 4 * D)
    gate_up_mine = trade_ranks(plan.by_rank(gate_up_weight, 2, hi_count))
    modulation = jnp.sum(lax.all_to_all(partial, AXES, 0, 0, tiled=True).astype(f32), axis=0)
    text_key_mine, text_value_mine = text_mine[..., :rank_width], text_mine[..., rank_width:]
    gate_mine, up_mine = gate_up_mine[..., :feed_width], gate_up_mine[..., feed_width:]
    qkv_z, down_rank, modulation, text_key_mine, text_value_mine, gate_mine, up_mine, captions_near = fence(
        qkv_z, down_rank, modulation, text_key_mine, text_value_mine, gate_mine, up_mine, captions_near
    )

    scale_attn, gate_attn, scale_mlp, gate_mlp = jnp.split(modulation, 4, axis=1)
    text_key_z = z_gather(text_key_mine)
    captions_far = swap(captions_near[0], "mid")
    qkv_rank = plan.across_hi(qkv_z)
    down_rank = plan.natural_hi(down_rank).reshape(feed_width, D)
    token_rows = tokens.astype(f32).reshape(item_count, item_len, D)
    normed = modulate(token_rows, gain_rows[0], scale_attn)
    normed = plan.ordered(normed.astype(bf16).reshape(row_count, D))
    mlp_gate = jnp.tanh(gate_mlp)[:, None, :]
    grad_top = out_cotangent.astype(f32).reshape(item_count, item_len, D)
    grad_result = (mlp_gate * grad_top).astype(bf16).reshape(row_count, D)
    normed_near, result_near = pair(normed), pair(grad_result)
    text_key_z, captions_far, qkv_rank, down_rank, normed_near, result_near, tables, scalars = fence(
        text_key_z, captions_far, qkv_rank, down_rank, normed_near, result_near, tables, scalars
    )

    text_value_z = z_gather(text_value_mine)
    text_key_rank = plan.across_hi(text_key_z)
    normed_far = swap(normed_near[0], "mid")
    captions_far = pair(captions_far)
    text_value_z, text_key_rank, normed_far, captions_far = fence(
        text_value_z, text_key_rank, normed_far, captions_far
    )

    gate_z = z_gather(gate_mine)
    text_value_rank = plan.across_hi(text_value_z)
    normed_far = pair(normed_far)
    if plan.aligned:
        blocks = [block.reshape(rep_count, -1, 3 * rank_width) for block in qkv_rank]
        out_rank = plan.natural_hi([block[:, RANKS * rows :].reshape(-1, D) for block in blocks])
        out_rank = out_rank.reshape(rank_width, D)
        qkv_rank = [block[:, : RANKS * rows].reshape(-1, 3 * rank_width) for block in blocks]
        qkv_rank = qkv_rank if hi_count == 2 else jnp.stack(qkv_rank)
    qkv_rank, text_key_rank = plan.halves(qkv_rank), plan.text_halves(text_key_rank)
    gate_z, text_value_rank, normed_far, qkv_rank, out_rank, text_key_rank = fence(
        gate_z, text_value_rank, normed_far, qkv_rank, out_rank, text_key_rank
    )

    up_z = z_gather(up_mine)
    gate_rank = plan.across_hi(gate_z)
    attend_weights = (qkv_rank, text_key_rank, plan.text_halves(text_value_rank), out_rank)
    normed_far, captions_far, kept_far, partial_far = attend(
        scalars[1], normed_far, captions_far, *attend_weights, tables
    )
    result_far = swap(result_near[0], "mid")
    up_z, gate_rank, result_far, normed_far, captions_far, kept_far, partial_far, attend_weights = fence(
        up_z, gate_rank, result_far, normed_far, captions_far, kept_far, partial_far, attend_weights
    )

    across = settle(partial_far).astype(bf16)
    across, normed_near, up_z = fence(across, normed_near, up_z)
    up_rank = plan.across_hi(up_z)
    arrived = settle_move(across)
    normed_near, captions_near, kept_near, partial_near = attend(
        scalars[0], normed_near, captions_near, *attend_weights, tables
    )
    result_far = pair(result_far)
    gate_rank = plan.halves(gate_rank)
    up_rank, arrived, normed_near, captions_near, kept_near, partial_near, result_far, gate_rank = fence(
        up_rank, arrived, normed_near, captions_near, kept_near, partial_near, result_far, gate_rank
    )

    branch = (settle(partial_near) + arrived.astype(f32)).reshape(item_count, item_len, D)
    attn_gate = jnp.tanh(gate_attn)[:, None, :]
    middle = token_rows + attn_gate * branch
    mlp_input = modulate(middle, gain_rows[4], scale_mlp)
    mlp_input = plan.ordered(mlp_input.astype(bf16).reshape(row_count, D))
    up_rank = plan.halves(up_rank)
    mlp_input, up_rank = fence(mlp_input, up_rank)

    feed_weights = (gate_rank, up_rank, down_rank)
    input_far = swap(mlp_input, "mid")
    input_near, result_near, hidden_near, gate_near, up_near, partial_near = feed(
        pair(mlp_input), result_near, *feed_weights
    )
    input_far, input_near, result_near, hidden_near, gate_near, up_near, partial_near = fence(
        input_far, input_near, result_near, hidden_near, gate_near, up_near, partial_near
    )
    input_far, result_far, hidden_far, gate_far, up_far, partial_far = feed(
        pair(input_far), result_far, *feed_weights
    )
    inputs, results = (input_near, input_far), (result_near, result_far)
    gate_rows, up_rows, hidden_rows = (gate_near, gate_far), (up_near, up_far), (hidden_near, hidden_far)
    across = settle(partial_far).astype(bf16)
    gate_moved = plan.product_moved(inputs, gate_rows)
    across, gate_moved, gate_rows, up_rows, hidden_rows = fence(
        across, gate_moved, gate_rows, up_rows, hidden_rows
    )
    arrived = settle_move(across)
    gate_moved = plan.move(gate_moved)
    up_moved = plan.product_moved(inputs, up_rows)
    hidden_first = hi_at * (feed_width // 2)
    down_moved = plan.product_moved(hidden_rows, results, feed_width // 2 - hidden_first)
    gate_kept = plan.product_kept(inputs, gate_rows)
    up_kept = plan.product_kept(inputs, up_rows)
    down_kept = plan.product_kept(hidden_rows, results, hidden_first)
    near = settle(partial_near)
    arrived, gate_moved, up_moved, down_moved, gate_kept, up_kept, down_kept, near = fence(
        arrived, gate_moved, up_moved, down_moved, gate_kept, up_kept, down_kept, near
    )

    up_moved = plan.move(up_moved)
    gate_grad = plan.by_rep(plan.total(gate_kept, gate_moved))
    gate_parts = plan.reduce(gate_grad)
    grad_mlp_input = plan.ordered(near + arrived.astype(f32))
    _, pull_mlp_norm = jax.vjp(modulate, middle, gain_rows[4], scale_mlp)
    grad_middle_norm, grad_mlp_gain, grad_scale_mlp = pull_mlp_norm(
        grad_mlp_input.reshape(item_count, item_len, D)
    )
    grad_middle = grad_top + grad_middle_norm
    grad_attn_gate = jnp.sum(grad_middle * branch, axis=1) * (1.0 - jnp.tanh(gate_attn) ** 2)
    grad_branch = (attn_gate * grad_middle).astype(bf16).reshape(row_count, D)
    (grad_branch,) = fence(grad_branch)

    branch_far = swap(grad_branch, "mid")
    back_weights = (qkv_rank, out_rank, tables)
    branch_near, qkv_near, text_near, rows_near, gain_near = attend_back(
        scalars[0], pair(grad_branch), kept_near, *back_weights
    )
    branch_far, up_moved, gate_parts, branch_near, qkv_near, text_near, rows_near, gain_near = fence(
        branch_far, up_moved, gate_parts, branch_near, qkv_near, text_near, rows_near, gain_near
    )

    up_grad = plan.by_rep(plan.total(up_kept, up_moved))
    up_grad, branch_far, down_moved = fence(up_grad, pair(branch_far), down_moved)
    up_parts = plan.reduce(up_grad)
    down_moved = plan.move(down_moved)
    branch_far, qkv_far, text_far, rows_far, gain_far = attend_back(
        scalars[1], branch_far, kept_far, *back_weights
    )
    captions, normed_rows = (captions_near, captions_far), (normed_near, normed_far)
    text_rows, qkv_rows, branches = (text_near, text_far), (qkv_near, qkv_far), (branch_near, branch_far)
    qkv_moved = plan.product_moved(normed_rows, qkv_rows)
    down_moved, up_parts, text_rows, qkv_rows, branches, rows_far, gain_far, qkv_moved, hidden_rows = fence(
        down_moved, up_parts, text_rows, qkv_rows, branches, rows_far, gain_far, qkv_moved, hidden_rows
    )

    qkv_moved = plan.move(qkv_moved)
    down_grad = plan.total(down_kept, down_moved).reshape(rep_count, -1, D)
    across = settle(rows_far).astype(bf16)
    mixed_rows = (kept_near[6], kept_far[6])
    across, down_grad, text_rows, qkv_rows, branches, hidden_rows, mixed_rows = fence(
        across, down_grad, text_rows, qkv_rows, branches, hidden_rows, mixed_rows
    )
    down_parts = plan.reduce(down_grad)
    arrived = settle_move(across)
    mixed_rows = [plan.ordered(rows) for rows in mixed_rows]
    if plan.aligned:
        halves = [slice(0, rank_width // 2), slice(rank_width // 2, None)]
        out_kept, out_moved = [
            product([side[:, lanes] for side in mixed_rows], branches, 0, rank_width // 2, bf16)
            for lanes in halves
        ]
        if hi_count == 2:
            out_moved = swap(out_moved, "hi")
        else:
            out_moved = plan.move(jnp.concatenate([out_kept, out_moved]))
    else:
        out_kept, out_moved = (), ()
    text_moved = plan.product_moved(captions, text_rows)
    qkv_kept = plan.product_kept(normed_rows, qkv_rows)
    result_far = result_part(hidden_rows[1], down_rank)
    qkv_moved, arrived, text_moved, out_kept, out_moved, qkv_kept, text_rows, hidden_rows, result_far = fence(
        qkv_moved, arrived, text_moved, out_kept, out_moved, qkv_kept, text_rows, hidden_rows, result_far
    )

    text_moved = plan.move(text_moved)
    qkv_grad = plan.by_rep(plan.total(qkv_kept, qkv_moved))
    if plan.aligned:
        out_grad = plan.total(out_kept.astype(f32), out_moved) if hi_count == 2 else out_moved
        out_grad = out_grad.reshape(rep_count, -1, 3 * rank_width)
        qkv_grad = jnp.concatenate([qkv_grad, out_grad], axis=1)
    else:
        at = (jnp.arange(RANKS) == plan.rank).astype(bf16)[:, None, None]
        out_grad = product(mixed_rows, branches, 0, rank_width, bf16)
        out_grad = (out_grad[None] * at).reshape(D, D)
    qkv_grad, text_rows, hidden_rows, rows_near = fence(qkv_grad, text_rows, hidden_rows, rows_near)
    qkv_parts = plan.reduce(qkv_grad)
    result_near = result_part(hidden_rows[0], down_rank)
    text_kept = plan.product_kept(captions, text_rows)
    result_arrived = settle_move(settle(result_far).astype(bf16))
    grad_normed = plan.ordered(settle(rows_near) + arrived.astype(f32))
    _, pull_attn_norm = jax.vjp(modulate, token_rows, gain_rows[0], scale_attn)
    grad_token_norm, grad_attn_gain, grad_scale_attn = pull_attn_norm(
        grad_normed.reshape(item_count, item_len, D)
    )
    text_kept, gate_parts, up_parts = fence(text_kept, gate_parts, up_parts)
    gate_up_parts = jnp.concatenate([gate_parts, up_parts], axis=-1)
    gate_up_parts = trade_ranks(gate_up_parts.reshape(RANKS, rows, -1))
    gate_up_weight_grad = plan.from_ranks(gate_up_parts, 2, hi_count).astype(f32)
    gain_terms = gain_near + gain_far
    gain_terms = gain_terms.at[3].multiply(1.0 - cross_gate**2)
    gain_terms = [plan.place_lanes(row) for row in gain_terms]
    (
        text_moved,
        down_parts,
        text_kept,
        qkv_parts,
        result_arrived,
        result_near,
        grad_scale_attn,
        grad_attn_gain,
        gate_up_weight_grad,
        gain_terms,
    ) = fence(
        text_moved,
        down_parts,
        text_kept,
        qkv_parts,
        result_arrived,
        result_near,
        grad_scale_attn,
        grad_attn_gain,
        gate_up_weight_grad,
        gain_terms,
    )

    text_grad = plan.text_by_rep(plan.total(text_kept, text_moved))
    text_grad, result_near, result_arrived, qkv_parts = fence(
        text_grad, result_near, result_arrived, qkv_parts
    )
    text_parts = plan.reduce(text_grad)
    if plan.aligned:
        out_parts = qkv_parts[RANKS * rows :].reshape(-1, D)
        qkv_parts = qkv_parts[: RANKS * rows]
    else:
        out_parts = lax.psum_scatter(out_grad, AXES, scatter_dimension=0, tiled=True)
    result = (settle(result_near) + result_arrived.astype(f32)).reshape(item_count, item_len, D)
    grad_mlp_gate = jnp.sum(grad_top * result, axis=1) * (1.0 - jnp.tanh(gate_mlp) ** 2)
    layer_out = (middle + mlp_gate * result).astype(bf16).reshape(row_count, D)
    tokens_grad = (grad_middle + grad_token_norm).reshape(row_count, D)

    def whole(parts, weight, sections, groups):
        blocks = trade_ranks(parts.reshape(RANKS, weight.shape[0], -1))
        return plan.from_ranks(blocks, sections, groups).astype(f32)

    qkv_blocks = trade_ranks(qkv_parts.reshape(RANKS, rows, -1))
    qkv_blocks, grad_mlp_gate = fence(qkv_blocks, grad_mlp_gate)
    qkv_weight_grad = plan.from_ranks(qkv_blocks, 3, plan.head_groups).astype(f32)

    grad_modulation = jnp.concatenate(
        [grad_scale_attn, grad_attn_gate, grad_scale_mlp, grad_mlp_gate], axis=1
    ).astype(bf16)
    gains_grad = jnp.stack(
        [grad_attn_gain, gain_terms[0], gain_terms[1], gain_terms[2], grad_mlp_gain, gain_terms[3]]
    ).astype(bf16)
    gain_blocks = jnp.moveaxis(gains_grad.reshape(6, devices, -1), 1, 0)
    gain_blocks = gain_blocks.reshape(devices, item_count, -1)
    modulations = jnp.broadcast_to(grad_modulation, (devices,) + grad_modulation.shape)
    both = lax.all_to_all(
        jnp.concatenate([modulations, gain_blocks], axis=2), AXES, 0, 0, tiled=True
    )
    both, layer_out, tokens_grad = fence(both, layer_out, tokens_grad)
    ada_weight_grad = lax.dot_general(
        activated_mine.reshape(devices, item_count, rows),
        both[:, :, : 4 * D],
        (((0, 1), (0, 1)), ((), ())),
        preferred_element_type=f32,
    )
    norm_gains_grad = jnp.sum(both[:, :, 4 * D :].astype(f32), axis=0).reshape(6, -1)
    both, text_parts = fence(both, text_parts)
    text_weight_grad = whole(text_parts, text_weight, 2, plan.head_groups)
    down_weight_grad, out_weight_grad = down_parts.astype(f32), out_parts.astype(f32)
    return (
        layer_out,
        tokens_grad,
        norm_gains_grad,
        ada_weight_grad,
        qkv_weight_grad,
        out_weight_grad,
        text_weight_grad,
        gate_up_weight_grad,
        down_weight_grad,
    )


def solution(mesh):
    grp, rep = mesh.devices.shape
    hi = grp // RANKS
    inner = Mesh(mesh.devices.reshape(hi, 2, 2, rep), AXES)
    rows = P(AXES, None)

    def step(*arrays):
        return local(hi, rep, *arrays)

    return jax.shard_map(
        step,
        mesh=inner,
        in_specs=(
            rows,
            rows,
            P(AXES, None, None),
            P(AXES),
            P(AXES),
            rows,
            P(None, AXES),
            rows,
            rows,
            rows,
            rows,
            rows,
            rows,
        ),
        out_specs=(rows, rows, P(None, AXES), rows, rows, rows, rows, rows, rows),
        check_vma=False,
    )
```

```python
import math

import jax
import jax.numpy as jnp
from jax import lax
from jax.experimental import pallas as pl
from jax.experimental.pallas import tpu as pltpu
from jax.sharding import Mesh
from jax.sharding import PartitionSpec as P

D = 1536
HEADS = 24
HEAD_DIM = 64
TEXT_DIM = 4096
FF = 4096
SIDE = 16
RANKS = 4
LANES = 128
MIB = 1 << 20
AXES = ("hi", "mid", "core", "rep")


EPSILON = 1e-06


def norm_rows(values, gain_row):
    return (
        values * lax.rsqrt(jnp.mean(values * values, axis=-1, keepdims=True) + EPSILON) * gain_row
    )


def rope_tables(item_kind, item_len):
    position = jnp.arange(item_len, dtype=jnp.int32)[None, :]
    half_side = SIDE // 2
    frame_index = position // (half_side * half_side)
    within = position % (half_side * half_side)
    is_clip = item_kind[:, None] == 1
    row_index = jnp.where(is_clip, frame_index * half_side + within // half_side, position // SIDE)
    columns = jnp.where(is_clip, within % half_side, position % SIDE)
    lane_index = jnp.arange(HEAD_DIM, dtype=jnp.int32)
    quarter = HEAD_DIM // 4
    frequency = jnp.exp(-(lane_index % quarter).astype(jnp.float32) * (math.log(10000.0) / quarter))
    coordinate = jnp.where(
        lane_index[None, None, :] < 2 * quarter, row_index[:, :, None], columns[:, :, None]
    ).astype(jnp.float32)
    angles = coordinate * frequency
    return (jnp.cos(angles), jnp.sin(angles))


def modulate(values, gain_row, scaling):
    return norm_rows(values, gain_row) * (1.0 + scaling[:, None, :])


def silu_product(gate_half, up_half):
    return jax.nn.silu(gate_half) * up_half


def dot(left, right):
    return jnp.dot(left, right, preferred_element_type=jnp.float32)


def dot_left(left, right):
    return lax.dot_general(left, right, (((0,), (0,)), ((), ())), preferred_element_type=jnp.float32)


def dot_right(left, right):
    return lax.dot_general(left, right, (((1,), (1,)), ((), ())), preferred_element_type=jnp.float32)


def lane_index(shape):
    return lax.broadcasted_iota(jnp.int32, shape, len(shape) - 1)

def head_sums(values):
    first = lane_index(values.shape) < HEAD_DIM
    low = jnp.sum(jnp.where(first, values, 0.0), axis=-1, keepdims=True)
    high = jnp.sum(jnp.where(first, 0.0, values), axis=-1, keepdims=True)
    return jnp.where(first, low, high)

def partner(values):
    quarter = HEAD_DIM // 4
    width = values.shape[-1]
    low = lane_index(values.shape) % (2 * quarter) < quarter
    return jnp.where(low, pltpu.roll(values, width - quarter, 1), pltpu.roll(values, quarter, 1))

def stack_heads(values):
    first = lane_index(values.shape) < HEAD_DIM
    zero = jnp.zeros_like(values)
    return jnp.concatenate([jnp.where(first, values, zero), jnp.where(first, zero, values)])

def join_heads(stacked):
    rows = stacked.shape[0] // 2
    first = lane_index((rows, stacked.shape[1])) < HEAD_DIM
    return jnp.where(first, stacked[:rows], stacked[rows:])

def inverse_rms(raw):
    return lax.rsqrt(head_sums(raw * raw) * (1.0 / HEAD_DIM) + EPSILON)

def rows_of(ref):
    return ref.shape[0]


def dot_cut(rows, mine, other):
    half = mine.shape[0]
    return dot(rows[:, :half], mine[...]) + dot(rows[:, half:], other[...])


def attend_kernel(
    kind_ref,
    len_ref,
    rows_ref,
    core_rows_ref,
    caption_ref,
    core_caption_ref,
    qkv_mine_ref,
    qkv_other_ref,
    key_mine_ref,
    key_other_ref,
    value_mine_ref,
    value_other_ref,
    out_weight_ref,
    gain_ref,
    cos_ref,
    sin_ref,
    rows_out_ref,
    caption_out_ref,
    qkv_ref,
    text_ref,
    text_value_ref,
    q_ref,
    k_ref,
    tk_ref,
    mixed_ref,
    read_ref,
    branch_ref,
    core_branch_ref,
):
    item = pl.program_id(0)
    own = item < pl.num_programs(0) // 2
    kind, length = kind_ref[item], len_ref[item]
    width = q_ref.shape[1]
    positions = pl.ds(kind * rows_of(q_ref), rows_of(q_ref))
    cosine, sine = cos_ref[positions, :], sin_ref[positions, :]
    scaling = HEAD_DIM ** (-0.5)

    @pl.when(own)
    def _():
        rows_out_ref[...] = rows_ref[...]
        caption_out_ref[...] = caption_ref[...]

    @pl.when(jnp.logical_not(own))
    def _():
        rows_out_ref[...] = core_rows_ref[...]
        caption_out_ref[...] = core_caption_ref[...]

    qkv_ref[...] = dot_cut(rows_out_ref, qkv_mine_ref, qkv_other_ref)
    text_ref[...] = dot_cut(caption_out_ref, key_mine_ref, key_other_ref)
    text_value_ref[...] = dot_cut(caption_out_ref, value_mine_ref, value_other_ref)
    for at in range(0, width, LANES):
        lanes = slice(at, at + LANES)
        turned = []
        for part, out_ref in ((0, q_ref), (1, k_ref)):
            raw = qkv_ref[:, part * width + at : part * width + at + LANES]
            normal = raw * inverse_rms(raw) * gain_ref[part : part + 1, lanes]
            rows = (normal * cosine + partner(normal) * sine).astype(jnp.bfloat16)
            out_ref[:, lanes] = rows
            turned.append(rows)
        queries, keys = turned
        values = qkv_ref[:, 2 * width + at : 2 * width + at + LANES].astype(jnp.bfloat16)
        text_raw = text_ref[:, lanes]
        text_keys = (text_raw * inverse_rms(text_raw) * gain_ref[2:3, lanes]).astype(jnp.bfloat16)
        tk_ref[:, lanes] = text_keys
        text_values = text_value_ref[:, lanes].astype(jnp.bfloat16)
        stacked = stack_heads(queries)
        scores = dot_right(stacked, keys) * scaling
        scores = jnp.exp(scores - jnp.max(scores, axis=-1, keepdims=True))
        own_out = dot(scores.astype(jnp.bfloat16), values) / jnp.sum(scores, axis=-1, keepdims=True)
        text = dot_right(stacked, text_keys) * scaling
        text = jnp.where(lane_index(text.shape) < length, text, -1e30)
        text = jnp.exp(text - jnp.max(text, axis=-1, keepdims=True))
        text_out = dot(text.astype(jnp.bfloat16), text_values) / jnp.sum(text, axis=-1, keepdims=True)
        read = join_heads(text_out)
        read_ref[:, lanes] = read
        mixed_ref[:, lanes] = (join_heads(own_out) + gain_ref[3:4, lanes] * read).astype(jnp.bfloat16)

    branch = dot(mixed_ref[...], out_weight_ref[...])

    @pl.when(own)
    def _():
        branch_ref[...] = branch

    @pl.when(jnp.logical_not(own))
    def _():
        core_branch_ref[...] = branch.astype(jnp.bfloat16)


def head_norm_back(grad, raw, gain_row):
    inverse = inverse_rms(raw)
    scaled = grad * gain_row
    normal = raw * inverse
    inner = head_sums(scaled * normal) * (1.0 / HEAD_DIM)
    return inverse * (scaled - normal * inner), jnp.sum(grad * normal, axis=0, keepdims=True)

def attend_back_kernel(
    kind_ref,
    len_ref,
    branch_ref,
    core_branch_ref,
    qkv_ref,
    text_ref,
    text_value_ref,
    q_ref,
    k_ref,
    tk_ref,
    read_ref,
    qkv_mine_ref,
    qkv_other_ref,
    out_weight_ref,
    gain_ref,
    cos_ref,
    sin_ref,
    branch_out_ref,
    gqkv_ref,
    gtext_ref,
    grad_rows_ref,
    core_grad_rows_ref,
    gains_ref,
    mixed_ref,
):
    item = pl.program_id(0)
    own = item < pl.num_programs(0) // 2
    kind, length = kind_ref[item], len_ref[item]
    width = q_ref.shape[1]
    positions = pl.ds(kind * rows_of(q_ref), rows_of(q_ref))
    cosine, sine = cos_ref[positions, :], sin_ref[positions, :]
    scaling = HEAD_DIM ** (-0.5)

    @pl.when(own)
    def _():
        branch_out_ref[...] = branch_ref[...]

    @pl.when(jnp.logical_not(own))
    def _():
        branch_out_ref[...] = core_branch_ref[...]

    mixed_ref[...] = dot_right(branch_out_ref[...], out_weight_ref[...])

    @pl.when(item == 0)
    def _():
        gains_ref[...] = jnp.zeros_like(gains_ref)

    def one(stacked, keys, values, stacked_grad, valid):
        scores = dot_right(keys, stacked) * scaling
        if valid is not None:
            scores = jnp.where(valid(scores.shape), scores, -1e30)
        probs = jnp.exp(scores - jnp.max(scores, axis=0, keepdims=True))
        probs = probs * (1.0 / jnp.sum(probs, axis=0, keepdims=True))
        grad_values = dot(probs.astype(jnp.bfloat16), stacked_grad)
        grad_probs = dot_right(values, stacked_grad)
        inner = jnp.sum(probs * grad_probs, axis=0, keepdims=True)
        grad_scores = (probs * (grad_probs - inner)).astype(jnp.bfloat16)
        grad_keys = dot(grad_scores, stacked) * scaling
        grad_queries = dot_left(keys, grad_scores)
        return grad_queries, grad_keys, grad_values

    for at in range(0, width, LANES):
        lanes = slice(at, at + LANES)
        grad = mixed_ref[:, lanes]
        cross = gain_ref[3:4, lanes]
        values = qkv_ref[:, 2 * width + at : 2 * width + at + LANES].astype(jnp.bfloat16)
        text_values = text_value_ref[:, lanes].astype(jnp.bfloat16)
        stacked = stack_heads(q_ref[:, lanes])
        own_queries, own_keys, own_values = one(
            stacked, k_ref[:, lanes], values, stack_heads(grad.astype(jnp.bfloat16)), None
        )
        read_queries, read_keys, read_values = one(
            stacked, tk_ref[:, lanes], text_values, stack_heads((cross * grad).astype(jnp.bfloat16)),
            lambda shape: lax.broadcasted_iota(jnp.int32, shape, 0) < length,
        )
        grad_queries = join_heads((own_queries + read_queries).T) * scaling
        for part, turned in ((0, grad_queries), (1, own_keys)):
            raw = qkv_ref[:, part * width + at : part * width + at + LANES]
            back = turned * cosine + partner(turned * sine)
            grad_raw, gain = head_norm_back(back, raw, gain_ref[part : part + 1, lanes])
            gqkv_ref[:, part * width + at : part * width + at + LANES] = grad_raw.astype(jnp.bfloat16)
            gains_ref[part : part + 1, lanes] += gain
        gqkv_ref[:, 2 * width + at : 2 * width + at + LANES] = own_values.astype(jnp.bfloat16)
        grad_text, gain = head_norm_back(read_keys, text_ref[:, lanes], gain_ref[2:3, lanes])
        gtext_ref[:, lanes] = grad_text.astype(jnp.bfloat16)
        gains_ref[2:3, lanes] += gain
        gtext_ref[:, width + at : width + at + LANES] = read_values.astype(jnp.bfloat16)
        gains_ref[3:4, lanes] += jnp.sum(grad * read_ref[:, lanes], axis=0, keepdims=True)

    half = qkv_mine_ref.shape[0]
    low = dot_right(gqkv_ref[...], qkv_mine_ref[...])
    high = dot_right(gqkv_ref[...], qkv_other_ref[...])

    @pl.when(own)
    def _():
        grad_rows_ref[:, :half] = low
        grad_rows_ref[:, half:] = high

    @pl.when(jnp.logical_not(own))
    def _():
        core_grad_rows_ref[:, :half] = low.astype(jnp.bfloat16)
        core_grad_rows_ref[:, half:] = high.astype(jnp.bfloat16)


def whole_spec(array):
    zeros = (0,) * len(array.shape)
    return pl.BlockSpec(array.shape, lambda *_: zeros, pipeline_mode=pl.Buffered(1))


def mine_spec(array, steps):
    half = steps // 2
    return pl.BlockSpec(
        (array.shape[0] // half, array.shape[1]), lambda i, *_: (jnp.minimum(i, half - 1), 0)
    )


def core_spec(array, steps):
    half = steps // 2
    return pl.BlockSpec(
        (array.shape[0] // half, array.shape[1]), lambda i, *_: (jnp.maximum(i - half, 0), 0)
    )


def pair_specs(pair_of_arrays, steps):
    return [mine_spec(pair_of_arrays[0], steps), core_spec(pair_of_arrays[1], steps)]


def step_spec(array, steps):
    return pl.BlockSpec((array.shape[0] // steps, array.shape[1]), lambda i, *_: (i, 0))


def summed_spec(array):
    return pl.BlockSpec(array.shape, lambda i, *_: (0, 0))


def shaped(count, columns, dtype=jnp.bfloat16):
    return jax.ShapeDtypeStruct((count, columns), dtype)


def parameters():
    return pltpu.CompilerParams(dimension_semantics=("arbitrary",), vmem_limit_bytes=58 * MIB)


def attend(scalars, rows, captions, qkv_rank, key_rank, value_rank, out_rank, tables):
    items = scalars[0].shape[0]
    count, width = 2 * rows[0].shape[0], out_rank.shape[0]
    text_count = 2 * captions[0].shape[0]
    outs = [
        shaped(count, D),
        shaped(text_count, TEXT_DIM),
        shaped(count, 3 * width, jnp.float32),
        shaped(text_count, width, jnp.float32),
        shaped(text_count, width, jnp.float32),
        shaped(count, width),
        shaped(count, width),
        shaped(text_count, width),
        shaped(count, width),
        shaped(count, width, jnp.float32),
    ]
    branch = (shaped(count // 2, D, jnp.float32), shaped(count // 2, D))
    whole = [*qkv_rank, *key_rank, *value_rank, out_rank, *tables]
    rows, captions, *kept, branch_mine, branch_core = pl.pallas_call(
        attend_kernel,
        grid_spec=pltpu.PrefetchScalarGridSpec(
            num_scalar_prefetch=2,
            grid=(items,),
            in_specs=pair_specs(rows, items)
            + pair_specs(captions, items)
            + [whole_spec(array) for array in whole],
            out_specs=[step_spec(array, items) for array in outs] + pair_specs(branch, items),
        ),
        out_shape=[*outs, *branch],
        compiler_params=parameters(),
        name="attend",
    )(*scalars, *rows, *captions, *whole)
    return rows, captions, kept, (branch_mine, branch_core)


def attend_back(scalars, grad_branch, kept, qkv_rank, out_rank, tables):
    items = scalars[0].shape[0]
    qkv_raw, text_raw, text_value_raw, queries, keys, text_keys, _, read = kept
    count, width = queries.shape
    outs = [
        shaped(count, D),
        shaped(count, 3 * width),
        shaped(text_raw.shape[0], 2 * width),
    ]
    rows = (shaped(count // 2, D, jnp.float32), shaped(count // 2, D))
    gains = shaped(4, width, jnp.float32)
    by_item = [qkv_raw, text_raw, text_value_raw, queries, keys, text_keys, read]
    whole = [*qkv_rank, out_rank, *tables]
    branch, qkv, text, rows_mine, rows_core, gains = pl.pallas_call(
        attend_back_kernel,
        grid_spec=pltpu.PrefetchScalarGridSpec(
            num_scalar_prefetch=2,
            grid=(items,),
            in_specs=pair_specs(grad_branch, items)
            + [step_spec(array, items) for array in by_item]
            + [whole_spec(array) for array in whole],
            out_specs=[step_spec(array, items) for array in outs]
            + pair_specs(rows, items)
            + [summed_spec(gains)],
            scratch_shapes=[pltpu.VMEM((count // items, width), jnp.float32)],
        ),
        out_shape=[*outs, *rows, gains],
        compiler_params=parameters(),
        name="attend_back",
    )(*scalars, *grad_branch, *by_item, *whole)
    return branch, qkv, text, (rows_mine, rows_core), gains


def row_cuts(lefts, rights):
    cuts, left, right, left_row, right_row = [], 0, 0, 0, 0
    while left < len(lefts):
        count = min(lefts[left].shape[0] - left_row, rights[right].shape[0] - right_row)
        cuts.append((left, left_row, right, right_row, count))
        left_row, right_row = left_row + count, right_row + count
        if left_row == lefts[left].shape[0]:
            left, left_row = left + 1, 0
        if right_row == rights[right].shape[0]:
            right, right_row = right + 1, 0
    return cuts


def product(lefts, rights, first, lanes, dtype):
    columns = rights[0].shape[1]
    if lanes % LANES:
        block = lanes
    else:
        block = 384 if lanes % 384 == 0 else math.gcd(lanes, 512)
    cuts = row_cuts(lefts, rights)

    def kernel(first_ref, *refs):
        left_refs, right_refs, out_ref = refs[: len(lefts)], refs[len(lefts) : -1], refs[-1]
        total = None
        for left, left_row, right, right_row, count in cuts:
            term = dot_left(
                left_refs[left][left_row : left_row + count, :],
                right_refs[right][right_row : right_row + count, :],
            )
            total = term if total is None else total + term
        out_ref[...] = total.astype(out_ref.dtype)

    return pl.pallas_call(
        kernel,
        grid_spec=pltpu.PrefetchScalarGridSpec(
            num_scalar_prefetch=1,
            grid=(lanes // block,),
            in_specs=[
                pl.BlockSpec((array.shape[0], block), lambda i, first: (0, first[0] // block + i))
                for array in lefts
            ]
            + [whole_spec(array) for array in rights],
            out_specs=pl.BlockSpec((block, columns), lambda i, first: (i, 0)),
        ),
        out_shape=shaped(lanes, columns, dtype),
        compiler_params=parameters(),
        name="product",
    )(jnp.reshape(first, (1,)).astype(jnp.int32), *lefts, *rights)


def feed_kernel(
    rows_ref,
    core_rows_ref,
    result_ref,
    core_result_ref,
    gate_mine_ref,
    gate_other_ref,
    up_mine_ref,
    up_other_ref,
    down_ref,
    rows,
    result,
    hidden_ref,
    grad_gate_ref,
    grad_up_ref,
    grad_ref,
    core_grad_ref,
):
    own = pl.program_id(0) < pl.num_programs(0) // 2

    @pl.when(own)
    def _():
        rows[...] = rows_ref[...]
        result[...] = result_ref[...]

    @pl.when(jnp.logical_not(own))
    def _():
        rows[...] = core_rows_ref[...]
        result[...] = core_result_ref[...]

    gate = dot_cut(rows, gate_mine_ref, gate_other_ref)
    up = dot_cut(rows, up_mine_ref, up_other_ref)
    grad_hidden = dot_right(result[...], down_ref[...])
    sigmoid = 1.0 / (1.0 + jnp.exp(-gate))
    silu = gate * sigmoid
    hidden_ref[...] = (silu * up).astype(jnp.bfloat16)
    grad_gate = (grad_hidden * up * (sigmoid + silu * (1.0 - sigmoid))).astype(jnp.bfloat16)
    grad_up = (grad_hidden * silu).astype(jnp.bfloat16)
    grad_gate_ref[...] = grad_gate
    grad_up_ref[...] = grad_up
    half = gate_mine_ref.shape[0]
    low = dot_right(grad_gate, gate_mine_ref[...]) + dot_right(grad_up, up_mine_ref[...])
    high = dot_right(grad_gate, gate_other_ref[...]) + dot_right(grad_up, up_other_ref[...])

    @pl.when(own)
    def _():
        grad_ref[:, :half] = low
        grad_ref[:, half:] = high

    @pl.when(jnp.logical_not(own))
    def _():
        core_grad_ref[:, :half] = low.astype(jnp.bfloat16)
        core_grad_ref[:, half:] = high.astype(jnp.bfloat16)


def feed(rows, grad_result, gate_rank, up_rank, down_rank):
    count, width = 2 * rows[0].shape[0], down_rank.shape[0]
    block = 256
    steps = count // block
    outs = [shaped(count, D)] * 2 + [shaped(count, width)] * 3
    grads = (shaped(count // 2, D, jnp.float32), shaped(count // 2, D))
    whole = [*gate_rank, *up_rank, down_rank]
    *outs, grad_mine, grad_core = pl.pallas_call(
        feed_kernel,
        grid=(steps,),
        in_specs=pair_specs(rows, steps)
        + pair_specs(grad_result, steps)
        + [whole_spec(array) for array in whole],
        out_specs=[step_spec(array, steps) for array in outs] + pair_specs(grads, steps),
        out_shape=[*outs, *grads],
        compiler_params=parameters(),
        name="feed",
    )(*rows, *grad_result, *whole)
    return *outs, (grad_mine, grad_core)


def result_kernel(hidden_ref, down_ref, result_ref, core_result_ref):
    own = pl.program_id(0) < pl.num_programs(0) // 2
    rows = dot(hidden_ref[...], down_ref[...])

    @pl.when(own)
    def _():
        result_ref[...] = rows

    @pl.when(jnp.logical_not(own))
    def _():
        core_result_ref[...] = rows.astype(jnp.bfloat16)


def result_part(hidden, down_rank):
    count = hidden.shape[0]
    steps = count // 256
    outs = (shaped(count // 2, D, jnp.float32), shaped(count // 2, D))
    return pl.pallas_call(
        result_kernel,
        grid=(steps,),
        in_specs=[step_spec(hidden, steps), whole_spec(down_rank)],
        out_specs=pair_specs(outs, steps),
        out_shape=outs,
        compiler_params=parameters(),
        name="result",
    )(hidden, down_rank)


def swap(block, axis, count=2, step=1):
    return lax.ppermute(block, axis, [(at, at ^ step) for at in range(count)])


def spread(block, axis, count):
    if count & (count - 1):
        return lax.all_gather(block, axis)
    block, step = block[None], 1
    while step < count:
        other = swap(block, axis, count, step)
        low = (lax.axis_index(axis) & step) == 0
        block = jnp.where(
            low, jnp.concatenate([block, other]), jnp.concatenate([other, block])
        )
        step *= 2
    return block


def fold(block, axis, count):
    if count & (count - 1):
        return lax.psum_scatter(block, axis, scatter_dimension=0)
    step = count // 2
    while step:
        half = block.shape[0] // 2
        low = (lax.axis_index(axis) & step) == 0
        lower, upper = block[:half], block[half:]
        block = jnp.where(low, lower, upper) + swap(
            jnp.where(low, upper, lower), axis, count, step
        )
        step //= 2
    return block[0]


def trade_ranks(block):
    return lax.all_to_all(block, ("mid", "core"), 0, 0, tiled=True)


def pick(stack, index):
    return lax.dynamic_index_in_dim(stack, index, 0, keepdims=False)


def pair(rows):
    return (rows, swap(rows, "core"))


def settle(partial):
    mine, core = partial
    return mine + swap(core, "core").astype(jnp.float32)


def settle_move(across):
    return swap(across, "mid")


class Layout:
    def __init__(self, hi, rep, out_rows):
        self.hi, self.rep = hi, rep
        self.aligned = (rep * out_rows) % HEAD_DIM == 0
        self.head_groups = hi if self.aligned else 1
        self.rank = lax.axis_index("mid") * 2 + lax.axis_index("core")

    def by_rank(self, weight, sections, groups):
        rows, columns = weight.shape
        width = columns // (sections * groups * RANKS)
        view = weight.reshape(rows, sections * groups, RANKS, width)
        view = jnp.transpose(view, (2, 0, 1, 3))
        return view.reshape(RANKS, rows, sections * groups * width)

    def from_ranks(self, blocks, sections, groups):
        _, rows, per_rank = blocks.shape
        width = per_rank // (sections * groups)
        view = blocks.reshape(RANKS, rows, sections * groups, width)
        return jnp.transpose(view, (1, 2, 0, 3)).reshape(rows, RANKS * per_rank)

    def ordered(self, values):
        if self.hi != 2:
            return values
        half = values.shape[-1] // 2
        turned = jnp.concatenate([values[..., half:], values[..., :half]], axis=-1)
        return jnp.where(lax.axis_index("hi") == 0, values, turned)

    def ordered_text(self, values):
        if self.hi != 2:
            return values
        view = values.reshape(values.shape[0], self.hi, RANKS, self.rep, -1)
        return self.ordered(jnp.swapaxes(view, 2, 3).reshape(values.shape))

    def text_halves(self, blocks):
        return tuple(blocks) if self.hi == 2 else self.halves(blocks)

    def text_by_rep(self, summed):
        return summed.reshape(self.rep, -1, summed.shape[1]) if self.hi == 2 else self.by_rep(summed)

    def across_hi(self, block):
        if self.hi == 2:
            return (block, swap(block, "hi"))
        return spread(block, "hi", self.hi)

    def natural_hi(self, blocks):
        if self.hi != 2:
            return blocks
        mine, other = blocks
        low = lax.axis_index("hi") == 0
        return jnp.stack([jnp.where(low, mine, other), jnp.where(low, other, mine)])

    def halves(self, blocks):
        if self.hi == 2:
            return tuple(self.natural_rows(block[None]) for block in blocks)
        return tuple(jnp.split(self.natural_rows(blocks), 2))

    def natural_rows(self, stacked):
        view = stacked.reshape(stacked.shape[0], self.rep, RANKS, -1, stacked.shape[-1])
        return jnp.transpose(view, (0, 2, 1, 3, 4)).reshape(-1, stacked.shape[-1])

    def product_moved(self, lefts, rights, first=None):
        lanes = lefts[0].shape[1]
        if self.hi != 2:
            return product(lefts, rights, 0, lanes, jnp.bfloat16)
        return product(lefts, rights, lanes // 2 if first is None else first, lanes // 2, jnp.bfloat16)

    def move(self, moved):
        if self.hi == 2:
            return swap(moved, "hi")
        return fold(moved.reshape(self.hi, -1, moved.shape[1]), "hi", self.hi)

    def product_kept(self, lefts, rights, first=0):
        if self.hi != 2:
            return None
        return product(lefts, rights, first, lefts[0].shape[1] // 2, jnp.float32)

    def total(self, kept, arrived):
        if kept is None:
            return arrived
        return (kept + arrived.astype(jnp.float32)).astype(jnp.bfloat16)

    def by_rep(self, summed):
        view = summed.reshape(RANKS, self.rep, -1, summed.shape[1])
        return jnp.transpose(view, (1, 0, 2, 3)).reshape(self.rep, -1, summed.shape[1])

    def reduce(self, blocks):
        flat = blocks.reshape(-1, blocks.shape[-1])
        return lax.psum_scatter(flat, "rep", scatter_dimension=0, tiled=True)

    def rank_lanes(self, rows, groups):
        view = rows.reshape(rows.shape[0], groups, RANKS, -1)
        return lax.dynamic_index_in_dim(view, self.rank, 2, keepdims=False).reshape(rows.shape[0], -1)

    def place_lanes(self, row):
        view = row.reshape(self.head_groups, 1, -1)
        at = (jnp.arange(RANKS) == self.rank).astype(row.dtype)[None, :, None]
        return (view * at).reshape(-1)


def fence(*values):
    return lax.optimization_barrier(values)


def local(
    hi_count,
    rep_count,
    tokens,
    condition,
    caption,
    caption_len,
    item_kind,
    out_cotangent,
    norm_gains,
    ada_weight,
    qkv_weight,
    out_weight,
    text_weight,
    gate_up_weight,
    down_weight,
):
    bf16, f32 = jnp.bfloat16, jnp.float32
    item_count = condition.shape[0]
    item_len = tokens.shape[0] // item_count
    row_count = item_count * item_len
    rows = qkv_weight.shape[0]
    plan = Layout(hi_count, rep_count, out_weight.shape[0])
    rank_width = HEADS // RANKS * HEAD_DIM
    hi_at, mid_at, core_at, rep_at = [lax.axis_index(name) for name in AXES]
    device_shape = (hi_count, 2, 2, rep_count)

    feed_width = FF // RANKS
    devices = hi_count * RANKS * rep_count
    block_at = (hi_at * RANKS + plan.rank) * rep_count + rep_at

    def z_gather(block):
        return lax.all_gather(block.reshape(-1, block.shape[-1]), "rep", tiled=True)

    down_z = z_gather(down_weight)
    qkv_mine = trade_ranks(plan.by_rank(qkv_weight, 3, plan.head_groups))
    qkv_mine = qkv_mine.reshape(RANKS * rows, 3 * rank_width)
    if plan.aligned:
        qkv_mine = jnp.concatenate([qkv_mine, out_weight.reshape(-1, 3 * rank_width)])
    else:
        out_whole = lax.all_gather(out_weight, AXES, axis=0, tiled=True)
        out_rank = pick(out_whole.reshape(RANKS, rank_width, D), plan.rank)

    head = condition.reshape(item_count, devices, rows)
    head = jnp.transpose(head, (1, 0, 2)).reshape(devices, -1)
    rest = jnp.concatenate(
        [norm_gains.reshape(-1), caption_len.astype(bf16), item_kind.astype(bf16)]
    )
    small = jnp.concatenate([head, jnp.broadcast_to(rest, (devices, rest.size))], axis=1)
    small = lax.all_to_all(small, AXES, 0, 0, tiled=True)
    cut = [head.shape[1], head.shape[1] + norm_gains.size]
    cut.append(cut[1] + item_count)
    conditions, gains, lengths, kinds = jnp.split(small, cut, axis=-1)
    activated_mine = jax.nn.silu(conditions.astype(f32)).astype(bf16).reshape(-1, rows)
    gain_rows = jnp.moveaxis(gains.astype(f32).reshape(devices, 6, -1), 1, 0).reshape(6, D)
    lengths, kinds = [
        values.reshape(device_shape + (item_count,)) for values in (lengths, kinds)
    ]

    def group_items(values):
        view = lax.dynamic_index_in_dim(pick(values, hi_at), rep_at, 2, keepdims=False)
        near, far = pick(view, mid_at), pick(view, 1 - mid_at)
        order = [core_at, 1 - core_at]
        return [
            jnp.concatenate([pick(side, at) for at in order]).astype(jnp.int32)
            for side in (near, far)
        ]

    lengths_sides = group_items(lengths)
    kinds_sides = group_items(kinds)
    cosine, sine = rope_tables(jnp.arange(2), item_len)
    signs = jnp.where(jnp.arange(HEAD_DIM) % (HEAD_DIM // 2) < HEAD_DIM // 4, -1.0, 1.0)
    cosine, sine = [
        jnp.tile(table, (1, 1, LANES // HEAD_DIM)).reshape(-1, LANES) for table in (cosine, sine * signs)
    ]
    head_gains = plan.rank_lanes(gain_rows, plan.head_groups)
    cross_gate = jnp.tanh(head_gains[5])
    head_gains = jnp.concatenate([head_gains[1:4], cross_gate[None]])
    tables = (head_gains, cosine, sine)
    scalars = list(zip(kinds_sides, lengths_sides, strict=True))

    down_z, qkv_mine, text_weight, activated_mine = fence(
        down_z, qkv_mine, text_weight, activated_mine
    )
    qkv_z = z_gather(qkv_mine)
    down_rank = plan.across_hi(down_z)
    text_mine = trade_ranks(plan.by_rank(text_weight, 2, plan.head_groups))
    captions_near = pair(plan.ordered_text(caption.reshape(-1, TEXT_DIM)))
    partial = dot(activated_mine, ada_weight).astype(bf16).reshape(devices, item_count, 4 * D)
    gate_up_mine = trade_ranks(plan.by_rank(gate_up_weight, 2, hi_count))
    modulation = jnp.sum(lax.all_to_all(partial, AXES, 0, 0, tiled=True).astype(f32), axis=0)
    text_key_mine, text_value_mine = text_mine[..., :rank_width], text_mine[..., rank_width:]
    gate_mine, up_mine = gate_up_mine[..., :feed_width], gate_up_mine[..., feed_width:]
    qkv_z, down_rank, modulation, text_key_mine, text_value_mine, gate_mine, up_mine, captions_near = fence(
        qkv_z, down_rank, modulation, text_key_mine, text_value_mine, gate_mine, up_mine, captions_near
    )

    scale_attn, gate_attn, scale_mlp, gate_mlp = jnp.split(modulation, 4, axis=1)
    text_key_z = z_gather(text_key_mine)
    captions_far = swap(captions_near[0], "mid")
    qkv_rank = plan.across_hi(qkv_z)
    token_rows = tokens.astype(f32).reshape(item_count, item_len, D)
    normed = modulate(token_rows, gain_rows[0], scale_attn)
    normed = plan.ordered(normed.astype(bf16).reshape(row_count, D))
    mlp_gate = jnp.tanh(gate_mlp)[:, None, :]
    grad_top = out_cotangent.astype(f32).reshape(item_count, item_len, D)
    grad_result = (mlp_gate * grad_top).astype(bf16).reshape(row_count, D)
    normed_near, result_near = pair(normed), pair(grad_result)
    text_key_z, captions_far, qkv_rank, normed_near, result_near, tables, scalars = fence(
        text_key_z, captions_far, qkv_rank, normed_near, result_near, tables, scalars
    )

    text_value_z = z_gather(text_value_mine)
    text_key_rank = plan.across_hi(text_key_z)
    normed_far = swap(normed_near[0], "mid")
    captions_far = pair(captions_far)
    text_value_z, text_key_rank, normed_far, captions_far = fence(
        text_value_z, text_key_rank, normed_far, captions_far
    )

    gate_z = z_gather(gate_mine)
    text_value_rank = plan.across_hi(text_value_z)
    normed_far = pair(normed_far)
    if plan.aligned:
        blocks = [block.reshape(rep_count, -1, 3 * rank_width) for block in qkv_rank]
        out_rank = plan.natural_hi([block[:, RANKS * rows :].reshape(-1, D) for block in blocks])
        out_rank = out_rank.reshape(rank_width, D)
        qkv_rank = [block[:, : RANKS * rows].reshape(-1, 3 * rank_width) for block in blocks]
        qkv_rank = qkv_rank if hi_count == 2 else jnp.stack(qkv_rank)
    qkv_rank, text_key_rank = plan.halves(qkv_rank), plan.text_halves(text_key_rank)
    gate_z, text_value_rank, normed_far, qkv_rank, out_rank, text_key_rank = fence(
        gate_z, text_value_rank, normed_far, qkv_rank, out_rank, text_key_rank
    )

    up_z = z_gather(up_mine)
    gate_rank = plan.across_hi(gate_z)
    attend_weights = (qkv_rank, text_key_rank, plan.text_halves(text_value_rank), out_rank)
    normed_far, captions_far, kept_far, partial_far = attend(
        scalars[1], normed_far, captions_far, *attend_weights, tables
    )
    down_rank = plan.natural_hi(down_rank).reshape(feed_width, D)
    result_far = swap(result_near[0], "mid")
    down_rank, up_z, gate_rank, result_far, normed_far, captions_far, kept_far, partial_far, attend_weights = fence(
        down_rank, up_z, gate_rank, result_far, normed_far, captions_far, kept_far, partial_far, attend_weights
    )

    across = settle(partial_far).astype(bf16)
    across, normed_near, up_z = fence(across, normed_near, up_z)
    up_rank = plan.across_hi(up_z)
    arrived = settle_move(across)
    normed_near, captions_near, kept_near, partial_near = attend(
        scalars[0], normed_near, captions_near, *attend_weights, tables
    )
    result_far = pair(result_far)
    gate_rank = plan.halves(gate_rank)
    up_rank, arrived, normed_near, captions_near, kept_near, partial_near, result_far, gate_rank = fence(
        up_rank, arrived, normed_near, captions_near, kept_near, partial_near, result_far, gate_rank
    )

    branch = (settle(partial_near) + arrived.astype(f32)).reshape(item_count, item_len, D)
    attn_gate = jnp.tanh(gate_attn)[:, None, :]
    middle = token_rows + attn_gate * branch
    mlp_input = modulate(middle, gain_rows[4], scale_mlp)
    mlp_input = plan.ordered(mlp_input.astype(bf16).reshape(row_count, D))
    up_rank = plan.halves(up_rank)
    mlp_input, up_rank = fence(mlp_input, up_rank)

    feed_weights = (gate_rank, up_rank, down_rank)
    input_far = swap(mlp_input, "mid")
    input_near, result_near, hidden_near, gate_near, up_near, partial_near = feed(
        pair(mlp_input), result_near, *feed_weights
    )
    input_far, input_near, result_near, hidden_near, gate_near, up_near, partial_near = fence(
        input_far, input_near, result_near, hidden_near, gate_near, up_near, partial_near
    )
    input_far, result_far, hidden_far, gate_far, up_far, partial_far = feed(
        pair(input_far), result_far, *feed_weights
    )
    inputs, results = (input_near, input_far), (result_near, result_far)
    gate_rows, up_rows, hidden_rows = (gate_near, gate_far), (up_near, up_far), (hidden_near, hidden_far)
    across = settle(partial_far).astype(bf16)
    gate_moved = plan.product_moved(inputs, gate_rows)
    across, gate_moved, gate_rows, up_rows, hidden_rows = fence(
        across, gate_moved, gate_rows, up_rows, hidden_rows
    )
    arrived = settle_move(across)
    gate_moved = plan.move(gate_moved)
    up_moved = plan.product_moved(inputs, up_rows)
    hidden_first = hi_at * (feed_width // 2)
    down_moved = plan.product_moved(hidden_rows, results, feed_width // 2 - hidden_first)
    gate_kept = plan.product_kept(inputs, gate_rows)
    up_kept = plan.product_kept(inputs, up_rows)
    down_kept = plan.product_kept(hidden_rows, results, hidden_first)
    near = settle(partial_near)
    arrived, gate_moved, up_moved, down_moved, gate_kept, up_kept, down_kept, near = fence(
        arrived, gate_moved, up_moved, down_moved, gate_kept, up_kept, down_kept, near
    )

    up_moved = plan.move(up_moved)
    gate_grad = plan.by_rep(plan.total(gate_kept, gate_moved))
    gate_parts = plan.reduce(gate_grad)
    grad_mlp_input = plan.ordered(near + arrived.astype(f32))
    _, pull_mlp_norm = jax.vjp(modulate, middle, gain_rows[4], scale_mlp)
    grad_middle_norm, grad_mlp_gain, grad_scale_mlp = pull_mlp_norm(
        grad_mlp_input.reshape(item_count, item_len, D)
    )
    grad_middle = grad_top + grad_middle_norm
    grad_attn_gate = jnp.sum(grad_middle * branch, axis=1) * (1.0 - jnp.tanh(gate_attn) ** 2)
    grad_branch = (attn_gate * grad_middle).astype(bf16).reshape(row_count, D)
    (grad_branch,) = fence(grad_branch)

    branch_far = swap(grad_branch, "mid")
    back_weights = (qkv_rank, out_rank, tables)
    branch_near, qkv_near, text_near, rows_near, gain_near = attend_back(
        scalars[0], pair(grad_branch), kept_near, *back_weights
    )
    branch_far, up_moved, gate_parts, branch_near, qkv_near, text_near, rows_near, gain_near = fence(
        branch_far, up_moved, gate_parts, branch_near, qkv_near, text_near, rows_near, gain_near
    )

    up_grad = plan.by_rep(plan.total(up_kept, up_moved))
    up_grad, branch_far, down_moved = fence(up_grad, pair(branch_far), down_moved)
    up_parts = plan.reduce(up_grad)
    down_moved = plan.move(down_moved)
    branch_far, qkv_far, text_far, rows_far, gain_far = attend_back(
        scalars[1], branch_far, kept_far, *back_weights
    )
    captions, normed_rows = (captions_near, captions_far), (normed_near, normed_far)
    text_rows, qkv_rows, branches = (text_near, text_far), (qkv_near, qkv_far), (branch_near, branch_far)
    qkv_moved = plan.product_moved(normed_rows, qkv_rows)
    down_moved, up_parts, text_rows, qkv_rows, branches, rows_far, gain_far, qkv_moved, hidden_rows = fence(
        down_moved, up_parts, text_rows, qkv_rows, branches, rows_far, gain_far, qkv_moved, hidden_rows
    )

    qkv_moved = plan.move(qkv_moved)
    down_grad = plan.total(down_kept, down_moved).reshape(rep_count, -1, D)
    across = settle(rows_far).astype(bf16)
    mixed_rows = (kept_near[6], kept_far[6])
    across, down_grad, text_rows, qkv_rows, branches, hidden_rows, mixed_rows = fence(
        across, down_grad, text_rows, qkv_rows, branches, hidden_rows, mixed_rows
    )
    down_parts = plan.reduce(down_grad)
    arrived = settle_move(across)
    mixed_rows = [plan.ordered(rows) for rows in mixed_rows]
    if plan.aligned:
        halves = [slice(0, rank_width // 2), slice(rank_width // 2, None)]
        out_kept, out_moved = [
            product([side[:, lanes] for side in mixed_rows], branches, 0, rank_width // 2, bf16)
            for lanes in halves
        ]
        if hi_count == 2:
            out_moved = swap(out_moved, "hi")
        else:
            out_moved = plan.move(jnp.concatenate([out_kept, out_moved]))
    else:
        out_kept, out_moved = (), ()
    text_moved = plan.product_moved(captions, text_rows)
    qkv_kept = plan.product_kept(normed_rows, qkv_rows)
    result_far = result_part(hidden_rows[1], down_rank)
    qkv_moved, arrived, text_moved, out_kept, out_moved, qkv_kept, text_rows, hidden_rows, result_far = fence(
        qkv_moved, arrived, text_moved, out_kept, out_moved, qkv_kept, text_rows, hidden_rows, result_far
    )

    text_moved = plan.move(text_moved)
    qkv_grad = plan.by_rep(plan.total(qkv_kept, qkv_moved))
    if plan.aligned:
        out_grad = plan.total(out_kept.astype(f32), out_moved) if hi_count == 2 else out_moved
        out_grad = out_grad.reshape(rep_count, -1, 3 * rank_width)
        qkv_grad = jnp.concatenate([qkv_grad, out_grad], axis=1)
    else:
        at = (jnp.arange(RANKS) == plan.rank).astype(bf16)[:, None, None]
        out_grad = product(mixed_rows, branches, 0, rank_width, bf16)
        out_grad = (out_grad[None] * at).reshape(D, D)
    qkv_grad, text_rows, hidden_rows, rows_near = fence(qkv_grad, text_rows, hidden_rows, rows_near)
    qkv_parts = plan.reduce(qkv_grad)
    result_near = result_part(hidden_rows[0], down_rank)
    text_kept = plan.product_kept(captions, text_rows)
    result_arrived = settle_move(settle(result_far).astype(bf16))
    grad_normed = plan.ordered(settle(rows_near) + arrived.astype(f32))
    _, pull_attn_norm = jax.vjp(modulate, token_rows, gain_rows[0], scale_attn)
    grad_token_norm, grad_attn_gain, grad_scale_attn = pull_attn_norm(
        grad_normed.reshape(item_count, item_len, D)
    )
    text_kept, gate_parts, up_parts = fence(text_kept, gate_parts, up_parts)
    gate_up_parts = jnp.concatenate([gate_parts, up_parts], axis=-1)
    gate_up_parts = trade_ranks(gate_up_parts.reshape(RANKS, rows, -1))
    gate_up_weight_grad = plan.from_ranks(gate_up_parts, 2, hi_count).astype(f32)
    gain_terms = gain_near + gain_far
    gain_terms = gain_terms.at[3].multiply(1.0 - cross_gate**2)
    gain_terms = [plan.place_lanes(row) for row in gain_terms]
    (
        text_moved,
        down_parts,
        text_kept,
        qkv_parts,
        result_arrived,
        result_near,
        grad_scale_attn,
        grad_attn_gain,
        gate_up_weight_grad,
        gain_terms,
    ) = fence(
        text_moved,
        down_parts,
        text_kept,
        qkv_parts,
        result_arrived,
        result_near,
        grad_scale_attn,
        grad_attn_gain,
        gate_up_weight_grad,
        gain_terms,
    )

    text_grad = plan.text_by_rep(plan.total(text_kept, text_moved))
    text_grad, result_near, result_arrived, qkv_parts = fence(
        text_grad, result_near, result_arrived, qkv_parts
    )
    text_parts = plan.reduce(text_grad)
    if plan.aligned:
        out_parts = qkv_parts[RANKS * rows :].reshape(-1, D)
        qkv_parts = qkv_parts[: RANKS * rows]
    else:
        out_parts = lax.psum_scatter(out_grad, AXES, scatter_dimension=0, tiled=True)
    result = (settle(result_near) + result_arrived.astype(f32)).reshape(item_count, item_len, D)
    grad_mlp_gate = jnp.sum(grad_top * result, axis=1) * (1.0 - jnp.tanh(gate_mlp) ** 2)
    layer_out = (middle + mlp_gate * result).astype(bf16).reshape(row_count, D)
    tokens_grad = (grad_middle + grad_token_norm).reshape(row_count, D)

    def whole(parts, weight, sections, groups):
        blocks = trade_ranks(parts.reshape(RANKS, weight.shape[0], -1))
        return plan.from_ranks(blocks, sections, groups).astype(f32)

    qkv_blocks = trade_ranks(qkv_parts.reshape(RANKS, rows, -1))
    qkv_blocks, grad_mlp_gate = fence(qkv_blocks, grad_mlp_gate)
    qkv_weight_grad = plan.from_ranks(qkv_blocks, 3, plan.head_groups).astype(f32)

    grad_modulation = jnp.concatenate(
        [grad_scale_attn, grad_attn_gate, grad_scale_mlp, grad_mlp_gate], axis=1
    ).astype(bf16)
    gains_grad = jnp.stack(
        [grad_attn_gain, gain_terms[0], gain_terms[1], gain_terms[2], grad_mlp_gain, gain_terms[3]]
    ).astype(bf16)
    gain_blocks = jnp.moveaxis(gains_grad.reshape(6, devices, -1), 1, 0)
    gain_blocks = gain_blocks.reshape(devices, item_count, -1)
    modulations = jnp.broadcast_to(grad_modulation, (devices,) + grad_modulation.shape)
    both = lax.all_to_all(
        jnp.concatenate([modulations, gain_blocks], axis=2), AXES, 0, 0, tiled=True
    )
    both, layer_out, tokens_grad = fence(both, layer_out, tokens_grad)
    ada_weight_grad = lax.dot_general(
        activated_mine.reshape(devices, item_count, rows),
        both[:, :, : 4 * D],
        (((0, 1), (0, 1)), ((), ())),
        preferred_element_type=f32,
    )
    norm_gains_grad = jnp.sum(both[:, :, 4 * D :].astype(f32), axis=0).reshape(6, -1)
    both, text_parts = fence(both, text_parts)
    text_weight_grad = whole(text_parts, text_weight, 2, plan.head_groups)
    down_weight_grad, out_weight_grad = down_parts.astype(f32), out_parts.astype(f32)
    return (
        layer_out,
        tokens_grad,
        norm_gains_grad,
        ada_weight_grad,
        qkv_weight_grad,
        out_weight_grad,
        text_weight_grad,
        gate_up_weight_grad,
        down_weight_grad,
    )


def solution(mesh):
    grp, rep = mesh.devices.shape
    hi = grp // RANKS
    inner = Mesh(mesh.devices.reshape(hi, 2, 2, rep), AXES)
    rows = P(AXES, None)

    def step(*arrays):
        return local(hi, rep, *arrays)

    return jax.shard_map(
        step,
        mesh=inner,
        in_specs=(
            rows,
            rows,
            P(AXES, None, None),
            P(AXES),
            P(AXES),
            rows,
            P(None, AXES),
            rows,
            rows,
            rows,
            rows,
            rows,
            rows,
        ),
        out_specs=(rows, rows, P(None, AXES), rows, rows, rows, rows, rows, rows),
        check_vma=False,
    )
```
